32 devices in a mesh: groups: 2 (over y), orb: 4 (over z), fit: 2 (over x), sub: 2 (over core).
Axes of the slice: x: 2, y: 2, z: 4, core: 2. Of those that a mesh axis runs over, the one named last changes fastest.
Arguments:
- blocks: float32 [16, 256, 2048], P(('groups', 'orb'), None, 'fit'), parts along dimension 0, may hold values from -4 to 4
- pno_coefficients: float32 [32, 64, 256], P(('groups', 'orb', 'sub')), parts along dimension 0, may hold values from -0.375 to 0.375
- domain_map: int32 [32, 256], P(('groups', 'orb', 'sub')), parts along dimension 0, may hold values from -1 to 255, as said below
- pair_first: int32 [32], P('groups'), parts along dimension 0, may hold values from 0 to 7, as said below
- pair_second: int32 [32], P('groups'), parts along dimension 0, may hold values from 0 to 7, as said below
- pno_ranks: int32 [32], P('groups'), parts along dimension 0, may hold values from 8 to 64
- neighbours: int32 [32, 4], P('groups'), parts along dimension 0, may hold values from 0 to 15, as said below
- couplings: float32 [32, 4], P(('groups', 'orb', 'sub')), parts along dimension 0, may hold values from -0.3 to 0.3
- intersections: float32 [32, 4, 4096], P(('groups', 'orb', 'sub')), parts along dimension 0, may hold values from -0.75 to 0.75
- pno_energy: float32 [32, 64], P(('groups', 'orb', 'sub')), parts along dimension 0, may hold values from 0.3 to 3
- occ_energy: float32 [16], P('groups'), parts along dimension 0, may hold values from -1.2 to -0.3
Outputs:
- amplitudes: float32 [32, 4096], P(('groups', 'orb', 'sub')), parts along dimension 0
- gradient: float32 [16, 256, 2048], P(('groups', 'orb'), 'sub', 'fit'), parts along dimension 0
The draws below stay inside these ranges and needn't reach their ends.
There are 2 independent parts, one for each index of `groups`. The reference program is written for one: setup_inputs(seed, part) draws one part's arguments, and reference() takes and returns one part's arrays. A program takes and returns all parts, laid end to end along the dimension named above; each array names one. Nothing has to cross between parts.
Inputs may be any that keep to these rules, and one draw needn't show every extreme that they name: `pair_first`: pair p belongs to orbital owner p // 4; its first orbital is one of that owner's 2 orbitals, o * 2 to (o + 1) * 2 - 1. `pair_second`: not below the pair's first orbital; among the owner's own orbitals or those of owner o + 1; for the last owner among its own. `neighbours`: device d holds pairs d * 2 to (d + 1) * 2 - 1. The neighbour pairs of one device's pairs lie on other devices, at most 2 of them on any one device. `domain_map`: in each row the entries other than -1 are distinct.
All inputs are finite; a program needn't handle non-finite values.
Results may differ from the reference program's by a relative error of at most 0.0003.
Values sent between devices are 32-bit elements; how exact they have to be, the bound alone decides.
No kernel may reach another device: no remote copies, remote signals or barrier semaphores. Data moves between devices by JAX's collectives and lax.ppermute only.
A program may use at most 64 MiB of HBM per device.

```python
import math
import jax
import jax.numpy as jnp
from jax import lax

NPAO = 256
NFIT = 2048
NPNO = 64
ORB_DEV = 2
PAIR_DEV = 2
NNB = 4
ITERS = 2
NOCC = 8
OWN_PAIRS = 4
NPAIR = 16


def pair_lists(key):
    first_key, second_key, third_key, fourth_key = jax.random.split(key, 4)
    pair_ids = jnp.arange(NPAIR, dtype=jnp.int32)
    owner_index = pair_ids // OWN_PAIRS
    last_owner = NOCC // ORB_DEV - 1
    first_orbital = owner_index * ORB_DEV + jax.random.randint(first_key, (NPAIR,), 0, ORB_DEV)
    upper_flag = (jax.random.randint(second_key, (NPAIR,), 0, 2) == 1) & (owner_index < last_owner)
    upper_orbital = (owner_index + 1) * ORB_DEV + jax.random.randint(third_key, (NPAIR,), 0, ORB_DEV)
    span_size = (owner_index + 1) * ORB_DEV - first_orbital
    own_orbital = first_orbital + jax.random.randint(fourth_key, (NPAIR,), 0, span_size)
    second_orbital = jnp.where(upper_flag, upper_orbital, own_orbital)
    return (first_orbital.astype(jnp.int32), second_orbital.astype(jnp.int32))


def draw_pair_first(key, part):
    return pair_lists(key)[0]


def draw_pair_second(key, part):
    return pair_lists(key)[1]


def draw_neighbours(key, part):
    key = jax.random.fold_in(key, 5)
    device_total = NPAIR // PAIR_DEV
    request_total = PAIR_DEV * NNB
    request_ids = jnp.arange(request_total, dtype=jnp.int32)

    def draw_device(device_id, device_key):
        order_key, slot_key = jax.random.split(device_key)
        offsets = 1 + jax.random.permutation(order_key, device_total - 1)
        source_device = (device_id + offsets[request_ids % (device_total - 1)]) % device_total
        slot_index = jax.random.randint(slot_key, (request_total,), 0, PAIR_DEV)
        return source_device * PAIR_DEV + slot_index
    key_list = jax.random.split(key, device_total)
    chosen = jax.vmap(draw_device)(jnp.arange(device_total, dtype=jnp.int32), key_list)
    return chosen.reshape(NPAIR, NNB).astype(jnp.int32)


def draw_domain_map(key, part):
    key = jax.random.fold_in(key, 7)
    order_key, keep_key = jax.random.split(key)
    key_list = jax.random.split(order_key, NPAIR)
    permuted = jax.vmap(lambda single_key: jax.random.permutation(single_key, NPAO))(key_list)
    keep_flag = jax.random.randint(keep_key, (NPAIR, NPAO), 0, 3) > 0
    return jnp.where(keep_flag, permuted, -1).astype(jnp.int32)


def with_ends(array, rng, smallest, top_value):
    extent = array.shape
    spot = [jax.random.randint(jax.random.fold_in(rng, axis), (), 0, extent[axis]) for axis in range(len(extent))]
    array = array.at[tuple(spot)].set(smallest)
    longest = extent.index(max(extent))
    spot[longest] = (spot[longest] + 1) % extent[longest]
    return array.at[tuple(spot)].set(top_value)


def block_levels(rng, shape, cuts, low, top_value):
    gain = 1.0
    for position, shards_of in cuts:
        draws = jax.random.uniform(jax.random.fold_in(jax.random.fold_in(rng, 6), position), (shards_of,), jnp.float32, low / len(cuts), top_value / len(cuts))
        gain = gain * jnp.repeat(jnp.exp(draws), shape[position] // shards_of).reshape((-1,) + (1,) * (len(shape) - 1 - position))
    return gain


def centred(rng, extent, scale, bound, cuts=(), kind=jnp.bfloat16):
    values = jax.random.normal(rng, extent, jnp.float32) * scale
    if len(cuts) > 0:
        values = block_levels(rng, extent, cuts, -0.22, 0.18) * values
    return jnp.clip(values, min=-bound, max=bound).astype(kind)


def setup_inputs(seed: int = 0, part: int = 0) -> dict:
    streams_of = jax.random.split(jax.random.key(seed), 12)
    part_keys = jax.random.split(jax.random.fold_in(streams_of[11], part), 12)
    blocks = centred(part_keys[0], (NOCC, NPAO, NFIT), 0.25, 4.0, ((0, 4), (2, 2)), jnp.float32)
    pno_coefficients = centred(part_keys[1], (NPAIR, NPNO, NPAO), NPAO ** -0.5, 0.375, ((0, 8),), jnp.float32)
    domain_map = draw_domain_map(jax.random.fold_in(jax.random.fold_in(streams_of[11], part), 71), part)
    pair_first = draw_pair_first(jax.random.fold_in(jax.random.fold_in(streams_of[11], part), 71), part)
    pair_second = draw_pair_second(jax.random.fold_in(jax.random.fold_in(streams_of[11], part), 71), part)
    pno_ranks = with_ends(jax.random.randint(part_keys[5], (NPAIR,), max(NPNO // 8, 1), NPNO + 1), jax.random.fold_in(part_keys[5], 1), max(NPNO // 8, 1), NPNO).astype(jnp.int32)
    neighbours = draw_neighbours(jax.random.fold_in(jax.random.fold_in(streams_of[11], part), 71), part)
    couplings = jnp.clip(jax.random.uniform(part_keys[7], (NPAIR, NNB), jnp.float32, -0.3, 0.3) * block_levels(part_keys[7], (NPAIR, NNB), ((0, 8),), -0.4, 0.0), -0.3, 0.3)
    intersections = centred(part_keys[8], (NPAIR, NNB, NPNO * NPNO), NPNO ** -0.5, 0.75, ((0, 8),), jnp.float32)
    pno_energy = jnp.clip(jnp.exp(math.log(3.0) - 2.3025851 * jax.random.uniform(part_keys[9], (NPAIR, NPNO), jnp.float32) ** block_levels(part_keys[9], (NPAIR, NPNO), ((0, 8),), -0.2, 0.2)), 0.3, 3.0)
    occ_energy = jnp.clip(jax.random.uniform(part_keys[10], (NOCC,), jnp.float32, -1.2, -0.3), -1.2, -0.3)
    return {"blocks": blocks, "pno_coefficients": pno_coefficients, "domain_map": domain_map, "pair_first": pair_first, "pair_second": pair_second, "pno_ranks": pno_ranks, "neighbours": neighbours, "couplings": couplings, "intersections": intersections, "pno_energy": pno_energy, "occ_energy": occ_energy}


highest = lax.Precision.HIGHEST


def reference(blocks, pno_coefficients, domain_map, pair_first, pair_second, pno_ranks, neighbours, couplings, intersections, pno_energy, occ_energy):
    columns = jnp.arange(NPAO, dtype=jnp.int32)

    def factors(pair_index):
        coefficients = pno_coefficients[pair_index]
        select = (domain_map[pair_index][:, None] == columns[None, :]).astype(jnp.float32)
        mapped = jnp.dot(coefficients, select, precision=highest)
        left_factor = jnp.dot(coefficients, blocks[pair_first[pair_index]], precision=highest)
        right_factor = jnp.dot(mapped, blocks[pair_second[pair_index]], precision=highest)
        return coefficients, mapped, left_factor, right_factor

    def project(pair_index):
        coefficients, mapped, left_factor, right_factor = factors(pair_index)
        return jnp.dot(left_factor, right_factor.T, precision=highest)

    integrals = lax.map(project, jnp.arange(NPAIR, dtype=jnp.int32))
    levels = jnp.arange(NPNO, dtype=jnp.int32)
    kept_levels = (levels[None, :] < pno_ranks[:, None]).astype(jnp.float32)
    pair_mask = kept_levels[:, :, None] * kept_levels[:, None, :]
    integrals = integrals * pair_mask
    denominator = (pno_energy[:, :, None] + pno_energy[:, None, :]
                   - occ_energy[pair_first][:, None, None] - occ_energy[pair_second][:, None, None])
    amplitudes = -integrals / denominator
    intersection = intersections.reshape(NPAIR, NNB, NPNO, NPNO)
    for sweep_index in range(ITERS):
        partner_amps = amplitudes[neighbours]
        inner_left = jnp.einsum('pkab,pkbc->pkac', intersection, partner_amps, precision=highest)
        sandwich = jnp.einsum('pkac,pkdc->pkad', inner_left, intersection, precision=highest)
        coupled = jnp.einsum('pk,pkad->pad', couplings, sandwich, precision=highest)
        amplitudes = pair_mask * (coupled - integrals) / denominator
    weights = pair_mask * (2.0 * amplitudes - jnp.swapaxes(amplitudes, 1, 2))

    def accumulate(pair_index, running):
        coefficients, mapped, left_factor, right_factor = factors(pair_index)
        weight = weights[pair_index]
        first_term = jnp.dot(coefficients.T, jnp.dot(weight, right_factor, precision=highest), precision=highest)
        second_term = jnp.dot(mapped.T, jnp.dot(weight.T, left_factor, precision=highest), precision=highest)
        running = running.at[pair_first[pair_index]].add(first_term)
        running = running.at[pair_second[pair_index]].add(second_term)
        return running

    gradient = lax.fori_loop(0, NPAIR, accumulate, jnp.zeros((NOCC, NPAO, NFIT), jnp.float32))
    return amplitudes.reshape(NPAIR, NPNO * NPNO), gradient
```

```python
import functools

import jax
import jax.numpy as jnp
from jax import lax
from jax.experimental import pallas as pl
from jax.experimental.pallas import tpu as pltpu
from jax.sharding import PartitionSpec as P

ITERS = 2
SMALL = 4
MIB = 1 << 20
EXTRA = 8

high = lax.Precision.HIGH
smem = pl.BlockSpec(memory_space=pltpu.SMEM)
vmem = pl.BlockSpec(memory_space=pltpu.VMEM)


def mm(a, b, contract=((1,), (0,))):
    return lax.dot_general(
        a, b, (contract, ((), ())), precision=high, preferred_element_type=jnp.float32
    )


def shifted(value, axis, steps):
    count = lax.axis_size(axis)
    initial, last = (max(0, -steps), min(count, count - steps))
    return lax.ppermute(value, axis, [(source, source + steps) for source in range(initial, last)])


def swapped(value, axis):
    return lax.ppermute(value, axis, [(0, 1), (1, 0)])


def owners_of(value):
    count = lax.axis_size("orb")
    if count > SMALL or count & (count - 1):
        return [lax.all_gather(value, "orb", axis=0, tiled=False)]
    return [value[None]] + [
        lax.ppermute(value, "orb", [(s, s ^ step) for s in range(count)])[None]
        for step in range(1, count)
    ]


def f32(flag):
    return flag.astype(jnp.float32)


class Sizes:
    def __init__(self, blocks, pno_coefficients, couplings):
        self.orbitals, self.paos, self.fits = blocks.shape
        self.pairs, self.pnos = pno_coefficients.shape[:2]
        self.links = couplings.shape[1]
        self.subs = lax.axis_size("sub")
        self.owners = lax.axis_size("orb")
        self.own = self.pairs * self.subs
        self.total = self.own * self.owners


def call(kernel, outs, ins, args, scratch=(), limit=16):
    return pl.pallas_call(
        kernel,
        out_shape=[jax.ShapeDtypeStruct(shape, jnp.float32) for shape in outs],
        in_specs=ins,
        out_specs=[vmem] * len(outs),
        scratch_shapes=list(scratch),
        compiler_params=pltpu.CompilerParams(vmem_limit_bytes=limit * MIB),
    )(*args)


def left_kernel(z, first, c_ref, map_ref, b_ref, lm_ref):
    owner, sub = lax.axis_index("orb"), lax.axis_index("sub")
    start = owner * z.own + sub * z.pairs
    rows = lax.broadcasted_iota(jnp.int32, (z.paos, z.paos), 0)
    for p in range(z.pairs):
        c = c_ref[p]
        select = f32(map_ref[p : p + 1, :] == rows)
        lm_ref[p, :, z.fits :] = mm(c, select, ((1,), (1,)))
        lm_ref[p, :, : z.fits] = mm(c, b_ref[first[start + p] - owner * z.orbitals])


def here_kernel(z, second, lm_ref, other_ref, b_ref, right_ref, sums_ref):
    owner, sub = lax.axis_index("orb"), lax.axis_index("sub")
    for side, ref in enumerate((lm_ref, other_ref)):
        start = owner * z.own + (sub if side == 0 else 1 - sub) * z.pairs
        for p in range(z.pairs):
            j = second[start + p] - owner * z.orbitals
            local = jnp.where(j < z.orbitals, 1.0, 0.0)
            mapped = ref[p, :, z.fits :] * local
            right = mm(mapped, b_ref[jnp.minimum(j, z.orbitals - 1)])
            right_ref[side * z.pairs + p] = right
            if side == 0:
                sums_ref[:, p * z.pnos : (p + 1) * z.pnos] = mm(
                    ref[p, :, : z.fits], right, ((1,), (1,))
                )


def below_kernel(z, second, below_ref, sums_ref, b_ref, right_ref, both_ref):
    owner, sub = lax.axis_index("orb"), lax.axis_index("sub")
    start = jnp.maximum(owner - 1, 0) * z.own + sub * z.pairs
    both_ref[0] = sums_ref[...]
    for p in range(z.pairs):
        j = second[start + p] - owner * z.orbitals
        held = jnp.where(j >= 0, 1.0, 0.0)
        mapped = below_ref[p, :, z.fits :] * held
        right = mm(mapped, b_ref[jnp.clip(j, 0, z.orbitals - 1)])
        right_ref[p] = right
        both_ref[1, :, p * z.pnos : (p + 1) * z.pnos] = mm(
            below_ref[p, :, : z.fits], right, ((1,), (1,))
        )


def final_kernel(z, part_count, *refs):
    (first, second, ranks, near, occupied, c_ref, c_other, lm_ref, lm_other, below_ref,
     below_other, here_ref, down_ref, down_other) = refs[:14]
    refs = refs[14:]
    packs, packs_other = refs[:part_count], refs[part_count : 2 * part_count]
    refs = refs[2 * part_count :]
    sums, sums_other = refs[:part_count], refs[part_count : 2 * part_count]
    amp_ref, grad_ref, s_ref, energy, total, start_amp, next_amp, inverse, diag, rows_ref = refs[
        2 * part_count :
    ]
    owner, sub = lax.axis_index("orb"), lax.axis_index("sub")
    n = z.pnos
    diag[...] = jnp.zeros_like(diag)

    def every_owner(action):
        for step in range(part_count):
            if part_count == 1 and z.owners > 1:
                @pl.loop(0, z.owners)
                def _(index):
                    action(step, index, index)
            else:
                action(step, 0, owner ^ step)

    def collect_pack(step, slot, who):
        for side, ref in ((sub, packs[step]), (1 - sub, packs_other[step])):
            for p in range(z.pairs):
                pair = who * z.own + side * z.pairs + p
                s_ref[pair] = ref[slot, p, :n, :]
                energy[pair] = ref[slot, p, n:, :]

    def collect_own(step, slot, who):
        for side, ref in ((sub, sums[step]), (1 - sub, sums_other[step])):
            for p in range(z.pairs):
                pair = who * z.own + side * z.pairs + p
                total[pair] = ref[slot, 0, :, p * n : (p + 1) * n]

    def collect_below(step, slot, who):
        @pl.when(who > 0)
        def _():
            for side, ref in ((sub, sums[step]), (1 - sub, sums_other[step])):
                for p in range(z.pairs):
                    pair = (who - 1) * z.own + side * z.pairs + p
                    total[pair] = total[pair] + ref[slot, 1, :, p * n : (p + 1) * n]

    every_owner(collect_pack)
    every_owner(collect_own)
    every_owner(collect_below)

    row_ids = lax.broadcasted_iota(jnp.int32, (n, n), 0)
    column_ids = lax.broadcasted_iota(jnp.int32, (n, n), 1)
    unroll = 4 if z.owners <= SMALL else 1

    def prepare(pair):
        level = energy[pair, 0:1, :n] * jnp.ones((n, 1), jnp.float32)
        shift = occupied[first[pair]] + occupied[second[pair]]
        rank = ranks[pair]
        kept = f32((row_ids < rank) & (column_ids < rank))
        scale = kept / (level + level.T - shift)
        inverse[pair] = scale
        start_amp[pair] = -total[pair] * scale

    def updated(pair, source, slot):
        for k in range(z.links):
            diag[slot, k * n : (k + 1) * n, k * n : (k + 1) * n] = source[near[pair, k]]
        s = s_ref[pair]
        inner = mm(s, diag[slot]) * energy[pair, 1:2, :]
        coupled = mm(inner, s, ((1,), (1,)))
        return (coupled - total[pair]) * inverse[pair]

    def over_pairs(action):
        if z.owners <= SMALL:
            for pair in range(z.total):
                action(pair, pair % 4)
        else:
            @pl.loop(0, z.total)
            def _(pair):
                action(pair, 0)

    over_pairs(lambda pair, slot: prepare(pair))

    def sweep(pair, slot):
        next_amp[pair] = updated(pair, start_amp, slot)

    over_pairs(sweep)

    half = z.paos // z.subs
    lanes = pl.ds(pl.multiple_of(sub * half, half), half)
    mapped_lanes = pl.ds(pl.multiple_of(z.fits + sub * half, half), half)
    orbital_base = owner * z.orbitals

    def place(index, value, orbital):
        for o in range(z.orbitals):
            rows_ref[index * n : (index + 1) * n, o * half : (o + 1) * half] = jnp.where(
                orbital == o, value, 0.0
            )

    def weights_of(pair, slot):
        amps = updated(pair, next_amp, slot)
        return amps, 2.0 * amps - amps.T

    slot = 0
    for side in range(z.subs):
        for p in range(z.pairs):
            index = side * z.pairs + p
            which = (sub if side == 0 else 1 - sub) * z.pairs + p
            pair = owner * z.own + which
            amps, weights = weights_of(pair, slot % 4)
            slot += 1
            if side == 0:
                amp_ref[p] = amps
            c = (c_ref if side == 0 else c_other)[p, :, lanes]
            mapped = (lm_ref if side == 0 else lm_other)[p, :, mapped_lanes]
            place(index, mm(weights.T, c), first[pair] - orbital_base)
            place(z.own + index, mm(weights, mapped), second[pair] - orbital_base)
            pair = jnp.maximum(owner - 1, 0) * z.own + which
            amps, weights = weights_of(pair, slot % 4)
            slot += 1
            mapped = (below_ref if side == 0 else below_other)[p, :, mapped_lanes]
            place(2 * z.own + index, mm(weights, mapped), second[pair] - orbital_base)

    width = z.own * n

    def factor(own, other, columns):
        return jnp.concatenate([own[:, :, columns], other[:, :, columns]]).reshape(width, -1)

    step = 256
    for start in range(0, z.fits, step):
        columns = slice(start, start + step)
        right = here_ref[:, :, columns].reshape(width, -1) + factor(down_ref, down_other, columns)
        value = mm(rows_ref[:width], right, ((0,), (0,)))
        value += mm(rows_ref[width : 2 * width], factor(lm_ref, lm_other, columns), ((0,), (0,)))
        value += mm(
            rows_ref[2 * width :], factor(below_ref, below_other, columns), ((0,), (0,))
        )
        grad_ref[:, :, columns] = value.reshape(z.orbitals, half, step)


def body(
    blocks,
    pno_coefficients,
    domain_map,
    pair_first,
    pair_second,
    pno_ranks,
    neighbours,
    couplings,
    intersections,
    pno_energy,
    occ_energy,
):
    z = Sizes(blocks, pno_coefficients, couplings)
    n, wide = z.pnos, z.fits + z.paos

    (lm,) = call(
        functools.partial(left_kernel, z),
        [(z.pairs, n, wide)],
        [smem, vmem, vmem, vmem],
        (pair_first, pno_coefficients, domain_map, blocks),
    )
    below = shifted(lm, "orb", 1)
    lm_other = swapped(lm, "sub")
    c_other = swapped(pno_coefficients, "sub")

    later = lax.optimization_barrier((intersections, pno_energy, couplings, lm))
    intersection, energy, coupling, lm = later
    pack = jnp.concatenate(
        [
            intersection.reshape(z.pairs, z.links, n, n)
            .transpose(0, 2, 1, 3)
            .reshape(z.pairs, n, z.links * n),
            jnp.pad(energy, ((0, 0), (0, (z.links - 1) * n)))[:, None, :],
            jnp.repeat(coupling, n, axis=1)[:, None, :],
            jnp.zeros((z.pairs, EXTRA - 2, z.links * n), jnp.float32),
        ],
        axis=1,
    )
    packs = owners_of(pack)
    packs_other = [swapped(part, "sub") for part in packs]

    right_here, sums = call(
        functools.partial(here_kernel, z),
        [(z.own, n, z.fits), (n, z.pairs * n)],
        [smem, vmem, vmem, vmem],
        (pair_second, lm, lm_other, blocks),
    )
    right_below, both = call(
        functools.partial(below_kernel, z),
        [(z.pairs, n, z.fits), (2, n, z.pairs * n)],
        [smem, vmem, vmem, vmem],
        (pair_second, below, sums, blocks),
    )
    if lax.axis_size("fit") == 2:
        both = both + swapped(both, "fit")
    else:
        both = lax.psum(both, "fit")
    parts = owners_of(both)
    parts_other = [swapped(part, "sub") for part in parts]
    down = shifted(right_below, "orb", -1)
    down_other = swapped(down, "sub")
    below_other = swapped(below, "sub")

    args = (
        pair_first, pair_second, pno_ranks, neighbours, occ_energy,
        pno_coefficients, c_other, lm, lm_other, below, below_other,
        right_here, down, down_other, *packs, *packs_other, *parts, *parts_other,
    )
    square = (z.total, n, n)
    amplitudes, gradient = call(
        functools.partial(final_kernel, z, len(packs)),
        [(z.pairs, n, n), (z.orbitals, z.paos // z.subs, z.fits)],
        [smem] * 5 + [vmem] * (len(args) - 5),
        args,
        [
            pltpu.VMEM((z.total, n, z.links * n), jnp.float32),
            pltpu.VMEM((z.total, EXTRA, z.links * n), jnp.float32),
            pltpu.VMEM(square, jnp.float32),
            pltpu.VMEM(square, jnp.float32),
            pltpu.VMEM(square, jnp.float32),
            pltpu.VMEM(square, jnp.float32),
            pltpu.VMEM((4, z.links * n, z.links * n), jnp.float32),
            pltpu.VMEM((3 * z.own * n, z.orbitals * (z.paos // z.subs)), jnp.float32),
        ],
        limit=48,
    )
    return (amplitudes.reshape(z.pairs, -1), gradient)


def solution(mesh):
    in_specs = (
        P(("groups", "orb"), None, "fit"),
        P(("groups", "orb", "sub"), None, None),
        P(("groups", "orb", "sub"), None),
        P("groups"),
        P("groups"),
        P("groups"),
        P("groups", None),
        P(("groups", "orb", "sub"), None),
        P(("groups", "orb", "sub"), None, None),
        P(("groups", "orb", "sub"), None),
        P("groups"),
    )
    out_specs = (P(("groups", "orb", "sub"), None), P(("groups", "orb"), "sub", "fit"))
    return jax.shard_map(body, mesh=mesh, in_specs=in_specs, out_specs=out_specs, check_vma=False)
```

```python
import functools

import jax
import jax.numpy as jnp
from jax import lax
from jax.experimental import pallas as pl
from jax.experimental.pallas import tpu as pltpu
from jax.sharding import PartitionSpec as P

ITERS = 2
SMALL = 4
MIB = 1 << 20
EXTRA = 8

high = lax.Precision.HIGH
smem = pl.BlockSpec(memory_space=pltpu.SMEM)
vmem = pl.BlockSpec(memory_space=pltpu.VMEM)


def mm(a, b, contract=((1,), (0,))):
    return lax.dot_general(
        a, b, (contract, ((), ())), precision=high, preferred_element_type=jnp.float32
    )


def shifted(value, axis, steps):
    count = lax.axis_size(axis)
    initial, last = (max(0, -steps), min(count, count - steps))
    return lax.ppermute(value, axis, [(source, source + steps) for source in range(initial, last)])


def swapped(value, axis):
    return lax.ppermute(value, axis, [(0, 1), (1, 0)])


def owners_of(value):
    count = lax.axis_size("orb")
    if count > SMALL or count & (count - 1):
        return [lax.all_gather(value, "orb", axis=0, tiled=False)]
    return [value[None]] + [
        lax.ppermute(value, "orb", [(s, s ^ step) for s in range(count)])[None]
        for step in range(1, count)
    ]


def f32(flag):
    return flag.astype(jnp.float32)


class Sizes:
    def __init__(self, blocks, pno_coefficients, couplings):
        self.orbitals, self.paos, self.fits = blocks.shape
        self.pairs, self.pnos = pno_coefficients.shape[:2]
        self.links = couplings.shape[1]
        self.subs = lax.axis_size("sub")
        self.owners = lax.axis_size("orb")
        self.own = self.pairs * self.subs
        self.total = self.own * self.owners


anywhere = pl.BlockSpec(memory_space=pl.ANY)
held_out = pl.BlockSpec(memory_space=pltpu.HBM)


def call(kernel, outs, ins, args, scratch=(), limit=16, out_specs=None):
    return pl.pallas_call(
        kernel,
        out_shape=[jax.ShapeDtypeStruct(shape, jnp.float32) for shape in outs],
        in_specs=ins,
        out_specs=out_specs or [vmem] * len(outs),
        scratch_shapes=list(scratch),
        compiler_params=pltpu.CompilerParams(vmem_limit_bytes=limit * MIB),
    )(*args)


def started(sources, targets, sems, base=0):
    copies = [
        pltpu.make_async_copy(source, target, sems.at[base + index])
        for index, (source, target) in enumerate(zip(sources, targets))
    ]
    for copy in copies:
        copy.start()
    return copies


def wait(copies):
    for copy in copies:
        copy.wait()


def side_start(z, owner, sub, side):
    return owner * z.own + (sub if side == 0 else 1 - sub) * z.pairs


def scale_of(z, pair, level, first, second, ranks, occupied):
    n = z.pnos
    row_ids = lax.broadcasted_iota(jnp.int32, (n, n), 0)
    column_ids = lax.broadcasted_iota(jnp.int32, (n, n), 1)
    level = level * jnp.ones((n, 1), jnp.float32)
    rank = ranks[pair]
    kept = f32((row_ids < rank) & (column_ids < rank))
    return kept / (level + level.T - (occupied[first[pair]] + occupied[second[pair]]))


def coupled_of(z, pair, source, near, s, coupling, diag, slot):
    n = z.pnos
    for k in range(z.links):
        diag[slot, k * n : (k + 1) * n, k * n : (k + 1) * n] = source[near[pair, k]]
    inner = mm(s, diag[slot]) * coupling
    return mm(inner, s, ((1,), (1,)))


def each_owner(z, parts, owner, action):
    if len(parts) == 1 and z.owners > 1:
        @pl.loop(0, z.owners)
        def _(index):
            action(0, index, index)
    else:
        for step in range(len(parts)):
            action(step, 0, owner ^ step)


def left_kernel(z, first_in, c_in, map_in, e_in, b_in, lm_ref, e_ref, first, c_ref, map_ref, b_ref,
                sems):
    owner, sub = lax.axis_index("orb"), lax.axis_index("sub")
    copies = started([first_in, c_in, map_in, e_in], [first, c_ref, map_ref, e_ref], sems)
    blocks = started(
        [b_in.at[o] for o in range(z.orbitals)], [b_ref.at[o] for o in range(z.orbitals)], sems, 4
    )
    wait(copies)
    start = side_start(z, owner, sub, 0)
    rows = lax.broadcasted_iota(jnp.int32, (z.paos, z.paos), 0)
    for p in range(z.pairs):
        select = f32(map_ref[p : p + 1, :] == rows)
        lm_ref[p, :, z.fits :] = mm(c_ref[p], select, ((1,), (1,)))
    wait(blocks)
    for p in range(z.pairs):
        lm_ref[p, :, : z.fits] = mm(c_ref[p], b_ref[first[start + p] - owner * z.orbitals])


def here_kernel(z, second, lm_ref, other_ref, b_ref, right_ref, sums_ref):
    owner, sub = lax.axis_index("orb"), lax.axis_index("sub")
    for side, ref in enumerate((lm_ref, other_ref)):
        start = side_start(z, owner, sub, side)
        for p in range(z.pairs):
            j = second[start + p] - owner * z.orbitals
            local = jnp.where(j < z.orbitals, 1.0, 0.0)
            mapped = ref[p, :, z.fits :] * local
            right = mm(mapped, b_ref[jnp.minimum(j, z.orbitals - 1)])
            right_ref[side * z.pairs + p] = right
            if side == 0:
                sums_ref[:, p * z.pnos : (p + 1) * z.pnos] = mm(
                    ref[p, :, : z.fits], right, ((1,), (1,))
                )


def below_kernel(z, first, second, ranks, occupied, e_ref, e_below, below_ref, sums_ref, b_ref,
                 right_ref, both_ref):
    owner, sub = lax.axis_index("orb"), lax.axis_index("sub")
    own_start = side_start(z, owner, sub, 0)
    start = side_start(z, jnp.maximum(owner - 1, 0), sub, 0)
    n = z.pnos
    for p in range(z.pairs):
        lanes = slice(p * n, (p + 1) * n)
        scale = scale_of(z, own_start + p, e_ref[p : p + 1, :], first, second, ranks, occupied)
        both_ref[0, :, lanes] = -sums_ref[:, lanes] * scale
        j = second[start + p] - owner * z.orbitals
        held = jnp.where(j >= 0, 1.0, 0.0)
        mapped = below_ref[p, :, z.fits :] * held
        right = mm(mapped, b_ref[jnp.clip(j, 0, z.orbitals - 1)])
        right_ref[p] = right
        part = mm(below_ref[p, :, : z.fits], right, ((1,), (1,)))
        scale = scale_of(z, start + p, e_below[p : p + 1, :], first, second, ranks, occupied)
        both_ref[1, :, lanes] = -part * scale


def sweep_kernel(z, part_count, first, second, ranks, near, occupied, pack, pack_other, *refs):
    parts, others = refs[:part_count], refs[part_count : 2 * part_count]
    own_ref, start_ref, amps, diag = refs[2 * part_count :]
    owner, sub = lax.axis_index("orb"), lax.axis_index("sub")
    n = z.pnos
    diag[...] = jnp.zeros_like(diag)

    def collect(step, slot, who):
        for side, ref in ((0, parts[step]), (1, others[step])):
            start = side_start(z, who, sub, side)
            for p in range(z.pairs):
                amps[start + p] = ref[slot, 0, :, p * n : (p + 1) * n]

    def collect_above(step, slot, who):
        @pl.when(who > 0)
        def _():
            for side, ref in ((0, parts[step]), (1, others[step])):
                start = side_start(z, who - 1, sub, side)
                for p in range(z.pairs):
                    amps[start + p] = amps[start + p] + ref[slot, 1, :, p * n : (p + 1) * n]

    each_owner(z, parts, owner, collect)
    each_owner(z, parts, owner, collect_above)
    for side, ref in enumerate((pack, pack_other)):
        start = side_start(z, owner, sub, side)
        start_below = side_start(z, jnp.maximum(owner - 1, 0), sub, side)
        for p in range(z.pairs):
            pair, index = start + p, side * z.pairs + p
            begin = amps[pair]
            start_ref[index] = begin
            start_ref[z.own + index] = amps[start_below + p]
            scale = scale_of(z, pair, ref[p, n : n + 1, :n], first, second, ranks, occupied)
            coupled = coupled_of(
                z, pair, amps, near, ref[p, :n, :], ref[p, n + 1 : n + 2, :], diag, index
            )
            own_ref[sub if side == 0 else 1 - sub, :, p * n : (p + 1) * n] = begin + coupled * scale


def final_kernel(z, part_count, first, second, ranks, near, occupied, *refs):
    (c_in, c_other, lm_in, lm_other, below_in, below_other, here_in, down_in, down_other,
     pack_in, pack_other, pack_below, pack_below_other, start_ref) = refs[:14]
    parts = refs[14 : 14 + part_count]
    amp_ref, grad_ref, packs, amps, diag, c_ref, m_ref, rhs, down, rows_ref, sems = refs[
        14 + part_count :
    ]
    owner, sub = lax.axis_index("orb"), lax.axis_index("sub")
    n, pairs, own = z.pnos, z.pairs, z.own
    half = z.paos // z.subs
    at = pl.ds(pl.multiple_of(sub * half, half), half)
    mapped_at = pl.ds(pl.multiple_of(z.fits + sub * half, half), half)
    fits = pl.ds(0, z.fits)
    pack_copies = started(
        [pack_in, pack_other, pack_below, pack_below_other],
        [packs.at[pl.ds(i * pairs, pairs)] for i in range(4)],
        sems,
    )
    small_copies = started(
        [c_in.at[:, :, at], c_other.at[:, :, at], lm_in.at[:, :, mapped_at],
         lm_other.at[:, :, mapped_at], below_in.at[:, :, mapped_at],
         below_other.at[:, :, mapped_at]],
        [c_ref.at[pl.ds(0, pairs)], c_ref.at[pl.ds(pairs, pairs)]]
        + [m_ref.at[pl.ds(i * pairs, pairs)] for i in range(4)],
        sems, 4,
    )
    large_copies = started(
        [here_in, lm_in.at[:, :, fits], lm_other.at[:, :, fits], below_in.at[:, :, fits],
         below_other.at[:, :, fits], down_in, down_other],
        [rhs.at[pl.ds(0, own)]] + [rhs.at[pl.ds(own + i * pairs, pairs)] for i in range(4)]
        + [down.at[pl.ds(0, pairs)], down.at[pl.ds(pairs, pairs)]],
        sems, 10,
    )
    diag[...] = jnp.zeros_like(diag)

    def collect(step, slot, who):
        for which in range(own):
            amps[who * own + which] = parts[step][
                slot, which // pairs, :, (which % pairs) * n : (which % pairs + 1) * n
            ]

    each_owner(z, parts, owner, collect)
    wait(pack_copies)
    wait(small_copies)
    orbital_base = owner * z.orbitals

    def place(index, value, orbital):
        for o in range(z.orbitals):
            rows_ref[index * n : (index + 1) * n, o * half : (o + 1) * half] = jnp.where(
                orbital == o, value, 0.0
            )

    def weights_of(pair, index):
        scale = scale_of(z, pair, packs[index, n : n + 1, :n], first, second, ranks, occupied)
        coupled = coupled_of(
            z, pair, amps, near, packs[index, :n, :], packs[index, n + 1 : n + 2, :], diag,
            index % own,
        )
        found = start_ref[index] + coupled * scale
        return found, 2.0 * found - found.T

    for side in range(z.subs):
        for p in range(pairs):
            index = side * pairs + p
            pair = side_start(z, owner, sub, side) + p
            found, weights = weights_of(pair, index)
            if side == 0:
                amp_ref[p] = found
            place(index, mm(weights.T, c_ref[index]), first[pair] - orbital_base)
            place(own + index, mm(weights, m_ref[index]), second[pair] - orbital_base)
            pair = side_start(z, jnp.maximum(owner - 1, 0), sub, side) + p
            found, weights = weights_of(pair, own + index)
            place(2 * own + index, mm(weights, m_ref[own + index]), second[pair] - orbital_base)

    wait(large_copies)
    width = own * n
    step = 256
    for start in range(0, z.fits, step):
        columns = slice(start, start + step)
        right = (rhs[:own, :, columns] + down[:, :, columns]).reshape(width, -1)
        value = mm(rows_ref[:width], right, ((0,), (0,)))
        value += mm(rows_ref[width:], rhs[own:, :, columns].reshape(2 * width, -1), ((0,), (0,)))
        grad_ref[:, :, columns] = value.reshape(z.orbitals, half, step)


def body(
    blocks,
    pno_coefficients,
    domain_map,
    pair_first,
    pair_second,
    pno_ranks,
    neighbours,
    couplings,
    intersections,
    pno_energy,
    occ_energy,
):
    z = Sizes(blocks, pno_coefficients, couplings)
    n, wide, pairs, own = z.pnos, z.fits + z.paos, z.pairs, z.own
    half = z.paos // z.subs
    room = 24 + z.owners // 8 * 4

    def scratch(*shape):
        return pltpu.VMEM(shape, jnp.float32)

    lm, energy = call(
        functools.partial(left_kernel, z),
        [(pairs, n, wide), pno_energy.shape],
        [anywhere] * 5,
        (pair_first, pno_coefficients, domain_map, pno_energy, blocks),
        [
            pltpu.SMEM(pair_first.shape, jnp.int32),
            scratch(*pno_coefficients.shape),
            pltpu.VMEM(domain_map.shape, jnp.int32),
            scratch(*blocks.shape),
            pltpu.SemaphoreType.DMA((4 + z.orbitals,)),
        ],
    )
    below = shifted(lm, "orb", 1)
    energy_below = shifted(energy, "orb", 1)
    lm_other = swapped(lm, "sub")

    later = lax.optimization_barrier((intersections, couplings, pno_coefficients, energy))
    intersection, coupling, coefficients, energy = later
    pack = jnp.concatenate(
        [
            intersection.reshape(pairs, z.links, n, n)
            .transpose(0, 2, 1, 3)
            .reshape(pairs, n, z.links * n),
            jnp.pad(energy, ((0, 0), (0, (z.links - 1) * n)))[:, None, :],
            jnp.repeat(coupling, n, axis=1)[:, None, :],
            jnp.zeros((pairs, EXTRA - 2, z.links * n), jnp.float32),
        ],
        axis=1,
    )
    c_other = swapped(coefficients, "sub")
    pack_other = swapped(pack, "sub")

    right_here, sums = call(
        functools.partial(here_kernel, z),
        [(own, n, z.fits), (n, pairs * n)],
        [smem, vmem, vmem, vmem],
        (pair_second, lm, lm_other, blocks),
    )
    lists = (pair_first, pair_second, pno_ranks)
    right_below, both = call(
        functools.partial(below_kernel, z),
        [(pairs, n, z.fits), (2, n, pairs * n)],
        [smem] * 4 + [vmem] * 5,
        (*lists, occ_energy, energy, energy_below, below, sums, blocks),
    )
    if lax.axis_size("fit") == 2:
        both = both + swapped(both, "fit")
    else:
        both = lax.psum(both, "fit")
    parts = owners_of(both)
    others = [swapped(part, "sub") for part in parts]
    down = shifted(right_below, "orb", -1)
    pack_late, _ = lax.optimization_barrier((pack, both))
    pack_below = shifted(pack_late, "orb", 1)

    lists = (*lists, neighbours, occ_energy)
    args = (*lists, pack, pack_other, *parts, *others)
    square = (z.total, n, n)
    own_amps, start_amps = call(
        functools.partial(sweep_kernel, z, len(parts)),
        [(z.subs, n, pairs * n), (2 * own, n, n)],
        [smem] * 5 + [vmem] * (len(args) - 5),
        args,
        [scratch(*square), scratch(own, z.links * n, z.links * n)],
    )
    amps = owners_of(own_amps)

    down, below, pack_below, _ = lax.optimization_barrier((down, below, pack_below, own_amps))
    down_other = swapped(down, "sub")
    below_other = swapped(below, "sub")
    pack_below_other = swapped(pack_below, "sub")
    args = (
        *lists, pno_coefficients, c_other, lm, lm_other, below, below_other,
        right_here, down, down_other, pack, pack_other, pack_below, pack_below_other,
        start_amps, *amps,
    )
    amplitudes, gradient = call(
        functools.partial(final_kernel, z, len(amps)),
        [(pairs, n, n), (z.orbitals, half, z.fits)],
        [smem] * 5 + [anywhere] * 13 + [vmem] * (len(args) - 18),
        args,
        [
            scratch(2 * own, n + EXTRA, z.links * n),
            scratch(*square),
            scratch(own, z.links * n, z.links * n),
            scratch(own, n, half),
            scratch(2 * own, n, half),
            scratch(3 * own, n, z.fits),
            scratch(own, n, z.fits),
            scratch(3 * own * n, z.orbitals * half),
            pltpu.SemaphoreType.DMA((17,)),
        ],
        limit=room,
    )
    return (amplitudes.reshape(pairs, -1), gradient)


def solution(mesh):
    in_specs = (
        P(("groups", "orb"), None, "fit"),
        P(("groups", "orb", "sub"), None, None),
        P(("groups", "orb", "sub"), None),
        P("groups"),
        P("groups"),
        P("groups"),
        P("groups", None),
        P(("groups", "orb", "sub"), None),
        P(("groups", "orb", "sub"), None, None),
        P(("groups", "orb", "sub"), None),
        P("groups"),
    )
    out_specs = (P(("groups", "orb", "sub"), None), P(("groups", "orb"), "sub", "fit"))
    return jax.shard_map(body, mesh=mesh, in_specs=in_specs, out_specs=out_specs, check_vma=False)
```

```python
import functools

import jax
import jax.numpy as jnp
from jax import lax
from jax.experimental import pallas as pl
from jax.experimental.pallas import tpu as pltpu
from jax.sharding import PartitionSpec as P

ITERS = 2
SMALL = 4
MIB = 1 << 20
EXTRA = 8

high = lax.Precision.HIGH
smem = pl.BlockSpec(memory_space=pltpu.SMEM)
vmem = pl.BlockSpec(memory_space=pltpu.VMEM)


def mm(a, b, contract=((1,), (0,))):
    return lax.dot_general(
        a, b, (contract, ((), ())), precision=high, preferred_element_type=jnp.float32
    )


def shifted(value, axis, steps):
    count = lax.axis_size(axis)
    initial, last = (max(0, -steps), min(count, count - steps))
    return lax.ppermute(value, axis, [(source, source + steps) for source in range(initial, last)])


def swapped(value, axis):
    return lax.ppermute(value, axis, [(0, 1), (1, 0)])


def owners_of(value):
    count = lax.axis_size("orb")
    if count > SMALL or count & (count - 1):
        return [lax.all_gather(value, "orb", axis=0, tiled=False)]
    return [value[None]] + [
        lax.ppermute(value, "orb", [(s, s ^ step) for s in range(count)])[None]
        for step in range(1, count)
    ]


def f32(flag):
    return flag.astype(jnp.float32)


class Sizes:
    def __init__(self, blocks, pno_coefficients, couplings):
        self.orbitals, self.paos, self.fits = blocks.shape
        self.pairs, self.pnos = pno_coefficients.shape[:2]
        self.links = couplings.shape[1]
        self.subs = lax.axis_size("sub")
        self.owners = lax.axis_size("orb")
        self.own = self.pairs * self.subs
        self.total = self.own * self.owners


anywhere = pl.BlockSpec(memory_space=pl.ANY)
held_out = pl.BlockSpec(memory_space=pltpu.HBM)


def call(kernel, outs, ins, args, scratch=(), limit=16, out_specs=None):
    return pl.pallas_call(
        kernel,
        out_shape=[jax.ShapeDtypeStruct(shape, jnp.float32) for shape in outs],
        in_specs=ins,
        out_specs=out_specs or [vmem] * len(outs),
        scratch_shapes=list(scratch),
        compiler_params=pltpu.CompilerParams(vmem_limit_bytes=limit * MIB),
    )(*args)


def started(sources, targets, sems, base=0):
    copies = [
        pltpu.make_async_copy(source, target, sems.at[base + index])
        for index, (source, target) in enumerate(zip(sources, targets))
    ]
    for copy in copies:
        copy.start()
    return copies


def wait(copies):
    for copy in copies:
        copy.wait()


def side_start(z, owner, sub, side):
    return owner * z.own + (sub if side == 0 else 1 - sub) * z.pairs


def scale_of(z, pair, level, first, second, ranks, occupied):
    n = z.pnos
    row_ids = lax.broadcasted_iota(jnp.int32, (n, n), 0)
    column_ids = lax.broadcasted_iota(jnp.int32, (n, n), 1)
    level = level * jnp.ones((n, 1), jnp.float32)
    rank = ranks[pair]
    kept = f32((row_ids < rank) & (column_ids < rank))
    return kept / (level + level.T - (occupied[first[pair]] + occupied[second[pair]]))


def split(value):
    high_part = value.astype(jnp.bfloat16)
    return high_part, (value - high_part.astype(jnp.float32)).astype(jnp.bfloat16)


def mm3(a, b, contract=((1,), (0,))):
    def one(x, y):
        return lax.dot_general(x, y, (contract, ((), ())), preferred_element_type=jnp.float32)

    return one(a[0], b[0]) + (one(a[0], b[1]) + one(a[1], b[0]))


def each_owner(z, parts, owner, action):
    if len(parts) == 1 and z.owners > 1:
        @pl.loop(0, z.owners)
        def _(index):
            action(0, index, index)
    else:
        for step in range(len(parts)):
            action(step, 0, owner ^ step)


def split_all(z, amps, amps_high, amps_low):
    def one(row):
        amps_high[row], amps_low[row] = split(amps[row])

    if z.owners <= SMALL:
        for row in range(z.own, z.own + z.total):
            one(row)
    else:
        @pl.loop(z.own, z.own + z.total)
        def _(row):
            one(row)


def coupled_of(z, pair_list, near, packs, amps_high, amps_low, diag_high, diag_low):
    n = z.pnos
    diag_high[...] = jnp.zeros_like(diag_high)
    diag_low[...] = jnp.zeros_like(diag_low)
    for index, pair in enumerate(pair_list):
        for k in range(z.links):
            row = near[pair, k] + z.own
            block = slice(k * n, (k + 1) * n)
            diag_high[index, block, block] = amps_high[row]
            diag_low[index, block, block] = amps_low[row]
    parts = [split(pack[:n, :]) for pack in packs]
    inner = [
        mm3(part, (diag_high[index], diag_low[index])) for index, part in enumerate(parts)
    ]
    inner = [split(value * pack[n : n + 1, :]) for value, pack in zip(inner, packs)]
    return [mm3(value, part, ((1,), (1,))) for value, part in zip(inner, parts)]


def mapped_kernel(z, c_in, map_in, e_in, mp_ref, c_ref, map_ref, e_ref, sems):
    n = z.pnos
    wait(started([c_in, map_in, e_in], [c_ref, map_ref, e_ref], sems))
    rows = lax.broadcasted_iota(jnp.int32, (z.paos, z.paos), 0)
    for p in range(z.pairs):
        select = f32(map_ref[p : p + 1, :] == rows).astype(jnp.bfloat16)
        c_high, c_low = split(c_ref[p])
        mp_ref[p, :n, :] = lax.dot_general(
            c_high, select, (((1,), (1,)), ((), ())), preferred_element_type=jnp.float32
        ) + lax.dot_general(
            c_low, select, (((1,), (1,)), ((), ())), preferred_element_type=jnp.float32
        )
        mp_ref[p, n:, :] = jnp.zeros((EXTRA, z.paos), jnp.float32)
        mp_ref[p, n : n + 1, :n] = e_ref[p : p + 1, :]


def left_kernel(z, first, c_ref, b_ref, order, left_ref):
    owner, sub = lax.axis_index("orb"), lax.axis_index("sub")
    start = side_start(z, owner, sub, 0)
    for p in range(z.pairs):
        left_ref[p] = mm(c_ref[p], b_ref[first[start + p] - owner * z.orbitals])


def below_kernel(z, second, mp_below, b_ref, right_ref):
    owner, sub = lax.axis_index("orb"), lax.axis_index("sub")
    start = side_start(z, jnp.maximum(owner - 1, 0), sub, 0)
    for p in range(z.pairs):
        j = second[start + p] - owner * z.orbitals
        held = jnp.where(j >= 0, 1.0, 0.0)
        mapped = mp_below[p, : z.pnos, :] * held
        right_ref[p] = mm(mapped, b_ref[jnp.clip(j, 0, z.orbitals - 1)])


def here_kernel(z, second, left_ref, mp_ref, mp_other, b_ref, pack, right_below, right_ref,
                sums_ref):
    owner, sub = lax.axis_index("orb"), lax.axis_index("sub")
    n = z.pnos
    for side, ref in enumerate((mp_ref, mp_other)):
        start = side_start(z, owner, sub, side)
        for p in range(z.pairs):
            j = second[start + p] - owner * z.orbitals
            local = jnp.where(j < z.orbitals, 1.0, 0.0)
            right = mm(ref[p, :n, :] * local, b_ref[jnp.minimum(j, z.orbitals - 1)])
            right_ref[side * z.pairs + p] = right
            if side == 0:
                sums_ref[:, p * n : (p + 1) * n] = mm(left_ref[p], right, ((1,), (1,)))


def sums_kernel(z, first, second, ranks, occupied, mp_ref, mp_below, left_below, right_below,
                sums_ref, both_ref):
    owner, sub = lax.axis_index("orb"), lax.axis_index("sub")
    own_start = side_start(z, owner, sub, 0)
    start = side_start(z, jnp.maximum(owner - 1, 0), sub, 0)
    n = z.pnos
    lists = (first, second, ranks, occupied)
    for p in range(z.pairs):
        lanes = slice(p * n, (p + 1) * n)
        scale = scale_of(z, own_start + p, mp_ref[p, n : n + 1, :n], *lists)
        both_ref[0, :, lanes] = -sums_ref[:, lanes] * scale
        part = mm(left_below[p], right_below[p], ((1,), (1,)))
        scale = scale_of(z, start + p, mp_below[p, n : n + 1, :n], *lists)
        both_ref[1, :, lanes] = -part * scale


def sweep_kernel(z, part_count, first, second, ranks, near, occupied, mp_ref, mp_other, pack,
                 pack_other, *refs):
    parts, others = refs[:part_count], refs[part_count : 2 * part_count]
    own_ref, start_ref, amps, amps_high, amps_low, diag_high, diag_low = refs[2 * part_count :]
    owner, sub = lax.axis_index("orb"), lax.axis_index("sub")
    n = z.pnos

    def collect(step, slot, who):
        for side, ref in ((0, parts[step]), (1, others[step])):
            row = side_start(z, who + 1, sub, side)
            for p in range(z.pairs):
                amps[row + p] = ref[slot, 0, :, p * n : (p + 1) * n]

    def collect_above(step, slot, who):
        for side, ref in ((0, parts[step]), (1, others[step])):
            row = side_start(z, who, sub, side)
            for p in range(z.pairs):
                amps[row + p] = amps[row + p] + ref[slot, 1, :, p * n : (p + 1) * n]

    amps[: z.own] = jnp.zeros((z.own, n, n), jnp.float32)
    each_owner(z, parts, owner, collect)
    each_owner(z, parts, owner, collect_above)
    split_all(z, amps, amps_high, amps_low)
    pair_list, scales = [], []
    for side, ref in enumerate((mp_ref, mp_other)):
        for p in range(z.pairs):
            pair = side_start(z, owner, sub, side) + p
            pair_list.append(pair)
            scales.append(
                scale_of(z, pair, ref[p, n : n + 1, :n], first, second, ranks, occupied)
            )
    packs = [ref.at[p] for ref in (pack, pack_other) for p in range(z.pairs)]
    coupled = coupled_of(z, pair_list, near, packs, amps_high, amps_low, diag_high, diag_low)
    for index, pair in enumerate(pair_list):
        side, p = divmod(index, z.pairs)
        begin = amps[pair + z.own]
        start_ref[index] = begin
        start_ref[z.own + index] = amps[
            side_start(z, jnp.maximum(owner - 1, 0), sub, side) + p + z.own
        ]
        own_ref[sub if side == 0 else 1 - sub, :, p * n : (p + 1) * n] = (
            begin + coupled[index] * scales[index]
        )


def final_kernel(z, part_count, first, second, ranks, near, occupied, *refs):
    (c_in, c_other, mp_in, mp_other, mp_below, mp_below_other, left_in, left_other, left_below,
     left_below_other, here_in, down_in, down_other, pack_in, pack_other, pack_below,
     pack_below_other, start_ref) = refs[:18]
    parts = refs[18 : 18 + part_count]
    (amp_ref, grad_out, packs, c_ref, m_ref, e_ref, rhs, down, grad, flat, amps, amps_high,
     amps_low, diag_high, diag_low, rows_high, rows_low, sems) = refs[18 + part_count :]
    owner, sub = lax.axis_index("orb"), lax.axis_index("sub")
    n, pairs, own = z.pnos, z.pairs, z.own
    half = z.paos // z.subs
    at = pl.ds(pl.multiple_of(sub * half, half), half)
    mapped_in = [mp_in, mp_other, mp_below, mp_below_other]

    def quarters(ref):
        return [ref.at[pl.ds(i * pairs, pairs)] for i in range(4)]

    pack_copies = started(
        [pack_in, pack_other, pack_below, pack_below_other]
        + [ref.at[:, pl.ds(n, EXTRA), :] for ref in mapped_in],
        quarters(packs) + quarters(e_ref),
        sems,
    )
    small_copies = started(
        [c_in.at[:, :, at], c_other.at[:, :, at]]
        + [ref.at[:, pl.ds(0, n), at] for ref in mapped_in],
        [c_ref.at[pl.ds(0, pairs)], c_ref.at[pl.ds(pairs, pairs)]] + quarters(m_ref),
        sems, 8,
    )
    large_copies = started(
        [here_in, left_in, left_other, left_below, left_below_other, down_in, down_other],
        [rhs.at[pl.ds(0, own)]] + [rhs.at[pl.ds(own + i * pairs, pairs)] for i in range(4)]
        + [down.at[pl.ds(0, pairs)], down.at[pl.ds(pairs, pairs)]],
        sems, 14,
    )

    def collect(step, slot, who):
        for which in range(own):
            amps[(who + 1) * own + which] = parts[step][
                slot, which // pairs, :, (which % pairs) * n : (which % pairs + 1) * n
            ]

    each_owner(z, parts, owner, collect)
    split_all(z, amps, amps_high, amps_low)
    pair_list = [
        side_start(z, who, sub, side) + p
        for who in (owner, jnp.maximum(owner - 1, 0))
        for side in range(z.subs)
        for p in range(pairs)
    ]
    wait(pack_copies)
    scales = [
        scale_of(z, pair, e_ref[index, 0:1, :n], first, second, ranks, occupied)
        for index, pair in enumerate(pair_list)
    ]
    coupled = coupled_of(
        z, pair_list, near, [packs.at[i] for i in range(2 * own)], amps_high, amps_low,
        diag_high, diag_low,
    )
    found = [
        start_ref[index] + value * scale
        for index, (value, scale) in enumerate(zip(coupled, scales))
    ]
    turned = [value.T for value in found]
    wait(small_copies)
    weights = [split(2.0 * a - b) for a, b in zip(found, turned)]
    weights_turned = [split(2.0 * b - a) for a, b in zip(found[:own], turned[:own])]
    terms = (
        [mm3(w, split(c_ref[i])) for i, w in enumerate(weights_turned)]
        + [mm3(w, split(m_ref[i])) for i, w in enumerate(weights)]
    )
    orbital_list = (
        [first[pair] - owner * z.orbitals for pair in pair_list[:own]]
        + [second[pair] - owner * z.orbitals for pair in pair_list]
    )
    for index in range(0, 3 * own, 2):
        for o in range(z.orbitals):
            block = jnp.concatenate(
                [
                    jnp.where(orbital_list[i] == o, terms[i], 0.0) for i in (index, index + 1)
                ]
            ).T
            place = (slice(o * half, (o + 1) * half), slice(index * n, (index + 2) * n))
            rows_high[place], rows_low[place] = split(block)

    for p in range(pairs):
        flat[p] = found[p]
        even = flat[p, pl.ds(0, n // 2, 2), :]
        odd = flat[p, pl.ds(1, n // 2, 2), :]
        lines = jnp.concatenate([even, odd], axis=1)
        for r in range(n // 2):
            amp_ref[p : p + 1, r * 2 * n : (r + 1) * 2 * n] = lines[r : r + 1, :]

    wait(large_copies)
    step = 256
    rows = (rows_high[...], rows_low[...])
    copies = []
    for index, start in enumerate(range(0, z.fits, step)):
        columns = slice(start, start + step)
        right = (rhs[:own, :, columns] + down[:, :, columns]).reshape(own * n, -1)
        factor = jnp.concatenate([right, rhs[own:, :, columns].reshape(2 * own * n, -1)])
        grad[:, :, columns] = mm3(rows, split(factor)).reshape(z.orbitals, half, step)
        window = pl.ds(start, step)
        copies += started(
            [grad.at[:, :, window]], [grad_out.at[:, :, window]], sems, 21 + index
        )
    wait(copies)


def gate(values, *after):
    return lax.optimization_barrier((tuple(values), after))[0]


def body(
    blocks,
    pno_coefficients,
    domain_map,
    pair_first,
    pair_second,
    pno_ranks,
    neighbours,
    couplings,
    intersections,
    pno_energy,
    occ_energy,
):
    z = Sizes(blocks, pno_coefficients, couplings)
    n, pairs, own, fits = z.pnos, z.pairs, z.own, z.fits
    half = z.paos // z.subs

    def scratch(*shape, kind=jnp.float32):
        return pltpu.VMEM(shape, kind)

    hbm = held_out
    (mp,) = call(
        functools.partial(mapped_kernel, z),
        [(pairs, n + EXTRA, z.paos)],
        [hbm] * 3,
        (pno_coefficients, domain_map, pno_energy),
        [
            scratch(*pno_coefficients.shape),
            pltpu.VMEM(domain_map.shape, jnp.int32),
            scratch(*pno_energy.shape),
            pltpu.SemaphoreType.DMA((3,)),
        ],
        limit=8,
    )
    mp_below = shifted(mp, "orb", 1)
    (left,) = call(
        functools.partial(left_kernel, z),
        [(pairs, n, fits)],
        [smem, vmem, vmem, anywhere],
        (pair_first, pno_coefficients, blocks, mp),
        limit=8,
    )
    left_below = shifted(left, "orb", 1)
    (right_below,) = call(
        functools.partial(below_kernel, z),
        [(pairs, n, fits)],
        [smem, vmem, vmem],
        (pair_second, mp_below, blocks),
        limit=8,
    )
    down = shifted(right_below, "orb", -1)

    intersection, coupling = gate((intersections, couplings), left)
    pack = jnp.concatenate(
        [
            intersection.reshape(pairs, z.links, n, n)
            .transpose(0, 2, 1, 3)
            .reshape(pairs, n, z.links * n),
            jnp.repeat(coupling, n, axis=1)[:, None, :],
            jnp.zeros((pairs, EXTRA - 1, z.links * n), jnp.float32),
        ],
        axis=1,
    )
    (coefficients,) = gate((pno_coefficients,), left)
    mp_other = swapped(mp, "sub")
    left_other = swapped(left, "sub")
    c_other = swapped(coefficients, "sub")
    pack_other = swapped(pack, "sub")
    pack_below = shifted(pack, "orb", 1)

    right_here, sums = call(
        functools.partial(here_kernel, z),
        [(own, n, fits), (n, pairs * n)],
        [smem, vmem, vmem, vmem, vmem, anywhere, anywhere],
        (pair_second, left, mp, mp_other, blocks, pack, right_below),
        limit=8,
    )
    lists = (pair_first, pair_second, pno_ranks)
    (both,) = call(
        functools.partial(sums_kernel, z),
        [(2, n, pairs * n)],
        [smem] * 4 + [vmem] * 5,
        (*lists, occ_energy, mp, mp_below, left_below, right_below, sums),
        limit=8,
    )
    if lax.axis_size("fit") == 2:
        both = both + swapped(both, "fit")
    else:
        both = lax.psum(both, "fit")
    parts = owners_of(both)
    others = [swapped(part, "sub") for part in parts]

    late = gate((mp_below, left_below, down, pack_below), both)
    mp_below_other, left_below_other, down_other, pack_below_other = [
        swapped(value, "sub") for value in late
    ]

    lists = (*lists, neighbours, occ_energy)
    args = (*lists, mp, mp_other, pack, pack_other, *parts, *others)
    rows = (z.total + own, n, n)
    bf16 = jnp.bfloat16
    wide = z.links * n
    own_amps, start_amps = call(
        functools.partial(sweep_kernel, z, len(parts)),
        [(z.subs, n, pairs * n), (2 * own, n, n)],
        [smem] * 5 + [vmem] * (len(args) - 5),
        args,
        [scratch(*rows), scratch(*rows, kind=bf16), scratch(*rows, kind=bf16)]
        + [scratch(own, wide, wide, kind=bf16)] * 2,
        limit=6 + z.owners // 2,
    )
    amps = owners_of(own_amps)

    args = (
        *lists, pno_coefficients, c_other, mp, mp_other, mp_below, mp_below_other,
        left, left_other, left_below, left_below_other, right_here, down, down_other,
        pack, pack_other, pack_below, pack_below_other, start_amps, *amps,
    )
    amplitudes, gradient = call(
        functools.partial(final_kernel, z, len(amps)),
        [(pairs, n * n), (z.orbitals, half, fits)],
        [smem] * 5 + [anywhere] * 17 + [vmem] * (len(args) - 22),
        args,
        [
            scratch(2 * own, n + EXTRA, wide),
            scratch(own, n, half),
            scratch(2 * own, n, half),
            scratch(2 * own, EXTRA, z.paos),
            scratch(3 * own, n, fits),
            scratch(own, n, fits),
            scratch(z.orbitals, half, fits),
            scratch(pairs, n, n),
            scratch(*rows),
            scratch(*rows, kind=bf16),
            scratch(*rows, kind=bf16),
        ]
        + [scratch(2 * own, wide, wide, kind=bf16)] * 2
        + [scratch(z.orbitals * half, 3 * own * n, kind=bf16)] * 2
        + [pltpu.SemaphoreType.DMA((21 + -(-fits // 256),))],
        limit=20 + z.owners // 2,
        out_specs=[vmem, hbm],
    )
    return (amplitudes, gradient)


def solution(mesh):
    in_specs = (
        P(("groups", "orb"), None, "fit"),
        P(("groups", "orb", "sub"), None, None),
        P(("groups", "orb", "sub"), None),
        P("groups"),
        P("groups"),
        P("groups"),
        P("groups", None),
        P(("groups", "orb", "sub"), None),
        P(("groups", "orb", "sub"), None, None),
        P(("groups", "orb", "sub"), None),
        P("groups"),
    )
    out_specs = (P(("groups", "orb", "sub"), None), P(("groups", "orb"), "sub", "fit"))
    return jax.shard_map(body, mesh=mesh, in_specs=in_specs, out_specs=out_specs, check_vma=False)
```

```python
import functools

import jax
import jax.numpy as jnp
from jax import lax
from jax.experimental import pallas as pl
from jax.experimental.pallas import tpu as pltpu
from jax.sharding import PartitionSpec as P

ITERS = 2
SMALL = 4
MIB = 1 << 20
EXTRA = 8

high = lax.Precision.HIGH
smem = pl.BlockSpec(memory_space=pltpu.SMEM)
vmem = pl.BlockSpec(memory_space=pltpu.VMEM)


def mm(a, b, contract=((1,), (0,))):
    return lax.dot_general(
        a, b, (contract, ((), ())), precision=high, preferred_element_type=jnp.float32
    )


def shifted(value, axis, steps):
    count = lax.axis_size(axis)
    initial, last = (max(0, -steps), min(count, count - steps))
    return lax.ppermute(value, axis, [(source, source + steps) for source in range(initial, last)])


def swapped(value, axis):
    return lax.ppermute(value, axis, [(0, 1), (1, 0)])


def everyone(value):
    return lax.all_to_all(value, ("orb", "sub"), 0, 0)


def f32(flag):
    return flag.astype(jnp.float32)


class Sizes:
    def __init__(self, blocks, pno_coefficients, couplings):
        self.orbitals, self.paos, self.fits = blocks.shape
        self.pairs, self.pnos = pno_coefficients.shape[:2]
        self.links = couplings.shape[1]
        self.subs = lax.axis_size("sub")
        self.owners = lax.axis_size("orb")
        self.own = self.pairs * self.subs
        self.total = self.own * self.owners


anywhere = pl.BlockSpec(memory_space=pl.ANY)
held_out = pl.BlockSpec(memory_space=pltpu.HBM)


def call(kernel, outs, ins, args, scratch=(), limit=16, out_specs=None):
    return pl.pallas_call(
        kernel,
        out_shape=[jax.ShapeDtypeStruct(shape, jnp.float32) for shape in outs],
        in_specs=ins,
        out_specs=out_specs or [vmem] * len(outs),
        scratch_shapes=list(scratch),
        compiler_params=pltpu.CompilerParams(vmem_limit_bytes=limit * MIB),
    )(*args)


def started(sources, targets, sems, base=0):
    copies = [
        pltpu.make_async_copy(source, target, sems.at[base + index])
        for index, (source, target) in enumerate(zip(sources, targets))
    ]
    for copy in copies:
        copy.start()
    return copies


def wait(copies):
    for copy in copies:
        copy.wait()


def side_start(z, owner, sub, side):
    return owner * z.own + (sub if side == 0 else 1 - sub) * z.pairs


def scale_of(z, pair, level, first, second, ranks, occupied):
    n = z.pnos
    row_ids = lax.broadcasted_iota(jnp.int32, (n, n), 0)
    column_ids = lax.broadcasted_iota(jnp.int32, (n, n), 1)
    level = level * jnp.ones((n, 1), jnp.float32)
    rank = ranks[pair]
    kept = f32((row_ids < rank) & (column_ids < rank))
    return kept / (level + level.T - (occupied[first[pair]] + occupied[second[pair]]))


def split(value):
    high_part = value.astype(jnp.bfloat16)
    return high_part, (value - high_part.astype(jnp.float32)).astype(jnp.bfloat16)


def mm3(a, b, contract=((1,), (0,))):
    def one(x, y):
        return lax.dot_general(x, y, (contract, ((), ())), preferred_element_type=jnp.float32)

    return one(a[0], b[0]) + (one(a[0], b[1]) + one(a[1], b[0]))


def split_all(z, amps, amps_high, amps_low):
    def one(row):
        amps_high[row], amps_low[row] = split(amps(row))

    if z.owners <= SMALL:
        for row in range(z.total):
            one(row)
    else:
        @pl.loop(0, z.total)
        def _(row):
            one(row)


def packed_pair(z, ref, row):
    if isinstance(row, int):
        side = row % z.pairs
        return ref[row // z.pairs, :, side * z.pnos : (side + 1) * z.pnos]
    block = ref[row // z.pairs]
    value = block[:, : z.pnos]
    for side in range(1, z.pairs):
        value = jnp.where(
            lax.rem(row, z.pairs) == side, block[:, side * z.pnos : (side + 1) * z.pnos], value
        )
    return value


def unpack(z, s_ref, index, block):
    n = z.pnos
    for k in range(0, z.links, 2):
        two = block[:, k * n : (k + 2) * n]
        for odd in range(2):
            part = two[:, odd * n : (odd + 1) * n]
            s_ref[index, k // 2, pl.ds(odd, n // 2, 2), :] = jnp.concatenate(
                [part[: n // 2], part[n // 2 :]], axis=1
            )


def unpacked(z, s_ref, index):
    return jnp.concatenate([s_ref[index, k] for k in range(z.links // 2)], axis=1)


def coupled_of(z, pair_list, near, s_ref, couplings, amps_high, amps_low, diag_high, diag_low):
    n = z.pnos
    diag_high[...] = jnp.zeros_like(diag_high)
    diag_low[...] = jnp.zeros_like(diag_low)
    for index, pair in enumerate(pair_list):
        for k in range(z.links):
            row = near[pair, k]
            block = slice(k * n, (k + 1) * n)
            diag_high[index, block, block] = amps_high[row]
            diag_low[index, block, block] = amps_low[row]
    parts = [split(unpacked(z, s_ref, index)) for index in range(len(pair_list))]
    inner = [
        mm3(part, (diag_high[index], diag_low[index])) for index, part in enumerate(parts)
    ]
    inner = [split(value * coupling) for value, coupling in zip(inner, couplings)]
    return [mm3(value, part, ((1,), (1,))) for value, part in zip(inner, parts)]


def mapped_kernel(z, c_in, map_in, e_in, coupling_in, b_in, mp_ref, b_ref, c_ref, map_ref, e_ref,
                  coupling, sems):
    n = z.pnos
    copies = started(
        [c_in, map_in, e_in, coupling_in, b_in], [c_ref, map_ref, e_ref, coupling, b_ref], sems
    )
    wait(copies[:4])
    rows = lax.broadcasted_iota(jnp.int32, (z.paos, z.paos), 0)
    lane_link = lax.broadcasted_iota(jnp.int32, (1, z.links * n), 1) // n
    for p in range(z.pairs):
        select = f32(map_ref[p : p + 1, :] == rows).astype(jnp.bfloat16)
        c_high, c_low = split(c_ref[p])
        mp_ref[p, :n, :] = lax.dot_general(
            c_high, select, (((1,), (1,)), ((), ())), preferred_element_type=jnp.float32
        ) + lax.dot_general(
            c_low, select, (((1,), (1,)), ((), ())), preferred_element_type=jnp.float32
        )
        mp_ref[p, n:, :] = jnp.zeros((EXTRA, z.paos), jnp.float32)
        mp_ref[p, n : n + 1, :n] = e_ref[p : p + 1, :]
        spread = jnp.zeros((1, z.links * n), jnp.float32)
        for k in range(z.links):
            spread = jnp.where(lane_link == k, coupling[p : p + 1, k : k + 1], spread)
        mp_ref[p, n + 1 : n + 2, :] = spread
    wait(copies[4:])


def left_kernel(z, first, c_ref, b_ref, q_ref, left_ref):
    owner, sub = lax.axis_index("orb"), lax.axis_index("sub")
    start = side_start(z, owner, sub, 0)
    for p in range(z.pairs):
        left_ref[p, :, : z.fits] = mm(c_ref[p], b_ref[first[start + p] - owner * z.orbitals])
        for k in range(0, z.links, 2):
            lanes = slice(z.fits + k * z.pnos, z.fits + (k + 2) * z.pnos)
            left_ref[p, :, lanes] = jnp.concatenate([q_ref[p, k], q_ref[p, k + 1]])


def below_kernel(z, second, mp_below, b_ref, right_ref):
    owner, sub = lax.axis_index("orb"), lax.axis_index("sub")
    start = side_start(z, jnp.maximum(owner - 1, 0), sub, 0)
    for p in range(z.pairs):
        j = second[start + p] - owner * z.orbitals
        held = jnp.where(j >= 0, 1.0, 0.0)
        mapped = mp_below[p, : z.pnos, :] * held
        right_ref[p] = mm(mapped, b_ref[jnp.clip(j, 0, z.orbitals - 1)])


def here_kernel(z, second, mp_ref, b_ref, right_below, left_other, c_other, right_ref):
    owner, sub = lax.axis_index("orb"), lax.axis_index("sub")
    start = side_start(z, owner, sub, 0)
    for p in range(z.pairs):
        j = second[start + p] - owner * z.orbitals
        local = jnp.where(j < z.orbitals, 1.0, 0.0)
        right_ref[p] = mm(
            mp_ref[p, : z.pnos, :] * local, b_ref[jnp.minimum(j, z.orbitals - 1)]
        )


def sums_kernel(z, first, second, ranks, occupied, mp_ref, left_ref, here_ref, down_ref, sums_ref,
                right_ref):
    owner, sub = lax.axis_index("orb"), lax.axis_index("sub")
    start = side_start(z, owner, sub, 0)
    n = z.pnos
    for p in range(z.pairs):
        right = here_ref[p] + down_ref[p]
        right_ref[p] = right
        scale = scale_of(
            z, start + p, mp_ref[p, n : n + 1, :n], first, second, ranks, occupied
        )
        part = mm(left_ref[p, :, : z.fits], right, ((1,), (1,)))
        sums_ref[:, p * n : (p + 1) * n] = -part * scale


def sweep_kernel(z, first, second, ranks, near, occupied, mp_ref, q_ref, all_ref, *refs):
    own_ref, amps_high, amps_low, diag_high, diag_low, s_ref = refs[-6:]
    owner, sub = lax.axis_index("orb"), lax.axis_index("sub")
    n = z.pnos
    split_all(z, functools.partial(packed_pair, z, all_ref), amps_high, amps_low)
    start = side_start(z, owner, sub, 0)
    pair_list = [start + p for p in range(z.pairs)]
    for p in range(z.pairs):
        unpack(z, s_ref, p, q_ref[p])
    scales = [
        scale_of(z, pair, mp_ref[p, n : n + 1, :n], first, second, ranks, occupied)
        for p, pair in enumerate(pair_list)
    ]
    couplings = [mp_ref[p, n + 1 : n + 2, :] for p in range(z.pairs)]
    coupled = coupled_of(
        z, pair_list, near, s_ref, couplings, amps_high, amps_low, diag_high, diag_low
    )
    begin = all_ref[owner * z.subs + sub]
    value = begin + jnp.concatenate([a * b for a, b in zip(coupled, scales)], axis=1)
    for copy in range(z.owners * z.subs):
        own_ref[copy] = value


def final_kernel(z, first, second, ranks, near, occupied, *refs):
    (c_in, c_other, mp_in, mp_other, mp_below, mp_below_other, left_in, left_other, left_below,
     left_below_other, right_in, right_other, start_ref, all_ref) = refs[:14]
    (amp_ref, grad_out, packs, c_ref, m_ref, e_ref, rhs, grad, flat, s_ref, amps_high, amps_low,
     diag_high, diag_low, rows_high, rows_low, sems) = refs[14:]
    owner, sub = lax.axis_index("orb"), lax.axis_index("sub")
    n, pairs, own = z.pnos, z.pairs, z.own
    half = z.paos // z.subs
    at = pl.ds(pl.multiple_of(sub * half, half), half)
    fits, links = pl.ds(0, z.fits), pl.ds(z.fits, z.links * n)
    mapped_in = [mp_in, mp_other, mp_below, mp_below_other]
    left_all = [left_in, left_other, left_below, left_below_other]

    def quarters(ref, base=0):
        return [ref.at[pl.ds(base + i * pairs, pairs)] for i in range(4)]

    pack_copies = started(
        [ref.at[:, :, links] for ref in left_all]
        + [ref.at[:, pl.ds(n, EXTRA), :] for ref in mapped_in],
        quarters(packs) + quarters(e_ref),
        sems,
    )
    small_copies = started(
        [c_in.at[:, :, at], c_other.at[:, :, at]]
        + [ref.at[:, pl.ds(0, n), at] for ref in mapped_in],
        [c_ref.at[pl.ds(0, pairs)], c_ref.at[pl.ds(pairs, pairs)]] + quarters(m_ref),
        sems, 8,
    )
    large_copies = started(
        [right_in, right_other] + [ref.at[:, :, fits] for ref in left_all],
        [rhs.at[pl.ds(0, pairs)], rhs.at[pl.ds(pairs, pairs)]] + quarters(rhs, own),
        sems, 14,
    )
    split_all(z, functools.partial(packed_pair, z, all_ref), amps_high, amps_low)
    pair_list = [
        side_start(z, who, sub, side) + p
        for who in (owner, jnp.maximum(owner - 1, 0))
        for side in range(z.subs)
        for p in range(pairs)
    ]
    wait(pack_copies)
    for index in range(2 * own):
        unpack(z, s_ref, index, packs[index])
    scales = [
        scale_of(z, pair, e_ref[index, 0:1, :n], first, second, ranks, occupied)
        for index, pair in enumerate(pair_list)
    ]
    couplings = [e_ref[index, 1:2, :] for index in range(2 * own)]
    coupled = coupled_of(
        z, pair_list, near, s_ref, couplings, amps_high, amps_low, diag_high, diag_low
    )
    found = []
    for base in range(0, 2 * own, pairs):
        block = start_ref[pair_list[base] // pairs]
        for p in range(pairs):
            index = base + p
            found.append(block[:, p * n : (p + 1) * n] + coupled[index] * scales[index])
    turned = [value.T for value in found]
    wait(small_copies)
    weights = [split(2.0 * a - b) for a, b in zip(found, turned)]
    weights_turned = [split(2.0 * b - a) for a, b in zip(found[:own], turned[:own])]
    terms = (
        [mm3(w, split(c_ref[i])) for i, w in enumerate(weights_turned)]
        + [mm3(w, split(m_ref[i])) for i, w in enumerate(weights)]
    )
    orbital_list = (
        [first[pair] - owner * z.orbitals for pair in pair_list[:own]]
        + [second[pair] - owner * z.orbitals for pair in pair_list]
    )
    for index in range(0, 3 * own, 2):
        for o in range(z.orbitals):
            block = jnp.concatenate(
                [
                    jnp.where(orbital_list[i] == o, terms[i], 0.0) for i in (index, index + 1)
                ]
            ).T
            place = (slice(o * half, (o + 1) * half), slice(index * n, (index + 2) * n))
            rows_high[place], rows_low[place] = split(block)

    for p in range(pairs):
        flat[p] = found[p]
        even = flat[p, pl.ds(0, n // 2, 2), :]
        odd = flat[p, pl.ds(1, n // 2, 2), :]
        lines = jnp.concatenate([even, odd], axis=1)
        for r in range(n // 2):
            amp_ref[p : p + 1, r * 2 * n : (r + 1) * 2 * n] = lines[r : r + 1, :]

    wait(large_copies)
    step = 256
    rows = (rows_high[...], rows_low[...])
    copies = []
    for index, start in enumerate(range(0, z.fits, step)):
        factor = rhs[:, :, start : start + step].reshape(3 * own * n, step)
        grad[:, :, start : start + step] = mm3(rows, split(factor)).reshape(
            z.orbitals, half, step
        )
        window = pl.ds(start, step)
        copies += started(
            [grad.at[:, :, window]], [grad_out.at[:, :, window]], sems, 20 + index
        )
    wait(copies)


def gate(values, *after):
    return lax.optimization_barrier((tuple(values), after))[0]


def body(
    blocks,
    pno_coefficients,
    domain_map,
    pair_first,
    pair_second,
    pno_ranks,
    neighbours,
    couplings,
    intersections,
    pno_energy,
    occ_energy,
):
    z = Sizes(blocks, pno_coefficients, couplings)
    n, pairs, own, fits = z.pnos, z.pairs, z.own, z.fits
    half = z.paos // z.subs
    devices = z.owners * z.subs
    wide = z.links * n

    def scratch(*shape, kind=jnp.float32):
        return pltpu.VMEM(shape, kind)

    hbm = held_out
    mp, held = call(
        functools.partial(mapped_kernel, z),
        [(pairs, n + EXTRA, z.paos), blocks.shape],
        [hbm] * 5,
        (pno_coefficients, domain_map, pno_energy, couplings, blocks),
        [
            scratch(*pno_coefficients.shape),
            pltpu.VMEM(domain_map.shape, jnp.int32),
            scratch(*pno_energy.shape),
            scratch(*couplings.shape),
            pltpu.SemaphoreType.DMA((5,)),
        ],
        limit=8,
    )
    mp_below = shifted(mp, "orb", 1)
    intersection, coefficients = gate((intersections, pno_coefficients), mp)
    (left,) = call(
        functools.partial(left_kernel, z),
        [(pairs, n, fits + wide)],
        [smem, vmem, vmem, vmem],
        (pair_first, coefficients, held,
         intersection.reshape(pairs, z.links, n // 2, 2 * n)),
        limit=8,
    )
    (right_below,) = call(
        functools.partial(below_kernel, z),
        [(pairs, n, fits)],
        [smem, vmem, vmem],
        (pair_second, mp_below, held),
        limit=8,
    )
    down = shifted(right_below, "orb", -1)
    left_late, mp_late, coefficients = gate((left, mp, coefficients), right_below)
    left_below = shifted(left_late, "orb", 1)
    mp_other = swapped(mp_late, "sub")
    left_other = swapped(left_late, "sub")
    c_other = swapped(coefficients, "sub")

    (right_here,) = call(
        functools.partial(here_kernel, z),
        [(pairs, n, fits)],
        [smem, vmem, vmem, anywhere, anywhere, anywhere],
        (pair_second, mp, held, right_below, left_other, c_other),
        limit=8,
    )
    lists = (pair_first, pair_second, pno_ranks)
    sums, right = call(
        functools.partial(sums_kernel, z),
        [(n, pairs * n), (pairs, n, fits)],
        [smem] * 4 + [vmem] * 4,
        (*lists, occ_energy, mp, left, right_here, down),
        limit=8,
    )
    if lax.axis_size("fit") == 2:
        sums = sums + swapped(sums, "fit")
    else:
        sums = lax.psum(sums, "fit")
    start_amps = everyone(jnp.broadcast_to(sums[None], (devices, *sums.shape)))

    mp_late, left_late, right_late = gate((mp_below, left_below, right), sums)
    mp_below_other, left_below_other, right_other = [
        swapped(value, "sub") for value in (mp_late, left_late, right_late)
    ]

    lists = (*lists, neighbours, occ_energy)
    rows = (z.total, n, n)
    bf16 = jnp.bfloat16
    (own_amps,) = call(
        functools.partial(sweep_kernel, z),
        [(devices, n, pairs * n)],
        [smem] * 5 + [vmem] * 3 + [anywhere] * 3,
        (*lists, mp, left[:, :, fits:], start_amps, mp_below_other, left_below_other, right_other),
        [scratch(*rows, kind=bf16), scratch(*rows, kind=bf16)]
        + [scratch(pairs, wide, wide, kind=bf16)] * 2
        + [scratch(pairs, z.links // 2, n, 2 * n)],
        limit=6 + z.owners // 2,
    )
    amps = everyone(own_amps)

    args = (
        *lists, pno_coefficients, c_other, mp, mp_other, mp_below, mp_below_other,
        left, left_other, left_below, left_below_other, right, right_other, start_amps, amps,
    )
    amplitudes, gradient = call(
        functools.partial(final_kernel, z),
        [(pairs, n * n), (z.orbitals, half, fits)],
        [smem] * 5 + [anywhere] * 12 + [vmem] * 2,
        args,
        [
            scratch(2 * own, n, wide),
            scratch(own, n, half),
            scratch(2 * own, n, half),
            scratch(2 * own, EXTRA, z.paos),
            scratch(3 * own, n, fits),
            scratch(z.orbitals, half, fits),
            scratch(pairs, n, n),
            scratch(2 * own, z.links // 2, n, 2 * n),
            scratch(*rows, kind=bf16),
            scratch(*rows, kind=bf16),
        ]
        + [scratch(2 * own, wide, wide, kind=bf16)] * 2
        + [scratch(z.orbitals * half, 3 * own * n, kind=bf16)] * 2
        + [pltpu.SemaphoreType.DMA((20 + -(-fits // 256),))],
        limit=20 + z.owners // 2,
        out_specs=[vmem, hbm],
    )
    return (amplitudes, gradient)


def solution(mesh):
    in_specs = (
        P(("groups", "orb"), None, "fit"),
        P(("groups", "orb", "sub"), None, None),
        P(("groups", "orb", "sub"), None),
        P("groups"),
        P("groups"),
        P("groups"),
        P("groups", None),
        P(("groups", "orb", "sub"), None),
        P(("groups", "orb", "sub"), None, None),
        P(("groups", "orb", "sub"), None),
        P("groups"),
    )
    out_specs = (P(("groups", "orb", "sub"), None), P(("groups", "orb"), "sub", "fit"))
    return jax.shard_map(body, mesh=mesh, in_specs=in_specs, out_specs=out_specs, check_vma=False)
```

```python
import functools

import jax
import jax.numpy as jnp
from jax import lax
from jax.experimental import pallas as pl
from jax.experimental.pallas import tpu as pltpu
from jax.sharding import PartitionSpec as P

ITERS = 2
SMALL = 4
MIB = 1 << 20
EXTRA = 8

high = lax.Precision.HIGH
smem = pl.BlockSpec(memory_space=pltpu.SMEM)
vmem = pl.BlockSpec(memory_space=pltpu.VMEM)


def mm(a, b, contract=((1,), (0,))):
    return lax.dot_general(
        a, b, (contract, ((), ())), precision=high, preferred_element_type=jnp.float32
    )


def shifted(value, axis, steps):
    count = lax.axis_size(axis)
    initial, last = (max(0, -steps), min(count, count - steps))
    return lax.ppermute(value, axis, [(source, source + steps) for source in range(initial, last)])


def swapped(value, axis):
    return lax.ppermute(value, axis, [(0, 1), (1, 0)])


def f32(flag):
    return flag.astype(jnp.float32)


class Sizes:
    def __init__(self, blocks, pno_coefficients, couplings):
        self.orbitals, self.paos, self.fits = blocks.shape
        self.pairs, self.pnos = pno_coefficients.shape[:2]
        self.links = couplings.shape[1]
        self.subs = lax.axis_size("sub")
        self.owners = lax.axis_size("orb")
        self.fit_count = lax.axis_size("fit")
        self.own = self.pairs * self.subs
        self.total = self.own * self.owners


anywhere = pl.BlockSpec(memory_space=pl.ANY)
held_out = pl.BlockSpec(memory_space=pltpu.HBM)


def call(kernel, outs, ins, args, scratch=(), limit=16, out_specs=None):
    return pl.pallas_call(
        kernel,
        out_shape=[jax.ShapeDtypeStruct(shape, jnp.float32) for shape in outs],
        in_specs=ins,
        out_specs=out_specs or [vmem] * len(outs),
        scratch_shapes=list(scratch),
        compiler_params=pltpu.CompilerParams(vmem_limit_bytes=limit and limit * MIB),
    )(*args)


def started(sources, targets, sems, base=0):
    copies = [
        pltpu.make_async_copy(source, target, sems.at[base + index])
        for index, (source, target) in enumerate(zip(sources, targets))
    ]
    for copy in copies:
        copy.start()
    return copies


def wait(copies):
    for copy in copies:
        copy.wait()


def side_start(z, owner, sub, side):
    return owner * z.own + (sub if side == 0 else 1 - sub) * z.pairs


def scale_of(z, pair, level, first, second, ranks, occupied):
    n = z.pnos
    row_ids = lax.broadcasted_iota(jnp.int32, (n, n), 0)
    column_ids = lax.broadcasted_iota(jnp.int32, (n, n), 1)
    level = level * jnp.ones((n, 1), jnp.float32)
    rank = ranks[pair]
    kept = f32((row_ids < rank) & (column_ids < rank))
    return kept / (level + level.T - (occupied[first[pair]] + occupied[second[pair]]))


def split(value):
    high_part = value.astype(jnp.bfloat16)
    return high_part, (value - high_part.astype(jnp.float32)).astype(jnp.bfloat16)


def mm3(a, b, contract=((1,), (0,))):
    def one(x, y):
        return lax.dot_general(x, y, (contract, ((), ())), preferred_element_type=jnp.float32)

    return one(a[0], b[0]) + (one(a[0], b[1]) + one(a[1], b[0]))


def mapped_kernel(z, c_in, map_in, e_in, coupling_in, mp_ref, c_ref, map_ref, e_ref, coupling,
                  sems):
    n = z.pnos
    copies = started(
        [c_in, map_in, e_in, coupling_in], [c_ref, map_ref, e_ref, coupling], sems
    )
    wait(copies)
    rows = lax.broadcasted_iota(jnp.int32, (z.paos, z.paos), 0)
    lane_link = lax.broadcasted_iota(jnp.int32, (1, z.links * n), 1) // n
    for p in range(z.pairs):
        select = f32(map_ref[p : p + 1, :] == rows).astype(jnp.bfloat16)
        c_high, c_low = split(c_ref[p])
        mp_ref[p, :n, :] = lax.dot_general(
            c_high, select, (((1,), (1,)), ((), ())), preferred_element_type=jnp.float32
        ) + lax.dot_general(
            c_low, select, (((1,), (1,)), ((), ())), preferred_element_type=jnp.float32
        )
        mp_ref[p, n:, :] = jnp.zeros((EXTRA, z.paos), jnp.float32)
        mp_ref[p, n : n + 1, :n] = e_ref[p : p + 1, :]
        spread = jnp.zeros((1, z.links * n), jnp.float32)
        for k in range(z.links):
            spread = jnp.where(lane_link == k, coupling[p : p + 1, k : k + 1], spread)
        mp_ref[p, n + 1 : n + 2, :] = spread


def small(z):
    return z.owners <= SMALL and z.pairs == z.fit_count == 2


def each_pair(z, action):
    if z.owners <= SMALL:
        for pair in range(z.total):
            action(pair)
    else:
        @pl.loop(0, z.total)
        def _(pair):
            action(pair)


def pack_kernel(z, s_ref, mp_ref, order, out_ref):
    n = z.pnos
    line = 2 * n
    base = z.links * n // 2
    for slot in range(1 if small(z) else z.pairs):
        p = lax.axis_index("fit") if small(z) else slot
        at = 0 if small(z) else slot
        for r in range(n // 2):
            lines = s_ref[p, :, r * line : (r + 1) * line]
            for k in range(z.links):
                row = k * n // 2 + r
                out_ref[at, row : row + 1, :] = lines[k : k + 1, :]
        out_ref[at, base:, :] = jnp.zeros((EXTRA, line), jnp.float32)
        out_ref[at, base : base + 1, :] = mp_ref[p, n : n + 1, :line]
        for k in range(z.links // 2):
            out_ref[at, base + 1 + k : base + 2 + k, :] = mp_ref[
                p, n + 1 : n + 2, k * line : (k + 1) * line
            ]
    if small(z):
        for copy in range(1, z.owners):
            out_ref[copy] = out_ref[0]


def below_kernel(z, second, mp_below, b_ref, order, right_ref):
    owner, sub = lax.axis_index("orb"), lax.axis_index("sub")
    start = side_start(z, jnp.maximum(owner - 1, 0), sub, 0)
    for p in range(z.pairs):
        j = second[start + p] - owner * z.orbitals
        held = jnp.where(j >= 0, 1.0, 0.0)
        mapped = mp_below[p, : z.pnos, :] * held
        right_ref[p] = mm(mapped, b_ref[jnp.clip(j, 0, z.orbitals - 1)])


def left_kernel(z, first, c_ref, b_ref, left_ref):
    owner, sub = lax.axis_index("orb"), lax.axis_index("sub")
    start = side_start(z, owner, sub, 0)
    for p in range(z.pairs):
        left_ref[p] = mm(c_ref[p], b_ref[first[start + p] - owner * z.orbitals])


def here_kernel(z, second, mp_ref, b_ref, order, right_ref):
    owner, sub = lax.axis_index("orb"), lax.axis_index("sub")
    start = side_start(z, owner, sub, 0)
    for p in range(z.pairs):
        j = second[start + p] - owner * z.orbitals
        local = jnp.where(j < z.orbitals, 1.0, 0.0)
        right_ref[p] = mm(
            mp_ref[p, : z.pnos, :] * local, b_ref[jnp.minimum(j, z.orbitals - 1)]
        )


def sums_kernel(z, first, second, ranks, occupied, mp_ref, left_ref, here_ref, down_ref, *refs):
    sums_ref, right_ref = refs[-2:]
    owner, sub = lax.axis_index("orb"), lax.axis_index("sub")
    start = side_start(z, owner, sub, 0)
    n = z.pnos
    for p in range(z.pairs):
        right = here_ref[p] + down_ref[p]
        right_ref[p] = right
        scale = scale_of(
            z, start + p, mp_ref[p, n : n + 1, :n], first, second, ranks, occupied
        )
        part = mm(left_ref[p], right, ((1,), (1,)))
        sums_ref[:, p * n : (p + 1) * n] = -part * scale


def unpack_kernel(z, first, second, ranks, occupied, *refs):
    packs = refs[:-5]
    high_ref, low_ref, scale_ref, coupling_ref, rows = refs[-5:]
    sub, fit = lax.axis_index("sub"), lax.axis_index("fit")
    n = z.pnos
    base = z.links * n // 2

    def one(pair, block, slot):
        for k in range(0, z.links, 2):
            two = [block(k * n // 2, n // 2), block((k + 1) * n // 2, n // 2)]
            for odd in range(2):
                rows[slot, k // 2, pl.ds(odd, n // 2, 2), :] = jnp.concatenate(
                    [part[:, odd * n : (odd + 1) * n] for part in two], axis=1
                )
        s = jnp.concatenate([rows[slot, k] for k in range(z.links // 2)], axis=1)
        high_ref[pair], low_ref[pair] = split(s)
        extra = block(base, EXTRA)
        scale_ref[pair] = scale_of(z, pair, extra[0:1, :n], first, second, ranks, occupied)
        coupling_ref[pair, 0:1, :] = jnp.concatenate(
            [extra[1 + k : 2 + k, :] for k in range(z.links // 2)], axis=1
        )

    if small(z):
        for index, ref in enumerate(packs):
            side = sub if index < 2 else 1 - sub
            which = fit if index % 2 == 0 else 1 - fit
            for who in range(z.owners):
                one(
                    who * z.own + side * z.pairs + which,
                    lambda start, size: ref[who, start : start + size, :],
                    index * z.owners + who,
                )
    else:
        each_pair(
            z, lambda pair: one(pair, lambda start, size: packs[0][pair, pl.ds(start, size), :], 0)
        )


def coupled_of(z, index, pair, near, s, coupling, amps_high, amps_low, diag_high, diag_low):
    n = z.pnos
    for k in range(z.links):
        row = near[pair, k]
        block = slice(k * n, (k + 1) * n)
        diag_high[index, block, block] = amps_high[row]
        diag_low[index, block, block] = amps_low[row]
    return split(mm3(s, (diag_high[index], diag_low[index])) * coupling)


def final_kernel(z, first, second, near, *refs):
    start_count = 2 if small(z) else 1
    starts = refs[:start_count]
    s_high, s_low, scale_ref, coupling_ref = refs[start_count : start_count + 4]
    (c_in, c_other, mp_in, mp_other, mp_below, mp_below_other, left_in, left_other, left_below,
     left_below_other, right_in, right_other) = refs[start_count + 4 : start_count + 16]
    (amp_ref, grad_out, c_ref, m_ref, rhs, grad, flat, amps, amps_high, amps_low, next_high,
     next_low, diag_high, diag_low, rows_high, rows_low, sems) = refs[start_count + 16 :]
    owner, sub = lax.axis_index("orb"), lax.axis_index("sub")
    n, pairs, own = z.pnos, z.pairs, z.own
    half = z.paos // z.subs
    at = pl.ds(pl.multiple_of(sub * half, half), half)

    def quarters(ref, base=0):
        return [ref.at[pl.ds(base + i * pairs, pairs)] for i in range(4)]

    small_copies = started(
        [c_in.at[:, :, at], c_other.at[:, :, at]]
        + [ref.at[:, pl.ds(0, n), at] for ref in (mp_in, mp_other, mp_below, mp_below_other)],
        [c_ref.at[pl.ds(0, pairs)], c_ref.at[pl.ds(pairs, pairs)]] + quarters(m_ref),
        sems,
    )
    large_copies = started(
        [right_in, right_other, left_in, left_other, left_below, left_below_other],
        [rhs.at[pl.ds(0, pairs)], rhs.at[pl.ds(pairs, pairs)]] + quarters(rhs, own),
        sems, 6,
    )
    diag_high[...] = jnp.zeros_like(diag_high)
    diag_low[...] = jnp.zeros_like(diag_low)

    def begin(pair, value):
        amps[pair] = value
        amps_high[pair], amps_low[pair] = split(value)

    if small(z):
        for side, ref in ((sub, starts[0]), (1 - sub, starts[1])):
            for who in range(z.owners):
                for p in range(pairs):
                    begin(who * own + side * pairs + p, ref[who, :, p * n : (p + 1) * n])
    else:
        @pl.loop(0, z.owners * z.subs)
        def _(device):
            for p in range(pairs):
                begin(device * pairs + p, starts[0][device, :, p * n : (p + 1) * n])

    def s_of(pair):
        return s_high[pair], s_low[pair]

    def swept(index, pair, high_amps, low_amps):
        s = s_of(pair)
        inner = coupled_of(
            z, index, pair, near, s, coupling_ref[pair, 0:1, :], high_amps, low_amps, diag_high,
            diag_low,
        )
        return amps[pair] + mm3(inner, s, ((1,), (1,))) * scale_ref[pair]

    if z.owners <= SMALL:
        group = diag_high.shape[0]
        for base in range(0, z.total, group):
            pair_list = range(base, min(base + group, z.total))
            inner = [
                coupled_of(
                    z, index, pair, near, s_of(pair), coupling_ref[pair, 0:1, :], amps_high,
                    amps_low, diag_high, diag_low,
                )
                for index, pair in enumerate(pair_list)
            ]
            for value, pair in zip(inner, pair_list):
                coupled = mm3(value, s_of(pair), ((1,), (1,)))
                next_high[pair], next_low[pair] = split(amps[pair] + coupled * scale_ref[pair])
    else:
        @pl.loop(0, z.total)
        def _(pair):
            next_high[pair], next_low[pair] = split(swept(0, pair, amps_high, amps_low))

    pair_list = [
        side_start(z, who, sub, side) + p
        for who in (owner, jnp.maximum(owner - 1, 0))
        for side in range(z.subs)
        for p in range(pairs)
    ]
    inner = [
        coupled_of(
            z, index, pair, near, s_of(pair), coupling_ref[pair, 0:1, :], next_high, next_low,
            diag_high, diag_low,
        )
        for index, pair in enumerate(pair_list)
    ]
    found = [
        amps[pair] + mm3(value, s_of(pair), ((1,), (1,))) * scale_ref[pair]
        for value, pair in zip(inner, pair_list)
    ]
    turned = [value.T for value in found]
    wait(small_copies)
    weights = [split(2.0 * a - b) for a, b in zip(found, turned)]
    weights_turned = [split(2.0 * b - a) for a, b in zip(found[:own], turned[:own])]
    terms = (
        [mm3(w, split(c_ref[i])) for i, w in enumerate(weights_turned)]
        + [mm3(w, split(m_ref[i])) for i, w in enumerate(weights)]
    )
    orbital_list = (
        [first[pair] - owner * z.orbitals for pair in pair_list[:own]]
        + [second[pair] - owner * z.orbitals for pair in pair_list]
    )
    for index in range(0, 3 * own, 2):
        for o in range(z.orbitals):
            block = jnp.concatenate(
                [
                    jnp.where(orbital_list[i] == o, terms[i], 0.0) for i in (index, index + 1)
                ]
            ).T
            place = (slice(o * half, (o + 1) * half), slice(index * n, (index + 2) * n))
            rows_high[place], rows_low[place] = split(block)

    for p in range(pairs):
        flat[p] = found[p]
        even = flat[p, pl.ds(0, n // 2, 2), :]
        odd = flat[p, pl.ds(1, n // 2, 2), :]
        lines = jnp.concatenate([even, odd], axis=1)
        for r in range(n // 2):
            amp_ref[p : p + 1, r * 2 * n : (r + 1) * 2 * n] = lines[r : r + 1, :]

    wait(large_copies)
    step = 256
    rows = (rows_high[...], rows_low[...])
    copies = []
    for index, start in enumerate(range(0, z.fits, step)):
        factor = rhs[:, :, start : start + step].reshape(3 * own * n, step)
        grad[:, :, start : start + step] = mm3(rows, split(factor)).reshape(
            z.orbitals, half, step
        )
        window = pl.ds(start, step)
        copies += started(
            [grad.at[:, :, window]], [grad_out.at[:, :, window]], sems, 12 + index
        )
    wait(copies)


def gate(values, *after):
    return lax.optimization_barrier((tuple(values), after))[0]


def body(
    blocks,
    pno_coefficients,
    domain_map,
    pair_first,
    pair_second,
    pno_ranks,
    neighbours,
    couplings,
    intersections,
    pno_energy,
    occ_energy,
):
    z = Sizes(blocks, pno_coefficients, couplings)
    n, pairs, own, fits = z.pnos, z.pairs, z.own, z.fits
    half = z.paos // z.subs
    wide = z.links * n
    hbm = held_out
    bf16 = jnp.bfloat16
    more = 0 if z.owners <= SMALL else z.owners

    def scratch(*shape, kind=jnp.float32):
        return pltpu.VMEM(shape, kind)

    (mp,) = call(
        functools.partial(mapped_kernel, z),
        [(pairs, n + EXTRA, z.paos)],
        [hbm] * 4,
        (pno_coefficients, domain_map, pno_energy, couplings),
        [
            scratch(*pno_coefficients.shape),
            pltpu.VMEM(domain_map.shape, jnp.int32),
            scratch(*pno_energy.shape),
            scratch(*couplings.shape),
            pltpu.SemaphoreType.DMA((4,)),
        ],
        limit=None,
    )
    mp_below = shifted(mp, "orb", 1)
    pack_shape = (z.owners if small(z) else pairs, z.links * n // 2 + EXTRA, 2 * n)
    (pack,) = call(
        functools.partial(pack_kernel, z),
        [pack_shape],
        [vmem, vmem, anywhere],
        (intersections, mp, mp),
        limit=8,
    )
    if small(z):
        packs = [lax.all_to_all(pack, "orb", 0, 0)]
    else:
        packs = [lax.all_gather(pack, ("orb", "sub"), axis=0, tiled=True)]
    (right_below,) = call(
        functools.partial(below_kernel, z),
        [(pairs, n, fits)],
        [smem, vmem, vmem, anywhere],
        (pair_second, mp_below, blocks, pack),
        limit=8,
    )
    down = shifted(right_below, "orb", -1)
    (coefficients,) = gate((pno_coefficients,), right_below)
    (left,) = call(
        functools.partial(left_kernel, z),
        [(pairs, n, fits)],
        [smem, vmem, vmem],
        (pair_first, coefficients, blocks),
        limit=8,
    )
    (right_here,) = call(
        functools.partial(here_kernel, z),
        [(pairs, n, fits)],
        [smem, vmem, vmem, anywhere],
        (pair_second, mp, blocks, left),
        limit=8,
    )
    left_late, mp_late, coefficients = gate((left, mp, coefficients), right_here)
    left_below = shifted(left_late, "orb", 1)
    mp_other = swapped(mp_late, "sub")
    left_other = swapped(left_late, "sub")
    c_other = swapped(coefficients, "sub")
    if small(z):
        packs.append(swapped(gate(packs, right_here)[0], "fit"))

    lists = (pair_first, pair_second, pno_ranks)
    part, right = call(
        functools.partial(sums_kernel, z),
        [(n, pairs * n), (pairs, n, fits)],
        [smem] * 4 + [vmem] * 4 + [anywhere] * 3,
        (*lists, occ_energy, mp, left, right_here, down, left_other, mp_other, c_other),
        limit=8,
    )
    if small(z):
        packs += [swapped(value, "sub") for value in gate(packs, part)]
        sums = part + swapped(part, "fit")
        start_amps = [
            lax.all_to_all(jnp.broadcast_to(sums[None], (z.owners, *sums.shape)), "orb", 0, 0)
        ]
        start_amps.append(swapped(start_amps[0], "sub"))
    else:
        sums = lax.psum(part, "fit")
        start_amps = [lax.all_gather(sums, ("orb", "sub"), axis=0, tiled=False)]

    right_late, mp_late = gate((right, mp_below), part)
    (left_late,) = gate((left_below,), sums)
    right_other, mp_below_other, left_below_other = [
        swapped(value, "sub") for value in (right_late, mp_late, left_late)
    ]

    split_shape = jax.ShapeDtypeStruct((z.total, n, wide), bf16)
    unpacked = pl.pallas_call(
        functools.partial(unpack_kernel, z),
        out_shape=[
            split_shape,
            split_shape,
            jax.ShapeDtypeStruct((z.total, n, n), jnp.float32),
            jax.ShapeDtypeStruct((z.total, EXTRA, wide), jnp.float32),
        ],
        in_specs=[smem] * 4 + [vmem] * len(packs),
        out_specs=[vmem] * 4,
        scratch_shapes=[scratch(z.total if small(z) else 1, z.links // 2, n, 2 * n)],
        compiler_params=pltpu.CompilerParams(vmem_limit_bytes=(16 + more) * MIB),
    )(*lists, occ_energy, *packs)

    args = (
        pair_first, pair_second, neighbours, *start_amps, *unpacked,
        pno_coefficients, c_other, mp, mp_other, mp_below, mp_below_other,
        left, left_other, left_below, left_below_other, right, right_other,
    )
    group = own * 2
    square = (z.total, n, n)
    amplitudes, gradient = call(
        functools.partial(final_kernel, z),
        [(pairs, n * n), (z.orbitals, half, fits)],
        [smem] * 3 + [vmem] * (len(start_amps) + 4) + [hbm] * 12,
        args,
        [
            scratch(own, n, half),
            scratch(2 * own, n, half),
            scratch(3 * own, n, fits),
            scratch(z.orbitals, half, fits),
            scratch(pairs, n, n),
            scratch(*square),
        ]
        + [scratch(*square, kind=bf16)] * 4
        + [scratch(group, wide, wide, kind=bf16)] * 2
        + [scratch(z.orbitals * half, 3 * own * n, kind=bf16)] * 2
        + [pltpu.SemaphoreType.DMA((12 + -(-fits // 256),))],
        limit=40 + more // 2,
        out_specs=[vmem, hbm],
    )
    return (amplitudes, gradient)


def solution(mesh):
    in_specs = (
        P(("groups", "orb"), None, "fit"),
        P(("groups", "orb", "sub"), None, None),
        P(("groups", "orb", "sub"), None),
        P("groups"),
        P("groups"),
        P("groups"),
        P("groups", None),
        P(("groups", "orb", "sub"), None),
        P(("groups", "orb", "sub"), None, None),
        P(("groups", "orb", "sub"), None),
        P("groups"),
    )
    out_specs = (P(("groups", "orb", "sub"), None), P(("groups", "orb"), "sub", "fit"))
    return jax.shard_map(body, mesh=mesh, in_specs=in_specs, out_specs=out_specs, check_vma=False)
```

```python
import functools

import jax
import jax.numpy as jnp
from jax import lax
from jax.experimental import pallas as pl
from jax.experimental.pallas import tpu as pltpu
from jax.sharding import PartitionSpec as P

ITERS = 2
SMALL = 4
MIB = 1 << 20
EXTRA = 8

high = lax.Precision.HIGH
LONG = pl.CostEstimate(flops=5 * 10**9, bytes_accessed=8 * MIB, transcendentals=0)
smem = pl.BlockSpec(memory_space=pltpu.SMEM)
vmem = pl.BlockSpec(memory_space=pltpu.VMEM)


def mm(a, b, contract=((1,), (0,))):
    return lax.dot_general(
        a, b, (contract, ((), ())), precision=high, preferred_element_type=jnp.float32
    )


def shifted(value, axis, steps):
    count = lax.axis_size(axis)
    initial, last = (max(0, -steps), min(count, count - steps))
    return lax.ppermute(value, axis, [(source, source + steps) for source in range(initial, last)])


def swapped(value, axis):
    return lax.ppermute(value, axis, [(0, 1), (1, 0)])


def f32(flag):
    return flag.astype(jnp.float32)


class Sizes:
    def __init__(self, blocks, pno_coefficients, couplings):
        self.orbitals, self.paos, self.fits = blocks.shape
        self.pairs, self.pnos = pno_coefficients.shape[:2]
        self.links = couplings.shape[1]
        self.subs = lax.axis_size("sub")
        self.owners = lax.axis_size("orb")
        self.fit_count = lax.axis_size("fit")
        self.own = self.pairs * self.subs
        self.total = self.own * self.owners


anywhere = pl.BlockSpec(memory_space=pl.ANY)
held_out = pl.BlockSpec(memory_space=pltpu.HBM)


def call(kernel, outs, ins, args, scratch=(), limit=16, out_specs=None, cost=None):
    return pl.pallas_call(
        kernel,
        out_shape=[jax.ShapeDtypeStruct(shape, jnp.float32) for shape in outs],
        in_specs=ins,
        out_specs=out_specs or [vmem] * len(outs),
        scratch_shapes=list(scratch),
        cost_estimate=cost,
        compiler_params=pltpu.CompilerParams(vmem_limit_bytes=limit and limit * MIB),
    )(*args)


def started(sources, targets, sems, base=0):
    copies = [
        pltpu.make_async_copy(source, target, sems.at[base + index])
        for index, (source, target) in enumerate(zip(sources, targets))
    ]
    for copy in copies:
        copy.start()
    return copies


def wait(copies):
    for copy in copies:
        copy.wait()


def side_start(z, owner, sub, side):
    return owner * z.own + (sub if side == 0 else 1 - sub) * z.pairs


def scale_of(z, pair, level, first, second, ranks, occupied):
    n = z.pnos
    row_ids = lax.broadcasted_iota(jnp.int32, (n, n), 0)
    column_ids = lax.broadcasted_iota(jnp.int32, (n, n), 1)
    level = level * jnp.ones((n, 1), jnp.float32)
    rank = ranks[pair]
    kept = f32((row_ids < rank) & (column_ids < rank))
    return kept / (level + level.T - (occupied[first[pair]] + occupied[second[pair]]))


def split(value):
    high_part = value.astype(jnp.bfloat16)
    return high_part, (value - high_part.astype(jnp.float32)).astype(jnp.bfloat16)


def mm3(a, b, contract=((1,), (0,))):
    def one(x, y):
        return lax.dot_general(x, y, (contract, ((), ())), preferred_element_type=jnp.float32)

    return one(a[0], b[0]) + (one(a[0], b[1]) + one(a[1], b[0]))


def small(z):
    return z.owners <= SMALL and z.pairs == z.fit_count == 2


def each_pair(z, action):
    if z.owners <= SMALL:
        for pair in range(z.total):
            action(pair)
    else:
        @pl.loop(0, z.total)
        def _(pair):
            action(pair)


def mapped_kernel(z, c_in, map_in, e_in, coupling_in, mp_ref, c_ref, map_ref, e_ref, coupling,
                  sems):
    n = z.pnos
    copies = started(
        [c_in, map_in, e_in, coupling_in], [c_ref, map_ref, e_ref, coupling], sems
    )
    wait(copies)
    rows = lax.broadcasted_iota(jnp.int32, (z.paos, z.paos), 0)
    lane_link = lax.broadcasted_iota(jnp.int32, (1, z.links * n), 1) // n
    for p in range(z.pairs):
        select = f32(map_ref[p : p + 1, :] == rows).astype(jnp.bfloat16)
        c_high, c_low = split(c_ref[p])
        mp_ref[p, :n, :] = lax.dot_general(
            c_high, select, (((1,), (1,)), ((), ())), preferred_element_type=jnp.float32
        ) + lax.dot_general(
            c_low, select, (((1,), (1,)), ((), ())), preferred_element_type=jnp.float32
        )
        mp_ref[p, n:, :] = jnp.zeros((EXTRA, z.paos), jnp.float32)
        mp_ref[p, n : n + 1, :n] = e_ref[p : p + 1, :]
        spread = jnp.zeros((1, z.links * n), jnp.float32)
        for k in range(z.links):
            spread = jnp.where(lane_link == k, coupling[p : p + 1, k : k + 1], spread)
        mp_ref[p, n + 1 : n + 2, :] = spread


def pack_kernel(z, s_in, mp_in, pack_ref, s_ref, mp_ref, sems):
    n = z.pnos
    line = 2 * n
    base = z.links * n // 2
    wait(started([s_in, mp_in.at[:, pl.ds(n, EXTRA), :]], [s_ref, mp_ref], sems))
    for slot in range(1 if small(z) else z.pairs):
        p = lax.axis_index("fit") if small(z) else slot
        for r in range(n // 2):
            lines = s_ref[p, :, r * line : (r + 1) * line]
            for k in range(z.links):
                row = k * n // 2 + r
                pack_ref[slot, row : row + 1, :] = lines[k : k + 1, :]
        pack_ref[slot, base:, :] = jnp.zeros((EXTRA, line), jnp.float32)
        pack_ref[slot, base : base + 1, :] = mp_ref[p, 0:1, :line]
        for k in range(z.links // 2):
            pack_ref[slot, base + 1 + k : base + 2 + k, :] = mp_ref[
                p, 1:2, k * line : (k + 1) * line
            ]
    if small(z):
        for copy in range(1, z.owners):
            pack_ref[copy] = pack_ref[0]


def below_kernel(z, second_in, mp_below, b_in, order, right_ref, second, m_ref, b_ref, sems):
    owner, sub = lax.axis_index("orb"), lax.axis_index("sub")
    start = side_start(z, jnp.maximum(owner - 1, 0), sub, 0)
    wait(started([second_in], [second], sems))
    m_copies = started([mp_below.at[:, pl.ds(0, z.pnos), :]], [m_ref], sems)
    b_copies, held = [], []
    for p in range(z.pairs):
        j = second[start + p] - owner * z.orbitals
        held.append(jnp.where(j >= 0, 1.0, 0.0))
        b_copies += started([b_in.at[jnp.clip(j, 0, z.orbitals - 1)]], [b_ref.at[p]], sems, 1 + p)
    wait(m_copies)
    for p in range(z.pairs):
        wait(b_copies[p : p + 1])
        right_ref[p] = mm(m_ref[p] * held[p], b_ref[p])


def local_kernel(z, first, second, c_ref, mp_ref, b_ref, left_ref, right_ref):
    owner, sub = lax.axis_index("orb"), lax.axis_index("sub")
    start = side_start(z, owner, sub, 0)
    base = owner * z.orbitals
    for p in range(z.pairs):
        left_ref[p] = mm(c_ref[p], b_ref[first[start + p] - base])
        j = second[start + p] - base
        local = jnp.where(j < z.orbitals, 1.0, 0.0)
        right_ref[p] = mm(
            mp_ref[p, : z.pnos, :] * local, b_ref[jnp.minimum(j, z.orbitals - 1)]
        )


def sums_kernel(z, first, second, ranks, occupied, mp_ref, left_ref, here_ref, down_ref, *refs):
    sums_ref, right_ref = refs[-2:]
    owner, sub = lax.axis_index("orb"), lax.axis_index("sub")
    start = side_start(z, owner, sub, 0)
    n = z.pnos
    for p in range(z.pairs):
        right = here_ref[p] + down_ref[p]
        right_ref[p] = right
        scale = scale_of(
            z, start + p, mp_ref[p, n : n + 1, :n], first, second, ranks, occupied
        )
        part = mm(left_ref[p], right, ((1,), (1,)))
        sums_ref[:, p * n : (p + 1) * n] = -part * scale


def unpack_kernel(z, first, second, ranks, occupied, *refs):
    packs = refs[:-5]
    high_ref, low_ref, scale_ref, coupling_ref, rows = refs[-5:]
    sub, fit = lax.axis_index("sub"), lax.axis_index("fit")
    n = z.pnos
    base = z.links * n // 2

    def one(pair, block, slot):
        for k in range(0, z.links, 2):
            two = [block(k * n // 2, n // 2), block((k + 1) * n // 2, n // 2)]
            for odd in range(2):
                rows[slot, k // 2, pl.ds(odd, n // 2, 2), :] = jnp.concatenate(
                    [part[:, odd * n : (odd + 1) * n] for part in two], axis=1
                )
        s = jnp.concatenate([rows[slot, k] for k in range(z.links // 2)], axis=1)
        high_ref[pair], low_ref[pair] = split(s)
        extra = block(base, EXTRA)
        scale_ref[pair] = scale_of(z, pair, extra[0:1, :n], first, second, ranks, occupied)
        coupling_ref[pair, 0:1, :] = jnp.concatenate(
            [extra[1 + k : 2 + k, :] for k in range(z.links // 2)], axis=1
        )

    if small(z):
        for index, ref in enumerate(packs):
            side = sub if index < 2 else 1 - sub
            which = fit if index % 2 == 0 else 1 - fit
            for who in range(z.owners):
                one(
                    who * z.own + side * z.pairs + which,
                    lambda start, size: ref[who, start : start + size, :],
                    index * z.owners + who,
                )
    else:
        each_pair(
            z, lambda pair: one(pair, lambda start, size: packs[0][pair, pl.ds(start, size), :], 0)
        )


def coupled_of(z, index, pair, near, s, coupling, amps_high, amps_low, diag_high, diag_low):
    n = z.pnos
    for k in range(z.links):
        row = near[pair, k]
        block = slice(k * n, (k + 1) * n)
        diag_high[index, block, block] = amps_high[row]
        diag_low[index, block, block] = amps_low[row]
    return split(mm3(s, (diag_high[index], diag_low[index])) * coupling)


def final_kernel(z, first, second, near, *refs):
    start_count = 2 if small(z) else 1
    starts = refs[:start_count]
    s_high, s_low, scale_ref, coupling_ref = refs[start_count : start_count + 4]
    (c_in, c_other, mp_in, mp_other, mp_below, mp_below_other, left_in, left_other, left_below,
     left_below_other, right_in, right_other) = refs[start_count + 4 : start_count + 16]
    (amp_ref, grad_out, c_ref, m_ref, rhs, grad, flat, amps, amps_high, amps_low, next_high,
     next_low, diag_high, diag_low, rows_high, rows_low, sems) = refs[start_count + 16 :]
    owner, sub = lax.axis_index("orb"), lax.axis_index("sub")
    n, pairs, own = z.pnos, z.pairs, z.own
    half = z.paos // z.subs
    at = pl.ds(pl.multiple_of(sub * half, half), half)

    def quarters(ref, base=0):
        return [ref.at[pl.ds(base + i * pairs, pairs)] for i in range(4)]

    small_copies = started(
        [c_in.at[:, :, at], c_other.at[:, :, at]]
        + [ref.at[:, pl.ds(0, n), at] for ref in (mp_in, mp_other, mp_below, mp_below_other)],
        [c_ref.at[pl.ds(0, pairs)], c_ref.at[pl.ds(pairs, pairs)]] + quarters(m_ref),
        sems,
    )
    large_copies = started(
        [right_in, right_other, left_in, left_other, left_below, left_below_other],
        [rhs.at[pl.ds(0, pairs)], rhs.at[pl.ds(pairs, pairs)]] + quarters(rhs, own),
        sems, 6,
    )
    diag_high[...] = jnp.zeros_like(diag_high)
    diag_low[...] = jnp.zeros_like(diag_low)

    def begin(pair, value):
        amps[pair] = value
        amps_high[pair], amps_low[pair] = split(value)

    if small(z):
        for side, ref in ((sub, starts[0]), (1 - sub, starts[1])):
            for who in range(z.owners):
                for p in range(pairs):
                    begin(who * own + side * pairs + p, ref[who, :, p * n : (p + 1) * n])
    else:
        @pl.loop(0, z.owners * z.subs)
        def _(device):
            for p in range(pairs):
                begin(device * pairs + p, starts[0][device, :, p * n : (p + 1) * n])

    def s_of(pair):
        return s_high[pair], s_low[pair]

    def swept(index, pair, high_amps, low_amps):
        s = s_of(pair)
        inner = coupled_of(
            z, index, pair, near, s, coupling_ref[pair, 0:1, :], high_amps, low_amps, diag_high,
            diag_low,
        )
        return amps[pair] + mm3(inner, s, ((1,), (1,))) * scale_ref[pair]

    if z.owners <= SMALL:
        group = diag_high.shape[0]
        for base in range(0, z.total, group):
            pair_list = range(base, min(base + group, z.total))
            inner = [
                coupled_of(
                    z, index, pair, near, s_of(pair), coupling_ref[pair, 0:1, :], amps_high,
                    amps_low, diag_high, diag_low,
                )
                for index, pair in enumerate(pair_list)
            ]
            for value, pair in zip(inner, pair_list):
                coupled = mm3(value, s_of(pair), ((1,), (1,)))
                next_high[pair], next_low[pair] = split(amps[pair] + coupled * scale_ref[pair])
    else:
        @pl.loop(0, z.total)
        def _(pair):
            next_high[pair], next_low[pair] = split(swept(0, pair, amps_high, amps_low))

    pair_list = [
        side_start(z, who, sub, side) + p
        for who in (owner, jnp.maximum(owner - 1, 0))
        for side in range(z.subs)
        for p in range(pairs)
    ]
    inner = [
        coupled_of(
            z, index, pair, near, s_of(pair), coupling_ref[pair, 0:1, :], next_high, next_low,
            diag_high, diag_low,
        )
        for index, pair in enumerate(pair_list)
    ]
    found = [
        amps[pair] + mm3(value, s_of(pair), ((1,), (1,))) * scale_ref[pair]
        for value, pair in zip(inner, pair_list)
    ]
    turned = [value.T for value in found]
    wait(small_copies)
    weights = [split(2.0 * a - b) for a, b in zip(found, turned)]
    weights_turned = [split(2.0 * b - a) for a, b in zip(found[:own], turned[:own])]
    terms = (
        [mm3(w, split(c_ref[i])) for i, w in enumerate(weights_turned)]
        + [mm3(w, split(m_ref[i])) for i, w in enumerate(weights)]
    )
    orbital_list = (
        [first[pair] - owner * z.orbitals for pair in pair_list[:own]]
        + [second[pair] - owner * z.orbitals for pair in pair_list]
    )
    for index in range(0, 3 * own, 2):
        for o in range(z.orbitals):
            block = jnp.concatenate(
                [
                    jnp.where(orbital_list[i] == o, terms[i], 0.0) for i in (index, index + 1)
                ]
            ).T
            place = (slice(o * half, (o + 1) * half), slice(index * n, (index + 2) * n))
            rows_high[place], rows_low[place] = split(block)

    for p in range(pairs):
        flat[p] = found[p]
        even = flat[p, pl.ds(0, n // 2, 2), :]
        odd = flat[p, pl.ds(1, n // 2, 2), :]
        lines = jnp.concatenate([even, odd], axis=1)
        for r in range(n // 2):
            amp_ref[p : p + 1, r * 2 * n : (r + 1) * 2 * n] = lines[r : r + 1, :]

    wait(large_copies)
    step = 256
    rows = (rows_high[...], rows_low[...])
    copies = []
    for index, start in enumerate(range(0, z.fits, step)):
        factor = rhs[:, :, start : start + step].reshape(3 * own * n, step)
        grad[:, :, start : start + step] = mm3(rows, split(factor)).reshape(
            z.orbitals, half, step
        )
        window = pl.ds(start, step)
        copies += started(
            [grad.at[:, :, window]], [grad_out.at[:, :, window]], sems, 12 + index
        )
    wait(copies)


def gate(values, *after):
    return lax.optimization_barrier((tuple(values), after))[0]


def body(
    blocks,
    pno_coefficients,
    domain_map,
    pair_first,
    pair_second,
    pno_ranks,
    neighbours,
    couplings,
    intersections,
    pno_energy,
    occ_energy,
):
    z = Sizes(blocks, pno_coefficients, couplings)
    n, pairs, own, fits = z.pnos, z.pairs, z.own, z.fits
    half = z.paos // z.subs
    wide = z.links * n
    hbm = held_out
    bf16 = jnp.bfloat16
    more = 0 if z.owners <= SMALL else z.owners

    def scratch(*shape, kind=jnp.float32):
        return pltpu.VMEM(shape, kind)

    pack_shape = (z.owners if small(z) else pairs, z.links * n // 2 + EXTRA, 2 * n)
    (mp,) = call(
        functools.partial(mapped_kernel, z),
        [(pairs, n + EXTRA, z.paos)],
        [hbm] * 4,
        (pno_coefficients, domain_map, pno_energy, couplings),
        [
            scratch(*pno_coefficients.shape),
            pltpu.VMEM(domain_map.shape, jnp.int32),
            scratch(*pno_energy.shape),
            scratch(*couplings.shape),
            pltpu.SemaphoreType.DMA((4,)),
        ],
        limit=None,
    )
    mp_below = shifted(mp, "orb", 1)
    (pack,) = call(
        functools.partial(pack_kernel, z),
        [pack_shape],
        [hbm] * 2,
        (intersections, mp),
        [
            scratch(*intersections.shape),
            scratch(pairs, EXTRA, z.paos),
            pltpu.SemaphoreType.DMA((2,)),
        ],
        limit=None,
    )
    if small(z):
        packs = [lax.all_to_all(pack, "orb", 0, 0)]
    else:
        packs = [lax.all_gather(pack, ("orb", "sub"), axis=0, tiled=True)]
    (right_below,) = call(
        functools.partial(below_kernel, z),
        [(pairs, n, fits)],
        [hbm] * 4,
        (pair_second, mp_below, blocks, pack),
        [
            pltpu.SMEM(pair_second.shape, jnp.int32),
            scratch(pairs, n, z.paos),
            scratch(pairs, *blocks.shape[1:]),
            pltpu.SemaphoreType.DMA((1 + pairs,)),
        ],
        limit=None,
    )
    down = shifted(right_below, "orb", -1)
    (coefficients,) = gate((pno_coefficients,), right_below)
    left, right_here = call(
        functools.partial(local_kernel, z),
        [(pairs, n, fits), (pairs, n, fits)],
        [smem, smem, vmem, vmem, vmem],
        (pair_first, pair_second, coefficients, mp, blocks),
        limit=8,
        cost=LONG,
    )
    left_late, mp_late, coefficients = gate((left, mp, coefficients), right_here)
    left_below = shifted(left_late, "orb", 1)
    mp_other = swapped(mp_late, "sub")
    left_other = swapped(left_late, "sub")
    c_other = swapped(coefficients, "sub")
    if small(z):
        packs.append(swapped(gate(packs, right_below)[0], "fit"))
        packs += [swapped(value, "sub") for value in gate(packs, right_here)]

    lists = (pair_first, pair_second, pno_ranks)
    split_shape = jax.ShapeDtypeStruct((z.total, n, wide), bf16)
    unpacked = pl.pallas_call(
        functools.partial(unpack_kernel, z),
        out_shape=[
            split_shape,
            split_shape,
            jax.ShapeDtypeStruct((z.total, n, n), jnp.float32),
            jax.ShapeDtypeStruct((z.total, EXTRA, wide), jnp.float32),
        ],
        in_specs=[smem] * 4 + [vmem] * len(packs),
        out_specs=[vmem] * 4,
        scratch_shapes=[scratch(z.total if small(z) else 1, z.links // 2, n, 2 * n)],
        cost_estimate=LONG,
        compiler_params=pltpu.CompilerParams(vmem_limit_bytes=(16 + more) * MIB),
    )(*lists, occ_energy, *packs)

    part, right = call(
        functools.partial(sums_kernel, z),
        [(n, pairs * n), (pairs, n, fits)],
        [smem] * 4 + [vmem] * 4 + [anywhere] * 4,
        (*lists, occ_energy, mp, left, right_here, down, left_other, mp_other, c_other,
         unpacked[0]),
        limit=8,
    )
    if small(z):
        sums = part + swapped(part, "fit")
        start_amps = [
            lax.all_to_all(jnp.broadcast_to(sums[None], (z.owners, *sums.shape)), "orb", 0, 0)
        ]
        start_amps.append(swapped(start_amps[0], "sub"))
    else:
        sums = lax.psum(part, "fit")
        start_amps = [lax.all_gather(sums, ("orb", "sub"), axis=0, tiled=False)]

    right_late, mp_late = gate((right, mp_below), part)
    (left_late,) = gate((left_below,), sums)
    right_other, mp_below_other, left_below_other = [
        swapped(value, "sub") for value in (right_late, mp_late, left_late)
    ]

    args = (
        pair_first, pair_second, neighbours, *start_amps, *unpacked,
        pno_coefficients, c_other, mp, mp_other, mp_below, mp_below_other,
        left, left_other, left_below, left_below_other, right, right_other,
    )
    group = own * 2
    square = (z.total, n, n)
    amplitudes, gradient = call(
        functools.partial(final_kernel, z),
        [(pairs, n * n), (z.orbitals, half, fits)],
        [smem] * 3 + [vmem] * (len(start_amps) + 4) + [hbm] * 12,
        args,
        [
            scratch(own, n, half),
            scratch(2 * own, n, half),
            scratch(3 * own, n, fits),
            scratch(z.orbitals, half, fits),
            scratch(pairs, n, n),
            scratch(*square),
        ]
        + [scratch(*square, kind=bf16)] * 4
        + [scratch(group, wide, wide, kind=bf16)] * 2
        + [scratch(z.orbitals * half, 3 * own * n, kind=bf16)] * 2
        + [pltpu.SemaphoreType.DMA((12 + -(-fits // 256),))],
        limit=40 + more // 2,
        out_specs=[vmem, hbm],
    )
    return (amplitudes, gradient)


def solution(mesh):
    in_specs = (
        P(("groups", "orb"), None, "fit"),
        P(("groups", "orb", "sub"), None, None),
        P(("groups", "orb", "sub"), None),
        P("groups"),
        P("groups"),
        P("groups"),
        P("groups", None),
        P(("groups", "orb", "sub"), None),
        P(("groups", "orb", "sub"), None, None),
        P(("groups", "orb", "sub"), None),
        P("groups"),
    )
    out_specs = (P(("groups", "orb", "sub"), None), P(("groups", "orb"), "sub", "fit"))
    return jax.shard_map(body, mesh=mesh, in_specs=in_specs, out_specs=out_specs, check_vma=False)
```

```python
import functools

import jax
import jax.numpy as jnp
from jax import lax
from jax.experimental import pallas as pl
from jax.experimental.pallas import tpu as pltpu
from jax.sharding import PartitionSpec as P

ITERS = 2
SMALL = 4
MIB = 1 << 20
EXTRA = 8

high = lax.Precision.HIGH
BRIEF = pl.CostEstimate(flops=1, bytes_accessed=1, transcendentals=0)
smem = pl.BlockSpec(memory_space=pltpu.SMEM)
vmem = pl.BlockSpec(memory_space=pltpu.VMEM)


def mm(a, b, contract=((1,), (0,))):
    return lax.dot_general(
        a, b, (contract, ((), ())), precision=high, preferred_element_type=jnp.float32
    )


def shifted(value, axis, steps):
    count = lax.axis_size(axis)
    initial, last = (max(0, -steps), min(count, count - steps))
    return lax.ppermute(value, axis, [(source, source + steps) for source in range(initial, last)])


def swapped(value, axis):
    return lax.ppermute(value, axis, [(0, 1), (1, 0)])


def f32(flag):
    return flag.astype(jnp.float32)


class Sizes:
    def __init__(self, blocks, pno_coefficients, couplings):
        self.orbitals, self.paos, self.fits = blocks.shape
        self.pairs, self.pnos = pno_coefficients.shape[:2]
        self.links = couplings.shape[1]
        self.subs = lax.axis_size("sub")
        self.owners = lax.axis_size("orb")
        self.fit_count = lax.axis_size("fit")
        self.own = self.pairs * self.subs
        self.total = self.own * self.owners


anywhere = pl.BlockSpec(memory_space=pl.ANY)
held_out = pl.BlockSpec(memory_space=pltpu.HBM)


def call(kernel, outs, ins, args, scratch=(), limit=16, out_specs=None, cost=BRIEF):
    return pl.pallas_call(
        kernel,
        out_shape=[jax.ShapeDtypeStruct(shape, jnp.float32) for shape in outs],
        in_specs=ins,
        out_specs=out_specs or [vmem] * len(outs),
        scratch_shapes=list(scratch),
        cost_estimate=cost,
        compiler_params=pltpu.CompilerParams(vmem_limit_bytes=limit and limit * MIB),
    )(*args)


def started(sources, targets, sems, base=0):
    copies = [
        pltpu.make_async_copy(source, target, sems.at[base + index])
        for index, (source, target) in enumerate(zip(sources, targets))
    ]
    for copy in copies:
        copy.start()
    return copies


def wait(copies):
    for copy in copies:
        copy.wait()


def side_start(z, owner, sub, side):
    return owner * z.own + (sub if side == 0 else 1 - sub) * z.pairs


def scale_of(z, pair, level, first, second, ranks, occupied):
    n = z.pnos
    row_ids = lax.broadcasted_iota(jnp.int32, (n, n), 0)
    column_ids = lax.broadcasted_iota(jnp.int32, (n, n), 1)
    level = level * jnp.ones((n, 1), jnp.float32)
    rank = ranks[pair]
    kept = f32((row_ids < rank) & (column_ids < rank))
    return kept / (level + level.T - (occupied[first[pair]] + occupied[second[pair]]))


def split(value):
    high_part = value.astype(jnp.bfloat16)
    return high_part, (value - high_part.astype(jnp.float32)).astype(jnp.bfloat16)


def mm3(a, b, contract=((1,), (0,))):
    def one(x, y):
        return lax.dot_general(x, y, (contract, ((), ())), preferred_element_type=jnp.float32)

    return one(a[0], b[0]) + (one(a[0], b[1]) + one(a[1], b[0]))


def small(z):
    return z.owners <= SMALL and z.pairs == z.fit_count == 2


def each_pair(z, action):
    if z.owners <= SMALL:
        for pair in range(z.total):
            action(pair)
    else:
        @pl.loop(0, z.total)
        def _(pair):
            action(pair)


def mapped_kernel(z, c_in, map_in, e_in, coupling_in, mp_ref, c_ref, map_ref, e_ref, coupling,
                  sems):
    n = z.pnos
    copies = started(
        [c_in, map_in, e_in, coupling_in], [c_ref, map_ref, e_ref, coupling], sems
    )
    wait(copies)
    rows = lax.broadcasted_iota(jnp.int32, (z.paos, z.paos), 0)
    lane_link = lax.broadcasted_iota(jnp.int32, (1, z.links * n), 1) // n
    for p in range(z.pairs):
        select = f32(map_ref[p : p + 1, :] == rows).astype(jnp.bfloat16)
        c_high, c_low = split(c_ref[p])
        mp_ref[p, :n, :] = lax.dot_general(
            c_high, select, (((1,), (1,)), ((), ())), preferred_element_type=jnp.float32
        ) + lax.dot_general(
            c_low, select, (((1,), (1,)), ((), ())), preferred_element_type=jnp.float32
        )
        mp_ref[p, n:, :] = jnp.zeros((EXTRA, z.paos), jnp.float32)
        mp_ref[p, n : n + 1, :n] = e_ref[p : p + 1, :]
        spread = jnp.zeros((1, z.links * n), jnp.float32)
        for k in range(z.links):
            spread = jnp.where(lane_link == k, coupling[p : p + 1, k : k + 1], spread)
        mp_ref[p, n + 1 : n + 2, :] = spread


def pack_kernel(z, s_in, mp_in, pack_ref, s_ref, mp_ref, sems):
    n = z.pnos
    line = 2 * n
    base = z.links * n // 2
    wait(started([s_in, mp_in.at[:, pl.ds(n, EXTRA), :]], [s_ref, mp_ref], sems))
    for slot in range(1 if small(z) else z.pairs):
        p = lax.axis_index("fit") if small(z) else slot
        for r in range(n // 2):
            lines = s_ref[p, :, r * line : (r + 1) * line]
            for k in range(z.links):
                row = k * n // 2 + r
                pack_ref[slot, row : row + 1, :] = lines[k : k + 1, :]
        pack_ref[slot, base:, :] = jnp.zeros((EXTRA, line), jnp.float32)
        pack_ref[slot, base : base + 1, :] = mp_ref[p, 0:1, :line]
        for k in range(z.links // 2):
            pack_ref[slot, base + 1 + k : base + 2 + k, :] = mp_ref[
                p, 1:2, k * line : (k + 1) * line
            ]
    if small(z):
        for copy in range(1, z.owners):
            pack_ref[copy] = pack_ref[0]


def below_kernel(z, second_in, mp_below, b_in, order, right_ref, second, m_ref, b_ref, sems):
    owner, sub = lax.axis_index("orb"), lax.axis_index("sub")
    start = side_start(z, jnp.maximum(owner - 1, 0), sub, 0)
    wait(started([second_in], [second], sems))
    m_copies = started([mp_below.at[:, pl.ds(0, z.pnos), :]], [m_ref], sems)
    b_copies, held = [], []
    for p in range(z.pairs):
        j = second[start + p] - owner * z.orbitals
        held.append(jnp.where(j >= 0, 1.0, 0.0))
        b_copies += started([b_in.at[jnp.clip(j, 0, z.orbitals - 1)]], [b_ref.at[p]], sems, 1 + p)
    wait(m_copies)
    for p in range(z.pairs):
        wait(b_copies[p : p + 1])
        right_ref[p] = mm(m_ref[p] * held[p], b_ref[p])


def local_kernel(z, first, second, c_ref, mp_ref, b_ref, left_ref, right_ref):
    owner, sub = lax.axis_index("orb"), lax.axis_index("sub")
    start = side_start(z, owner, sub, 0)
    base = owner * z.orbitals
    for p in range(z.pairs):
        left_ref[p] = mm(c_ref[p], b_ref[first[start + p] - base])
        j = second[start + p] - base
        local = jnp.where(j < z.orbitals, 1.0, 0.0)
        right_ref[p] = mm(
            mp_ref[p, : z.pnos, :] * local, b_ref[jnp.minimum(j, z.orbitals - 1)]
        )


def sums_kernel(z, first, second, ranks, occupied, mp_ref, left_ref, here_ref, down_ref, *refs):
    sums_ref, right_ref = refs[-2:]
    owner, sub = lax.axis_index("orb"), lax.axis_index("sub")
    start = side_start(z, owner, sub, 0)
    n = z.pnos
    for p in range(z.pairs):
        right = here_ref[p] + down_ref[p]
        right_ref[p] = right
        scale = scale_of(
            z, start + p, mp_ref[p, n : n + 1, :n], first, second, ranks, occupied
        )
        part = mm(left_ref[p], right, ((1,), (1,)))
        sums_ref[:, p * n : (p + 1) * n] = -part * scale


def unpack_kernel(z, first, second, ranks, occupied, *refs):
    packs = refs[:-5]
    high_ref, low_ref, scale_ref, coupling_ref, rows = refs[-5:]
    sub, fit = lax.axis_index("sub"), lax.axis_index("fit")
    n = z.pnos
    base = z.links * n // 2

    def one(pair, block, slot):
        for k in range(0, z.links, 2):
            two = [block(k * n // 2, n // 2), block((k + 1) * n // 2, n // 2)]
            for odd in range(2):
                rows[slot, k // 2, pl.ds(odd, n // 2, 2), :] = jnp.concatenate(
                    [part[:, odd * n : (odd + 1) * n] for part in two], axis=1
                )
        s = jnp.concatenate([rows[slot, k] for k in range(z.links // 2)], axis=1)
        high_ref[pair], low_ref[pair] = split(s)
        extra = block(base, EXTRA)
        scale_ref[pair] = scale_of(z, pair, extra[0:1, :n], first, second, ranks, occupied)
        coupling_ref[pair, 0:1, :] = jnp.concatenate(
            [extra[1 + k : 2 + k, :] for k in range(z.links // 2)], axis=1
        )

    if small(z):
        for index, ref in enumerate(packs):
            side = sub if index < 2 else 1 - sub
            which = fit if index % 2 == 0 else 1 - fit
            for who in range(z.owners):
                one(
                    who * z.own + side * z.pairs + which,
                    lambda start, size: ref[who, start : start + size, :],
                    index * z.owners + who,
                )
    else:
        each_pair(
            z, lambda pair: one(pair, lambda start, size: packs[0][pair, pl.ds(start, size), :], 0)
        )


def coupled_of(z, index, pair, near, s, coupling, amps_high, amps_low, diag_high, diag_low):
    n = z.pnos
    for k in range(z.links):
        row = near[pair, k]
        block = slice(k * n, (k + 1) * n)
        diag_high[index, block, block] = amps_high[row]
        diag_low[index, block, block] = amps_low[row]
    return split(mm3(s, (diag_high[index], diag_low[index])) * coupling)


def final_kernel(z, first, second, near, *refs):
    start_count = 2 if small(z) else 1
    starts = refs[:start_count]
    s_high, s_low, scale_ref, coupling_ref = refs[start_count : start_count + 4]
    (c_in, c_other, mp_in, mp_other, mp_below, mp_below_other, left_in, left_other, left_below,
     left_below_other, right_in, right_other) = refs[start_count + 4 : start_count + 16]
    (amp_ref, grad_out, c_ref, m_ref, rhs, grad, flat, amps, amps_high, amps_low, next_high,
     next_low, diag_high, diag_low, rows_high, rows_low, sems) = refs[start_count + 16 :]
    owner, sub = lax.axis_index("orb"), lax.axis_index("sub")
    n, pairs, own = z.pnos, z.pairs, z.own
    half = z.paos // z.subs
    at = pl.ds(pl.multiple_of(sub * half, half), half)

    def quarters(ref, base=0):
        return [ref.at[pl.ds(base + i * pairs, pairs)] for i in range(4)]

    small_copies = started(
        [c_in.at[:, :, at], c_other.at[:, :, at]]
        + [ref.at[:, pl.ds(0, n), at] for ref in (mp_in, mp_other, mp_below, mp_below_other)],
        [c_ref.at[pl.ds(0, pairs)], c_ref.at[pl.ds(pairs, pairs)]] + quarters(m_ref),
        sems,
    )
    large_copies = started(
        [right_in, right_other, left_in, left_other, left_below, left_below_other],
        [rhs.at[pl.ds(0, pairs)], rhs.at[pl.ds(pairs, pairs)]] + quarters(rhs, own),
        sems, 6,
    )
    diag_high[...] = jnp.zeros_like(diag_high)
    diag_low[...] = jnp.zeros_like(diag_low)

    def begin(pair, value):
        amps[pair] = value
        amps_high[pair], amps_low[pair] = split(value)

    if small(z):
        for side, ref in ((sub, starts[0]), (1 - sub, starts[1])):
            for who in range(z.owners):
                for p in range(pairs):
                    begin(who * own + side * pairs + p, ref[who, :, p * n : (p + 1) * n])
    else:
        @pl.loop(0, z.owners * z.subs)
        def _(device):
            for p in range(pairs):
                begin(device * pairs + p, starts[0][device, :, p * n : (p + 1) * n])

    def s_of(pair):
        return s_high[pair], s_low[pair]

    def swept(index, pair, high_amps, low_amps):
        s = s_of(pair)
        inner = coupled_of(
            z, index, pair, near, s, coupling_ref[pair, 0:1, :], high_amps, low_amps, diag_high,
            diag_low,
        )
        return amps[pair] + mm3(inner, s, ((1,), (1,))) * scale_ref[pair]

    if z.owners <= SMALL:
        group = diag_high.shape[0]
        for base in range(0, z.total, group):
            pair_list = range(base, min(base + group, z.total))
            inner = [
                coupled_of(
                    z, index, pair, near, s_of(pair), coupling_ref[pair, 0:1, :], amps_high,
                    amps_low, diag_high, diag_low,
                )
                for index, pair in enumerate(pair_list)
            ]
            for value, pair in zip(inner, pair_list):
                coupled = mm3(value, s_of(pair), ((1,), (1,)))
                next_high[pair], next_low[pair] = split(amps[pair] + coupled * scale_ref[pair])
    else:
        @pl.loop(0, z.total)
        def _(pair):
            next_high[pair], next_low[pair] = split(swept(0, pair, amps_high, amps_low))

    pair_list = [
        side_start(z, who, sub, side) + p
        for who in (owner, jnp.maximum(owner - 1, 0))
        for side in range(z.subs)
        for p in range(pairs)
    ]
    inner = [
        coupled_of(
            z, index, pair, near, s_of(pair), coupling_ref[pair, 0:1, :], next_high, next_low,
            diag_high, diag_low,
        )
        for index, pair in enumerate(pair_list)
    ]
    found = [
        amps[pair] + mm3(value, s_of(pair), ((1,), (1,))) * scale_ref[pair]
        for value, pair in zip(inner, pair_list)
    ]
    turned = [value.T for value in found]
    wait(small_copies)
    weights = [split(2.0 * a - b) for a, b in zip(found, turned)]
    weights_turned = [split(2.0 * b - a) for a, b in zip(found[:own], turned[:own])]
    terms = (
        [mm3(w, split(c_ref[i])) for i, w in enumerate(weights_turned)]
        + [mm3(w, split(m_ref[i])) for i, w in enumerate(weights)]
    )
    orbital_list = (
        [first[pair] - owner * z.orbitals for pair in pair_list[:own]]
        + [second[pair] - owner * z.orbitals for pair in pair_list]
    )
    for index in range(0, 3 * own, 2):
        for o in range(z.orbitals):
            block = jnp.concatenate(
                [
                    jnp.where(orbital_list[i] == o, terms[i], 0.0) for i in (index, index + 1)
                ]
            ).T
            place = (slice(o * half, (o + 1) * half), slice(index * n, (index + 2) * n))
            rows_high[place], rows_low[place] = split(block)

    for p in range(pairs):
        flat[p] = found[p]
        even = flat[p, pl.ds(0, n // 2, 2), :]
        odd = flat[p, pl.ds(1, n // 2, 2), :]
        lines = jnp.concatenate([even, odd], axis=1)
        for r in range(n // 2):
            amp_ref[p : p + 1, r * 2 * n : (r + 1) * 2 * n] = lines[r : r + 1, :]

    wait(large_copies)
    step = 256
    rows = (rows_high[...], rows_low[...])
    copies = []
    for index, start in enumerate(range(0, z.fits, step)):
        factor = rhs[:, :, start : start + step].reshape(3 * own * n, step)
        grad[:, :, start : start + step] = mm3(rows, split(factor)).reshape(
            z.orbitals, half, step
        )
        window = pl.ds(start, step)
        copies += started(
            [grad.at[:, :, window]], [grad_out.at[:, :, window]], sems, 12 + index
        )
    wait(copies)


def gate(values, *after):
    return lax.optimization_barrier((tuple(values), after))[0]


def body(
    blocks,
    pno_coefficients,
    domain_map,
    pair_first,
    pair_second,
    pno_ranks,
    neighbours,
    couplings,
    intersections,
    pno_energy,
    occ_energy,
):
    z = Sizes(blocks, pno_coefficients, couplings)
    n, pairs, own, fits = z.pnos, z.pairs, z.own, z.fits
    half = z.paos // z.subs
    wide = z.links * n
    hbm = held_out
    bf16 = jnp.bfloat16
    more = 0 if z.owners <= SMALL else z.owners

    def scratch(*shape, kind=jnp.float32):
        return pltpu.VMEM(shape, kind)

    pack_shape = (z.owners if small(z) else pairs, z.links * n // 2 + EXTRA, 2 * n)
    (mp,) = call(
        functools.partial(mapped_kernel, z),
        [(pairs, n + EXTRA, z.paos)],
        [hbm] * 4,
        (pno_coefficients, domain_map, pno_energy, couplings),
        [
            scratch(*pno_coefficients.shape),
            pltpu.VMEM(domain_map.shape, jnp.int32),
            scratch(*pno_energy.shape),
            scratch(*couplings.shape),
            pltpu.SemaphoreType.DMA((4,)),
        ],
        limit=None,
    )
    mp_below = shifted(mp, "orb", 1)
    (pack,) = call(
        functools.partial(pack_kernel, z),
        [pack_shape],
        [hbm] * 2,
        (intersections, mp),
        [
            scratch(*intersections.shape),
            scratch(pairs, EXTRA, z.paos),
            pltpu.SemaphoreType.DMA((2,)),
        ],
        limit=None,
    )
    if small(z):
        packs = [lax.all_to_all(pack, "orb", 0, 0)]
    else:
        packs = [lax.all_gather(pack, ("orb", "sub"), axis=0, tiled=True)]
    (right_below,) = call(
        functools.partial(below_kernel, z),
        [(pairs, n, fits)],
        [hbm] * 4,
        (pair_second, mp_below, blocks, pack),
        [
            pltpu.SMEM(pair_second.shape, jnp.int32),
            scratch(pairs, n, z.paos),
            scratch(pairs, *blocks.shape[1:]),
            pltpu.SemaphoreType.DMA((1 + pairs,)),
        ],
        limit=None,
    )
    down = shifted(right_below, "orb", -1)
    (coefficients,) = gate((pno_coefficients,), right_below)
    left, right_here = call(
        functools.partial(local_kernel, z),
        [(pairs, n, fits), (pairs, n, fits)],
        [smem, smem, vmem, vmem, vmem],
        (pair_first, pair_second, coefficients, mp, blocks),
        limit=8,
        cost=BRIEF,
    )
    left_late, mp_late, coefficients = gate((left, mp, coefficients), right_here)
    mp_other = swapped(mp_late, "sub")
    left_other = swapped(left_late, "sub")
    c_other = swapped(coefficients, "sub")
    if small(z):
        packs.append(swapped(gate(packs, right_here)[0], "fit"))
        packs += [swapped(value, "sub") for value in gate(packs, right_here)]
    left_below = shifted(gate((left,), packs[1] if small(z) else right_here)[0], "orb", 1)

    lists = (pair_first, pair_second, pno_ranks)
    split_shape = jax.ShapeDtypeStruct((z.total, n, wide), bf16)
    unpacked = pl.pallas_call(
        functools.partial(unpack_kernel, z),
        out_shape=[
            split_shape,
            split_shape,
            jax.ShapeDtypeStruct((z.total, n, n), jnp.float32),
            jax.ShapeDtypeStruct((z.total, EXTRA, wide), jnp.float32),
        ],
        in_specs=[smem] * 4 + [vmem] * len(packs),
        out_specs=[vmem] * 4,
        scratch_shapes=[scratch(z.total if small(z) else 1, z.links // 2, n, 2 * n)],
        cost_estimate=BRIEF,
        compiler_params=pltpu.CompilerParams(vmem_limit_bytes=(16 + more) * MIB),
    )(*lists, occ_energy, *packs)

    part, right = call(
        functools.partial(sums_kernel, z),
        [(n, pairs * n), (pairs, n, fits)],
        [smem] * 4 + [vmem] * 4 + [anywhere] * 4,
        (*lists, occ_energy, mp, left, right_here, down, left_other, mp_other, c_other,
         unpacked[0]),
        limit=8,
    )
    if small(z):
        sums = part + swapped(part, "fit")
        start_amps = [
            lax.all_to_all(jnp.broadcast_to(sums[None], (z.owners, *sums.shape)), "orb", 0, 0)
        ]
        start_amps.append(swapped(start_amps[0], "sub"))
    else:
        sums = lax.psum(part, "fit")
        start_amps = [lax.all_gather(sums, ("orb", "sub"), axis=0, tiled=False)]

    right_late, mp_late = gate((right, mp_below), part)
    (left_late,) = gate((left_below,), sums)
    right_other, mp_below_other, left_below_other = [
        swapped(value, "sub") for value in (right_late, mp_late, left_late)
    ]

    args = (
        pair_first, pair_second, neighbours, *start_amps, *unpacked,
        pno_coefficients, c_other, mp, mp_other, mp_below, mp_below_other,
        left, left_other, left_below, left_below_other, right, right_other,
    )
    group = own * 2
    square = (z.total, n, n)
    amplitudes, gradient = call(
        functools.partial(final_kernel, z),
        [(pairs, n * n), (z.orbitals, half, fits)],
        [smem] * 3 + [vmem] * (len(start_amps) + 4) + [hbm] * 12,
        args,
        [
            scratch(own, n, half),
            scratch(2 * own, n, half),
            scratch(3 * own, n, fits),
            scratch(z.orbitals, half, fits),
            scratch(pairs, n, n),
            scratch(*square),
        ]
        + [scratch(*square, kind=bf16)] * 4
        + [scratch(group, wide, wide, kind=bf16)] * 2
        + [scratch(z.orbitals * half, 3 * own * n, kind=bf16)] * 2
        + [pltpu.SemaphoreType.DMA((12 + -(-fits // 256),))],
        limit=40 + more // 2,
        out_specs=[vmem, hbm],
    )
    return (amplitudes, gradient)


def solution(mesh):
    in_specs = (
        P(("groups", "orb"), None, "fit"),
        P(("groups", "orb", "sub"), None, None),
        P(("groups", "orb", "sub"), None),
        P("groups"),
        P("groups"),
        P("groups"),
        P("groups", None),
        P(("groups", "orb", "sub"), None),
        P(("groups", "orb", "sub"), None, None),
        P(("groups", "orb", "sub"), None),
        P("groups"),
    )
    out_specs = (P(("groups", "orb", "sub"), None), P(("groups", "orb"), "sub", "fit"))
    return jax.shard_map(body, mesh=mesh, in_specs=in_specs, out_specs=out_specs, check_vma=False)
```

```python
import functools

import jax
import jax.numpy as jnp
from jax import lax
from jax.experimental import pallas as pl
from jax.experimental.pallas import tpu as pltpu
from jax.sharding import PartitionSpec as P

ITERS = 2
SMALL = 4
MIB = 1 << 20
EXTRA = 8

high = lax.Precision.HIGH
BRIEF = pl.CostEstimate(flops=1, bytes_accessed=1, transcendentals=0)
smem = pl.BlockSpec(memory_space=pltpu.SMEM)
vmem = pl.BlockSpec(memory_space=pltpu.VMEM)


def mm(a, b, contract=((1,), (0,))):
    return lax.dot_general(
        a, b, (contract, ((), ())), precision=high, preferred_element_type=jnp.float32
    )


def shifted(value, axis, steps):
    count = lax.axis_size(axis)
    initial, last = (max(0, -steps), min(count, count - steps))
    return lax.ppermute(value, axis, [(source, source + steps) for source in range(initial, last)])


def swapped(value, axis):
    return lax.ppermute(value, axis, [(0, 1), (1, 0)])


def f32(flag):
    return flag.astype(jnp.float32)


class Sizes:
    def __init__(self, blocks, pno_coefficients, couplings):
        self.orbitals, self.paos, self.fits = blocks.shape
        self.pairs, self.pnos = pno_coefficients.shape[:2]
        self.links = couplings.shape[1]
        self.subs = lax.axis_size("sub")
        self.owners = lax.axis_size("orb")
        self.fit_count = lax.axis_size("fit")
        self.own = self.pairs * self.subs
        self.total = self.own * self.owners


anywhere = pl.BlockSpec(memory_space=pl.ANY)
held_out = pl.BlockSpec(memory_space=pltpu.HBM)


def call(kernel, outs, ins, args, scratch=(), limit=16, out_specs=None, cost=BRIEF):
    return pl.pallas_call(
        kernel,
        out_shape=[jax.ShapeDtypeStruct(shape, jnp.float32) for shape in outs],
        in_specs=ins,
        out_specs=out_specs or [vmem] * len(outs),
        scratch_shapes=list(scratch),
        cost_estimate=cost,
        compiler_params=pltpu.CompilerParams(vmem_limit_bytes=limit and limit * MIB),
    )(*args)


def started(sources, targets, sems, base=0):
    copies = [
        pltpu.make_async_copy(source, target, sems.at[base + index])
        for index, (source, target) in enumerate(zip(sources, targets))
    ]
    for copy in copies:
        copy.start()
    return copies


def wait(copies):
    for copy in copies:
        copy.wait()


def side_start(z, owner, sub, side):
    return owner * z.own + (sub if side == 0 else 1 - sub) * z.pairs


def scale_of(z, pair, level, first, second, ranks, occupied):
    n = z.pnos
    row_ids = lax.broadcasted_iota(jnp.int32, (n, n), 0)
    column_ids = lax.broadcasted_iota(jnp.int32, (n, n), 1)
    level = level * jnp.ones((n, 1), jnp.float32)
    rank = ranks[pair]
    kept = f32((row_ids < rank) & (column_ids < rank))
    return kept / (level + level.T - (occupied[first[pair]] + occupied[second[pair]]))


def split(value):
    high_part = value.astype(jnp.bfloat16)
    return high_part, (value - high_part.astype(jnp.float32)).astype(jnp.bfloat16)


def mm3(a, b, contract=((1,), (0,))):
    def one(x, y):
        return lax.dot_general(x, y, (contract, ((), ())), preferred_element_type=jnp.float32)

    return one(a[0], b[0]) + (one(a[0], b[1]) + one(a[1], b[0]))


def small(z):
    return z.owners <= SMALL and z.pairs == z.fit_count == 2


def each_pair(z, action):
    if z.owners <= SMALL:
        for pair in range(z.total):
            action(pair)
    else:
        @pl.loop(0, z.total)
        def _(pair):
            action(pair)


def mapped_kernel(z, c_in, map_in, e_in, coupling_in, mp_ref, c_ref, map_ref, e_ref, coupling,
                  sems):
    n = z.pnos
    copies = started(
        [c_in, map_in, e_in, coupling_in], [c_ref, map_ref, e_ref, coupling], sems
    )
    wait(copies)
    rows = lax.broadcasted_iota(jnp.int32, (z.paos, z.paos), 0)
    lane_link = lax.broadcasted_iota(jnp.int32, (1, z.links * n), 1) // n
    for p in range(z.pairs):
        select = f32(map_ref[p : p + 1, :] == rows).astype(jnp.bfloat16)
        c_high, c_low = split(c_ref[p])
        mp_ref[p, :n, :] = lax.dot_general(
            c_high, select, (((1,), (1,)), ((), ())), preferred_element_type=jnp.float32
        ) + lax.dot_general(
            c_low, select, (((1,), (1,)), ((), ())), preferred_element_type=jnp.float32
        )
        mp_ref[p, n:, :] = jnp.zeros((EXTRA, z.paos), jnp.float32)
        mp_ref[p, n : n + 1, :n] = e_ref[p : p + 1, :]
        spread = jnp.zeros((1, z.links * n), jnp.float32)
        for k in range(z.links):
            spread = jnp.where(lane_link == k, coupling[p : p + 1, k : k + 1], spread)
        mp_ref[p, n + 1 : n + 2, :] = spread


def pack_kernel(z, s_in, mp_in, pack_ref, s_ref, mp_ref, sems):
    n = z.pnos
    line = 2 * n
    base = z.links * n // 2
    wait(started([s_in, mp_in.at[:, pl.ds(n, EXTRA), :]], [s_ref, mp_ref], sems))
    for slot in range(1 if small(z) else z.pairs):
        p = lax.axis_index("fit") if small(z) else slot
        for r in range(n // 2):
            lines = s_ref[p, :, r * line : (r + 1) * line]
            for k in range(z.links):
                row = k * n // 2 + r
                pack_ref[slot, row : row + 1, :] = lines[k : k + 1, :]
        pack_ref[slot, base:, :] = jnp.zeros((EXTRA, line), jnp.float32)
        pack_ref[slot, base : base + 1, :] = mp_ref[p, 0:1, :line]
        for k in range(z.links // 2):
            pack_ref[slot, base + 1 + k : base + 2 + k, :] = mp_ref[
                p, 1:2, k * line : (k + 1) * line
            ]
    if small(z):
        for copy in range(1, z.owners):
            pack_ref[copy] = pack_ref[0]


def below_kernel(z, second, mp_below, b_ref, right_ref):
    owner, sub = lax.axis_index("orb"), lax.axis_index("sub")
    start = side_start(z, jnp.maximum(owner - 1, 0), sub, 0)
    for p in range(z.pairs):
        j = second[start + p] - owner * z.orbitals
        held = jnp.where(j >= 0, 1.0, 0.0)
        mapped = mp_below[p, : z.pnos, :] * held
        right_ref[p] = mm(mapped, b_ref[jnp.clip(j, 0, z.orbitals - 1)])


def local_kernel(z, first, second, c_ref, mp_ref, b_ref, left_ref, right_ref):
    owner, sub = lax.axis_index("orb"), lax.axis_index("sub")
    start = side_start(z, owner, sub, 0)
    base = owner * z.orbitals
    for p in range(z.pairs):
        left_ref[p] = mm(c_ref[p], b_ref[first[start + p] - base])
        j = second[start + p] - base
        local = jnp.where(j < z.orbitals, 1.0, 0.0)
        right_ref[p] = mm(
            mp_ref[p, : z.pnos, :] * local, b_ref[jnp.minimum(j, z.orbitals - 1)]
        )


def sums_kernel(z, first, second, ranks, occupied, mp_ref, left_ref, here_ref, down_ref, *refs):
    sums_ref, right_ref = refs[-2:]
    owner, sub = lax.axis_index("orb"), lax.axis_index("sub")
    start = side_start(z, owner, sub, 0)
    n = z.pnos
    for p in range(z.pairs):
        right = here_ref[p] + down_ref[p]
        right_ref[p] = right
        scale = scale_of(
            z, start + p, mp_ref[p, n : n + 1, :n], first, second, ranks, occupied
        )
        part = mm(left_ref[p], right, ((1,), (1,)))
        sums_ref[:, p * n : (p + 1) * n] = -part * scale


def unpack(z, pair, block, rows, slot, s_high, s_low, scale_ref, coupling_ref, lists):
    n = z.pnos
    for k in range(0, z.links, 2):
        two = [block(k * n // 2, n // 2), block((k + 1) * n // 2, n // 2)]
        for odd in range(2):
            rows[slot, k // 2, pl.ds(odd, n // 2, 2), :] = jnp.concatenate(
                [part[:, odd * n : (odd + 1) * n] for part in two], axis=1
            )
    s = jnp.concatenate([rows[slot, k] for k in range(z.links // 2)], axis=1)
    s_high[pair], s_low[pair] = split(s)
    extra = block(z.links * n // 2, EXTRA)
    scale_ref[pair] = scale_of(z, pair, extra[0:1, :n], *lists)
    coupling_ref[pair, 0:1, :] = jnp.concatenate(
        [extra[1 + k : 2 + k, :] for k in range(z.links // 2)], axis=1
    )


def coupled_of(z, index, pair, near, s, coupling, amps_high, amps_low, diag_high, diag_low):
    n = z.pnos
    for k in range(z.links):
        row = near[pair, k]
        block = slice(k * n, (k + 1) * n)
        diag_high[index, block, block] = amps_high[row]
        diag_low[index, block, block] = amps_low[row]
    return split(mm3(s, (diag_high[index], diag_low[index])) * coupling)


def final_kernel(z, first, second, ranks, near, occupied, *refs):
    start_count, pack_count = (2, 4) if small(z) else (1, 1)
    starts = refs[:start_count]
    pack_in = refs[start_count : start_count + pack_count]
    (c_in, c_other, mp_in, mp_other, mp_below, mp_below_other, left_in, left_other, left_below,
     left_below_other, right_in, right_other) = refs[start_count + pack_count :][:12]
    (amp_ref, grad_out, packs, s_high, s_low, scale_ref, coupling_ref, s_rows, c_ref, m_ref, rhs,
     grad, flat, amps, amps_high, amps_low, next_high, next_low, diag_high, diag_low, rows_high,
     rows_low, sems) = refs[start_count + pack_count + 12 :]
    owner, sub = lax.axis_index("orb"), lax.axis_index("sub")
    fit = lax.axis_index("fit")
    n, pairs, own = z.pnos, z.pairs, z.own
    half = z.paos // z.subs
    at = pl.ds(pl.multiple_of(sub * half, half), half)
    lists = (first, second, ranks, occupied)

    def quarters(ref, base=0):
        return [ref.at[pl.ds(base + i * pairs, pairs)] for i in range(4)]

    pack_copies = started(pack_in, [packs.at[i] for i in range(pack_count)], sems)
    small_copies = started(
        [c_in.at[:, :, at], c_other.at[:, :, at]]
        + [ref.at[:, pl.ds(0, n), at] for ref in (mp_in, mp_other, mp_below, mp_below_other)],
        [c_ref.at[pl.ds(0, pairs)], c_ref.at[pl.ds(pairs, pairs)]] + quarters(m_ref),
        sems, 4,
    )
    large_copies = started(
        [right_in, right_other, left_in, left_other, left_below, left_below_other],
        [rhs.at[pl.ds(0, pairs)], rhs.at[pl.ds(pairs, pairs)]] + quarters(rhs, own),
        sems, 10,
    )
    diag_high[...] = jnp.zeros_like(diag_high)
    diag_low[...] = jnp.zeros_like(diag_low)

    def begin(pair, value):
        amps[pair] = value
        amps_high[pair], amps_low[pair] = split(value)

    if small(z):
        for side, ref in ((sub, starts[0]), (1 - sub, starts[1])):
            for who in range(z.owners):
                for p in range(pairs):
                    begin(who * own + side * pairs + p, ref[who, :, p * n : (p + 1) * n])
    else:
        @pl.loop(0, z.owners * z.subs)
        def _(device):
            for p in range(pairs):
                begin(device * pairs + p, starts[0][device, :, p * n : (p + 1) * n])

    wait(pack_copies)
    if small(z):
        for index in range(pack_count):
            side = sub if index < 2 else 1 - sub
            which = fit if index % 2 == 0 else 1 - fit
            for who in range(z.owners):
                unpack(
                    z, who * own + side * pairs + which,
                    lambda start, size: packs[index, who, start : start + size, :], s_rows,
                    index * z.owners + who, s_high, s_low, scale_ref, coupling_ref, lists,
                )
    else:
        @pl.loop(0, z.total)
        def _(pair):
            unpack(
                z, pair, lambda start, size: packs[0, pair, pl.ds(start, size), :], s_rows, 0,
                s_high, s_low, scale_ref, coupling_ref, lists,
            )

    def s_of(pair):
        return s_high[pair], s_low[pair]

    def swept(index, pair, high_amps, low_amps):
        s = s_of(pair)
        inner = coupled_of(
            z, index, pair, near, s, coupling_ref[pair, 0:1, :], high_amps, low_amps, diag_high,
            diag_low,
        )
        return amps[pair] + mm3(inner, s, ((1,), (1,))) * scale_ref[pair]

    if z.owners <= SMALL:
        group = diag_high.shape[0]
        for base in range(0, z.total, group):
            pair_list = range(base, min(base + group, z.total))
            inner = [
                coupled_of(
                    z, index, pair, near, s_of(pair), coupling_ref[pair, 0:1, :], amps_high,
                    amps_low, diag_high, diag_low,
                )
                for index, pair in enumerate(pair_list)
            ]
            for value, pair in zip(inner, pair_list):
                coupled = mm3(value, s_of(pair), ((1,), (1,)))
                next_high[pair], next_low[pair] = split(amps[pair] + coupled * scale_ref[pair])
    else:
        @pl.loop(0, z.total)
        def _(pair):
            next_high[pair], next_low[pair] = split(swept(0, pair, amps_high, amps_low))

    pair_list = [
        side_start(z, who, sub, side) + p
        for who in (owner, jnp.maximum(owner - 1, 0))
        for side in range(z.subs)
        for p in range(pairs)
    ]
    inner = [
        coupled_of(
            z, index, pair, near, s_of(pair), coupling_ref[pair, 0:1, :], next_high, next_low,
            diag_high, diag_low,
        )
        for index, pair in enumerate(pair_list)
    ]
    found = [
        amps[pair] + mm3(value, s_of(pair), ((1,), (1,))) * scale_ref[pair]
        for value, pair in zip(inner, pair_list)
    ]
    turned = [value.T for value in found]
    wait(small_copies)
    weights = [split(2.0 * a - b) for a, b in zip(found, turned)]
    weights_turned = [split(2.0 * b - a) for a, b in zip(found[:own], turned[:own])]
    terms = (
        [mm3(w, split(c_ref[i])) for i, w in enumerate(weights_turned)]
        + [mm3(w, split(m_ref[i])) for i, w in enumerate(weights)]
    )
    orbital_list = (
        [first[pair] - owner * z.orbitals for pair in pair_list[:own]]
        + [second[pair] - owner * z.orbitals for pair in pair_list]
    )
    for index in range(0, 3 * own, 2):
        for o in range(z.orbitals):
            block = jnp.concatenate(
                [
                    jnp.where(orbital_list[i] == o, terms[i], 0.0) for i in (index, index + 1)
                ]
            ).T
            place = (slice(o * half, (o + 1) * half), slice(index * n, (index + 2) * n))
            rows_high[place], rows_low[place] = split(block)

    for p in range(pairs):
        flat[p] = found[p]
        even = flat[p, pl.ds(0, n // 2, 2), :]
        odd = flat[p, pl.ds(1, n // 2, 2), :]
        lines = jnp.concatenate([even, odd], axis=1)
        for r in range(n // 2):
            amp_ref[p : p + 1, r * 2 * n : (r + 1) * 2 * n] = lines[r : r + 1, :]

    wait(large_copies)
    step = 256
    rows = (rows_high[...], rows_low[...])
    copies = []
    for index, start in enumerate(range(0, z.fits, step)):
        factor = rhs[:, :, start : start + step].reshape(3 * own * n, step)
        grad[:, :, start : start + step] = mm3(rows, split(factor)).reshape(
            z.orbitals, half, step
        )
        window = pl.ds(start, step)
        copies += started(
            [grad.at[:, :, window]], [grad_out.at[:, :, window]], sems, 16 + index
        )
    wait(copies)


def gate(values, *after):
    return lax.optimization_barrier((tuple(values), after))[0]


def body(
    blocks,
    pno_coefficients,
    domain_map,
    pair_first,
    pair_second,
    pno_ranks,
    neighbours,
    couplings,
    intersections,
    pno_energy,
    occ_energy,
):
    z = Sizes(blocks, pno_coefficients, couplings)
    n, pairs, own, fits = z.pnos, z.pairs, z.own, z.fits
    half = z.paos // z.subs
    wide = z.links * n
    hbm = held_out
    bf16 = jnp.bfloat16
    more = 0 if z.owners <= SMALL else z.owners

    def scratch(*shape, kind=jnp.float32):
        return pltpu.VMEM(shape, kind)

    pack_shape = (z.owners if small(z) else pairs, z.links * n // 2 + EXTRA, 2 * n)
    (mp,) = call(
        functools.partial(mapped_kernel, z),
        [(pairs, n + EXTRA, z.paos)],
        [hbm] * 4,
        (pno_coefficients, domain_map, pno_energy, couplings),
        [
            scratch(*pno_coefficients.shape),
            pltpu.VMEM(domain_map.shape, jnp.int32),
            scratch(*pno_energy.shape),
            scratch(*couplings.shape),
            pltpu.SemaphoreType.DMA((4,)),
        ],
        limit=None,
    )
    mp_below = shifted(mp, "orb", 1)
    left, right_here = call(
        functools.partial(local_kernel, z),
        [(pairs, n, fits), (pairs, n, fits)],
        [smem, smem, vmem, vmem, vmem],
        (pair_first, pair_second, pno_coefficients, mp, blocks),
        limit=8,
    )
    (right_below,) = call(
        functools.partial(below_kernel, z),
        [(pairs, n, fits)],
        [smem, vmem, vmem],
        (pair_second, gate((mp_below,), left)[0], blocks),
        limit=8,
    )
    down = shifted(right_below, "orb", -1)
    late = gate((intersections, mp, left, pno_coefficients), right_below)
    intersection, mp_late, left_late, coefficients = late
    (pack,) = call(
        functools.partial(pack_kernel, z),
        [pack_shape],
        [hbm] * 2,
        (intersection, mp_late),
        [
            scratch(*intersections.shape),
            scratch(pairs, EXTRA, z.paos),
            pltpu.SemaphoreType.DMA((2,)),
        ],
        limit=8,
    )
    if small(z):
        packs = [lax.all_to_all(pack, "orb", 0, 0)]
    else:
        packs = [lax.all_gather(pack, ("orb", "sub"), axis=0, tiled=True)]
    left_below = shifted(left_late, "orb", 1)
    mp_other = swapped(mp_late, "sub")
    left_other = swapped(left_late, "sub")
    c_other = swapped(coefficients, "sub")

    lists = (pair_first, pair_second, pno_ranks)
    (down,) = gate((down,), mp_other, left_other, c_other)
    part, right = call(
        functools.partial(sums_kernel, z),
        [(n, pairs * n), (pairs, n, fits)],
        [smem] * 4 + [vmem] * 4,
        (*lists, occ_energy, mp, left, right_here, down),
        limit=8,
    )
    (pack_late,) = gate(packs, part)
    if small(z):
        packs = [pack_late, swapped(pack_late, "fit")]
        packs.append(swapped(pack_late, "sub"))
        sums = part + swapped(part, "fit")
        start_amps = [
            lax.all_to_all(jnp.broadcast_to(sums[None], (z.owners, *sums.shape)), "orb", 0, 0)
        ]
        start_amps.append(swapped(start_amps[0], "sub"))
        packs.append(swapped(gate(packs[1:2], start_amps[0])[0], "sub"))
    else:
        sums = lax.psum(part, "fit")
        start_amps = [lax.all_gather(sums, ("orb", "sub"), axis=0, tiled=False)]

    right_late, mp_late = gate((right, mp_below), part)
    (left_late,) = gate((left_below,), sums)
    right_other, mp_below_other, left_below_other = [
        swapped(value, "sub") for value in (right_late, mp_late, left_late)
    ]

    args = (
        *lists, neighbours, occ_energy, *start_amps, *packs,
        pno_coefficients, c_other, mp, mp_other, mp_below, mp_below_other,
        left, left_other, left_below, left_below_other, right, right_other,
    )
    square = (z.total, n, n)
    amplitudes, gradient = call(
        functools.partial(final_kernel, z),
        [(pairs, n * n), (z.orbitals, half, fits)],
        [smem] * 5 + [vmem] * len(start_amps) + [hbm] * (12 + len(packs)),
        args,
        [
            scratch(len(packs), *packs[0].shape),
            scratch(z.total, n, wide, kind=bf16),
            scratch(z.total, n, wide, kind=bf16),
            scratch(*square),
            scratch(z.total, EXTRA, wide),
            scratch(z.total if small(z) else 1, z.links // 2, n, 2 * n),
            scratch(own, n, half),
            scratch(2 * own, n, half),
            scratch(3 * own, n, fits),
            scratch(z.orbitals, half, fits),
            scratch(pairs, n, n),
            scratch(*square),
        ]
        + [scratch(*square, kind=bf16)] * 4
        + [scratch(2 * own, wide, wide, kind=bf16)] * 2
        + [scratch(z.orbitals * half, 3 * own * n, kind=bf16)] * 2
        + [pltpu.SemaphoreType.DMA((16 + -(-fits // 256),))],
        limit=40 + more // 2,
        out_specs=[vmem, hbm],
    )
    return (amplitudes, gradient)


def solution(mesh):
    in_specs = (
        P(("groups", "orb"), None, "fit"),
        P(("groups", "orb", "sub"), None, None),
        P(("groups", "orb", "sub"), None),
        P("groups"),
        P("groups"),
        P("groups"),
        P("groups", None),
        P(("groups", "orb", "sub"), None),
        P(("groups", "orb", "sub"), None, None),
        P(("groups", "orb", "sub"), None),
        P("groups"),
    )
    out_specs = (P(("groups", "orb", "sub"), None), P(("groups", "orb"), "sub", "fit"))
    return jax.shard_map(body, mesh=mesh, in_specs=in_specs, out_specs=out_specs, check_vma=False)
```

```python
import functools

import jax
import jax.numpy as jnp
from jax import lax
from jax.experimental import pallas as pl
from jax.experimental.pallas import tpu as pltpu
from jax.sharding import PartitionSpec as P

ITERS = 2
SMALL = 4
MIB = 1 << 20
EXTRA = 8

high = lax.Precision.HIGH
BRIEF = pl.CostEstimate(flops=1, bytes_accessed=1, transcendentals=0)
smem = pl.BlockSpec(memory_space=pltpu.SMEM)
vmem = pl.BlockSpec(memory_space=pltpu.VMEM)


def mm(a, b, contract=((1,), (0,))):
    return lax.dot_general(
        a, b, (contract, ((), ())), precision=high, preferred_element_type=jnp.float32
    )


def shifted(value, axis, steps):
    count = lax.axis_size(axis)
    initial, last = (max(0, -steps), min(count, count - steps))
    return lax.ppermute(value, axis, [(source, source + steps) for source in range(initial, last)])


def swapped(value, axis):
    return lax.ppermute(value, axis, [(0, 1), (1, 0)])


def f32(flag):
    return flag.astype(jnp.float32)


class Sizes:
    def __init__(self, blocks, pno_coefficients, couplings):
        self.orbitals, self.paos, self.fits = blocks.shape
        self.pairs, self.pnos = pno_coefficients.shape[:2]
        self.links = couplings.shape[1]
        self.subs = lax.axis_size("sub")
        self.owners = lax.axis_size("orb")
        self.fit_count = lax.axis_size("fit")
        self.own = self.pairs * self.subs
        self.total = self.own * self.owners


anywhere = pl.BlockSpec(memory_space=pl.ANY)
held_out = pl.BlockSpec(memory_space=pltpu.HBM)


def call(kernel, outs, ins, args, scratch=(), limit=16, out_specs=None, cost=BRIEF):
    return pl.pallas_call(
        kernel,
        out_shape=[jax.ShapeDtypeStruct(shape, jnp.float32) for shape in outs],
        in_specs=ins,
        out_specs=out_specs or [vmem] * len(outs),
        scratch_shapes=list(scratch),
        cost_estimate=cost,
        compiler_params=pltpu.CompilerParams(vmem_limit_bytes=limit and limit * MIB),
    )(*args)


def started(sources, targets, sems, base=0):
    copies = [
        pltpu.make_async_copy(source, target, sems.at[base + index])
        for index, (source, target) in enumerate(zip(sources, targets))
    ]
    for copy in copies:
        copy.start()
    return copies


def wait(copies):
    for copy in copies:
        copy.wait()


def side_start(z, owner, sub, side):
    return owner * z.own + (sub if side == 0 else 1 - sub) * z.pairs


def scale_of(z, pair, level, first, second, ranks, occupied):
    n = z.pnos
    row_ids = lax.broadcasted_iota(jnp.int32, (n, n), 0)
    column_ids = lax.broadcasted_iota(jnp.int32, (n, n), 1)
    level = level * jnp.ones((n, 1), jnp.float32)
    rank = ranks[pair]
    kept = f32((row_ids < rank) & (column_ids < rank))
    return kept / (level + level.T - (occupied[first[pair]] + occupied[second[pair]]))


def split(value):
    high_part = value.astype(jnp.bfloat16)
    return high_part, (value - high_part.astype(jnp.float32)).astype(jnp.bfloat16)


def mm3(a, b, contract=((1,), (0,))):
    def one(x, y):
        return lax.dot_general(x, y, (contract, ((), ())), preferred_element_type=jnp.float32)

    return one(a[0], b[0]) + (one(a[0], b[1]) + one(a[1], b[0]))


def small(z):
    return z.owners <= SMALL and z.pairs == z.fit_count == 2


def each_pair(z, action):
    if z.owners <= SMALL:
        for pair in range(z.total):
            action(pair)
    else:
        @pl.loop(0, z.total)
        def _(pair):
            action(pair)


def mapped_kernel(z, c_in, map_in, e_in, coupling_in, mp_ref, c_ref, map_ref, e_ref, coupling,
                  sems):
    n = z.pnos
    copies = started(
        [c_in, map_in, e_in, coupling_in], [c_ref, map_ref, e_ref, coupling], sems
    )
    wait(copies)
    rows = lax.broadcasted_iota(jnp.int32, (z.paos, z.paos), 0)
    lane_link = lax.broadcasted_iota(jnp.int32, (1, z.links * n), 1) // n
    for p in range(z.pairs):
        select = f32(map_ref[p : p + 1, :] == rows).astype(jnp.bfloat16)
        c_high, c_low = split(c_ref[p])
        mp_ref[p, :n, :] = lax.dot_general(
            c_high, select, (((1,), (1,)), ((), ())), preferred_element_type=jnp.float32
        ) + lax.dot_general(
            c_low, select, (((1,), (1,)), ((), ())), preferred_element_type=jnp.float32
        )
        mp_ref[p, n:, :] = jnp.zeros((EXTRA, z.paos), jnp.float32)
        mp_ref[p, n : n + 1, :n] = e_ref[p : p + 1, :]
        spread = jnp.zeros((1, z.links * n), jnp.float32)
        for k in range(z.links):
            spread = jnp.where(lane_link == k, coupling[p : p + 1, k : k + 1], spread)
        mp_ref[p, n + 1 : n + 2, :] = spread


def pack_kernel(z, s_in, mp_in, pack_ref, s_ref, mp_ref, sems):
    n = z.pnos
    line = 2 * n
    base = z.links * n // 2
    wait(started([s_in, mp_in.at[:, pl.ds(n, EXTRA), :]], [s_ref, mp_ref], sems))
    for slot in range(1 if small(z) else z.pairs):
        p = lax.axis_index("fit") if small(z) else slot
        for r in range(n // 2):
            lines = s_ref[p, :, r * line : (r + 1) * line]
            for k in range(z.links):
                row = k * n // 2 + r
                pack_ref[slot, row : row + 1, :] = lines[k : k + 1, :]
        pack_ref[slot, base:, :] = jnp.zeros((EXTRA, line), jnp.float32)
        pack_ref[slot, base : base + 1, :] = mp_ref[p, 0:1, :line]
        for k in range(z.links // 2):
            pack_ref[slot, base + 1 + k : base + 2 + k, :] = mp_ref[
                p, 1:2, k * line : (k + 1) * line
            ]
    if small(z):
        for copy in range(1, z.owners):
            pack_ref[copy] = pack_ref[0]


def below_kernel(z, second, mp_below, b_ref, right_ref):
    owner, sub = lax.axis_index("orb"), lax.axis_index("sub")
    start = side_start(z, jnp.maximum(owner - 1, 0), sub, 0)
    for p in range(z.pairs):
        j = second[start + p] - owner * z.orbitals
        held = jnp.where(j >= 0, 1.0, 0.0)
        mapped = mp_below[p, : z.pnos, :] * held
        right_ref[p] = mm(mapped, b_ref[jnp.clip(j, 0, z.orbitals - 1)])


def local_kernel(z, first, second, c_ref, mp_ref, b_ref, left_ref, right_ref):
    owner, sub = lax.axis_index("orb"), lax.axis_index("sub")
    start = side_start(z, owner, sub, 0)
    base = owner * z.orbitals
    for p in range(z.pairs):
        left_ref[p] = mm(c_ref[p], b_ref[first[start + p] - base])
        j = second[start + p] - base
        local = jnp.where(j < z.orbitals, 1.0, 0.0)
        right_ref[p] = mm(
            mp_ref[p, : z.pnos, :] * local, b_ref[jnp.minimum(j, z.orbitals - 1)]
        )


def sums_kernel(z, first, second, ranks, occupied, mp_ref, left_ref, here_ref, down_ref, *refs):
    sums_ref, right_ref = refs[-2:]
    owner, sub = lax.axis_index("orb"), lax.axis_index("sub")
    start = side_start(z, owner, sub, 0)
    n = z.pnos
    for p in range(z.pairs):
        right = here_ref[p] + down_ref[p]
        right_ref[p] = right
        scale = scale_of(
            z, start + p, mp_ref[p, n : n + 1, :n], first, second, ranks, occupied
        )
        part = mm(left_ref[p], right, ((1,), (1,)))
        sums_ref[:, p * n : (p + 1) * n] = -part * scale


def unpack(z, pair, block, rows, slot, s_high, s_low, scale_ref, coupling_ref, lists):
    n = z.pnos
    for k in range(0, z.links, 2):
        two = [block(k * n // 2, n // 2), block((k + 1) * n // 2, n // 2)]
        for odd in range(2):
            rows[slot, k // 2, pl.ds(odd, n // 2, 2), :] = jnp.concatenate(
                [part[:, odd * n : (odd + 1) * n] for part in two], axis=1
            )
    s = jnp.concatenate([rows[slot, k] for k in range(z.links // 2)], axis=1)
    s_high[pair], s_low[pair] = split(s)
    extra = block(z.links * n // 2, EXTRA)
    scale_ref[pair] = scale_of(z, pair, extra[0:1, :n], *lists)
    coupling_ref[pair, 0:1, :] = jnp.concatenate(
        [extra[1 + k : 2 + k, :] for k in range(z.links // 2)], axis=1
    )


def coupled_of(z, index, pair, near, s, coupling, amps_high, amps_low, diag_high, diag_low):
    n = z.pnos
    for k in range(z.links):
        row = near[pair, k]
        block = slice(k * n, (k + 1) * n)
        diag_high[index, block, block] = amps_high[row]
        diag_low[index, block, block] = amps_low[row]
    return split(mm3(s, (diag_high[index], diag_low[index])) * coupling)


def final_kernel(z, first, second, ranks, near, occupied, *refs):
    start_count, pack_count = (2, 4) if small(z) else (1, 1)
    starts = refs[:start_count]
    pack_in = refs[start_count : start_count + pack_count]
    (c_in, c_other, mp_in, mp_other, mp_below, mp_below_other, left_in, left_other, left_below,
     left_below_other, right_in, right_other) = refs[start_count + pack_count :][:12]
    (amp_ref, grad_out, packs, s_high, s_low, scale_ref, coupling_ref, s_rows, c_ref, m_ref, rhs,
     grad, flat, amps, amps_high, amps_low, next_high, next_low, diag_high, diag_low, rows_high,
     rows_low, sems) = refs[start_count + pack_count + 12 :]
    owner, sub = lax.axis_index("orb"), lax.axis_index("sub")
    fit = lax.axis_index("fit")
    n, pairs, own = z.pnos, z.pairs, z.own
    half = z.paos // z.subs
    at = pl.ds(pl.multiple_of(sub * half, half), half)
    lists = (first, second, ranks, occupied)

    def quarters(ref, base=0):
        return [ref.at[pl.ds(base + i * pairs, pairs)] for i in range(4)]

    pack_copies = started(pack_in, [packs.at[i] for i in range(pack_count)], sems)
    small_copies = started(
        [c_in.at[:, :, at], c_other.at[:, :, at]]
        + [ref.at[:, pl.ds(0, n), at] for ref in (mp_in, mp_other, mp_below, mp_below_other)],
        [c_ref.at[pl.ds(0, pairs)], c_ref.at[pl.ds(pairs, pairs)]] + quarters(m_ref),
        sems, 4,
    )
    large_copies = started(
        [right_in, right_other, left_in, left_other, left_below, left_below_other],
        [rhs.at[pl.ds(0, pairs)], rhs.at[pl.ds(pairs, pairs)]] + quarters(rhs, own),
        sems, 10,
    )
    diag_high[...] = jnp.zeros_like(diag_high)
    diag_low[...] = jnp.zeros_like(diag_low)

    def begin(pair, value):
        amps[pair] = value
        amps_high[pair], amps_low[pair] = split(value)

    if small(z):
        for side, ref in ((sub, starts[0]), (1 - sub, starts[1])):
            for who in range(z.owners):
                for p in range(pairs):
                    begin(who * own + side * pairs + p, ref[who, :, p * n : (p + 1) * n])
    else:
        @pl.loop(0, z.owners * z.subs)
        def _(device):
            for p in range(pairs):
                begin(device * pairs + p, starts[0][device, :, p * n : (p + 1) * n])

    wait(pack_copies)
    if small(z):
        for index in range(pack_count):
            side = sub if index < 2 else 1 - sub
            which = fit if index % 2 == 0 else 1 - fit
            for who in range(z.owners):
                unpack(
                    z, who * own + side * pairs + which,
                    lambda start, size: packs[index, who, start : start + size, :], s_rows,
                    index * z.owners + who, s_high, s_low, scale_ref, coupling_ref, lists,
                )
    else:
        @pl.loop(0, z.total)
        def _(pair):
            unpack(
                z, pair, lambda start, size: packs[0, pair, pl.ds(start, size), :], s_rows, 0,
                s_high, s_low, scale_ref, coupling_ref, lists,
            )

    def s_of(pair):
        return s_high[pair], s_low[pair]

    def swept(index, pair, high_amps, low_amps):
        s = s_of(pair)
        inner = coupled_of(
            z, index, pair, near, s, coupling_ref[pair, 0:1, :], high_amps, low_amps, diag_high,
            diag_low,
        )
        return amps[pair] + mm3(inner, s, ((1,), (1,))) * scale_ref[pair]

    if z.owners <= SMALL:
        group = diag_high.shape[0]
        for base in range(0, z.total, group):
            pair_list = range(base, min(base + group, z.total))
            inner = [
                coupled_of(
                    z, index, pair, near, s_of(pair), coupling_ref[pair, 0:1, :], amps_high,
                    amps_low, diag_high, diag_low,
                )
                for index, pair in enumerate(pair_list)
            ]
            for value, pair in zip(inner, pair_list):
                coupled = mm3(value, s_of(pair), ((1,), (1,)))
                next_high[pair], next_low[pair] = split(amps[pair] + coupled * scale_ref[pair])
    else:
        @pl.loop(0, z.total)
        def _(pair):
            next_high[pair], next_low[pair] = split(swept(0, pair, amps_high, amps_low))

    pair_list = [
        side_start(z, who, sub, side) + p
        for who in (owner, jnp.maximum(owner - 1, 0))
        for side in range(z.subs)
        for p in range(pairs)
    ]
    inner = [
        coupled_of(
            z, index, pair, near, s_of(pair), coupling_ref[pair, 0:1, :], next_high, next_low,
            diag_high, diag_low,
        )
        for index, pair in enumerate(pair_list)
    ]
    found = [
        amps[pair] + mm3(value, s_of(pair), ((1,), (1,))) * scale_ref[pair]
        for value, pair in zip(inner, pair_list)
    ]
    turned = [value.T for value in found]
    wait(small_copies)
    weights = [split(2.0 * a - b) for a, b in zip(found, turned)]
    weights_turned = [split(2.0 * b - a) for a, b in zip(found[:own], turned[:own])]
    terms = (
        [mm3(w, split(c_ref[i])) for i, w in enumerate(weights_turned)]
        + [mm3(w, split(m_ref[i])) for i, w in enumerate(weights)]
    )
    orbital_list = (
        [first[pair] - owner * z.orbitals for pair in pair_list[:own]]
        + [second[pair] - owner * z.orbitals for pair in pair_list]
    )
    for index in range(0, 3 * own, 2):
        for o in range(z.orbitals):
            block = jnp.concatenate(
                [
                    jnp.where(orbital_list[i] == o, terms[i], 0.0) for i in (index, index + 1)
                ]
            ).T
            place = (slice(o * half, (o + 1) * half), slice(index * n, (index + 2) * n))
            rows_high[place], rows_low[place] = split(block)

    for p in range(pairs):
        flat[p] = found[p]
        even = flat[p, pl.ds(0, n // 2, 2), :]
        odd = flat[p, pl.ds(1, n // 2, 2), :]
        lines = jnp.concatenate([even, odd], axis=1)
        for r in range(n // 2):
            amp_ref[p : p + 1, r * 2 * n : (r + 1) * 2 * n] = lines[r : r + 1, :]

    wait(large_copies)
    step = 256
    rows = (rows_high[...], rows_low[...])
    copies = []
    for index, start in enumerate(range(0, z.fits, step)):
        factor = rhs[:, :, start : start + step].reshape(3 * own * n, step)
        grad[:, :, start : start + step] = mm3(rows, split(factor)).reshape(
            z.orbitals, half, step
        )
        window = pl.ds(start, step)
        copies += started(
            [grad.at[:, :, window]], [grad_out.at[:, :, window]], sems, 16 + index
        )
    wait(copies)


def gate(values, *after):
    return lax.optimization_barrier((tuple(values), after))[0]


def body(
    blocks,
    pno_coefficients,
    domain_map,
    pair_first,
    pair_second,
    pno_ranks,
    neighbours,
    couplings,
    intersections,
    pno_energy,
    occ_energy,
):
    z = Sizes(blocks, pno_coefficients, couplings)
    n, pairs, own, fits = z.pnos, z.pairs, z.own, z.fits
    half = z.paos // z.subs
    wide = z.links * n
    hbm = held_out
    bf16 = jnp.bfloat16
    more = 0 if z.owners <= SMALL else z.owners

    def scratch(*shape, kind=jnp.float32):
        return pltpu.VMEM(shape, kind)

    pack_shape = (z.owners if small(z) else pairs, z.links * n // 2 + EXTRA, 2 * n)
    (mp,) = call(
        functools.partial(mapped_kernel, z),
        [(pairs, n + EXTRA, z.paos)],
        [hbm] * 4,
        (pno_coefficients, domain_map, pno_energy, couplings),
        [
            scratch(*pno_coefficients.shape),
            pltpu.VMEM(domain_map.shape, jnp.int32),
            scratch(*pno_energy.shape),
            scratch(*couplings.shape),
            pltpu.SemaphoreType.DMA((4,)),
        ],
        limit=None,
    )
    mp_below = shifted(mp, "orb", 1)
    (right_below,) = call(
        functools.partial(below_kernel, z),
        [(pairs, n, fits)],
        [smem, vmem, vmem],
        (pair_second, mp_below, blocks),
        limit=8,
    )
    down = shifted(right_below, "orb", -1)
    late = gate((intersections, mp, pno_coefficients), right_below)
    intersection, mp_late, coefficients = late
    left, right_here = call(
        functools.partial(local_kernel, z),
        [(pairs, n, fits), (pairs, n, fits)],
        [smem, smem, vmem, vmem, vmem],
        (pair_first, pair_second, coefficients, mp_late, blocks),
        limit=8,
    )
    (pack,) = call(
        functools.partial(pack_kernel, z),
        [pack_shape],
        [hbm] * 2,
        (intersection, mp_late),
        [
            scratch(*intersections.shape),
            scratch(pairs, EXTRA, z.paos),
            pltpu.SemaphoreType.DMA((2,)),
        ],
        limit=8,
    )
    if small(z):
        packs = [lax.all_to_all(pack, "orb", 0, 0)]
    else:
        packs = [lax.all_gather(pack, ("orb", "sub"), axis=0, tiled=True)]
    left_below = shifted(gate((left,), pack)[0], "orb", 1)
    mp_other = swapped(mp_late, "sub")
    left_other = swapped(left, "sub")
    c_other = swapped(coefficients, "sub")

    lists = (pair_first, pair_second, pno_ranks)
    (down,) = gate((down,), packs[0], mp_other, left_other, c_other)
    part, right = call(
        functools.partial(sums_kernel, z),
        [(n, pairs * n), (pairs, n, fits)],
        [smem] * 4 + [vmem] * 4,
        (*lists, occ_energy, mp, left, right_here, down),
        limit=8,
    )
    (pack_late,) = gate(packs, part)
    if small(z):
        packs = [pack_late, swapped(pack_late, "fit")]
        packs.append(swapped(pack_late, "sub"))
        sums = part + swapped(part, "fit")
        start_amps = [
            lax.all_to_all(jnp.broadcast_to(sums[None], (z.owners, *sums.shape)), "orb", 0, 0)
        ]
        start_amps.append(swapped(start_amps[0], "sub"))
        packs.append(swapped(gate(packs[1:2], start_amps[0])[0], "sub"))
    else:
        sums = lax.psum(part, "fit")
        start_amps = [lax.all_gather(sums, ("orb", "sub"), axis=0, tiled=False)]

    right_late, mp_late = gate((right, mp_below), part)
    (left_late,) = gate((left_below,), sums)
    right_other, mp_below_other, left_below_other = [
        swapped(value, "sub") for value in (right_late, mp_late, left_late)
    ]

    args = (
        *lists, neighbours, occ_energy, *start_amps, *packs,
        pno_coefficients, c_other, mp, mp_other, mp_below, mp_below_other,
        left, left_other, left_below, left_below_other, right, right_other,
    )
    square = (z.total, n, n)
    amplitudes, gradient = call(
        functools.partial(final_kernel, z),
        [(pairs, n * n), (z.orbitals, half, fits)],
        [smem] * 5 + [vmem] * len(start_amps) + [hbm] * (12 + len(packs)),
        args,
        [
            scratch(len(packs), *packs[0].shape),
            scratch(z.total, n, wide, kind=bf16),
            scratch(z.total, n, wide, kind=bf16),
            scratch(*square),
            scratch(z.total, EXTRA, wide),
            scratch(z.total if small(z) else 1, z.links // 2, n, 2 * n),
            scratch(own, n, half),
            scratch(2 * own, n, half),
            scratch(3 * own, n, fits),
            scratch(z.orbitals, half, fits),
            scratch(pairs, n, n),
            scratch(*square),
        ]
        + [scratch(*square, kind=bf16)] * 4
        + [scratch(2 * own, wide, wide, kind=bf16)] * 2
        + [scratch(z.orbitals * half, 3 * own * n, kind=bf16)] * 2
        + [pltpu.SemaphoreType.DMA((16 + -(-fits // 256),))],
        limit=60,
        out_specs=[vmem, hbm],
    )
    return (amplitudes, gradient)


def solution(mesh):
    in_specs = (
        P(("groups", "orb"), None, "fit"),
        P(("groups", "orb", "sub"), None, None),
        P(("groups", "orb", "sub"), None),
        P("groups"),
        P("groups"),
        P("groups"),
        P("groups", None),
        P(("groups", "orb", "sub"), None),
        P(("groups", "orb", "sub"), None, None),
        P(("groups", "orb", "sub"), None),
        P("groups"),
    )
    out_specs = (P(("groups", "orb", "sub"), None), P(("groups", "orb"), "sub", "fit"))
    return jax.shard_map(body, mesh=mesh, in_specs=in_specs, out_specs=out_specs, check_vma=False)
```

```python
import functools

import jax
import jax.numpy as jnp
from jax import lax
from jax.experimental import pallas as pl
from jax.experimental.pallas import tpu as pltpu
from jax.sharding import PartitionSpec as P

ITERS = 2
SMALL = 4
MIB = 1 << 20
EXTRA = 8

high = lax.Precision.HIGH
BRIEF = pl.CostEstimate(flops=1, bytes_accessed=1, transcendentals=0)
smem = pl.BlockSpec(memory_space=pltpu.SMEM)
vmem = pl.BlockSpec(memory_space=pltpu.VMEM)


def mm(a, b, contract=((1,), (0,))):
    return lax.dot_general(
        a, b, (contract, ((), ())), precision=high, preferred_element_type=jnp.float32
    )


def shifted(value, axis, steps):
    count = lax.axis_size(axis)
    initial, last = (max(0, -steps), min(count, count - steps))
    return lax.ppermute(value, axis, [(source, source + steps) for source in range(initial, last)])


def swapped(value, axis):
    return lax.ppermute(value, axis, [(0, 1), (1, 0)])


def f32(flag):
    return flag.astype(jnp.float32)


class Sizes:
    def __init__(self, blocks, pno_coefficients, couplings):
        self.orbitals, self.paos, self.fits = blocks.shape
        self.pairs, self.pnos = pno_coefficients.shape[:2]
        self.links = couplings.shape[1]
        self.subs = lax.axis_size("sub")
        self.owners = lax.axis_size("orb")
        self.fit_count = lax.axis_size("fit")
        self.own = self.pairs * self.subs
        self.total = self.own * self.owners


anywhere = pl.BlockSpec(memory_space=pl.ANY)
held_out = pl.BlockSpec(memory_space=pltpu.HBM)


def call(kernel, outs, ins, args, scratch=(), limit=16, out_specs=None, cost=None):
    return pl.pallas_call(
        kernel,
        out_shape=[jax.ShapeDtypeStruct(shape, jnp.float32) for shape in outs],
        in_specs=ins,
        out_specs=out_specs or [vmem] * len(outs),
        scratch_shapes=list(scratch),
        cost_estimate=cost,
        compiler_params=pltpu.CompilerParams(vmem_limit_bytes=limit and limit * MIB),
    )(*args)


def started(sources, targets, sems, base=0):
    copies = [
        pltpu.make_async_copy(source, target, sems.at[base + index])
        for index, (source, target) in enumerate(zip(sources, targets))
    ]
    for copy in copies:
        copy.start()
    return copies


def wait(copies):
    for copy in copies:
        copy.wait()


def side_start(z, owner, sub, side):
    return owner * z.own + (sub if side == 0 else 1 - sub) * z.pairs


def scale_of(z, pair, level, first, second, ranks, occupied):
    n = z.pnos
    row_ids = lax.broadcasted_iota(jnp.int32, (n, n), 0)
    column_ids = lax.broadcasted_iota(jnp.int32, (n, n), 1)
    level = level * jnp.ones((n, 1), jnp.float32)
    rank = ranks[pair]
    kept = f32((row_ids < rank) & (column_ids < rank))
    return kept / (level + level.T - (occupied[first[pair]] + occupied[second[pair]]))


def split(value):
    high_part = value.astype(jnp.bfloat16)
    return high_part, (value - high_part.astype(jnp.float32)).astype(jnp.bfloat16)


def mm3(a, b, contract=((1,), (0,))):
    def one(x, y):
        return lax.dot_general(x, y, (contract, ((), ())), preferred_element_type=jnp.float32)

    return one(a[0], b[0]) + (one(a[0], b[1]) + one(a[1], b[0]))


def small(z):
    return z.owners <= SMALL and z.pairs == z.fit_count == 2


def each_pair(z, action):
    if z.owners <= SMALL:
        for pair in range(z.total):
            action(pair)
    else:
        @pl.loop(0, z.total)
        def _(pair):
            action(pair)


def mapped_kernel(z, c_in, map_in, e_in, coupling_in, mp_ref, c_ref, map_ref, e_ref, coupling,
                  sems):
    n = z.pnos
    copies = started(
        [c_in, map_in, e_in, coupling_in], [c_ref, map_ref, e_ref, coupling], sems
    )
    wait(copies)
    rows = lax.broadcasted_iota(jnp.int32, (z.paos, z.paos), 0)
    lane_link = lax.broadcasted_iota(jnp.int32, (1, z.links * n), 1) // n
    for p in range(z.pairs):
        select = f32(map_ref[p : p + 1, :] == rows).astype(jnp.bfloat16)
        c_high, c_low = split(c_ref[p])
        mp_ref[p, :n, :] = lax.dot_general(
            c_high, select, (((1,), (1,)), ((), ())), preferred_element_type=jnp.float32
        ) + lax.dot_general(
            c_low, select, (((1,), (1,)), ((), ())), preferred_element_type=jnp.float32
        )
        mp_ref[p, n:, :] = jnp.zeros((EXTRA, z.paos), jnp.float32)
        mp_ref[p, n : n + 1, :n] = e_ref[p : p + 1, :]
        spread = jnp.zeros((1, z.links * n), jnp.float32)
        for k in range(z.links):
            spread = jnp.where(lane_link == k, coupling[p : p + 1, k : k + 1], spread)
        mp_ref[p, n + 1 : n + 2, :] = spread


def pack_kernel(z, s_in, mp_in, pack_ref, s_ref, mp_ref, sems):
    n = z.pnos
    line = 2 * n
    base = z.links * n // 2
    wait(started([s_in, mp_in.at[:, pl.ds(n, EXTRA), :]], [s_ref, mp_ref], sems))
    for slot in range(1 if small(z) else z.pairs):
        p = lax.axis_index("fit") if small(z) else slot
        for r in range(n // 2):
            lines = s_ref[p, :, r * line : (r + 1) * line]
            for k in range(z.links):
                row = k * n // 2 + r
                pack_ref[slot, row : row + 1, :] = lines[k : k + 1, :]
        pack_ref[slot, base:, :] = jnp.zeros((EXTRA, line), jnp.float32)
        pack_ref[slot, base : base + 1, :] = mp_ref[p, 0:1, :line]
        for k in range(z.links // 2):
            pack_ref[slot, base + 1 + k : base + 2 + k, :] = mp_ref[
                p, 1:2, k * line : (k + 1) * line
            ]
    if small(z):
        for copy in range(1, z.owners):
            pack_ref[copy] = pack_ref[0]


def below_kernel(z, second, mp_below, b_ref, right_ref):
    owner, sub = lax.axis_index("orb"), lax.axis_index("sub")
    start = side_start(z, jnp.maximum(owner - 1, 0), sub, 0)
    for p in range(z.pairs):
        j = second[start + p] - owner * z.orbitals
        held = jnp.where(j >= 0, 1.0, 0.0)
        mapped = mp_below[p, : z.pnos, :] * held
        right_ref[p] = mm(mapped, b_ref[jnp.clip(j, 0, z.orbitals - 1)])


def local_kernel(z, first, second, c_ref, mp_ref, b_ref, left_ref, right_ref):
    owner, sub = lax.axis_index("orb"), lax.axis_index("sub")
    start = side_start(z, owner, sub, 0)
    base = owner * z.orbitals
    for p in range(z.pairs):
        left_ref[p] = mm(c_ref[p], b_ref[first[start + p] - base])
        j = second[start + p] - base
        local = jnp.where(j < z.orbitals, 1.0, 0.0)
        right_ref[p] = mm(
            mp_ref[p, : z.pnos, :] * local, b_ref[jnp.minimum(j, z.orbitals - 1)]
        )


def sums_kernel(z, first, second, ranks, occupied, mp_ref, left_ref, here_ref, down_ref, *refs):
    sums_ref, right_ref = refs[-2:]
    owner, sub = lax.axis_index("orb"), lax.axis_index("sub")
    start = side_start(z, owner, sub, 0)
    n = z.pnos
    for p in range(z.pairs):
        right = here_ref[p] + down_ref[p]
        right_ref[p] = right
        scale = scale_of(
            z, start + p, mp_ref[p, n : n + 1, :n], first, second, ranks, occupied
        )
        part = mm(left_ref[p], right, ((1,), (1,)))
        sums_ref[:, p * n : (p + 1) * n] = -part * scale


def unpack(z, pair, block, rows, slot, s_high, s_low, scale_ref, coupling_ref, lists):
    n = z.pnos
    for k in range(0, z.links, 2):
        two = [block(k * n // 2, n // 2), block((k + 1) * n // 2, n // 2)]
        for odd in range(2):
            rows[slot, k // 2, pl.ds(odd, n // 2, 2), :] = jnp.concatenate(
                [part[:, odd * n : (odd + 1) * n] for part in two], axis=1
            )
    s = jnp.concatenate([rows[slot, k] for k in range(z.links // 2)], axis=1)
    s_high[pair], s_low[pair] = split(s)
    extra = block(z.links * n // 2, EXTRA)
    scale_ref[pair] = scale_of(z, pair, extra[0:1, :n], *lists)
    coupling_ref[pair, 0:1, :] = jnp.concatenate(
        [extra[1 + k : 2 + k, :] for k in range(z.links // 2)], axis=1
    )


def coupled_of(z, index, pair, near, s, coupling, amps_high, amps_low, diag_high, diag_low):
    n = z.pnos
    for k in range(z.links):
        row = near[k, pair]
        block = slice(k * n, (k + 1) * n)
        diag_high[index, block, block] = amps_high[row]
        diag_low[index, block, block] = amps_low[row]
    return split(mm3(s, (diag_high[index], diag_low[index])) * coupling)


def final_kernel(z, first, second, ranks, near, occupied, *refs):
    start_count, pack_count = (2, 4) if small(z) else (1, 1)
    starts = refs[:start_count]
    pack_in = refs[start_count : start_count + pack_count]
    (c_in, c_other, mp_in, mp_other, mp_below, mp_below_other, left_in, left_other, left_below,
     left_below_other, right_in, right_other) = refs[start_count + pack_count :][:12]
    (amp_ref, grad_out, packs, s_high, s_low, scale_ref, coupling_ref, s_rows, c_ref, m_ref, rhs,
     grad, flat, amps, amps_high, amps_low, next_high, next_low, diag_high, diag_low, rows_high,
     rows_low, sems) = refs[start_count + pack_count + 12 :]
    owner, sub = lax.axis_index("orb"), lax.axis_index("sub")
    fit = lax.axis_index("fit")
    n, pairs, own = z.pnos, z.pairs, z.own
    half = z.paos // z.subs
    at = pl.ds(pl.multiple_of(sub * half, half), half)
    lists = (first, second, ranks, occupied)

    def quarters(ref, base=0):
        return [ref.at[pl.ds(base + i * pairs, pairs)] for i in range(4)]

    pack_copies = started(pack_in, [packs.at[i] for i in range(pack_count)], sems)
    small_copies = started(
        [c_in.at[:, :, at], c_other.at[:, :, at]]
        + [ref.at[:, pl.ds(0, n), at] for ref in (mp_in, mp_other, mp_below, mp_below_other)],
        [c_ref.at[pl.ds(0, pairs)], c_ref.at[pl.ds(pairs, pairs)]] + quarters(m_ref),
        sems, 4,
    )
    large_copies = started(
        [right_in, right_other, left_in, left_other, left_below, left_below_other],
        [rhs.at[pl.ds(0, pairs)], rhs.at[pl.ds(pairs, pairs)]] + quarters(rhs, own),
        sems, 10,
    )
    diag_high[...] = jnp.zeros_like(diag_high)
    diag_low[...] = jnp.zeros_like(diag_low)

    def begin(pair, value):
        amps[pair] = value
        amps_high[pair], amps_low[pair] = split(value)

    if small(z):
        for side, ref in ((sub, starts[0]), (1 - sub, starts[1])):
            for who in range(z.owners):
                for p in range(pairs):
                    begin(who * own + side * pairs + p, ref[who, :, p * n : (p + 1) * n])
    else:
        @pl.loop(0, z.owners * z.subs)
        def _(device):
            for p in range(pairs):
                begin(device * pairs + p, starts[0][device, :, p * n : (p + 1) * n])

    wait(pack_copies)
    if small(z):
        for index in range(pack_count):
            side = sub if index < 2 else 1 - sub
            which = fit if index % 2 == 0 else 1 - fit
            for who in range(z.owners):
                unpack(
                    z, who * own + side * pairs + which,
                    lambda start, size: packs[index, who, start : start + size, :], s_rows,
                    index * z.owners + who, s_high, s_low, scale_ref, coupling_ref, lists,
                )
    else:
        @pl.loop(0, z.total)
        def _(pair):
            unpack(
                z, pair, lambda start, size: packs[0, pair, pl.ds(start, size), :], s_rows, 0,
                s_high, s_low, scale_ref, coupling_ref, lists,
            )

    def s_of(pair):
        return s_high[pair], s_low[pair]

    def swept(index, pair, high_amps, low_amps):
        s = s_of(pair)
        inner = coupled_of(
            z, index, pair, near, s, coupling_ref[pair, 0:1, :], high_amps, low_amps, diag_high,
            diag_low,
        )
        return amps[pair] + mm3(inner, s, ((1,), (1,))) * scale_ref[pair]

    if z.owners <= SMALL:
        group = diag_high.shape[0]
        for base in range(0, z.total, group):
            pair_list = range(base, min(base + group, z.total))
            inner = [
                coupled_of(
                    z, index, pair, near, s_of(pair), coupling_ref[pair, 0:1, :], amps_high,
                    amps_low, diag_high, diag_low,
                )
                for index, pair in enumerate(pair_list)
            ]
            for value, pair in zip(inner, pair_list):
                coupled = mm3(value, s_of(pair), ((1,), (1,)))
                next_high[pair], next_low[pair] = split(amps[pair] + coupled * scale_ref[pair])
    else:
        @pl.loop(0, z.total)
        def _(pair):
            next_high[pair], next_low[pair] = split(swept(0, pair, amps_high, amps_low))

    pair_list = [
        side_start(z, who, sub, side) + p
        for who in (owner, jnp.maximum(owner - 1, 0))
        for side in range(z.subs)
        for p in range(pairs)
    ]
    inner = [
        coupled_of(
            z, index, pair, near, s_of(pair), coupling_ref[pair, 0:1, :], next_high, next_low,
            diag_high, diag_low,
        )
        for index, pair in enumerate(pair_list)
    ]
    found = [
        amps[pair] + mm3(value, s_of(pair), ((1,), (1,))) * scale_ref[pair]
        for value, pair in zip(inner, pair_list)
    ]
    turned = [value.T for value in found]
    wait(small_copies)
    weights = [split(2.0 * a - b) for a, b in zip(found, turned)]
    weights_turned = [split(2.0 * b - a) for a, b in zip(found[:own], turned[:own])]
    terms = (
        [mm3(w, split(c_ref[i])) for i, w in enumerate(weights_turned)]
        + [mm3(w, split(m_ref[i])) for i, w in enumerate(weights)]
    )
    orbital_list = (
        [first[pair] - owner * z.orbitals for pair in pair_list[:own]]
        + [second[pair] - owner * z.orbitals for pair in pair_list]
    )
    for index in range(0, 3 * own, 2):
        for o in range(z.orbitals):
            block = jnp.concatenate(
                [
                    jnp.where(orbital_list[i] == o, terms[i], 0.0) for i in (index, index + 1)
                ]
            ).T
            place = (slice(o * half, (o + 1) * half), slice(index * n, (index + 2) * n))
            rows_high[place], rows_low[place] = split(block)

    for p in range(pairs):
        flat[p] = found[p]
        even = flat[p, pl.ds(0, n // 2, 2), :]
        odd = flat[p, pl.ds(1, n // 2, 2), :]
        lines = jnp.concatenate([even, odd], axis=1)
        for r in range(n // 2):
            amp_ref[p : p + 1, r * 2 * n : (r + 1) * 2 * n] = lines[r : r + 1, :]

    wait(large_copies)
    step = 256
    rows = (rows_high[...], rows_low[...])
    copies = []
    for index, start in enumerate(range(0, z.fits, step)):
        factor = rhs[:, :, start : start + step].reshape(3 * own * n, step)
        grad[:, :, start : start + step] = mm3(rows, split(factor)).reshape(
            z.orbitals, half, step
        )
        window = pl.ds(start, step)
        copies += started(
            [grad.at[:, :, window]], [grad_out.at[:, :, window]], sems, 16 + index
        )
    wait(copies)


def gate(values, *after):
    return lax.optimization_barrier((tuple(values), after))[0]


def body(
    blocks,
    pno_coefficients,
    domain_map,
    pair_first,
    pair_second,
    pno_ranks,
    neighbours,
    couplings,
    intersections,
    pno_energy,
    occ_energy,
):
    z = Sizes(blocks, pno_coefficients, couplings)
    n, pairs, own, fits = z.pnos, z.pairs, z.own, z.fits
    half = z.paos // z.subs
    wide = z.links * n
    hbm = held_out
    bf16 = jnp.bfloat16
    more = 0 if z.owners <= SMALL else z.owners

    def scratch(*shape, kind=jnp.float32):
        return pltpu.VMEM(shape, kind)

    pack_shape = (z.owners if small(z) else pairs, z.links * n // 2 + EXTRA, 2 * n)
    (mp,) = call(
        functools.partial(mapped_kernel, z),
        [(pairs, n + EXTRA, z.paos)],
        [hbm] * 4,
        (pno_coefficients, domain_map, pno_energy, couplings),
        [
            scratch(*pno_coefficients.shape),
            pltpu.VMEM(domain_map.shape, jnp.int32),
            scratch(*pno_energy.shape),
            scratch(*couplings.shape),
            pltpu.SemaphoreType.DMA((4,)),
        ],
        limit=None,
    )
    mp_below = shifted(mp, "orb", 1)
    (pack,) = call(
        functools.partial(pack_kernel, z),
        [pack_shape],
        [hbm] * 2,
        (intersections, mp),
        [
            scratch(*intersections.shape),
            scratch(pairs, EXTRA, z.paos),
            pltpu.SemaphoreType.DMA((2,)),
        ],
        limit=None,
    )
    if small(z):
        packs = [lax.all_to_all(pack, "orb", 0, 0)]
    else:
        packs = [lax.all_gather(pack, ("orb", "sub"), axis=0, tiled=True)]
    (right_below,) = call(
        functools.partial(below_kernel, z),
        [(pairs, n, fits)],
        [smem, vmem, vmem],
        (pair_second, gate((mp_below,), pack)[0], blocks),
        limit=8,
    )
    down = shifted(right_below, "orb", -1)
    mp_late, coefficients = gate((mp, pno_coefficients), right_below)
    left, right_here = call(
        functools.partial(local_kernel, z),
        [(pairs, n, fits), (pairs, n, fits)],
        [smem, smem, vmem, vmem, vmem],
        (pair_first, pair_second, coefficients, mp_late, blocks),
        limit=8,
        cost=BRIEF,
    )
    if small(z):
        packs.append(swapped(gate(packs, right_here)[0], "fit"))
    left_below = shifted(left, "orb", 1)
    mp_other = swapped(gate((mp,), right_here)[0], "sub")
    left_other = swapped(left, "sub")
    c_other = swapped(gate((coefficients,), right_here)[0], "sub")

    lists = (pair_first, pair_second, pno_ranks)
    (down,) = gate((down,), mp_other, left_other, c_other)
    part, right = call(
        functools.partial(sums_kernel, z),
        [(n, pairs * n), (pairs, n, fits)],
        [smem] * 4 + [vmem] * 4,
        (*lists, occ_energy, mp, left, right_here, down),
        limit=8,
    )
    if small(z):
        packs += [swapped(value, "sub") for value in gate(packs, part)]
        sums = part + swapped(part, "fit")
        start_amps = [
            lax.all_to_all(jnp.broadcast_to(sums[None], (z.owners, *sums.shape)), "orb", 0, 0)
        ]
        start_amps.append(swapped(start_amps[0], "sub"))
    else:
        sums = lax.psum(part, "fit")
        start_amps = [lax.all_gather(sums, ("orb", "sub"), axis=0, tiled=False)]

    right_late, mp_late = gate((right, mp_below), part)
    (left_late,) = gate((left_below,), sums)
    right_other, mp_below_other, left_below_other = [
        swapped(value, "sub") for value in (right_late, mp_late, left_late)
    ]

    args = (
        *lists, neighbours.T, occ_energy, *start_amps, *packs,
        pno_coefficients, c_other, mp, mp_other, mp_below, mp_below_other,
        left, left_other, left_below, left_below_other, right, right_other,
    )
    square = (z.total, n, n)
    amplitudes, gradient = call(
        functools.partial(final_kernel, z),
        [(pairs, n * n), (z.orbitals, half, fits)],
        [smem] * 5 + [vmem] * len(start_amps) + [hbm] * (12 + len(packs)),
        args,
        [
            scratch(len(packs), *packs[0].shape),
            scratch(z.total, n, wide, kind=bf16),
            scratch(z.total, n, wide, kind=bf16),
            scratch(*square),
            scratch(z.total, EXTRA, wide),
            scratch(z.total if small(z) else 1, z.links // 2, n, 2 * n),
            scratch(own, n, half),
            scratch(2 * own, n, half),
            scratch(3 * own, n, fits),
            scratch(z.orbitals, half, fits),
            scratch(pairs, n, n),
            scratch(*square),
        ]
        + [scratch(*square, kind=bf16)] * 4
        + [scratch(2 * own, wide, wide, kind=bf16)] * 2
        + [scratch(z.orbitals * half, 3 * own * n, kind=bf16)] * 2
        + [pltpu.SemaphoreType.DMA((16 + -(-fits // 256),))],
        limit=60,
        out_specs=[vmem, hbm],
    )
    return (amplitudes, gradient)


def solution(mesh):
    in_specs = (
        P(("groups", "orb"), None, "fit"),
        P(("groups", "orb", "sub"), None, None),
        P(("groups", "orb", "sub"), None),
        P("groups"),
        P("groups"),
        P("groups"),
        P("groups", None),
        P(("groups", "orb", "sub"), None),
        P(("groups", "orb", "sub"), None, None),
        P(("groups", "orb", "sub"), None),
        P("groups"),
    )
    out_specs = (P(("groups", "orb", "sub"), None), P(("groups", "orb"), "sub", "fit"))
    return jax.shard_map(body, mesh=mesh, in_specs=in_specs, out_specs=out_specs, check_vma=False)
```

```python
import functools

import jax
import jax.numpy as jnp
from jax import lax
from jax.experimental import pallas as pl
from jax.experimental.pallas import tpu as pltpu
from jax.sharding import PartitionSpec as P

ITERS = 2
SMALL = 4
MIB = 1 << 20
EXTRA = 8

high = lax.Precision.HIGH
BRIEF = pl.CostEstimate(flops=1, bytes_accessed=1, transcendentals=0)
smem = pl.BlockSpec(memory_space=pltpu.SMEM)
vmem = pl.BlockSpec(memory_space=pltpu.VMEM)


def mm(a, b, contract=((1,), (0,))):
    return lax.dot_general(
        a, b, (contract, ((), ())), precision=high, preferred_element_type=jnp.float32
    )


def shifted(value, axis, steps):
    count = lax.axis_size(axis)
    initial, last = (max(0, -steps), min(count, count - steps))
    return lax.ppermute(value, axis, [(source, source + steps) for source in range(initial, last)])


def swapped(value, axis):
    return lax.ppermute(value, axis, [(0, 1), (1, 0)])


def f32(flag):
    return flag.astype(jnp.float32)


class Sizes:
    def __init__(self, blocks, pno_coefficients, couplings):
        self.orbitals, self.paos, self.fits = blocks.shape
        self.pairs, self.pnos = pno_coefficients.shape[:2]
        self.links = couplings.shape[1]
        self.subs = lax.axis_size("sub")
        self.owners = lax.axis_size("orb")
        self.fit_count = lax.axis_size("fit")
        self.own = self.pairs * self.subs
        self.total = self.own * self.owners


anywhere = pl.BlockSpec(memory_space=pl.ANY)
held_out = pl.BlockSpec(memory_space=pltpu.HBM)


def call(kernel, outs, ins, args, scratch=(), limit=16, out_specs=None, cost=None):
    return pl.pallas_call(
        kernel,
        out_shape=[jax.ShapeDtypeStruct(shape, jnp.float32) for shape in outs],
        in_specs=ins,
        out_specs=out_specs or [vmem] * len(outs),
        scratch_shapes=list(scratch),
        cost_estimate=cost,
        compiler_params=pltpu.CompilerParams(vmem_limit_bytes=limit and limit * MIB),
    )(*args)


def started(sources, targets, sems, base=0):
    copies = [
        pltpu.make_async_copy(source, target, sems.at[base + index])
        for index, (source, target) in enumerate(zip(sources, targets))
    ]
    for copy in copies:
        copy.start()
    return copies


def wait(copies):
    for copy in copies:
        copy.wait()


def side_start(z, owner, sub, side):
    return owner * z.own + (sub if side == 0 else 1 - sub) * z.pairs


def scale_of(z, pair, level, first, second, ranks, occupied):
    n = z.pnos
    row_ids = lax.broadcasted_iota(jnp.int32, (n, n), 0)
    column_ids = lax.broadcasted_iota(jnp.int32, (n, n), 1)
    level = level * jnp.ones((n, 1), jnp.float32)
    rank = ranks[pair]
    kept = f32((row_ids < rank) & (column_ids < rank))
    return kept / (level + level.T - (occupied[first[pair]] + occupied[second[pair]]))


def split(value):
    high_part = value.astype(jnp.bfloat16)
    return high_part, (value - high_part.astype(jnp.float32)).astype(jnp.bfloat16)


def mm3(a, b, contract=((1,), (0,))):
    def one(x, y):
        return lax.dot_general(x, y, (contract, ((), ())), preferred_element_type=jnp.float32)

    return one(a[0], b[0]) + (one(a[0], b[1]) + one(a[1], b[0]))


def small(z):
    return z.owners <= SMALL and z.pairs == z.fit_count == 2


def each_pair(z, action):
    if z.owners <= SMALL:
        for pair in range(z.total):
            action(pair)
    else:
        @pl.loop(0, z.total)
        def _(pair):
            action(pair)


def mapped_kernel(z, c_in, map_in, e_in, coupling_in, mp_ref, c_ref, map_ref, e_ref, coupling,
                  sems):
    n = z.pnos
    copies = started(
        [c_in, map_in, e_in, coupling_in], [c_ref, map_ref, e_ref, coupling], sems
    )
    wait(copies)
    rows = lax.broadcasted_iota(jnp.int32, (z.paos, z.paos), 0)
    lane_link = lax.broadcasted_iota(jnp.int32, (1, z.links * n), 1) // n
    for p in range(z.pairs):
        select = f32(map_ref[p : p + 1, :] == rows).astype(jnp.bfloat16)
        c_high, c_low = split(c_ref[p])
        mp_ref[p, :n, :] = lax.dot_general(
            c_high, select, (((1,), (1,)), ((), ())), preferred_element_type=jnp.float32
        ) + lax.dot_general(
            c_low, select, (((1,), (1,)), ((), ())), preferred_element_type=jnp.float32
        )
        mp_ref[p, n:, :] = jnp.zeros((EXTRA, z.paos), jnp.float32)
        mp_ref[p, n : n + 1, :n] = e_ref[p : p + 1, :]
        spread = jnp.zeros((1, z.links * n), jnp.float32)
        for k in range(z.links):
            spread = jnp.where(lane_link == k, coupling[p : p + 1, k : k + 1], spread)
        mp_ref[p, n + 1 : n + 2, :] = spread


def pack_kernel(z, s_in, mp_in, pack_ref, s_ref, mp_ref, sems):
    n = z.pnos
    line = 2 * n
    base = z.links * n // 2
    wait(started([s_in, mp_in.at[:, pl.ds(n, EXTRA), :]], [s_ref, mp_ref], sems))
    for slot in range(1 if small(z) else z.pairs):
        p = lax.axis_index("fit") if small(z) else slot
        for r in range(n // 2):
            lines = s_ref[p, :, r * line : (r + 1) * line]
            for k in range(z.links):
                row = k * n // 2 + r
                pack_ref[slot, row : row + 1, :] = lines[k : k + 1, :]
        pack_ref[slot, base:, :] = jnp.zeros((EXTRA, line), jnp.float32)
        pack_ref[slot, base : base + 1, :] = mp_ref[p, 0:1, :line]
        for k in range(z.links // 2):
            pack_ref[slot, base + 1 + k : base + 2 + k, :] = mp_ref[
                p, 1:2, k * line : (k + 1) * line
            ]
    if small(z):
        for copy in range(1, z.owners):
            pack_ref[copy] = pack_ref[0]


def below_kernel(z, second, mp_below, b_ref, order, right_ref):
    owner, sub = lax.axis_index("orb"), lax.axis_index("sub")
    start = side_start(z, jnp.maximum(owner - 1, 0), sub, 0)
    for p in range(z.pairs):
        j = second[start + p] - owner * z.orbitals
        held = jnp.where(j >= 0, 1.0, 0.0)
        mapped = mp_below[p, : z.pnos, :] * held
        right_ref[p] = mm(mapped, b_ref[jnp.clip(j, 0, z.orbitals - 1)])


def local_kernel(z, first, second, c_ref, mp_ref, b_ref, left_ref, right_ref):
    owner, sub = lax.axis_index("orb"), lax.axis_index("sub")
    start = side_start(z, owner, sub, 0)
    base = owner * z.orbitals
    for p in range(z.pairs):
        left_ref[p] = mm(c_ref[p], b_ref[first[start + p] - base])
        j = second[start + p] - base
        local = jnp.where(j < z.orbitals, 1.0, 0.0)
        right_ref[p] = mm(
            mp_ref[p, : z.pnos, :] * local, b_ref[jnp.minimum(j, z.orbitals - 1)]
        )


def sums_kernel(z, first, second, ranks, occupied, mp_ref, left_ref, here_ref, down_ref, *refs):
    sums_ref, right_ref = refs[-2:]
    owner, sub = lax.axis_index("orb"), lax.axis_index("sub")
    start = side_start(z, owner, sub, 0)
    n = z.pnos
    for p in range(z.pairs):
        right = here_ref[p] + down_ref[p]
        right_ref[p] = right
        scale = scale_of(
            z, start + p, mp_ref[p, n : n + 1, :n], first, second, ranks, occupied
        )
        part = mm(left_ref[p], right, ((1,), (1,)))
        sums_ref[:, p * n : (p + 1) * n] = -part * scale


def unpack(z, pair, block, rows, slot, s_high, s_low, scale_ref, coupling_ref, lists):
    n = z.pnos
    for k in range(0, z.links, 2):
        two = [block(k * n // 2, n // 2), block((k + 1) * n // 2, n // 2)]
        for odd in range(2):
            rows[slot, k // 2, pl.ds(odd, n // 2, 2), :] = jnp.concatenate(
                [part[:, odd * n : (odd + 1) * n] for part in two], axis=1
            )
    s = jnp.concatenate([rows[slot, k] for k in range(z.links // 2)], axis=1)
    s_high[pair], s_low[pair] = split(s)
    extra = block(z.links * n // 2, EXTRA)
    scale_ref[pair] = scale_of(z, pair, extra[0:1, :n], *lists)
    coupling_ref[pair, 0:1, :] = jnp.concatenate(
        [extra[1 + k : 2 + k, :] for k in range(z.links // 2)], axis=1
    )


def coupled_of(z, index, pair, near, s, coupling, amps_high, amps_low, diag_high, diag_low):
    n = z.pnos
    for k in range(z.links):
        row = near[k, pair]
        block = slice(k * n, (k + 1) * n)
        diag_high[index, block, block] = amps_high[row]
        diag_low[index, block, block] = amps_low[row]
    return split(mm3(s, (diag_high[index], diag_low[index])) * coupling)


def final_kernel(z, first, second, ranks, near, occupied, *refs):
    start_count, pack_count = (2, 4) if small(z) else (1, 1)
    starts = refs[:start_count]
    pack_in = refs[start_count : start_count + pack_count]
    (c_in, c_other, mp_in, mp_other, mp_below, mp_below_other, left_in, left_other, left_below,
     left_below_other, right_in, right_other) = refs[start_count + pack_count :][:12]
    (amp_ref, grad_out, packs, s_high, s_low, scale_ref, coupling_ref, s_rows, c_ref, m_ref, rhs,
     grad, flat, amps, amps_high, amps_low, next_high, next_low, diag_high, diag_low, rows_high,
     rows_low, sems) = refs[start_count + pack_count + 12 :]
    owner, sub = lax.axis_index("orb"), lax.axis_index("sub")
    fit = lax.axis_index("fit")
    n, pairs, own = z.pnos, z.pairs, z.own
    half = z.paos // z.subs
    at = pl.ds(pl.multiple_of(sub * half, half), half)
    lists = (first, second, ranks, occupied)

    def quarters(ref, base=0):
        return [ref.at[pl.ds(base + i * pairs, pairs)] for i in range(4)]

    pack_copies = started(pack_in, [packs.at[i] for i in range(pack_count)], sems)
    small_copies = started(
        [c_in.at[:, :, at], c_other.at[:, :, at]]
        + [ref.at[:, pl.ds(0, n), at] for ref in (mp_in, mp_other, mp_below, mp_below_other)],
        [c_ref.at[pl.ds(0, pairs)], c_ref.at[pl.ds(pairs, pairs)]] + quarters(m_ref),
        sems, 4,
    )
    large_copies = started(
        [right_in, right_other, left_in, left_other, left_below, left_below_other],
        [rhs.at[pl.ds(0, pairs)], rhs.at[pl.ds(pairs, pairs)]] + quarters(rhs, own),
        sems, 10,
    )
    diag_high[...] = jnp.zeros_like(diag_high)
    diag_low[...] = jnp.zeros_like(diag_low)

    def begin(pair, value):
        amps[pair] = value
        amps_high[pair], amps_low[pair] = split(value)

    if small(z):
        for side, ref in ((sub, starts[0]), (1 - sub, starts[1])):
            for who in range(z.owners):
                for p in range(pairs):
                    begin(who * own + side * pairs + p, ref[who, :, p * n : (p + 1) * n])
    else:
        @pl.loop(0, z.owners * z.subs)
        def _(device):
            for p in range(pairs):
                begin(device * pairs + p, starts[0][device, :, p * n : (p + 1) * n])

    wait(pack_copies)
    if small(z):
        for index in range(pack_count):
            side = sub if index < 2 else 1 - sub
            which = fit if index % 2 == 0 else 1 - fit
            for who in range(z.owners):
                unpack(
                    z, who * own + side * pairs + which,
                    lambda start, size: packs[index, who, start : start + size, :], s_rows,
                    index * z.owners + who, s_high, s_low, scale_ref, coupling_ref, lists,
                )
    else:
        @pl.loop(0, z.total)
        def _(pair):
            unpack(
                z, pair, lambda start, size: packs[0, pair, pl.ds(start, size), :], s_rows, 0,
                s_high, s_low, scale_ref, coupling_ref, lists,
            )

    def s_of(pair):
        return s_high[pair], s_low[pair]

    def swept(index, pair, high_amps, low_amps):
        s = s_of(pair)
        inner = coupled_of(
            z, index, pair, near, s, coupling_ref[pair, 0:1, :], high_amps, low_amps, diag_high,
            diag_low,
        )
        return amps[pair] + mm3(inner, s, ((1,), (1,))) * scale_ref[pair]

    if z.owners <= SMALL:
        group = diag_high.shape[0]
        for base in range(0, z.total, group):
            pair_list = range(base, min(base + group, z.total))
            inner = [
                coupled_of(
                    z, index, pair, near, s_of(pair), coupling_ref[pair, 0:1, :], amps_high,
                    amps_low, diag_high, diag_low,
                )
                for index, pair in enumerate(pair_list)
            ]
            for value, pair in zip(inner, pair_list):
                coupled = mm3(value, s_of(pair), ((1,), (1,)))
                next_high[pair], next_low[pair] = split(amps[pair] + coupled * scale_ref[pair])
    else:
        @pl.loop(0, z.total)
        def _(pair):
            next_high[pair], next_low[pair] = split(swept(0, pair, amps_high, amps_low))

    pair_list = [
        side_start(z, who, sub, side) + p
        for who in (owner, jnp.maximum(owner - 1, 0))
        for side in range(z.subs)
        for p in range(pairs)
    ]
    inner = [
        coupled_of(
            z, index, pair, near, s_of(pair), coupling_ref[pair, 0:1, :], next_high, next_low,
            diag_high, diag_low,
        )
        for index, pair in enumerate(pair_list)
    ]
    found = [
        amps[pair] + mm3(value, s_of(pair), ((1,), (1,))) * scale_ref[pair]
        for value, pair in zip(inner, pair_list)
    ]
    turned = [value.T for value in found]
    wait(small_copies)
    weights = [split(2.0 * a - b) for a, b in zip(found, turned)]
    weights_turned = [split(2.0 * b - a) for a, b in zip(found[:own], turned[:own])]
    terms = (
        [mm3(w, split(c_ref[i])) for i, w in enumerate(weights_turned)]
        + [mm3(w, split(m_ref[i])) for i, w in enumerate(weights)]
    )
    orbital_list = (
        [first[pair] - owner * z.orbitals for pair in pair_list[:own]]
        + [second[pair] - owner * z.orbitals for pair in pair_list]
    )
    for index in range(0, 3 * own, 2):
        for o in range(z.orbitals):
            block = jnp.concatenate(
                [
                    jnp.where(orbital_list[i] == o, terms[i], 0.0) for i in (index, index + 1)
                ]
            ).T
            place = (slice(o * half, (o + 1) * half), slice(index * n, (index + 2) * n))
            rows_high[place], rows_low[place] = split(block)

    for p in range(pairs):
        flat[p] = found[p]
        even = flat[p, pl.ds(0, n // 2, 2), :]
        odd = flat[p, pl.ds(1, n // 2, 2), :]
        lines = jnp.concatenate([even, odd], axis=1)
        for r in range(n // 2):
            amp_ref[p : p + 1, r * 2 * n : (r + 1) * 2 * n] = lines[r : r + 1, :]

    wait(large_copies)
    step = 256
    rows = (rows_high[...], rows_low[...])
    copies = []
    for index, start in enumerate(range(0, z.fits, step)):
        factor = rhs[:, :, start : start + step].reshape(3 * own * n, step)
        grad[:, :, start : start + step] = mm3(rows, split(factor)).reshape(
            z.orbitals, half, step
        )
        window = pl.ds(start, step)
        copies += started(
            [grad.at[:, :, window]], [grad_out.at[:, :, window]], sems, 16 + index
        )
    wait(copies)


def gate(values, *after):
    return lax.optimization_barrier((tuple(values), after))[0]


def body(
    blocks,
    pno_coefficients,
    domain_map,
    pair_first,
    pair_second,
    pno_ranks,
    neighbours,
    couplings,
    intersections,
    pno_energy,
    occ_energy,
):
    z = Sizes(blocks, pno_coefficients, couplings)
    n, pairs, own, fits = z.pnos, z.pairs, z.own, z.fits
    half = z.paos // z.subs
    wide = z.links * n
    hbm = held_out
    bf16 = jnp.bfloat16
    more = 0 if z.owners <= SMALL else z.owners

    def scratch(*shape, kind=jnp.float32):
        return pltpu.VMEM(shape, kind)

    pack_shape = (z.owners if small(z) else pairs, z.links * n // 2 + EXTRA, 2 * n)
    (mp,) = call(
        functools.partial(mapped_kernel, z),
        [(pairs, n + EXTRA, z.paos)],
        [hbm] * 4,
        (pno_coefficients, domain_map, pno_energy, couplings),
        [
            scratch(*pno_coefficients.shape),
            pltpu.VMEM(domain_map.shape, jnp.int32),
            scratch(*pno_energy.shape),
            scratch(*couplings.shape),
            pltpu.SemaphoreType.DMA((4,)),
        ],
        limit=None,
    )
    mp_below = shifted(mp, "orb", 1)
    pack_shape = (z.owners if small(z) else pairs, z.links * n // 2 + EXTRA, 2 * n)
    (pack,) = call(
        functools.partial(pack_kernel, z),
        [pack_shape],
        [hbm] * 2,
        (intersections, mp),
        [
            scratch(*intersections.shape),
            scratch(pairs, EXTRA, z.paos),
            pltpu.SemaphoreType.DMA((2,)),
        ],
        limit=None,
    )
    if small(z):
        packs = [lax.all_to_all(pack, "orb", 0, 0)]
    else:
        packs = [lax.all_gather(pack, ("orb", "sub"), axis=0, tiled=True)]
    (right_below,) = call(
        functools.partial(below_kernel, z),
        [(pairs, n, fits)],
        [smem, vmem, vmem, anywhere],
        (pair_second, mp_below, blocks, pack),
        limit=8,
    )
    down = shifted(right_below, "orb", -1)
    (coefficients,) = gate((pno_coefficients,), right_below)
    left, right_here = call(
        functools.partial(local_kernel, z),
        [(pairs, n, fits), (pairs, n, fits)],
        [smem, smem, vmem, vmem, vmem],
        (pair_first, pair_second, coefficients, mp, blocks),
        limit=8,
    )
    left_late, mp_late, coefficients = gate((left, mp, coefficients), right_here)
    left_below = shifted(left_late, "orb", 1)
    mp_other = swapped(mp_late, "sub")
    left_other = swapped(left_late, "sub")
    c_other = swapped(coefficients, "sub")
    if small(z):
        packs.append(swapped(gate(packs, right_here)[0], "fit"))

    lists = (pair_first, pair_second, pno_ranks)
    part, right = call(
        functools.partial(sums_kernel, z),
        [(n, pairs * n), (pairs, n, fits)],
        [smem] * 4 + [vmem] * 4 + [anywhere] * 3,
        (*lists, occ_energy, mp, left, right_here, down, left_other, mp_other, c_other),
        limit=8,
    )
    if small(z):
        packs += [swapped(value, "sub") for value in gate(packs, part)]
        sums = part + swapped(part, "fit")
        start_amps = [
            lax.all_to_all(jnp.broadcast_to(sums[None], (z.owners, *sums.shape)), "orb", 0, 0)
        ]
        start_amps.append(swapped(start_amps[0], "sub"))
    else:
        sums = lax.psum(part, "fit")
        start_amps = [lax.all_gather(sums, ("orb", "sub"), axis=0, tiled=False)]

    right_late, mp_late = gate((right, mp_below), part)
    (left_late,) = gate((left_below,), sums)
    right_other, mp_below_other, left_below_other = [
        swapped(value, "sub") for value in (right_late, mp_late, left_late)
    ]

    args = (
        *lists, neighbours.T, occ_energy, *start_amps, *packs,
        pno_coefficients, c_other, mp, mp_other, mp_below, mp_below_other,
        left, left_other, left_below, left_below_other, right, right_other,
    )
    square = (z.total, n, n)
    amplitudes, gradient = call(
        functools.partial(final_kernel, z),
        [(pairs, n * n), (z.orbitals, half, fits)],
        [smem] * 5 + [vmem] * len(start_amps) + [hbm] * (12 + len(packs)),
        args,
        [
            scratch(len(packs), *packs[0].shape),
            scratch(z.total, n, wide, kind=bf16),
            scratch(z.total, n, wide, kind=bf16),
            scratch(*square),
            scratch(z.total, EXTRA, wide),
            scratch(z.total if small(z) else 1, z.links // 2, n, 2 * n),
            scratch(own, n, half),
            scratch(2 * own, n, half),
            scratch(3 * own, n, fits),
            scratch(z.orbitals, half, fits),
            scratch(pairs, n, n),
            scratch(*square),
        ]
        + [scratch(*square, kind=bf16)] * 4
        + [scratch(2 * own, wide, wide, kind=bf16)] * 2
        + [scratch(z.orbitals * half, 3 * own * n, kind=bf16)] * 2
        + [pltpu.SemaphoreType.DMA((16 + -(-fits // 256),))],
        limit=60,
        out_specs=[vmem, hbm],
    )
    return (amplitudes, gradient)


def solution(mesh):
    in_specs = (
        P(("groups", "orb"), None, "fit"),
        P(("groups", "orb", "sub"), None, None),
        P(("groups", "orb", "sub"), None),
        P("groups"),
        P("groups"),
        P("groups"),
        P("groups", None),
        P(("groups", "orb", "sub"), None),
        P(("groups", "orb", "sub"), None, None),
        P(("groups", "orb", "sub"), None),
        P("groups"),
    )
    out_specs = (P(("groups", "orb", "sub"), None), P(("groups", "orb"), "sub", "fit"))
    return jax.shard_map(body, mesh=mesh, in_specs=in_specs, out_specs=out_specs, check_vma=False)
```

```python
import functools

import jax
import jax.numpy as jnp
from jax import lax
from jax.experimental import pallas as pl
from jax.experimental.pallas import tpu as pltpu
from jax.sharding import PartitionSpec as P

ITERS = 2
SMALL = 4
MIB = 1 << 20
EXTRA = 8

high = lax.Precision.HIGH
BRIEF = pl.CostEstimate(flops=1, bytes_accessed=1, transcendentals=0)
smem = pl.BlockSpec(memory_space=pltpu.SMEM)
vmem = pl.BlockSpec(memory_space=pltpu.VMEM)


def mm(a, b, contract=((1,), (0,))):
    return lax.dot_general(
        a, b, (contract, ((), ())), precision=high, preferred_element_type=jnp.float32
    )


def shifted(value, axis, steps):
    count = lax.axis_size(axis)
    initial, last = (max(0, -steps), min(count, count - steps))
    return lax.ppermute(value, axis, [(source, source + steps) for source in range(initial, last)])


def swapped(value, axis):
    return lax.ppermute(value, axis, [(0, 1), (1, 0)])


def f32(flag):
    return flag.astype(jnp.float32)


class Sizes:
    def __init__(self, blocks, pno_coefficients, couplings):
        self.orbitals, self.paos, self.fits = blocks.shape
        self.pairs, self.pnos = pno_coefficients.shape[:2]
        self.links = couplings.shape[1]
        self.subs = lax.axis_size("sub")
        self.owners = lax.axis_size("orb")
        self.fit_count = lax.axis_size("fit")
        self.own = self.pairs * self.subs
        self.total = self.own * self.owners


anywhere = pl.BlockSpec(memory_space=pl.ANY)
held_out = pl.BlockSpec(memory_space=pltpu.HBM)


def call(kernel, outs, ins, args, scratch=(), limit=16, out_specs=None, cost=None):
    return pl.pallas_call(
        kernel,
        out_shape=[jax.ShapeDtypeStruct(shape, jnp.float32) for shape in outs],
        in_specs=ins,
        out_specs=out_specs or [vmem] * len(outs),
        scratch_shapes=list(scratch),
        cost_estimate=cost,
        compiler_params=pltpu.CompilerParams(vmem_limit_bytes=limit and limit * MIB),
    )(*args)


def started(sources, targets, sems, base=0):
    copies = [
        pltpu.make_async_copy(source, target, sems.at[base + index])
        for index, (source, target) in enumerate(zip(sources, targets))
    ]
    for copy in copies:
        copy.start()
    return copies


def wait(copies):
    for copy in copies:
        copy.wait()


def side_start(z, owner, sub, side):
    return owner * z.own + (sub if side == 0 else 1 - sub) * z.pairs


def scale_of(z, pair, level, first, second, ranks, occupied):
    n = z.pnos
    row_ids = lax.broadcasted_iota(jnp.int32, (n, n), 0)
    column_ids = lax.broadcasted_iota(jnp.int32, (n, n), 1)
    level = level * jnp.ones((n, 1), jnp.float32)
    rank = ranks[pair]
    kept = f32((row_ids < rank) & (column_ids < rank))
    return kept / (level + level.T - (occupied[first[pair]] + occupied[second[pair]]))


def split(value):
    high_part = value.astype(jnp.bfloat16)
    return high_part, (value - high_part.astype(jnp.float32)).astype(jnp.bfloat16)


def mm3(a, b, contract=((1,), (0,))):
    def one(x, y):
        return lax.dot_general(x, y, (contract, ((), ())), preferred_element_type=jnp.float32)

    return one(a[0], b[0]) + (one(a[0], b[1]) + one(a[1], b[0]))


def small(z):
    return z.owners <= SMALL and z.pairs == z.fit_count == 2


def each_pair(z, action):
    if z.owners <= SMALL:
        for pair in range(z.total):
            action(pair)
    else:
        @pl.loop(0, z.total)
        def _(pair):
            action(pair)


def mapped_kernel(z, c_in, map_in, e_in, coupling_in, mp_ref, c_ref, map_ref, e_ref, coupling,
                  sems):
    n = z.pnos
    copies = started(
        [c_in, map_in, e_in, coupling_in], [c_ref, map_ref, e_ref, coupling], sems
    )
    wait(copies)
    rows = lax.broadcasted_iota(jnp.int32, (z.paos, z.paos), 0)
    lane_link = lax.broadcasted_iota(jnp.int32, (1, z.links * n), 1) // n
    for p in range(z.pairs):
        select = f32(map_ref[p : p + 1, :] == rows).astype(jnp.bfloat16)
        c_high, c_low = split(c_ref[p])
        mp_ref[p, :n, :] = lax.dot_general(
            c_high, select, (((1,), (1,)), ((), ())), preferred_element_type=jnp.float32
        ) + lax.dot_general(
            c_low, select, (((1,), (1,)), ((), ())), preferred_element_type=jnp.float32
        )
        mp_ref[p, n:, :] = jnp.zeros((EXTRA, z.paos), jnp.float32)
        mp_ref[p, n : n + 1, :n] = e_ref[p : p + 1, :]
        spread = jnp.zeros((1, z.links * n), jnp.float32)
        for k in range(z.links):
            spread = jnp.where(lane_link == k, coupling[p : p + 1, k : k + 1], spread)
        mp_ref[p, n + 1 : n + 2, :] = spread


def pack_kernel(z, s_in, mp_in, pack_ref, s_ref, mp_ref, sems):
    n = z.pnos
    line = 2 * n
    base = z.links * n // 2
    wait(started([s_in, mp_in.at[:, pl.ds(n, EXTRA), :]], [s_ref, mp_ref], sems))
    for slot in range(1 if small(z) else z.pairs):
        p = lax.axis_index("fit") if small(z) else slot
        for r in range(n // 2):
            lines = s_ref[p, :, r * line : (r + 1) * line]
            for k in range(z.links):
                row = k * n // 2 + r
                pack_ref[slot, row : row + 1, :] = lines[k : k + 1, :]
        pack_ref[slot, base:, :] = jnp.zeros((EXTRA, line), jnp.float32)
        pack_ref[slot, base : base + 1, :] = mp_ref[p, 0:1, :line]
        for k in range(z.links // 2):
            pack_ref[slot, base + 1 + k : base + 2 + k, :] = mp_ref[
                p, 1:2, k * line : (k + 1) * line
            ]
    if small(z):
        for copy in range(1, z.owners):
            pack_ref[copy] = pack_ref[0]


def below_kernel(z, second, mp_below, b_ref, right_ref):
    owner, sub = lax.axis_index("orb"), lax.axis_index("sub")
    start = side_start(z, jnp.maximum(owner - 1, 0), sub, 0)
    for p in range(z.pairs):
        j = second[start + p] - owner * z.orbitals
        held = jnp.where(j >= 0, 1.0, 0.0)
        mapped = mp_below[p, : z.pnos, :] * held
        right_ref[p] = mm(mapped, b_ref[jnp.clip(j, 0, z.orbitals - 1)])


def local_kernel(z, first, second, c_ref, mp_ref, b_ref, left_ref, right_ref):
    owner, sub = lax.axis_index("orb"), lax.axis_index("sub")
    start = side_start(z, owner, sub, 0)
    base = owner * z.orbitals
    for p in range(z.pairs):
        left_ref[p] = mm(c_ref[p], b_ref[first[start + p] - base])
        j = second[start + p] - base
        local = jnp.where(j < z.orbitals, 1.0, 0.0)
        right_ref[p] = mm(
            mp_ref[p, : z.pnos, :] * local, b_ref[jnp.minimum(j, z.orbitals - 1)]
        )


def sums_kernel(z, first, second, ranks, occupied, mp_ref, left_ref, here_ref, down_ref, *refs):
    sums_ref, right_ref = refs[-2:]
    owner, sub = lax.axis_index("orb"), lax.axis_index("sub")
    start = side_start(z, owner, sub, 0)
    n = z.pnos
    for p in range(z.pairs):
        right = here_ref[p] + down_ref[p]
        right_ref[p] = right
        scale = scale_of(
            z, start + p, mp_ref[p, n : n + 1, :n], first, second, ranks, occupied
        )
        part = mm(left_ref[p], right, ((1,), (1,)))
        sums_ref[:, p * n : (p + 1) * n] = -part * scale


def unpack(z, pair, block, rows, slot, s_high, s_low, scale_ref, coupling_ref, lists):
    n = z.pnos
    for k in range(0, z.links, 2):
        two = [block(k * n // 2, n // 2), block((k + 1) * n // 2, n // 2)]
        for odd in range(2):
            rows[slot, k // 2, pl.ds(odd, n // 2, 2), :] = jnp.concatenate(
                [part[:, odd * n : (odd + 1) * n] for part in two], axis=1
            )
    s = jnp.concatenate([rows[slot, k] for k in range(z.links // 2)], axis=1)
    s_high[pair], s_low[pair] = split(s)
    extra = block(z.links * n // 2, EXTRA)
    scale_ref[pair] = scale_of(z, pair, extra[0:1, :n], *lists)
    coupling_ref[pair, 0:1, :] = jnp.concatenate(
        [extra[1 + k : 2 + k, :] for k in range(z.links // 2)], axis=1
    )


def coupled_of(z, index, pair, near, s, coupling, amps_high, amps_low, diag_high, diag_low):
    n = z.pnos
    for k in range(z.links):
        row = near[k, pair]
        block = slice(k * n, (k + 1) * n)
        diag_high[index, block, block] = amps_high[row]
        diag_low[index, block, block] = amps_low[row]
    return split(mm3(s, (diag_high[index], diag_low[index])) * coupling)


def final_kernel(z, first, second, ranks, near, occupied, *refs):
    start_count, pack_count = (2, 4) if small(z) else (1, 1)
    starts_in = refs[:start_count]
    pack_in = refs[start_count : start_count + pack_count]
    (c_in, c_other, mp_in, mp_other, mp_below, mp_below_other, left_in, left_other, left_below,
     left_below_other, right_in, right_other) = refs[start_count + pack_count :][:12]
    (amp_out, grad_out, starts, amp_ref, packs, s_high, s_low, scale_ref, coupling_ref, s_rows, c_ref, m_ref, rhs,
     grad, flat, amps, amps_high, amps_low, next_high, next_low, diag_high, diag_low, rows_high,
     rows_low, sems) = refs[start_count + pack_count + 12 :]
    owner, sub = lax.axis_index("orb"), lax.axis_index("sub")
    fit = lax.axis_index("fit")
    n, pairs, own = z.pnos, z.pairs, z.own
    half = z.paos // z.subs
    at = pl.ds(pl.multiple_of(sub * half, half), half)
    lists = (first, second, ranks, occupied)

    def quarters(ref, base=0):
        return [ref.at[pl.ds(base + i * pairs, pairs)] for i in range(4)]

    start_copies = started(starts_in, [starts.at[i] for i in range(start_count)], sems, 16)
    pack_copies = started(pack_in, [packs.at[i] for i in range(pack_count)], sems)
    small_copies = started(
        [c_in.at[:, :, at], c_other.at[:, :, at]]
        + [ref.at[:, pl.ds(0, n), at] for ref in (mp_in, mp_other, mp_below, mp_below_other)],
        [c_ref.at[pl.ds(0, pairs)], c_ref.at[pl.ds(pairs, pairs)]] + quarters(m_ref),
        sems, 4,
    )
    large_copies = started(
        [right_in, right_other, left_in, left_other, left_below, left_below_other],
        [rhs.at[pl.ds(0, pairs)], rhs.at[pl.ds(pairs, pairs)]] + quarters(rhs, own),
        sems, 10,
    )
    diag_high[...] = jnp.zeros_like(diag_high)
    diag_low[...] = jnp.zeros_like(diag_low)

    wait(start_copies)

    def begin(pair, value):
        amps[pair] = value
        amps_high[pair], amps_low[pair] = split(value)

    if small(z):
        for index, side in enumerate((sub, 1 - sub)):
            for who in range(z.owners):
                for p in range(pairs):
                    begin(
                        who * own + side * pairs + p,
                        starts[index, who, :, p * n : (p + 1) * n],
                    )
    else:
        @pl.loop(0, z.owners * z.subs)
        def _(device):
            for p in range(pairs):
                begin(device * pairs + p, starts[0, device, :, p * n : (p + 1) * n])

    wait(pack_copies)
    if small(z):
        for index in range(pack_count):
            side = sub if index < 2 else 1 - sub
            which = fit if index % 2 == 0 else 1 - fit
            for who in range(z.owners):
                unpack(
                    z, who * own + side * pairs + which,
                    lambda start, size: packs[index, who, start : start + size, :], s_rows,
                    index * z.owners + who, s_high, s_low, scale_ref, coupling_ref, lists,
                )
    else:
        @pl.loop(0, z.total)
        def _(pair):
            unpack(
                z, pair, lambda start, size: packs[0, pair, pl.ds(start, size), :], s_rows, 0,
                s_high, s_low, scale_ref, coupling_ref, lists,
            )

    def s_of(pair):
        return s_high[pair], s_low[pair]

    def swept(index, pair, high_amps, low_amps):
        s = s_of(pair)
        inner = coupled_of(
            z, index, pair, near, s, coupling_ref[pair, 0:1, :], high_amps, low_amps, diag_high,
            diag_low,
        )
        return amps[pair] + mm3(inner, s, ((1,), (1,))) * scale_ref[pair]

    if z.owners <= SMALL:
        group = diag_high.shape[0]
        for base in range(0, z.total, group):
            pair_list = range(base, min(base + group, z.total))
            inner = [
                coupled_of(
                    z, index, pair, near, s_of(pair), coupling_ref[pair, 0:1, :], amps_high,
                    amps_low, diag_high, diag_low,
                )
                for index, pair in enumerate(pair_list)
            ]
            for value, pair in zip(inner, pair_list):
                coupled = mm3(value, s_of(pair), ((1,), (1,)))
                next_high[pair], next_low[pair] = split(amps[pair] + coupled * scale_ref[pair])
    else:
        @pl.loop(0, z.total)
        def _(pair):
            next_high[pair], next_low[pair] = split(swept(0, pair, amps_high, amps_low))

    pair_list = [
        side_start(z, who, sub, side) + p
        for who in (owner, jnp.maximum(owner - 1, 0))
        for side in range(z.subs)
        for p in range(pairs)
    ]
    inner = [
        coupled_of(
            z, index, pair, near, s_of(pair), coupling_ref[pair, 0:1, :], next_high, next_low,
            diag_high, diag_low,
        )
        for index, pair in enumerate(pair_list)
    ]
    found = [
        amps[pair] + mm3(value, s_of(pair), ((1,), (1,))) * scale_ref[pair]
        for value, pair in zip(inner, pair_list)
    ]
    turned = [value.T for value in found]
    wait(small_copies)
    weights = [split(2.0 * a - b) for a, b in zip(found, turned)]
    weights_turned = [split(2.0 * b - a) for a, b in zip(found[:own], turned[:own])]
    terms = (
        [mm3(w, split(c_ref[i])) for i, w in enumerate(weights_turned)]
        + [mm3(w, split(m_ref[i])) for i, w in enumerate(weights)]
    )
    orbital_list = (
        [first[pair] - owner * z.orbitals for pair in pair_list[:own]]
        + [second[pair] - owner * z.orbitals for pair in pair_list]
    )
    for index in range(0, 3 * own, 2):
        for o in range(z.orbitals):
            block = jnp.concatenate(
                [
                    jnp.where(orbital_list[i] == o, terms[i], 0.0) for i in (index, index + 1)
                ]
            ).T
            place = (slice(o * half, (o + 1) * half), slice(index * n, (index + 2) * n))
            rows_high[place], rows_low[place] = split(block)

    for p in range(pairs):
        flat[p] = found[p]
        even = flat[p, pl.ds(0, n // 2, 2), :]
        odd = flat[p, pl.ds(1, n // 2, 2), :]
        lines = jnp.concatenate([even, odd], axis=1)
        for r in range(n // 2):
            amp_ref[p : p + 1, r * 2 * n : (r + 1) * 2 * n] = lines[r : r + 1, :]
    copies = started([amp_ref], [amp_out], sems, 18)

    wait(large_copies)
    step = 256
    rows = (rows_high[...], rows_low[...])
    for index, start in enumerate(range(0, z.fits, step)):
        factor = rhs[:, :, start : start + step].reshape(3 * own * n, step)
        grad[:, :, start : start + step] = mm3(rows, split(factor)).reshape(
            z.orbitals, half, step
        )
        window = pl.ds(start, step)
        copies += started(
            [grad.at[:, :, window]], [grad_out.at[:, :, window]], sems, 19 + index
        )
    wait(copies)


def gate(values, *after):
    return lax.optimization_barrier((tuple(values), after))[0]


def body(
    blocks,
    pno_coefficients,
    domain_map,
    pair_first,
    pair_second,
    pno_ranks,
    neighbours,
    couplings,
    intersections,
    pno_energy,
    occ_energy,
):
    z = Sizes(blocks, pno_coefficients, couplings)
    n, pairs, own, fits = z.pnos, z.pairs, z.own, z.fits
    half = z.paos // z.subs
    wide = z.links * n
    hbm = held_out
    bf16 = jnp.bfloat16
    more = 0 if z.owners <= SMALL else z.owners

    def scratch(*shape, kind=jnp.float32):
        return pltpu.VMEM(shape, kind)

    pack_shape = (z.owners if small(z) else pairs, z.links * n // 2 + EXTRA, 2 * n)
    (mp,) = call(
        functools.partial(mapped_kernel, z),
        [(pairs, n + EXTRA, z.paos)],
        [hbm] * 4,
        (pno_coefficients, domain_map, pno_energy, couplings),
        [
            scratch(*pno_coefficients.shape),
            pltpu.VMEM(domain_map.shape, jnp.int32),
            scratch(*pno_energy.shape),
            scratch(*couplings.shape),
            pltpu.SemaphoreType.DMA((4,)),
        ],
        limit=None,
    )
    mp_below = shifted(mp, "orb", 1)
    (pack,) = call(
        functools.partial(pack_kernel, z),
        [pack_shape],
        [hbm] * 2,
        (intersections, mp),
        [
            scratch(*intersections.shape),
            scratch(pairs, EXTRA, z.paos),
            pltpu.SemaphoreType.DMA((2,)),
        ],
        limit=None,
    )
    if small(z):
        packs = [lax.all_to_all(pack, "orb", 0, 0)]
    else:
        packs = [lax.all_gather(pack, ("orb", "sub"), axis=0, tiled=True)]
    (right_below,) = call(
        functools.partial(below_kernel, z),
        [(pairs, n, fits)],
        [smem, vmem, vmem],
        (pair_second, gate((mp_below,), pack)[0], blocks),
        limit=8,
    )
    down = shifted(right_below, "orb", -1)
    mp_late, coefficients = gate((mp, pno_coefficients), right_below)
    left, right_here = call(
        functools.partial(local_kernel, z),
        [(pairs, n, fits), (pairs, n, fits)],
        [smem, smem, vmem, vmem, vmem],
        (pair_first, pair_second, coefficients, mp_late, blocks),
        limit=8,
        cost=BRIEF,
    )
    left_below = shifted(gate((left,), packs[0])[0], "orb", 1)
    mp_other = swapped(gate((mp,), right_here)[0], "sub")
    left_other = swapped(left, "sub")
    c_other = swapped(gate((coefficients,), right_here)[0], "sub")

    lists = (pair_first, pair_second, pno_ranks)
    (down,) = gate((down,), mp_other, left_other, c_other)
    part, right = call(
        functools.partial(sums_kernel, z),
        [(n, pairs * n), (pairs, n, fits)],
        [smem] * 4 + [vmem] * 4,
        (*lists, occ_energy, mp, left, right_here, down),
        limit=8,
    )
    if small(z):
        packs.append(None)
        packs.append(swapped(gate(packs[:1], part)[0], "sub"))
        sums = part + swapped(part, "fit")
        packs[1] = swapped(gate(packs[:1], sums)[0], "fit")
        start_amps = [
            lax.all_to_all(jnp.broadcast_to(sums[None], (z.owners, *sums.shape)), "orb", 0, 0)
        ]
        start_amps.append(swapped(start_amps[0], "sub"))
        packs.append(swapped(gate(packs[1:2], start_amps[0])[0], "sub"))
    else:
        sums = lax.psum(part, "fit")
        start_amps = [lax.all_gather(sums, ("orb", "sub"), axis=0, tiled=False)]

    right_late, mp_late = gate((right, mp_below), part)
    (left_late,) = gate((left_below,), sums)
    right_other, mp_below_other, left_below_other = [
        swapped(value, "sub") for value in (right_late, mp_late, left_late)
    ]

    args = (
        *lists, neighbours.T, occ_energy, *start_amps, *packs,
        pno_coefficients, c_other, mp, mp_other, mp_below, mp_below_other,
        left, left_other, left_below, left_below_other, right, right_other,
    )
    square = (z.total, n, n)
    amplitudes, gradient = call(
        functools.partial(final_kernel, z),
        [(pairs, n * n), (z.orbitals, half, fits)],
        [smem] * 5 + [hbm] * (12 + len(start_amps) + len(packs)),
        args,
        [
            scratch(len(start_amps), *start_amps[0].shape),
            scratch(pairs, n * n),
            scratch(len(packs), *packs[0].shape),
            scratch(z.total, n, wide, kind=bf16),
            scratch(z.total, n, wide, kind=bf16),
            scratch(*square),
            scratch(z.total, EXTRA, wide),
            scratch(z.total if small(z) else 1, z.links // 2, n, 2 * n),
            scratch(own, n, half),
            scratch(2 * own, n, half),
            scratch(3 * own, n, fits),
            scratch(z.orbitals, half, fits),
            scratch(pairs, n, n),
            scratch(*square),
        ]
        + [scratch(*square, kind=bf16)] * 4
        + [scratch(2 * own, wide, wide, kind=bf16)] * 2
        + [scratch(z.orbitals * half, 3 * own * n, kind=bf16)] * 2
        + [pltpu.SemaphoreType.DMA((19 + -(-fits // 256),))],
        limit=60,
        out_specs=[hbm, hbm],
    )
    return (amplitudes, gradient)


def solution(mesh):
    in_specs = (
        P(("groups", "orb"), None, "fit"),
        P(("groups", "orb", "sub"), None, None),
        P(("groups", "orb", "sub"), None),
        P("groups"),
        P("groups"),
        P("groups"),
        P("groups", None),
        P(("groups", "orb", "sub"), None),
        P(("groups", "orb", "sub"), None, None),
        P(("groups", "orb", "sub"), None),
        P("groups"),
    )
    out_specs = (P(("groups", "orb", "sub"), None), P(("groups", "orb"), "sub", "fit"))
    return jax.shard_map(body, mesh=mesh, in_specs=in_specs, out_specs=out_specs, check_vma=False)
```

```python
import functools

import jax
import jax.numpy as jnp
from jax import lax
from jax.experimental import pallas as pl
from jax.experimental.pallas import tpu as pltpu
from jax.sharding import PartitionSpec as P

ITERS = 2
SMALL = 4
MIB = 1 << 20
EXTRA = 8

high = lax.Precision.HIGH
BRIEF = pl.CostEstimate(flops=1, bytes_accessed=1, transcendentals=0)
smem = pl.BlockSpec(memory_space=pltpu.SMEM)
vmem = pl.BlockSpec(memory_space=pltpu.VMEM)


def mm(a, b, contract=((1,), (0,))):
    return lax.dot_general(
        a, b, (contract, ((), ())), precision=high, preferred_element_type=jnp.float32
    )


def shifted(value, axis, steps):
    count = lax.axis_size(axis)
    initial, last = (max(0, -steps), min(count, count - steps))
    return lax.ppermute(value, axis, [(source, source + steps) for source in range(initial, last)])


def swapped(value, axis):
    return lax.ppermute(value, axis, [(0, 1), (1, 0)])


def f32(flag):
    return flag.astype(jnp.float32)


class Sizes:
    def __init__(self, blocks, pno_coefficients, couplings):
        self.orbitals, self.paos, self.fits = blocks.shape
        self.pairs, self.pnos = pno_coefficients.shape[:2]
        self.links = couplings.shape[1]
        self.subs = lax.axis_size("sub")
        self.owners = lax.axis_size("orb")
        self.fit_count = lax.axis_size("fit")
        self.own = self.pairs * self.subs
        self.total = self.own * self.owners


anywhere = pl.BlockSpec(memory_space=pl.ANY)
held_out = pl.BlockSpec(memory_space=pltpu.HBM)


def call(kernel, outs, ins, args, scratch=(), limit=16, out_specs=None, cost=None):
    return pl.pallas_call(
        kernel,
        out_shape=[jax.ShapeDtypeStruct(shape, jnp.float32) for shape in outs],
        in_specs=ins,
        out_specs=out_specs or [vmem] * len(outs),
        scratch_shapes=list(scratch),
        cost_estimate=cost,
        compiler_params=pltpu.CompilerParams(vmem_limit_bytes=limit and limit * MIB),
    )(*args)


def started(sources, targets, sems, base=0):
    copies = [
        pltpu.make_async_copy(source, target, sems.at[base + index])
        for index, (source, target) in enumerate(zip(sources, targets))
    ]
    for copy in copies:
        copy.start()
    return copies


def wait(copies):
    for copy in copies:
        copy.wait()


def side_start(z, owner, sub, side):
    return owner * z.own + (sub if side == 0 else 1 - sub) * z.pairs


def scale_of(z, pair, level, first, second, ranks, occupied):
    n = z.pnos
    row_ids = lax.broadcasted_iota(jnp.int32, (n, n), 0)
    column_ids = lax.broadcasted_iota(jnp.int32, (n, n), 1)
    level = level * jnp.ones((n, 1), jnp.float32)
    rank = ranks[pair]
    kept = f32((row_ids < rank) & (column_ids < rank))
    return kept / (level + level.T - (occupied[first[pair]] + occupied[second[pair]]))


def split(value):
    high_part = value.astype(jnp.bfloat16)
    return high_part, (value - high_part.astype(jnp.float32)).astype(jnp.bfloat16)


def mm3(a, b, contract=((1,), (0,))):
    def one(x, y):
        return lax.dot_general(x, y, (contract, ((), ())), preferred_element_type=jnp.float32)

    return one(a[0], b[0]) + (one(a[0], b[1]) + one(a[1], b[0]))


def small(z):
    return z.owners <= SMALL and z.pairs == z.fit_count == 2


def each_pair(z, action):
    if z.owners <= SMALL:
        for pair in range(z.total):
            action(pair)
    else:
        @pl.loop(0, z.total)
        def _(pair):
            action(pair)


def mapped_kernel(z, c_in, map_in, e_in, coupling_in, mp_ref, c_ref, map_ref, e_ref, coupling,
                  sems):
    n = z.pnos
    copies = started(
        [c_in, map_in, e_in, coupling_in], [c_ref, map_ref, e_ref, coupling], sems
    )
    wait(copies)
    rows = lax.broadcasted_iota(jnp.int32, (z.paos, z.paos), 0)
    lane_link = lax.broadcasted_iota(jnp.int32, (1, z.links * n), 1) // n
    for p in range(z.pairs):
        select = f32(map_ref[p : p + 1, :] == rows).astype(jnp.bfloat16)
        c_high, c_low = split(c_ref[p])
        mp_ref[p, :n, :] = lax.dot_general(
            c_high, select, (((1,), (1,)), ((), ())), preferred_element_type=jnp.float32
        ) + lax.dot_general(
            c_low, select, (((1,), (1,)), ((), ())), preferred_element_type=jnp.float32
        )
        mp_ref[p, n:, :] = jnp.zeros((EXTRA, z.paos), jnp.float32)
        mp_ref[p, n : n + 1, :n] = e_ref[p : p + 1, :]
        spread = jnp.zeros((1, z.links * n), jnp.float32)
        for k in range(z.links):
            spread = jnp.where(lane_link == k, coupling[p : p + 1, k : k + 1], spread)
        mp_ref[p, n + 1 : n + 2, :] = spread


def pack_kernel(z, s_in, mp_in, pack_ref, s_ref, mp_ref, sems):
    n = z.pnos
    line = 2 * n
    base = z.links * n // 2
    wait(started([s_in, mp_in.at[:, pl.ds(n, EXTRA), :]], [s_ref, mp_ref], sems))
    for slot in range(1 if small(z) else z.pairs):
        p = lax.axis_index("fit") if small(z) else slot
        for r in range(n // 2):
            lines = s_ref[p, :, r * line : (r + 1) * line]
            for k in range(z.links):
                row = k * n // 2 + r
                pack_ref[slot, row : row + 1, :] = lines[k : k + 1, :]
        pack_ref[slot, base:, :] = jnp.zeros((EXTRA, line), jnp.float32)
        pack_ref[slot, base : base + 1, :] = mp_ref[p, 0:1, :line]
        for k in range(z.links // 2):
            pack_ref[slot, base + 1 + k : base + 2 + k, :] = mp_ref[
                p, 1:2, k * line : (k + 1) * line
            ]
    if small(z):
        for copy in range(1, z.owners):
            pack_ref[copy] = pack_ref[0]


def below_kernel(z, second, mp_below, b_ref, right_ref):
    owner, sub = lax.axis_index("orb"), lax.axis_index("sub")
    start = side_start(z, jnp.maximum(owner - 1, 0), sub, 0)
    for p in range(z.pairs):
        j = second[start + p] - owner * z.orbitals
        held = jnp.where(j >= 0, 1.0, 0.0)
        mapped = mp_below[p, : z.pnos, :] * held
        right_ref[p] = mm(mapped, b_ref[jnp.clip(j, 0, z.orbitals - 1)])


def local_kernel(z, first, second, c_ref, mp_ref, b_ref, left_ref, right_ref):
    owner, sub = lax.axis_index("orb"), lax.axis_index("sub")
    start = side_start(z, owner, sub, 0)
    base = owner * z.orbitals
    for p in range(z.pairs):
        left_ref[p] = mm(c_ref[p], b_ref[first[start + p] - base])
        j = second[start + p] - base
        local = jnp.where(j < z.orbitals, 1.0, 0.0)
        right_ref[p] = mm(
            mp_ref[p, : z.pnos, :] * local, b_ref[jnp.minimum(j, z.orbitals - 1)]
        )


def sums_kernel(z, first, second, ranks, occupied, mp_ref, left_ref, here_ref, down_ref, *refs):
    sums_ref, right_ref = refs[-2:]
    owner, sub = lax.axis_index("orb"), lax.axis_index("sub")
    start = side_start(z, owner, sub, 0)
    n = z.pnos
    for p in range(z.pairs):
        right = here_ref[p] + down_ref[p]
        right_ref[p] = right
        scale = scale_of(
            z, start + p, mp_ref[p, n : n + 1, :n], first, second, ranks, occupied
        )
        part = mm(left_ref[p], right, ((1,), (1,)))
        sums_ref[:, p * n : (p + 1) * n] = -part * scale


def unpack(z, pair, block, rows, slot, s_high, s_low, scale_ref, coupling_ref, lists):
    n = z.pnos
    for k in range(0, z.links, 2):
        two = [block(k * n // 2, n // 2), block((k + 1) * n // 2, n // 2)]
        for odd in range(2):
            rows[slot, k // 2, pl.ds(odd, n // 2, 2), :] = jnp.concatenate(
                [part[:, odd * n : (odd + 1) * n] for part in two], axis=1
            )
    s = jnp.concatenate([rows[slot, k] for k in range(z.links // 2)], axis=1)
    s_high[pair], s_low[pair] = split(s)
    extra = block(z.links * n // 2, EXTRA)
    scale_ref[pair] = scale_of(z, pair, extra[0:1, :n], *lists)
    coupling_ref[pair, 0:1, :] = jnp.concatenate(
        [extra[1 + k : 2 + k, :] for k in range(z.links // 2)], axis=1
    )


def coupled_of(z, index, pair, near, s, coupling, amps_high, amps_low, diag_high, diag_low):
    n = z.pnos
    for k in range(z.links):
        row = near[k, pair]
        block = slice(k * n, (k + 1) * n)
        diag_high[index, block, block] = amps_high[row]
        diag_low[index, block, block] = amps_low[row]
    return split(mm3(s, (diag_high[index], diag_low[index])) * coupling)


def final_kernel(z, first, second, ranks, near, occupied, *refs):
    start_count, pack_count = (2, 4) if small(z) else (1, 1)
    starts_in = refs[:start_count]
    pack_in = refs[start_count : start_count + pack_count]
    (c_in, c_other, mp_in, mp_other, mp_below, mp_below_other, left_in, left_other, left_below,
     left_below_other, right_in, right_other) = refs[start_count + pack_count :][:12]
    (amp_out, grad_out, starts, amp_ref, packs, s_high, s_low, scale_ref, coupling_ref, s_rows, c_ref, m_ref, rhs,
     grad, flat, amps, amps_high, amps_low, next_high, next_low, diag_high, diag_low, rows_high,
     rows_low, sems) = refs[start_count + pack_count + 12 :]
    owner, sub = lax.axis_index("orb"), lax.axis_index("sub")
    fit = lax.axis_index("fit")
    n, pairs, own = z.pnos, z.pairs, z.own
    half = z.paos // z.subs
    at = pl.ds(pl.multiple_of(sub * half, half), half)
    lists = (first, second, ranks, occupied)

    def quarters(ref, base=0):
        return [ref.at[pl.ds(base + i * pairs, pairs)] for i in range(4)]

    start_copies = started(starts_in, [starts.at[i] for i in range(start_count)], sems, 16)
    pack_copies = started(pack_in, [packs.at[i] for i in range(pack_count)], sems)
    small_copies = started(
        [c_in.at[:, :, at], c_other.at[:, :, at]]
        + [ref.at[:, pl.ds(0, n), at] for ref in (mp_in, mp_other, mp_below, mp_below_other)],
        [c_ref.at[pl.ds(0, pairs)], c_ref.at[pl.ds(pairs, pairs)]] + quarters(m_ref),
        sems, 4,
    )
    large_copies = started(
        [right_in, right_other, left_in, left_other, left_below, left_below_other],
        [rhs.at[pl.ds(0, pairs)], rhs.at[pl.ds(pairs, pairs)]] + quarters(rhs, own),
        sems, 10,
    )
    diag_high[...] = jnp.zeros_like(diag_high)
    diag_low[...] = jnp.zeros_like(diag_low)

    wait(start_copies)

    def begin(pair, value):
        amps[pair] = value
        amps_high[pair], amps_low[pair] = split(value)

    if small(z):
        for index, side in enumerate((sub, 1 - sub)):
            for who in range(z.owners):
                for p in range(pairs):
                    begin(
                        who * own + side * pairs + p,
                        starts[index, who, :, p * n : (p + 1) * n],
                    )
    else:
        @pl.loop(0, z.owners * z.subs)
        def _(device):
            for p in range(pairs):
                begin(device * pairs + p, starts[0, device, :, p * n : (p + 1) * n])

    wait(pack_copies)
    if small(z):
        for index in range(pack_count):
            side = sub if index < 2 else 1 - sub
            which = fit if index % 2 == 0 else 1 - fit
            for who in range(z.owners):
                unpack(
                    z, who * own + side * pairs + which,
                    lambda start, size: packs[index, who, start : start + size, :], s_rows,
                    index * z.owners + who, s_high, s_low, scale_ref, coupling_ref, lists,
                )
    else:
        @pl.loop(0, z.total)
        def _(pair):
            unpack(
                z, pair, lambda start, size: packs[0, pair, pl.ds(start, size), :], s_rows, 0,
                s_high, s_low, scale_ref, coupling_ref, lists,
            )

    def s_of(pair):
        return s_high[pair], s_low[pair]

    def swept(index, pair, high_amps, low_amps):
        s = s_of(pair)
        inner = coupled_of(
            z, index, pair, near, s, coupling_ref[pair, 0:1, :], high_amps, low_amps, diag_high,
            diag_low,
        )
        return amps[pair] + mm3(inner, s, ((1,), (1,))) * scale_ref[pair]

    if z.owners <= SMALL:
        group = diag_high.shape[0]
        for base in range(0, z.total, group):
            pair_list = range(base, min(base + group, z.total))
            inner = [
                coupled_of(
                    z, index, pair, near, s_of(pair), coupling_ref[pair, 0:1, :], amps_high,
                    amps_low, diag_high, diag_low,
                )
                for index, pair in enumerate(pair_list)
            ]
            for value, pair in zip(inner, pair_list):
                coupled = mm3(value, s_of(pair), ((1,), (1,)))
                next_high[pair], next_low[pair] = split(amps[pair] + coupled * scale_ref[pair])
    else:
        @pl.loop(0, z.total)
        def _(pair):
            next_high[pair], next_low[pair] = split(swept(0, pair, amps_high, amps_low))

    pair_list = [
        side_start(z, who, sub, side) + p
        for who in (owner, jnp.maximum(owner - 1, 0))
        for side in range(z.subs)
        for p in range(pairs)
    ]
    inner = [
        coupled_of(
            z, index, pair, near, s_of(pair), coupling_ref[pair, 0:1, :], next_high, next_low,
            diag_high, diag_low,
        )
        for index, pair in enumerate(pair_list)
    ]
    found = [
        amps[pair] + mm3(value, s_of(pair), ((1,), (1,))) * scale_ref[pair]
        for value, pair in zip(inner, pair_list)
    ]
    turned = [value.T for value in found]
    wait(small_copies)
    weights = [split(2.0 * a - b) for a, b in zip(found, turned)]
    weights_turned = [split(2.0 * b - a) for a, b in zip(found[:own], turned[:own])]
    terms = (
        [mm3(w, split(c_ref[i])) for i, w in enumerate(weights_turned)]
        + [mm3(w, split(m_ref[i])) for i, w in enumerate(weights)]
    )
    orbital_list = (
        [first[pair] - owner * z.orbitals for pair in pair_list[:own]]
        + [second[pair] - owner * z.orbitals for pair in pair_list]
    )
    for index in range(0, 3 * own, 2):
        for o in range(z.orbitals):
            block = jnp.concatenate(
                [
                    jnp.where(orbital_list[i] == o, terms[i], 0.0) for i in (index, index + 1)
                ]
            ).T
            place = (slice(o * half, (o + 1) * half), slice(index * n, (index + 2) * n))
            rows_high[place], rows_low[place] = split(block)

    for p in range(pairs):
        flat[p] = found[p]
        even = flat[p, pl.ds(0, n // 2, 2), :]
        odd = flat[p, pl.ds(1, n // 2, 2), :]
        lines = jnp.concatenate([even, odd], axis=1)
        for r in range(n // 2):
            amp_ref[p : p + 1, r * 2 * n : (r + 1) * 2 * n] = lines[r : r + 1, :]
    copies = started([amp_ref], [amp_out], sems, 18)

    wait(large_copies)
    step = 256
    rows = (rows_high[...], rows_low[...])
    for index, start in enumerate(range(0, z.fits, step)):
        factor = rhs[:, :, start : start + step].reshape(3 * own * n, step)
        grad[:, :, start : start + step] = mm3(rows, split(factor)).reshape(
            z.orbitals, half, step
        )
        window = pl.ds(start, step)
        copies += started(
            [grad.at[:, :, window]], [grad_out.at[:, :, window]], sems, 19 + index
        )
    wait(copies)


def gate(values, *after):
    return lax.optimization_barrier((tuple(values), after))[0]


def body(
    blocks,
    pno_coefficients,
    domain_map,
    pair_first,
    pair_second,
    pno_ranks,
    neighbours,
    couplings,
    intersections,
    pno_energy,
    occ_energy,
):
    z = Sizes(blocks, pno_coefficients, couplings)
    n, pairs, own, fits = z.pnos, z.pairs, z.own, z.fits
    half = z.paos // z.subs
    wide = z.links * n
    hbm = held_out
    bf16 = jnp.bfloat16
    more = 0 if z.owners <= SMALL else z.owners

    def scratch(*shape, kind=jnp.float32):
        return pltpu.VMEM(shape, kind)

    pack_shape = (z.owners if small(z) else pairs, z.links * n // 2 + EXTRA, 2 * n)
    (mp,) = call(
        functools.partial(mapped_kernel, z),
        [(pairs, n + EXTRA, z.paos)],
        [hbm] * 4,
        (pno_coefficients, domain_map, pno_energy, couplings),
        [
            scratch(*pno_coefficients.shape),
            pltpu.VMEM(domain_map.shape, jnp.int32),
            scratch(*pno_energy.shape),
            scratch(*couplings.shape),
            pltpu.SemaphoreType.DMA((4,)),
        ],
        limit=None,
    )
    mp_below = shifted(mp, "orb", 1)
    (pack,) = call(
        functools.partial(pack_kernel, z),
        [pack_shape],
        [hbm] * 2,
        (intersections, mp),
        [
            scratch(*intersections.shape),
            scratch(pairs, EXTRA, z.paos),
            pltpu.SemaphoreType.DMA((2,)),
        ],
        limit=None,
    )
    if small(z):
        packs = [lax.all_to_all(pack, "orb", 0, 0)]
    else:
        packs = [lax.all_gather(pack, ("orb", "sub"), axis=0, tiled=True)]
    (right_below,) = call(
        functools.partial(below_kernel, z),
        [(pairs, n, fits)],
        [smem, vmem, vmem],
        (pair_second, gate((mp_below,), pack)[0], blocks),
        limit=8,
    )
    down = shifted(right_below, "orb", -1)
    mp_late, coefficients = gate((mp, pno_coefficients), right_below)
    left, right_here = call(
        functools.partial(local_kernel, z),
        [(pairs, n, fits), (pairs, n, fits)],
        [smem, smem, vmem, vmem, vmem],
        (pair_first, pair_second, coefficients, mp_late, blocks),
        limit=8,
        cost=BRIEF,
    )
    mp_other = swapped(gate((mp,), right_here)[0], "sub")
    left_other = swapped(left, "sub")
    c_other = swapped(gate((coefficients,), right_here)[0], "sub")

    lists = (pair_first, pair_second, pno_ranks)
    (down,) = gate((down,), mp_other, left_other, c_other)
    part, right = call(
        functools.partial(sums_kernel, z),
        [(n, pairs * n), (pairs, n, fits)],
        [smem] * 4 + [vmem] * 4,
        (*lists, occ_energy, mp, left, right_here, down),
        limit=8,
    )
    if small(z):
        packs.append(None)
        packs.append(swapped(gate(packs[:1], part)[0], "sub"))
        sums = part + swapped(part, "fit")
        packs[1] = swapped(gate(packs[:1], part)[0], "fit")
        start_amps = [
            lax.all_to_all(jnp.broadcast_to(sums[None], (z.owners, *sums.shape)), "orb", 0, 0)
        ]
        start_amps.append(swapped(start_amps[0], "sub"))
        packs.append(swapped(gate(packs[1:2], start_amps[0])[0], "sub"))
    else:
        sums = lax.psum(part, "fit")
        start_amps = [lax.all_gather(sums, ("orb", "sub"), axis=0, tiled=False)]

    right_late, mp_late = gate((right, mp_below), part)
    left_below = shifted(gate((left,), part)[0], "orb", 1)
    (left_late,) = gate((left_below,), start_amps[0])
    right_other, mp_below_other, left_below_other = [
        swapped(value, "sub") for value in (right_late, mp_late, left_late)
    ]

    args = (
        *lists, neighbours.T, occ_energy, *start_amps, *packs,
        pno_coefficients, c_other, mp, mp_other, mp_below, mp_below_other,
        left, left_other, left_below, left_below_other, right, right_other,
    )
    square = (z.total, n, n)
    amplitudes, gradient = call(
        functools.partial(final_kernel, z),
        [(pairs, n * n), (z.orbitals, half, fits)],
        [smem] * 5 + [hbm] * (12 + len(start_amps) + len(packs)),
        args,
        [
            scratch(len(start_amps), *start_amps[0].shape),
            scratch(pairs, n * n),
            scratch(len(packs), *packs[0].shape),
            scratch(z.total, n, wide, kind=bf16),
            scratch(z.total, n, wide, kind=bf16),
            scratch(*square),
            scratch(z.total, EXTRA, wide),
            scratch(z.total if small(z) else 1, z.links // 2, n, 2 * n),
            scratch(own, n, half),
            scratch(2 * own, n, half),
            scratch(3 * own, n, fits),
            scratch(z.orbitals, half, fits),
            scratch(pairs, n, n),
            scratch(*square),
        ]
        + [scratch(*square, kind=bf16)] * 4
        + [scratch(2 * own, wide, wide, kind=bf16)] * 2
        + [scratch(z.orbitals * half, 3 * own * n, kind=bf16)] * 2
        + [pltpu.SemaphoreType.DMA((19 + -(-fits // 256),))],
        limit=60,
        out_specs=[hbm, hbm],
    )
    return (amplitudes, gradient)


def solution(mesh):
    in_specs = (
        P(("groups", "orb"), None, "fit"),
        P(("groups", "orb", "sub"), None, None),
        P(("groups", "orb", "sub"), None),
        P("groups"),
        P("groups"),
        P("groups"),
        P("groups", None),
        P(("groups", "orb", "sub"), None),
        P(("groups", "orb", "sub"), None, None),
        P(("groups", "orb", "sub"), None),
        P("groups"),
    )
    out_specs = (P(("groups", "orb", "sub"), None), P(("groups", "orb"), "sub", "fit"))
    return jax.shard_map(body, mesh=mesh, in_specs=in_specs, out_specs=out_specs, check_vma=False)
```

```python
import functools

import jax
import jax.numpy as jnp
from jax import lax
from jax.experimental import pallas as pl
from jax.experimental.pallas import tpu as pltpu
from jax.sharding import PartitionSpec as P

ITERS = 2
SMALL = 4
MIB = 1 << 20
EXTRA = 8

high = lax.Precision.HIGH
BRIEF = pl.CostEstimate(flops=1, bytes_accessed=1, transcendentals=0)
smem = pl.BlockSpec(memory_space=pltpu.SMEM)
vmem = pl.BlockSpec(memory_space=pltpu.VMEM)


def mm(a, b, contract=((1,), (0,))):
    return lax.dot_general(
        a, b, (contract, ((), ())), precision=high, preferred_element_type=jnp.float32
    )


def shifted(value, axis, steps):
    count = lax.axis_size(axis)
    initial, last = (max(0, -steps), min(count, count - steps))
    return lax.ppermute(value, axis, [(source, source + steps) for source in range(initial, last)])


def swapped(value, axis):
    return lax.ppermute(value, axis, [(0, 1), (1, 0)])


def f32(flag):
    return flag.astype(jnp.float32)


class Sizes:
    def __init__(self, blocks, pno_coefficients, couplings):
        self.orbitals, self.paos, self.fits = blocks.shape
        self.pairs, self.pnos = pno_coefficients.shape[:2]
        self.links = couplings.shape[1]
        self.subs = lax.axis_size("sub")
        self.owners = lax.axis_size("orb")
        self.fit_count = lax.axis_size("fit")
        self.own = self.pairs * self.subs
        self.total = self.own * self.owners


anywhere = pl.BlockSpec(memory_space=pl.ANY)
held_out = pl.BlockSpec(memory_space=pltpu.HBM)


def call(kernel, outs, ins, args, scratch=(), limit=16, out_specs=None, cost=None):
    return pl.pallas_call(
        kernel,
        out_shape=[jax.ShapeDtypeStruct(shape, jnp.float32) for shape in outs],
        in_specs=ins,
        out_specs=out_specs or [vmem] * len(outs),
        scratch_shapes=list(scratch),
        cost_estimate=cost,
        compiler_params=pltpu.CompilerParams(vmem_limit_bytes=limit and limit * MIB),
    )(*args)


def started(sources, targets, sems, base=0):
    copies = [
        pltpu.make_async_copy(source, target, sems.at[base + index])
        for index, (source, target) in enumerate(zip(sources, targets))
    ]
    for copy in copies:
        copy.start()
    return copies


def wait(copies):
    for copy in copies:
        copy.wait()


def side_start(z, owner, sub, side):
    return owner * z.own + (sub if side == 0 else 1 - sub) * z.pairs


def scale_of(z, pair, level, first, second, ranks, occupied):
    n = z.pnos
    row_ids = lax.broadcasted_iota(jnp.int32, (n, n), 0)
    column_ids = lax.broadcasted_iota(jnp.int32, (n, n), 1)
    level = level * jnp.ones((n, 1), jnp.float32)
    rank = ranks[pair]
    kept = f32((row_ids < rank) & (column_ids < rank))
    return kept / (level + level.T - (occupied[first[pair]] + occupied[second[pair]]))


def split(value):
    high_part = value.astype(jnp.bfloat16)
    return high_part, (value - high_part.astype(jnp.float32)).astype(jnp.bfloat16)


def mm3(a, b, contract=((1,), (0,))):
    def one(x, y):
        return lax.dot_general(x, y, (contract, ((), ())), preferred_element_type=jnp.float32)

    return one(a[0], b[0]) + (one(a[0], b[1]) + one(a[1], b[0]))


def small(z):
    return z.owners <= SMALL and z.pairs == z.fit_count == 2


def each_pair(z, action):
    if z.owners <= SMALL:
        for pair in range(z.total):
            action(pair)
    else:
        @pl.loop(0, z.total)
        def _(pair):
            action(pair)


def mapped_kernel(z, c_in, map_in, e_in, coupling_in, mp_ref, c_ref, map_ref, e_ref, coupling,
                  sems):
    n = z.pnos
    copies = started(
        [c_in, map_in, e_in, coupling_in], [c_ref, map_ref, e_ref, coupling], sems
    )
    wait(copies)
    rows = lax.broadcasted_iota(jnp.int32, (z.paos, z.paos), 0)
    lane_link = lax.broadcasted_iota(jnp.int32, (1, z.links * n), 1) // n
    for p in range(z.pairs):
        select = f32(map_ref[p : p + 1, :] == rows).astype(jnp.bfloat16)
        c_high, c_low = split(c_ref[p])
        mp_ref[p, :n, :] = lax.dot_general(
            c_high, select, (((1,), (1,)), ((), ())), preferred_element_type=jnp.float32
        ) + lax.dot_general(
            c_low, select, (((1,), (1,)), ((), ())), preferred_element_type=jnp.float32
        )
        mp_ref[p, n:, :] = jnp.zeros((EXTRA, z.paos), jnp.float32)
        mp_ref[p, n : n + 1, :n] = e_ref[p : p + 1, :]
        spread = jnp.zeros((1, z.links * n), jnp.float32)
        for k in range(z.links):
            spread = jnp.where(lane_link == k, coupling[p : p + 1, k : k + 1], spread)
        mp_ref[p, n + 1 : n + 2, :] = spread


def pack_kernel(z, s_in, mp_in, pack_ref, s_ref, mp_ref, sems):
    n = z.pnos
    line = 2 * n
    base = z.links * n // 2
    wait(started([s_in, mp_in.at[:, pl.ds(n, EXTRA), :]], [s_ref, mp_ref], sems))
    for slot in range(1 if small(z) else z.pairs):
        p = lax.axis_index("fit") if small(z) else slot
        for r in range(n // 2):
            lines = s_ref[p, :, r * line : (r + 1) * line]
            for k in range(z.links):
                row = k * n // 2 + r
                pack_ref[slot, row : row + 1, :] = lines[k : k + 1, :]
        pack_ref[slot, base:, :] = jnp.zeros((EXTRA, line), jnp.float32)
        pack_ref[slot, base : base + 1, :] = mp_ref[p, 0:1, :line]
        for k in range(z.links // 2):
            pack_ref[slot, base + 1 + k : base + 2 + k, :] = mp_ref[
                p, 1:2, k * line : (k + 1) * line
            ]
    if small(z):
        for copy in range(1, z.owners):
            pack_ref[copy] = pack_ref[0]


def below_kernel(z, second, mp_below, b_ref, right_ref):
    owner, sub = lax.axis_index("orb"), lax.axis_index("sub")
    start = side_start(z, jnp.maximum(owner - 1, 0), sub, 0)
    for p in range(z.pairs):
        j = second[start + p] - owner * z.orbitals
        held = jnp.where(j >= 0, 1.0, 0.0)
        mapped = mp_below[p, : z.pnos, :] * held
        right_ref[p] = mm(mapped, b_ref[jnp.clip(j, 0, z.orbitals - 1)])


def local_kernel(z, first, second, c_ref, mp_ref, b_ref, left_ref, right_ref):
    owner, sub = lax.axis_index("orb"), lax.axis_index("sub")
    start = side_start(z, owner, sub, 0)
    base = owner * z.orbitals
    for p in range(z.pairs):
        left_ref[p] = mm(c_ref[p], b_ref[first[start + p] - base])
        j = second[start + p] - base
        local = jnp.where(j < z.orbitals, 1.0, 0.0)
        right_ref[p] = mm(
            mp_ref[p, : z.pnos, :] * local, b_ref[jnp.minimum(j, z.orbitals - 1)]
        )


def sums_kernel(z, first, second, ranks, occupied, mp_ref, left_ref, here_ref, down_ref, *refs):
    sums_ref, right_ref = refs[-2:]
    owner, sub = lax.axis_index("orb"), lax.axis_index("sub")
    start = side_start(z, owner, sub, 0)
    n = z.pnos
    for p in range(z.pairs):
        right = here_ref[p] + down_ref[p]
        right_ref[p] = right
        scale = scale_of(
            z, start + p, mp_ref[p, n : n + 1, :n], first, second, ranks, occupied
        )
        part = mm(left_ref[p], right, ((1,), (1,)))
        sums_ref[:, p * n : (p + 1) * n] = -part * scale


def unpack(z, pair, block, rows, slot, s_high, s_low, scale_ref, coupling_ref, lists):
    n = z.pnos
    for k in range(0, z.links, 2):
        two = [block(k * n // 2, n // 2), block((k + 1) * n // 2, n // 2)]
        for odd in range(2):
            rows[slot, k // 2, pl.ds(odd, n // 2, 2), :] = jnp.concatenate(
                [part[:, odd * n : (odd + 1) * n] for part in two], axis=1
            )
    s = jnp.concatenate([rows[slot, k] for k in range(z.links // 2)], axis=1)
    s_high[pair], s_low[pair] = split(s)
    extra = block(z.links * n // 2, EXTRA)
    scale_ref[pair] = scale_of(z, pair, extra[0:1, :n], *lists)
    coupling_ref[pair, 0:1, :] = jnp.concatenate(
        [extra[1 + k : 2 + k, :] for k in range(z.links // 2)], axis=1
    )


def coupled_of(z, index, pair, near, s, coupling, amps_high, amps_low, diag_high, diag_low):
    n = z.pnos
    for k in range(z.links):
        row = near[k, pair]
        block = slice(k * n, (k + 1) * n)
        diag_high[index, block, block] = amps_high[row]
        diag_low[index, block, block] = amps_low[row]
    return split(mm3(s, (diag_high[index], diag_low[index])) * coupling)


def final_kernel(z, first, second, ranks, near, occupied, *refs):
    start_count, pack_count = (2, 4) if small(z) else (1, 1)
    starts_in = refs[:start_count]
    pack_in = refs[start_count : start_count + pack_count]
    (c_in, c_other, mp_in, mp_other, mp_below, mp_below_other, left_in, left_other, left_below,
     left_below_other, right_in, right_other) = refs[start_count + pack_count :][:12]
    (amp_out, grad_out, starts, amp_ref, packs, s_high, s_low, scale_ref, coupling_ref, s_rows, c_ref, m_ref, rhs,
     grad, flat, amps, amps_high, amps_low, next_high, next_low, diag_high, diag_low, rows_high,
     rows_low, sems) = refs[start_count + pack_count + 12 :]
    owner, sub = lax.axis_index("orb"), lax.axis_index("sub")
    fit = lax.axis_index("fit")
    n, pairs, own = z.pnos, z.pairs, z.own
    half = z.paos // z.subs
    at = pl.ds(pl.multiple_of(sub * half, half), half)
    lists = (first, second, ranks, occupied)

    def quarters(ref, base=0):
        return [ref.at[pl.ds(base + i * pairs, pairs)] for i in range(4)]

    start_copies = started(starts_in, [starts.at[i] for i in range(start_count)], sems, 16)
    pack_copies = started(pack_in, [packs.at[i] for i in range(pack_count)], sems)
    small_copies = started(
        [c_in.at[:, :, at], c_other.at[:, :, at]]
        + [ref.at[:, pl.ds(0, n), at] for ref in (mp_in, mp_other, mp_below, mp_below_other)],
        [c_ref.at[pl.ds(0, pairs)], c_ref.at[pl.ds(pairs, pairs)]] + quarters(m_ref),
        sems, 4,
    )
    large_copies = started(
        [right_in, right_other, left_in, left_other, left_below, left_below_other],
        [rhs.at[pl.ds(0, pairs)], rhs.at[pl.ds(pairs, pairs)]] + quarters(rhs, own),
        sems, 10,
    )
    diag_high[...] = jnp.zeros_like(diag_high)
    diag_low[...] = jnp.zeros_like(diag_low)

    wait(start_copies)

    def begin(pair, value):
        amps[pair] = value
        amps_high[pair], amps_low[pair] = split(value)

    if small(z):
        for index, side in enumerate((sub, 1 - sub)):
            for who in range(z.owners):
                for p in range(pairs):
                    begin(
                        who * own + side * pairs + p,
                        starts[index, who, :, p * n : (p + 1) * n],
                    )
    else:
        @pl.loop(0, z.owners * z.subs)
        def _(device):
            for p in range(pairs):
                begin(device * pairs + p, starts[0, device, :, p * n : (p + 1) * n])

    wait(pack_copies)
    if small(z):
        for index in range(pack_count):
            side = sub if index < 2 else 1 - sub
            which = fit if index % 2 == 0 else 1 - fit
            for who in range(z.owners):
                unpack(
                    z, who * own + side * pairs + which,
                    lambda start, size: packs[index, who, start : start + size, :], s_rows,
                    index * z.owners + who, s_high, s_low, scale_ref, coupling_ref, lists,
                )
    else:
        @pl.loop(0, z.total)
        def _(pair):
            unpack(
                z, pair, lambda start, size: packs[0, pair, pl.ds(start, size), :], s_rows, 0,
                s_high, s_low, scale_ref, coupling_ref, lists,
            )

    def s_of(pair):
        return s_high[pair], s_low[pair]

    def swept(index, pair, high_amps, low_amps):
        s = s_of(pair)
        inner = coupled_of(
            z, index, pair, near, s, coupling_ref[pair, 0:1, :], high_amps, low_amps, diag_high,
            diag_low,
        )
        return amps[pair] + mm3(inner, s, ((1,), (1,))) * scale_ref[pair]

    if z.owners <= SMALL:
        group = diag_high.shape[0]
        for base in range(0, z.total, group):
            pair_list = range(base, min(base + group, z.total))
            inner = [
                coupled_of(
                    z, index, pair, near, s_of(pair), coupling_ref[pair, 0:1, :], amps_high,
                    amps_low, diag_high, diag_low,
                )
                for index, pair in enumerate(pair_list)
            ]
            for value, pair in zip(inner, pair_list):
                coupled = mm3(value, s_of(pair), ((1,), (1,)))
                next_high[pair], next_low[pair] = split(amps[pair] + coupled * scale_ref[pair])
    else:
        @pl.loop(0, z.total)
        def _(pair):
            next_high[pair], next_low[pair] = split(swept(0, pair, amps_high, amps_low))

    pair_list = [
        side_start(z, who, sub, side) + p
        for who in (owner, jnp.maximum(owner - 1, 0))
        for side in range(z.subs)
        for p in range(pairs)
    ]
    inner = [
        coupled_of(
            z, index, pair, near, s_of(pair), coupling_ref[pair, 0:1, :], next_high, next_low,
            diag_high, diag_low,
        )
        for index, pair in enumerate(pair_list)
    ]
    found = [
        amps[pair] + mm3(value, s_of(pair), ((1,), (1,))) * scale_ref[pair]
        for value, pair in zip(inner, pair_list)
    ]
    turned = [value.T for value in found]
    wait(small_copies)
    weights = [split(2.0 * a - b) for a, b in zip(found, turned)]
    weights_turned = [split(2.0 * b - a) for a, b in zip(found[:own], turned[:own])]
    terms = (
        [mm3(w, split(c_ref[i])) for i, w in enumerate(weights_turned)]
        + [mm3(w, split(m_ref[i])) for i, w in enumerate(weights)]
    )
    orbital_list = (
        [first[pair] - owner * z.orbitals for pair in pair_list[:own]]
        + [second[pair] - owner * z.orbitals for pair in pair_list]
    )
    for index in range(0, 3 * own, 2):
        for o in range(z.orbitals):
            block = jnp.concatenate(
                [
                    jnp.where(orbital_list[i] == o, terms[i], 0.0) for i in (index, index + 1)
                ]
            ).T
            place = (slice(o * half, (o + 1) * half), slice(index * n, (index + 2) * n))
            rows_high[place], rows_low[place] = split(block)

    for p in range(pairs):
        flat[p] = found[p]
        even = flat[p, pl.ds(0, n // 2, 2), :]
        odd = flat[p, pl.ds(1, n // 2, 2), :]
        lines = jnp.concatenate([even, odd], axis=1)
        for r in range(n // 2):
            amp_ref[p : p + 1, r * 2 * n : (r + 1) * 2 * n] = lines[r : r + 1, :]
    copies = started([amp_ref], [amp_out], sems, 18)

    wait(large_copies)
    step = 256
    rows = (rows_high[...], rows_low[...])
    for index, start in enumerate(range(0, z.fits, step)):
        factor = rhs[:, :, start : start + step].reshape(3 * own * n, step)
        grad[:, :, start : start + step] = mm3(rows, split(factor)).reshape(
            z.orbitals, half, step
        )
        window = pl.ds(start, step)
        copies += started(
            [grad.at[:, :, window]], [grad_out.at[:, :, window]], sems, 19 + index
        )
    wait(copies)


def gate(values, *after):
    return lax.optimization_barrier((tuple(values), after))[0]


def body(
    blocks,
    pno_coefficients,
    domain_map,
    pair_first,
    pair_second,
    pno_ranks,
    neighbours,
    couplings,
    intersections,
    pno_energy,
    occ_energy,
):
    z = Sizes(blocks, pno_coefficients, couplings)
    n, pairs, own, fits = z.pnos, z.pairs, z.own, z.fits
    half = z.paos // z.subs
    wide = z.links * n
    hbm = held_out
    bf16 = jnp.bfloat16
    more = 0 if z.owners <= SMALL else z.owners

    def scratch(*shape, kind=jnp.float32):
        return pltpu.VMEM(shape, kind)

    pack_shape = (z.owners if small(z) else pairs, z.links * n // 2 + EXTRA, 2 * n)
    (mp,) = call(
        functools.partial(mapped_kernel, z),
        [(pairs, n + EXTRA, z.paos)],
        [hbm] * 4,
        (pno_coefficients, domain_map, pno_energy, couplings),
        [
            scratch(*pno_coefficients.shape),
            pltpu.VMEM(domain_map.shape, jnp.int32),
            scratch(*pno_energy.shape),
            scratch(*couplings.shape),
            pltpu.SemaphoreType.DMA((4,)),
        ],
        limit=None,
    )
    mp_below = shifted(mp, "orb", 1)
    (pack,) = call(
        functools.partial(pack_kernel, z),
        [pack_shape],
        [hbm] * 2,
        (intersections, mp),
        [
            scratch(*intersections.shape),
            scratch(pairs, EXTRA, z.paos),
            pltpu.SemaphoreType.DMA((2,)),
        ],
        limit=None,
    )
    (right_below,) = call(
        functools.partial(below_kernel, z),
        [(pairs, n, fits)],
        [smem, vmem, vmem],
        (pair_second, gate((mp_below,), pack)[0], blocks),
        limit=8,
    )
    down = shifted(right_below, "orb", -1)
    mp_late, coefficients, pack, mp_below_late = gate(
        (mp, pno_coefficients, pack, mp_below), right_below
    )
    mp_below_other = swapped(mp_below_late, "sub")
    if small(z):
        packs = [lax.all_to_all(pack, "orb", 0, 0)]
    else:
        packs = [lax.all_gather(pack, ("orb", "sub"), axis=0, tiled=True)]
    left, right_here = call(
        functools.partial(local_kernel, z),
        [(pairs, n, fits), (pairs, n, fits)],
        [smem, smem, vmem, vmem, vmem],
        (pair_first, pair_second, coefficients, mp_late, blocks),
        limit=8,
        cost=BRIEF,
    )
    mp_other = swapped(gate((mp,), right_here)[0], "sub")
    left_other = swapped(left, "sub")
    c_other = swapped(gate((coefficients,), right_here)[0], "sub")

    lists = (pair_first, pair_second, pno_ranks)
    (down,) = gate((down,), mp_other, left_other, c_other, mp_below_other)
    part, right = call(
        functools.partial(sums_kernel, z),
        [(n, pairs * n), (pairs, n, fits)],
        [smem] * 4 + [vmem] * 4,
        (*lists, occ_energy, mp, left, right_here, down),
        limit=8,
    )
    if small(z):
        packs.append(None)
        packs.append(swapped(gate(packs[:1], part)[0], "sub"))
        sums = part + swapped(part, "fit")
        (sums,) = gate((sums,), packs[2])
        packs[1] = swapped(gate(packs[:1], part)[0], "fit")
        start_amps = [
            lax.all_to_all(jnp.broadcast_to(sums[None], (z.owners, *sums.shape)), "orb", 0, 0)
        ]
        start_amps.append(swapped(start_amps[0], "sub"))
        packs.append(swapped(gate(packs[1:2], start_amps[0])[0], "sub"))
    else:
        sums = lax.psum(part, "fit")
        start_amps = [lax.all_gather(sums, ("orb", "sub"), axis=0, tiled=False)]

    right_other = swapped(right, "sub")
    left_below = shifted(gate((left,), right_other)[0], "orb", 1)
    left_below_other = swapped(gate((left_below,), start_amps[0])[0], "sub")

    args = (
        *lists, neighbours.T, occ_energy, *start_amps, *packs,
        pno_coefficients, c_other, mp, mp_other, mp_below, mp_below_other,
        left, left_other, left_below, left_below_other, right, right_other,
    )
    square = (z.total, n, n)
    amplitudes, gradient = call(
        functools.partial(final_kernel, z),
        [(pairs, n * n), (z.orbitals, half, fits)],
        [smem] * 5 + [hbm] * (12 + len(start_amps) + len(packs)),
        args,
        [
            scratch(len(start_amps), *start_amps[0].shape),
            scratch(pairs, n * n),
            scratch(len(packs), *packs[0].shape),
            scratch(z.total, n, wide, kind=bf16),
            scratch(z.total, n, wide, kind=bf16),
            scratch(*square),
            scratch(z.total, EXTRA, wide),
            scratch(z.total if small(z) else 1, z.links // 2, n, 2 * n),
            scratch(own, n, half),
            scratch(2 * own, n, half),
            scratch(3 * own, n, fits),
            scratch(z.orbitals, half, fits),
            scratch(pairs, n, n),
            scratch(*square),
        ]
        + [scratch(*square, kind=bf16)] * 4
        + [scratch(2 * own, wide, wide, kind=bf16)] * 2
        + [scratch(z.orbitals * half, 3 * own * n, kind=bf16)] * 2
        + [pltpu.SemaphoreType.DMA((19 + -(-fits // 256),))],
        limit=60,
        out_specs=[hbm, hbm],
    )
    return (amplitudes, gradient)


def solution(mesh):
    in_specs = (
        P(("groups", "orb"), None, "fit"),
        P(("groups", "orb", "sub"), None, None),
        P(("groups", "orb", "sub"), None),
        P("groups"),
        P("groups"),
        P("groups"),
        P("groups", None),
        P(("groups", "orb", "sub"), None),
        P(("groups", "orb", "sub"), None, None),
        P(("groups", "orb", "sub"), None),
        P("groups"),
    )
    out_specs = (P(("groups", "orb", "sub"), None), P(("groups", "orb"), "sub", "fit"))
    return jax.shard_map(body, mesh=mesh, in_specs=in_specs, out_specs=out_specs, check_vma=False)
```

```python
import functools

import jax
import jax.numpy as jnp
from jax import lax
from jax.experimental import pallas as pl
from jax.experimental.pallas import tpu as pltpu
from jax.sharding import PartitionSpec as P

ITERS = 2
SMALL = 4
MIB = 1 << 20
EXTRA = 8

high = lax.Precision.HIGH
BRIEF = pl.CostEstimate(flops=1, bytes_accessed=1, transcendentals=0)
smem = pl.BlockSpec(memory_space=pltpu.SMEM)
vmem = pl.BlockSpec(memory_space=pltpu.VMEM)


def mm(a, b, contract=((1,), (0,))):
    return lax.dot_general(
        a, b, (contract, ((), ())), precision=high, preferred_element_type=jnp.float32
    )


def shifted(value, axis, steps):
    count = lax.axis_size(axis)
    initial, last = (max(0, -steps), min(count, count - steps))
    return lax.ppermute(value, axis, [(source, source + steps) for source in range(initial, last)])


def swapped(value, axis):
    return lax.ppermute(value, axis, [(0, 1), (1, 0)])


def f32(flag):
    return flag.astype(jnp.float32)


class Sizes:
    def __init__(self, blocks, pno_coefficients, couplings):
        self.orbitals, self.paos, self.fits = blocks.shape
        self.pairs, self.pnos = pno_coefficients.shape[:2]
        self.links = couplings.shape[1]
        self.subs = lax.axis_size("sub")
        self.owners = lax.axis_size("orb")
        self.fit_count = lax.axis_size("fit")
        self.own = self.pairs * self.subs
        self.total = self.own * self.owners


anywhere = pl.BlockSpec(memory_space=pl.ANY)
held_out = pl.BlockSpec(memory_space=pltpu.HBM)


def call(kernel, outs, ins, args, scratch=(), limit=16, out_specs=None, cost=None):
    return pl.pallas_call(
        kernel,
        out_shape=[jax.ShapeDtypeStruct(shape, jnp.float32) for shape in outs],
        in_specs=ins,
        out_specs=out_specs or [vmem] * len(outs),
        scratch_shapes=list(scratch),
        cost_estimate=cost,
        compiler_params=pltpu.CompilerParams(vmem_limit_bytes=limit and limit * MIB),
    )(*args)


def started(sources, targets, sems, base=0):
    copies = [
        pltpu.make_async_copy(source, target, sems.at[base + index])
        for index, (source, target) in enumerate(zip(sources, targets))
    ]
    for copy in copies:
        copy.start()
    return copies


def wait(copies):
    for copy in copies:
        copy.wait()


def side_start(z, owner, sub, side):
    return owner * z.own + (sub if side == 0 else 1 - sub) * z.pairs


def scale_of(z, pair, level, first, second, ranks, occupied):
    n = z.pnos
    row_ids = lax.broadcasted_iota(jnp.int32, (n, n), 0)
    column_ids = lax.broadcasted_iota(jnp.int32, (n, n), 1)
    level = level * jnp.ones((n, 1), jnp.float32)
    rank = ranks[pair]
    kept = f32((row_ids < rank) & (column_ids < rank))
    return kept / (level + level.T - (occupied[first[pair]] + occupied[second[pair]]))


def split(value):
    high_part = value.astype(jnp.bfloat16)
    return high_part, (value - high_part.astype(jnp.float32)).astype(jnp.bfloat16)


def mm3(a, b, contract=((1,), (0,))):
    def one(x, y):
        return lax.dot_general(x, y, (contract, ((), ())), preferred_element_type=jnp.float32)

    return one(a[0], b[0]) + (one(a[0], b[1]) + one(a[1], b[0]))


def small(z):
    return z.owners <= SMALL and z.pairs == z.fit_count == 2


def each_pair(z, action):
    if z.owners <= SMALL:
        for pair in range(z.total):
            action(pair)
    else:
        @pl.loop(0, z.total)
        def _(pair):
            action(pair)


def mapped_kernel(z, c_in, map_in, e_in, coupling_in, mp_ref, c_ref, map_ref, e_ref, coupling,
                  sems):
    n = z.pnos
    copies = started(
        [c_in, map_in, e_in, coupling_in], [c_ref, map_ref, e_ref, coupling], sems
    )
    wait(copies)
    rows = lax.broadcasted_iota(jnp.int32, (z.paos, z.paos), 0)
    lane_link = lax.broadcasted_iota(jnp.int32, (1, z.links * n), 1) // n
    for p in range(z.pairs):
        select = f32(map_ref[p : p + 1, :] == rows).astype(jnp.bfloat16)
        c_high, c_low = split(c_ref[p])
        mp_ref[p, :n, :] = lax.dot_general(
            c_high, select, (((1,), (1,)), ((), ())), preferred_element_type=jnp.float32
        ) + lax.dot_general(
            c_low, select, (((1,), (1,)), ((), ())), preferred_element_type=jnp.float32
        )
        mp_ref[p, n:, :] = jnp.zeros((EXTRA, z.paos), jnp.float32)
        mp_ref[p, n : n + 1, :n] = e_ref[p : p + 1, :]
        spread = jnp.zeros((1, z.links * n), jnp.float32)
        for k in range(z.links):
            spread = jnp.where(lane_link == k, coupling[p : p + 1, k : k + 1], spread)
        mp_ref[p, n + 1 : n + 2, :] = spread


def pack_kernel(z, s_in, mp_in, pack_ref, s_ref, mp_ref, sems):
    n = z.pnos
    line = 2 * n
    base = z.links * n // 2
    wait(started([s_in, mp_in.at[:, pl.ds(n, EXTRA), :]], [s_ref, mp_ref], sems))
    for slot in range(1 if small(z) else z.pairs):
        p = lax.axis_index("fit") if small(z) else slot
        for r in range(n // 2):
            lines = s_ref[p, :, r * line : (r + 1) * line]
            for k in range(z.links):
                row = k * n // 2 + r
                pack_ref[slot, row : row + 1, :] = lines[k : k + 1, :]
        pack_ref[slot, base:, :] = jnp.zeros((EXTRA, line), jnp.float32)
        pack_ref[slot, base : base + 1, :] = mp_ref[p, 0:1, :line]
        for k in range(z.links // 2):
            pack_ref[slot, base + 1 + k : base + 2 + k, :] = mp_ref[
                p, 1:2, k * line : (k + 1) * line
            ]
    if small(z):
        for copy in range(1, z.owners):
            pack_ref[copy] = pack_ref[0]


def below_kernel(z, second, mp_below, b_ref, right_ref):
    owner, sub = lax.axis_index("orb"), lax.axis_index("sub")
    start = side_start(z, jnp.maximum(owner - 1, 0), sub, 0)
    for p in range(z.pairs):
        j = second[start + p] - owner * z.orbitals
        held = jnp.where(j >= 0, 1.0, 0.0)
        mapped = mp_below[p, : z.pnos, :] * held
        right_ref[p] = mm(mapped, b_ref[jnp.clip(j, 0, z.orbitals - 1)])


def local_kernel(z, first, second, c_ref, mp_ref, b_ref, left_ref, right_ref):
    owner, sub = lax.axis_index("orb"), lax.axis_index("sub")
    start = side_start(z, owner, sub, 0)
    base = owner * z.orbitals
    for p in range(z.pairs):
        left_ref[p] = mm(c_ref[p], b_ref[first[start + p] - base])
        j = second[start + p] - base
        local = jnp.where(j < z.orbitals, 1.0, 0.0)
        right_ref[p] = mm(
            mp_ref[p, : z.pnos, :] * local, b_ref[jnp.minimum(j, z.orbitals - 1)]
        )


def sums_kernel(z, first, second, ranks, occupied, mp_ref, left_ref, here_ref, down_ref, *refs):
    sums_ref, right_ref = refs[-2:]
    owner, sub = lax.axis_index("orb"), lax.axis_index("sub")
    start = side_start(z, owner, sub, 0)
    n = z.pnos
    for p in range(z.pairs):
        right = here_ref[p] + down_ref[p]
        right_ref[p] = right
        scale = scale_of(
            z, start + p, mp_ref[p, n : n + 1, :n], first, second, ranks, occupied
        )
        part = mm(left_ref[p], right, ((1,), (1,)))
        sums_ref[:, p * n : (p + 1) * n] = -part * scale


def unpack(z, pair, block, rows, slot, s_high, s_low, scale_ref, coupling_ref, lists):
    n = z.pnos
    for k in range(0, z.links, 2):
        two = [block(k * n // 2, n // 2), block((k + 1) * n // 2, n // 2)]
        for odd in range(2):
            rows[slot, k // 2, pl.ds(odd, n // 2, 2), :] = jnp.concatenate(
                [part[:, odd * n : (odd + 1) * n] for part in two], axis=1
            )
    s = jnp.concatenate([rows[slot, k] for k in range(z.links // 2)], axis=1)
    s_high[pair], s_low[pair] = split(s)
    extra = block(z.links * n // 2, EXTRA)
    scale_ref[pair] = scale_of(z, pair, extra[0:1, :n], *lists)
    coupling_ref[pair, 0:1, :] = jnp.concatenate(
        [extra[1 + k : 2 + k, :] for k in range(z.links // 2)], axis=1
    )


def coupled_of(z, index, pair, near, s, coupling, amps_high, amps_low, diag_high, diag_low):
    n = z.pnos
    for k in range(z.links):
        row = near[k, pair]
        block = slice(k * n, (k + 1) * n)
        diag_high[index, block, block] = amps_high[row]
        diag_low[index, block, block] = amps_low[row]
    return split(mm3(s, (diag_high[index], diag_low[index])) * coupling)


def final_kernel(z, first, second, ranks, near, occupied, *refs):
    start_count, pack_count = (2, 4) if small(z) else (1, 1)
    starts_in = refs[:start_count]
    pack_in = refs[start_count : start_count + pack_count]
    (c_in, c_other, mp_in, mp_other, mp_below, mp_below_other, left_in, left_other, left_below,
     left_below_other, right_in, right_other) = refs[start_count + pack_count :][:12]
    (amp_out, grad_out, starts, amp_ref, packs, s_high, s_low, scale_ref, coupling_ref, s_rows, c_ref, m_ref, rhs,
     grad, flat, amps, amps_high, amps_low, next_high, next_low, diag_high, diag_low, rows_high,
     rows_low, sems) = refs[start_count + pack_count + 12 :]
    owner, sub = lax.axis_index("orb"), lax.axis_index("sub")
    fit = lax.axis_index("fit")
    n, pairs, own = z.pnos, z.pairs, z.own
    half = z.paos // z.subs
    at = pl.ds(pl.multiple_of(sub * half, half), half)
    lists = (first, second, ranks, occupied)

    def quarters(ref, base=0):
        return [ref.at[pl.ds(base + i * pairs, pairs)] for i in range(4)]

    start_copies = started(starts_in, [starts.at[i] for i in range(start_count)], sems, 16)
    pack_copies = started(pack_in, [packs.at[i] for i in range(pack_count)], sems)
    small_copies = started(
        [c_in.at[:, :, at], c_other.at[:, :, at]]
        + [ref.at[:, pl.ds(0, n), at] for ref in (mp_in, mp_other, mp_below, mp_below_other)],
        [c_ref.at[pl.ds(0, pairs)], c_ref.at[pl.ds(pairs, pairs)]] + quarters(m_ref),
        sems, 4,
    )
    large_copies = started(
        [right_in, right_other, left_in, left_other, left_below, left_below_other],
        [rhs.at[pl.ds(0, pairs)], rhs.at[pl.ds(pairs, pairs)]] + quarters(rhs, own),
        sems, 10,
    )
    diag_high[...] = jnp.zeros_like(diag_high)
    diag_low[...] = jnp.zeros_like(diag_low)

    wait(start_copies)

    def begin(pair, value):
        amps[pair] = value
        amps_high[pair], amps_low[pair] = split(value)

    if small(z):
        for index, side in enumerate((sub, 1 - sub)):
            for who in range(z.owners):
                for p in range(pairs):
                    begin(
                        who * own + side * pairs + p,
                        starts[index, who, :, p * n : (p + 1) * n],
                    )
    else:
        @pl.loop(0, z.owners * z.subs)
        def _(device):
            for p in range(pairs):
                begin(device * pairs + p, starts[0, device, :, p * n : (p + 1) * n])

    wait(pack_copies)
    if small(z):
        for index in range(pack_count):
            side = sub if index < 2 else 1 - sub
            which = fit if index % 2 == 0 else 1 - fit
            for who in range(z.owners):
                unpack(
                    z, who * own + side * pairs + which,
                    lambda start, size: packs[index, who, start : start + size, :], s_rows,
                    index * z.owners + who, s_high, s_low, scale_ref, coupling_ref, lists,
                )
    else:
        @pl.loop(0, z.total)
        def _(pair):
            unpack(
                z, pair, lambda start, size: packs[0, pair, pl.ds(start, size), :], s_rows, 0,
                s_high, s_low, scale_ref, coupling_ref, lists,
            )

    def s_of(pair):
        return s_high[pair], s_low[pair]

    def swept(index, pair, high_amps, low_amps):
        s = s_of(pair)
        inner = coupled_of(
            z, index, pair, near, s, coupling_ref[pair, 0:1, :], high_amps, low_amps, diag_high,
            diag_low,
        )
        return amps[pair] + mm3(inner, s, ((1,), (1,))) * scale_ref[pair]

    if z.owners <= SMALL:
        group = diag_high.shape[0]
        for base in range(0, z.total, group):
            pair_list = range(base, min(base + group, z.total))
            inner = [
                coupled_of(
                    z, index, pair, near, s_of(pair), coupling_ref[pair, 0:1, :], amps_high,
                    amps_low, diag_high, diag_low,
                )
                for index, pair in enumerate(pair_list)
            ]
            for value, pair in zip(inner, pair_list):
                coupled = mm3(value, s_of(pair), ((1,), (1,)))
                next_high[pair], next_low[pair] = split(amps[pair] + coupled * scale_ref[pair])
    else:
        @pl.loop(0, z.total)
        def _(pair):
            next_high[pair], next_low[pair] = split(swept(0, pair, amps_high, amps_low))

    pair_list = [
        side_start(z, who, sub, side) + p
        for who in (owner, jnp.maximum(owner - 1, 0))
        for side in range(z.subs)
        for p in range(pairs)
    ]
    inner = [
        coupled_of(
            z, index, pair, near, s_of(pair), coupling_ref[pair, 0:1, :], next_high, next_low,
            diag_high, diag_low,
        )
        for index, pair in enumerate(pair_list)
    ]
    found = [
        amps[pair] + mm3(value, s_of(pair), ((1,), (1,))) * scale_ref[pair]
        for value, pair in zip(inner, pair_list)
    ]
    turned = [value.T for value in found]
    wait(small_copies)
    weights = [split(2.0 * a - b) for a, b in zip(found, turned)]
    weights_turned = [split(2.0 * b - a) for a, b in zip(found[:own], turned[:own])]
    terms = (
        [mm3(w, split(c_ref[i])) for i, w in enumerate(weights_turned)]
        + [mm3(w, split(m_ref[i])) for i, w in enumerate(weights)]
    )
    orbital_list = (
        [first[pair] - owner * z.orbitals for pair in pair_list[:own]]
        + [second[pair] - owner * z.orbitals for pair in pair_list]
    )
    for index in range(0, 3 * own, 2):
        for o in range(z.orbitals):
            block = jnp.concatenate(
                [
                    jnp.where(orbital_list[i] == o, terms[i], 0.0) for i in (index, index + 1)
                ]
            ).T
            place = (slice(o * half, (o + 1) * half), slice(index * n, (index + 2) * n))
            rows_high[place], rows_low[place] = split(block)

    for p in range(pairs):
        flat[p] = found[p]
        even = flat[p, pl.ds(0, n // 2, 2), :]
        odd = flat[p, pl.ds(1, n // 2, 2), :]
        lines = jnp.concatenate([even, odd], axis=1)
        for r in range(n // 2):
            amp_ref[p : p + 1, r * 2 * n : (r + 1) * 2 * n] = lines[r : r + 1, :]
    copies = started([amp_ref], [amp_out], sems, 18)

    wait(large_copies)
    step = 256
    rows = (rows_high[...], rows_low[...])
    for index, start in enumerate(range(0, z.fits, step)):
        factor = rhs[:, :, start : start + step].reshape(3 * own * n, step)
        grad[:, :, start : start + step] = mm3(rows, split(factor)).reshape(
            z.orbitals, half, step
        )
        window = pl.ds(start, step)
        copies += started(
            [grad.at[:, :, window]], [grad_out.at[:, :, window]], sems, 19 + index
        )
    wait(copies)


def gate(values, *after):
    return lax.optimization_barrier((tuple(values), after))[0]


def body(
    blocks,
    pno_coefficients,
    domain_map,
    pair_first,
    pair_second,
    pno_ranks,
    neighbours,
    couplings,
    intersections,
    pno_energy,
    occ_energy,
):
    z = Sizes(blocks, pno_coefficients, couplings)
    n, pairs, own, fits = z.pnos, z.pairs, z.own, z.fits
    half = z.paos // z.subs
    wide = z.links * n
    hbm = held_out
    bf16 = jnp.bfloat16
    more = 0 if z.owners <= SMALL else z.owners

    def scratch(*shape, kind=jnp.float32):
        return pltpu.VMEM(shape, kind)

    pack_shape = (z.owners if small(z) else pairs, z.links * n // 2 + EXTRA, 2 * n)
    (mp,) = call(
        functools.partial(mapped_kernel, z),
        [(pairs, n + EXTRA, z.paos)],
        [hbm] * 4,
        (pno_coefficients, domain_map, pno_energy, couplings),
        [
            scratch(*pno_coefficients.shape),
            pltpu.VMEM(domain_map.shape, jnp.int32),
            scratch(*pno_energy.shape),
            scratch(*couplings.shape),
            pltpu.SemaphoreType.DMA((4,)),
        ],
        limit=None,
    )
    mp_below = shifted(mp, "orb", 1)
    (pack,) = call(
        functools.partial(pack_kernel, z),
        [pack_shape],
        [hbm] * 2,
        (intersections, mp),
        [
            scratch(*intersections.shape),
            scratch(pairs, EXTRA, z.paos),
            pltpu.SemaphoreType.DMA((2,)),
        ],
        limit=None,
    )
    if small(z):
        packs = [lax.all_to_all(pack, "orb", 0, 0)]
    else:
        packs = [lax.all_gather(pack, ("orb", "sub"), axis=0, tiled=True)]
    (right_below,) = call(
        functools.partial(below_kernel, z),
        [(pairs, n, fits)],
        [smem, vmem, vmem],
        (pair_second, gate((mp_below,), pack)[0], blocks),
        limit=8,
    )
    down = shifted(right_below, "orb", -1)
    mp_late, coefficients, mp_below_late = gate((mp, pno_coefficients, mp_below), right_below)
    mp_below_other = swapped(mp_below_late, "sub")
    left, right_here = call(
        functools.partial(local_kernel, z),
        [(pairs, n, fits), (pairs, n, fits)],
        [smem, smem, vmem, vmem, vmem],
        (pair_first, pair_second, coefficients, mp_late, blocks),
        limit=8,
        cost=BRIEF,
    )
    left_below = shifted(left, "orb", 1)
    mp_other = swapped(gate((mp,), right_here)[0], "sub")
    left_other = swapped(left, "sub")
    c_other = swapped(gate((coefficients,), right_here)[0], "sub")

    lists = (pair_first, pair_second, pno_ranks)
    (down,) = gate((down,), mp_other, left_other, c_other, mp_below_other)
    part, right = call(
        functools.partial(sums_kernel, z),
        [(n, pairs * n), (pairs, n, fits)],
        [smem] * 4 + [vmem] * 4,
        (*lists, occ_energy, mp, left, right_here, down),
        limit=8,
    )
    if small(z):
        packs.append(None)
        packs.append(swapped(gate(packs[:1], part)[0], "sub"))
        sums = part + swapped(part, "fit")
        packs[1] = swapped(gate(packs[:1], part)[0], "fit")
        start_amps = [
            lax.all_to_all(jnp.broadcast_to(sums[None], (z.owners, *sums.shape)), "orb", 0, 0)
        ]
        start_amps.append(swapped(start_amps[0], "sub"))
        packs.append(swapped(gate(packs[1:2], start_amps[0])[0], "sub"))
    else:
        sums = lax.psum(part, "fit")
        start_amps = [lax.all_gather(sums, ("orb", "sub"), axis=0, tiled=False)]

    right_other = swapped(right, "sub")
    left_below_other = swapped(gate((left_below,), sums)[0], "sub")

    args = (
        *lists, neighbours.T, occ_energy, *start_amps, *packs,
        pno_coefficients, c_other, mp, mp_other, mp_below, mp_below_other,
        left, left_other, left_below, left_below_other, right, right_other,
    )
    square = (z.total, n, n)
    amplitudes, gradient = call(
        functools.partial(final_kernel, z),
        [(pairs, n * n), (z.orbitals, half, fits)],
        [smem] * 5 + [hbm] * (12 + len(start_amps) + len(packs)),
        args,
        [
            scratch(len(start_amps), *start_amps[0].shape),
            scratch(pairs, n * n),
            scratch(len(packs), *packs[0].shape),
            scratch(z.total, n, wide, kind=bf16),
            scratch(z.total, n, wide, kind=bf16),
            scratch(*square),
            scratch(z.total, EXTRA, wide),
            scratch(z.total if small(z) else 1, z.links // 2, n, 2 * n),
            scratch(own, n, half),
            scratch(2 * own, n, half),
            scratch(3 * own, n, fits),
            scratch(z.orbitals, half, fits),
            scratch(pairs, n, n),
            scratch(*square),
        ]
        + [scratch(*square, kind=bf16)] * 4
        + [scratch(2 * own, wide, wide, kind=bf16)] * 2
        + [scratch(z.orbitals * half, 3 * own * n, kind=bf16)] * 2
        + [pltpu.SemaphoreType.DMA((19 + -(-fits // 256),))],
        limit=60,
        out_specs=[hbm, hbm],
    )
    return (amplitudes, gradient)


def solution(mesh):
    in_specs = (
        P(("groups", "orb"), None, "fit"),
        P(("groups", "orb", "sub"), None, None),
        P(("groups", "orb", "sub"), None),
        P("groups"),
        P("groups"),
        P("groups"),
        P("groups", None),
        P(("groups", "orb", "sub"), None),
        P(("groups", "orb", "sub"), None, None),
        P(("groups", "orb", "sub"), None),
        P("groups"),
    )
    out_specs = (P(("groups", "orb", "sub"), None), P(("groups", "orb"), "sub", "fit"))
    return jax.shard_map(body, mesh=mesh, in_specs=in_specs, out_specs=out_specs, check_vma=False)
```

```python
import functools

import jax
import jax.numpy as jnp
from jax import lax
from jax.experimental import pallas as pl
from jax.experimental.pallas import tpu as pltpu
from jax.sharding import PartitionSpec as P

ITERS = 2
SMALL = 4
MIB = 1 << 20
EXTRA = 8

high = lax.Precision.HIGH
BRIEF = pl.CostEstimate(flops=1, bytes_accessed=1, transcendentals=0)
smem = pl.BlockSpec(memory_space=pltpu.SMEM)
vmem = pl.BlockSpec(memory_space=pltpu.VMEM)


def mm(a, b, contract=((1,), (0,))):
    return lax.dot_general(
        a, b, (contract, ((), ())), precision=high, preferred_element_type=jnp.float32
    )


def shifted(value, axis, steps):
    count = lax.axis_size(axis)
    initial, last = (max(0, -steps), min(count, count - steps))
    return lax.ppermute(value, axis, [(source, source + steps) for source in range(initial, last)])


def swapped(value, axis):
    return lax.ppermute(value, axis, [(0, 1), (1, 0)])


def f32(flag):
    return flag.astype(jnp.float32)


class Sizes:
    def __init__(self, blocks, pno_coefficients, couplings):
        self.orbitals, self.paos, self.fits = blocks.shape
        self.pairs, self.pnos = pno_coefficients.shape[:2]
        self.links = couplings.shape[1]
        self.subs = lax.axis_size("sub")
        self.owners = lax.axis_size("orb")
        self.fit_count = lax.axis_size("fit")
        self.own = self.pairs * self.subs
        self.total = self.own * self.owners


anywhere = pl.BlockSpec(memory_space=pl.ANY)
held_out = pl.BlockSpec(memory_space=pltpu.HBM)


def call(kernel, outs, ins, args, scratch=(), limit=16, out_specs=None, cost=None):
    return pl.pallas_call(
        kernel,
        out_shape=[jax.ShapeDtypeStruct(shape, jnp.float32) for shape in outs],
        in_specs=ins,
        out_specs=out_specs or [vmem] * len(outs),
        scratch_shapes=list(scratch),
        cost_estimate=cost,
        compiler_params=pltpu.CompilerParams(vmem_limit_bytes=limit and limit * MIB),
    )(*args)


def started(sources, targets, sems, base=0):
    copies = [
        pltpu.make_async_copy(source, target, sems.at[base + index])
        for index, (source, target) in enumerate(zip(sources, targets))
    ]
    for copy in copies:
        copy.start()
    return copies


def wait(copies):
    for copy in copies:
        copy.wait()


def side_start(z, owner, sub, side):
    return owner * z.own + (sub if side == 0 else 1 - sub) * z.pairs


def scale_of(z, pair, level, first, second, ranks, occupied):
    n = z.pnos
    row_ids = lax.broadcasted_iota(jnp.int32, (n, n), 0)
    column_ids = lax.broadcasted_iota(jnp.int32, (n, n), 1)
    level = level * jnp.ones((n, 1), jnp.float32)
    rank = ranks[pair]
    kept = f32((row_ids < rank) & (column_ids < rank))
    return kept / (level + level.T - (occupied[first[pair]] + occupied[second[pair]]))


def split(value):
    high_part = value.astype(jnp.bfloat16)
    return high_part, (value - high_part.astype(jnp.float32)).astype(jnp.bfloat16)


def mm3(a, b, contract=((1,), (0,))):
    def one(x, y):
        return lax.dot_general(x, y, (contract, ((), ())), preferred_element_type=jnp.float32)

    return one(a[0], b[0]) + (one(a[0], b[1]) + one(a[1], b[0]))


def small(z):
    return z.owners <= SMALL and z.pairs == z.fit_count == 2


def each_pair(z, action):
    if z.owners <= SMALL:
        for pair in range(z.total):
            action(pair)
    else:
        @pl.loop(0, z.total)
        def _(pair):
            action(pair)


def mapped_kernel(z, c_in, map_in, e_in, coupling_in, mp_ref, c_ref, map_ref, e_ref, coupling,
                  sems):
    n = z.pnos
    copies = started(
        [c_in, map_in, e_in, coupling_in], [c_ref, map_ref, e_ref, coupling], sems
    )
    wait(copies)
    rows = lax.broadcasted_iota(jnp.int32, (z.paos, z.paos), 0)
    lane_link = lax.broadcasted_iota(jnp.int32, (1, z.links * n), 1) // n
    for p in range(z.pairs):
        select = f32(map_ref[p : p + 1, :] == rows).astype(jnp.bfloat16)
        c_high, c_low = split(c_ref[p])
        mp_ref[p, :n, :] = lax.dot_general(
            c_high, select, (((1,), (1,)), ((), ())), preferred_element_type=jnp.float32
        ) + lax.dot_general(
            c_low, select, (((1,), (1,)), ((), ())), preferred_element_type=jnp.float32
        )
        mp_ref[p, n:, :] = jnp.zeros((EXTRA, z.paos), jnp.float32)
        mp_ref[p, n : n + 1, :n] = e_ref[p : p + 1, :]
        spread = jnp.zeros((1, z.links * n), jnp.float32)
        for k in range(z.links):
            spread = jnp.where(lane_link == k, coupling[p : p + 1, k : k + 1], spread)
        mp_ref[p, n + 1 : n + 2, :] = spread


def pack_kernel(z, s_in, mp_in, pack_ref, s_ref, mp_ref, sems):
    n = z.pnos
    line = 2 * n
    base = z.links * n // 2
    wait(started([s_in, mp_in.at[:, pl.ds(n, EXTRA), :]], [s_ref, mp_ref], sems))
    for slot in range(1 if small(z) else z.pairs):
        p = lax.axis_index("fit") if small(z) else slot
        for r in range(n // 2):
            lines = s_ref[p, :, r * line : (r + 1) * line]
            for k in range(z.links):
                row = k * n // 2 + r
                pack_ref[slot, row : row + 1, :] = lines[k : k + 1, :]
        pack_ref[slot, base:, :] = jnp.zeros((EXTRA, line), jnp.float32)
        pack_ref[slot, base : base + 1, :] = mp_ref[p, 0:1, :line]
        for k in range(z.links // 2):
            pack_ref[slot, base + 1 + k : base + 2 + k, :] = mp_ref[
                p, 1:2, k * line : (k + 1) * line
            ]
    if small(z):
        for copy in range(1, z.owners):
            pack_ref[copy] = pack_ref[0]


def below_kernel(z, second, mp_below, b_ref, touched, right_ref):
    owner, sub = lax.axis_index("orb"), lax.axis_index("sub")
    start = side_start(z, jnp.maximum(owner - 1, 0), sub, 0)
    for p in range(z.pairs):
        j = second[start + p] - owner * z.orbitals
        held = jnp.where(j >= 0, 1.0, 0.0)
        mapped = mp_below[p, : z.pnos, :] * held
        right_ref[p] = mm(mapped, b_ref[jnp.clip(j, 0, z.orbitals - 1)])


def early_kernel(z, second, mp_ref, b_ref, out_ref):
    out_ref[...] = b_ref[0, :EXTRA, :128] + mp_ref[...] + second[0].astype(jnp.float32)


def local_kernel(z, first, second, c_ref, mp_ref, b_ref, left_ref, right_ref):
    owner, sub = lax.axis_index("orb"), lax.axis_index("sub")
    start = side_start(z, owner, sub, 0)
    base = owner * z.orbitals
    for p in range(z.pairs):
        left_ref[p] = mm(c_ref[p], b_ref[first[start + p] - base])
        j = second[start + p] - base
        local = jnp.where(j < z.orbitals, 1.0, 0.0)
        right_ref[p] = mm(
            mp_ref[p, : z.pnos, :] * local, b_ref[jnp.minimum(j, z.orbitals - 1)]
        )


def sums_kernel(z, first, second, ranks, occupied, mp_ref, left_ref, here_ref, down_ref, *refs):
    sums_ref, right_ref = refs[-2:]
    owner, sub = lax.axis_index("orb"), lax.axis_index("sub")
    start = side_start(z, owner, sub, 0)
    n = z.pnos
    for p in range(z.pairs):
        right = here_ref[p] + down_ref[p]
        right_ref[p] = right
        scale = scale_of(
            z, start + p, mp_ref[p, n : n + 1, :n], first, second, ranks, occupied
        )
        part = mm(left_ref[p], right, ((1,), (1,)))
        sums_ref[:, p * n : (p + 1) * n] = -part * scale


def unpack(z, pair, block, rows, slot, s_high, s_low, scale_ref, coupling_ref, lists):
    n = z.pnos
    for k in range(0, z.links, 2):
        two = [block(k * n // 2, n // 2), block((k + 1) * n // 2, n // 2)]
        for odd in range(2):
            rows[slot, k // 2, pl.ds(odd, n // 2, 2), :] = jnp.concatenate(
                [part[:, odd * n : (odd + 1) * n] for part in two], axis=1
            )
    s = jnp.concatenate([rows[slot, k] for k in range(z.links // 2)], axis=1)
    s_high[pair], s_low[pair] = split(s)
    extra = block(z.links * n // 2, EXTRA)
    scale_ref[pair] = scale_of(z, pair, extra[0:1, :n], *lists)
    coupling_ref[pair, 0:1, :] = jnp.concatenate(
        [extra[1 + k : 2 + k, :] for k in range(z.links // 2)], axis=1
    )


def coupled_of(z, index, pair, near, s, coupling, amps_high, amps_low, diag_high, diag_low):
    n = z.pnos
    for k in range(z.links):
        row = near[k, pair]
        block = slice(k * n, (k + 1) * n)
        diag_high[index, block, block] = amps_high[row]
        diag_low[index, block, block] = amps_low[row]
    return split(mm3(s, (diag_high[index], diag_low[index])) * coupling)


def final_kernel(z, first, second, ranks, near, occupied, *refs):
    start_count, pack_count = (2, 4) if small(z) else (1, 1)
    starts_in = refs[:start_count]
    pack_in = refs[start_count : start_count + pack_count]
    (c_in, c_other, mp_in, mp_other, mp_below, mp_below_other, left_in, left_other, left_below,
     left_below_other, right_in, right_other) = refs[start_count + pack_count :][:12]
    (amp_out, grad_out, starts, amp_ref, packs, s_high, s_low, scale_ref, coupling_ref, s_rows, c_ref, m_ref, rhs,
     grad, flat, amps, amps_high, amps_low, next_high, next_low, diag_high, diag_low, rows_high,
     rows_low, sems) = refs[start_count + pack_count + 12 :]
    owner, sub = lax.axis_index("orb"), lax.axis_index("sub")
    fit = lax.axis_index("fit")
    n, pairs, own = z.pnos, z.pairs, z.own
    half = z.paos // z.subs
    at = pl.ds(pl.multiple_of(sub * half, half), half)
    lists = (first, second, ranks, occupied)

    def quarters(ref, base=0):
        return [ref.at[pl.ds(base + i * pairs, pairs)] for i in range(4)]

    start_copies = started(starts_in, [starts.at[i] for i in range(start_count)], sems, 16)
    pack_copies = started(pack_in, [packs.at[i] for i in range(pack_count)], sems)
    small_copies = started(
        [c_in.at[:, :, at], c_other.at[:, :, at]]
        + [ref.at[:, pl.ds(0, n), at] for ref in (mp_in, mp_other, mp_below, mp_below_other)],
        [c_ref.at[pl.ds(0, pairs)], c_ref.at[pl.ds(pairs, pairs)]] + quarters(m_ref),
        sems, 4,
    )
    large_copies = started(
        [right_in, right_other, left_in, left_other, left_below, left_below_other],
        [rhs.at[pl.ds(0, pairs)], rhs.at[pl.ds(pairs, pairs)]] + quarters(rhs, own),
        sems, 10,
    )
    diag_high[...] = jnp.zeros_like(diag_high)
    diag_low[...] = jnp.zeros_like(diag_low)

    wait(start_copies)

    def begin(pair, value):
        amps[pair] = value
        amps_high[pair], amps_low[pair] = split(value)

    if small(z):
        for index, side in enumerate((sub, 1 - sub)):
            for who in range(z.owners):
                for p in range(pairs):
                    begin(
                        who * own + side * pairs + p,
                        starts[index, who, :, p * n : (p + 1) * n],
                    )
    else:
        @pl.loop(0, z.owners * z.subs)
        def _(device):
            for p in range(pairs):
                begin(device * pairs + p, starts[0, device, :, p * n : (p + 1) * n])

    wait(pack_copies)
    if small(z):
        for index in range(pack_count):
            side = sub if index < 2 else 1 - sub
            which = fit if index % 2 == 0 else 1 - fit
            for who in range(z.owners):
                unpack(
                    z, who * own + side * pairs + which,
                    lambda start, size: packs[index, who, start : start + size, :], s_rows,
                    index * z.owners + who, s_high, s_low, scale_ref, coupling_ref, lists,
                )
    else:
        @pl.loop(0, z.total)
        def _(pair):
            unpack(
                z, pair, lambda start, size: packs[0, pair, pl.ds(start, size), :], s_rows, 0,
                s_high, s_low, scale_ref, coupling_ref, lists,
            )

    def s_of(pair):
        return s_high[pair], s_low[pair]

    def swept(index, pair, high_amps, low_amps):
        s = s_of(pair)
        inner = coupled_of(
            z, index, pair, near, s, coupling_ref[pair, 0:1, :], high_amps, low_amps, diag_high,
            diag_low,
        )
        return amps[pair] + mm3(inner, s, ((1,), (1,))) * scale_ref[pair]

    if z.owners <= SMALL:
        group = diag_high.shape[0]
        for base in range(0, z.total, group):
            pair_list = range(base, min(base + group, z.total))
            inner = [
                coupled_of(
                    z, index, pair, near, s_of(pair), coupling_ref[pair, 0:1, :], amps_high,
                    amps_low, diag_high, diag_low,
                )
                for index, pair in enumerate(pair_list)
            ]
            for value, pair in zip(inner, pair_list):
                coupled = mm3(value, s_of(pair), ((1,), (1,)))
                next_high[pair], next_low[pair] = split(amps[pair] + coupled * scale_ref[pair])
    else:
        @pl.loop(0, z.total)
        def _(pair):
            next_high[pair], next_low[pair] = split(swept(0, pair, amps_high, amps_low))

    pair_list = [
        side_start(z, who, sub, side) + p
        for who in (owner, jnp.maximum(owner - 1, 0))
        for side in range(z.subs)
        for p in range(pairs)
    ]
    inner = [
        coupled_of(
            z, index, pair, near, s_of(pair), coupling_ref[pair, 0:1, :], next_high, next_low,
            diag_high, diag_low,
        )
        for index, pair in enumerate(pair_list)
    ]
    found = [
        amps[pair] + mm3(value, s_of(pair), ((1,), (1,))) * scale_ref[pair]
        for value, pair in zip(inner, pair_list)
    ]
    turned = [value.T for value in found]
    wait(small_copies)
    weights = [split(2.0 * a - b) for a, b in zip(found, turned)]
    weights_turned = [split(2.0 * b - a) for a, b in zip(found[:own], turned[:own])]
    terms = (
        [mm3(w, split(c_ref[i])) for i, w in enumerate(weights_turned)]
        + [mm3(w, split(m_ref[i])) for i, w in enumerate(weights)]
    )
    orbital_list = (
        [first[pair] - owner * z.orbitals for pair in pair_list[:own]]
        + [second[pair] - owner * z.orbitals for pair in pair_list]
    )
    for index in range(0, 3 * own, 2):
        for o in range(z.orbitals):
            block = jnp.concatenate(
                [
                    jnp.where(orbital_list[i] == o, terms[i], 0.0) for i in (index, index + 1)
                ]
            ).T
            place = (slice(o * half, (o + 1) * half), slice(index * n, (index + 2) * n))
            rows_high[place], rows_low[place] = split(block)

    for p in range(pairs):
        flat[p] = found[p]
        even = flat[p, pl.ds(0, n // 2, 2), :]
        odd = flat[p, pl.ds(1, n // 2, 2), :]
        lines = jnp.concatenate([even, odd], axis=1)
        for r in range(n // 2):
            amp_ref[p : p + 1, r * 2 * n : (r + 1) * 2 * n] = lines[r : r + 1, :]
    copies = started([amp_ref], [amp_out], sems, 18)

    wait(large_copies)
    step = 256
    rows = (rows_high[...], rows_low[...])
    for index, start in enumerate(range(0, z.fits, step)):
        factor = rhs[:, :, start : start + step].reshape(3 * own * n, step)
        grad[:, :, start : start + step] = mm3(rows, split(factor)).reshape(
            z.orbitals, half, step
        )
        window = pl.ds(start, step)
        copies += started(
            [grad.at[:, :, window]], [grad_out.at[:, :, window]], sems, 19 + index
        )
    wait(copies)


def gate(values, *after):
    return lax.optimization_barrier((tuple(values), after))[0]


def body(
    blocks,
    pno_coefficients,
    domain_map,
    pair_first,
    pair_second,
    pno_ranks,
    neighbours,
    couplings,
    intersections,
    pno_energy,
    occ_energy,
):
    z = Sizes(blocks, pno_coefficients, couplings)
    n, pairs, own, fits = z.pnos, z.pairs, z.own, z.fits
    half = z.paos // z.subs
    wide = z.links * n
    hbm = held_out
    bf16 = jnp.bfloat16
    more = 0 if z.owners <= SMALL else z.owners

    def scratch(*shape, kind=jnp.float32):
        return pltpu.VMEM(shape, kind)

    pack_shape = (z.owners if small(z) else pairs, z.links * n // 2 + EXTRA, 2 * n)
    (mp,) = call(
        functools.partial(mapped_kernel, z),
        [(pairs, n + EXTRA, z.paos)],
        [hbm] * 4,
        (pno_coefficients, domain_map, pno_energy, couplings),
        [
            scratch(*pno_coefficients.shape),
            pltpu.VMEM(domain_map.shape, jnp.int32),
            scratch(*pno_energy.shape),
            scratch(*couplings.shape),
            pltpu.SemaphoreType.DMA((4,)),
        ],
        limit=None,
    )
    mp_below = shifted(mp, "orb", 1)
    (pack,) = call(
        functools.partial(pack_kernel, z),
        [pack_shape],
        [hbm] * 2,
        (intersections, mp),
        [
            scratch(*intersections.shape),
            scratch(pairs, EXTRA, z.paos),
            pltpu.SemaphoreType.DMA((2,)),
        ],
        limit=None,
    )
    if small(z):
        packs = [lax.all_to_all(pack, "orb", 0, 0)]
    else:
        packs = [lax.all_gather(pack, ("orb", "sub"), axis=0, tiled=True)]
    (touched,) = call(
        functools.partial(early_kernel, z),
        [(EXTRA, 128)],
        [smem, vmem, vmem],
        (pair_second, mp[0, :EXTRA, :128], blocks),
        limit=8,
    )
    (right_below,) = call(
        functools.partial(below_kernel, z),
        [(pairs, n, fits)],
        [smem, vmem, vmem, vmem],
        (pair_second, gate((mp_below,), pack)[0], blocks, touched),
        limit=8,
    )
    down = shifted(right_below, "orb", -1)
    mp_late, coefficients, mp_below_late = gate((mp, pno_coefficients, mp_below), right_below)
    mp_below_other = swapped(mp_below_late, "sub")
    left, right_here = call(
        functools.partial(local_kernel, z),
        [(pairs, n, fits), (pairs, n, fits)],
        [smem, smem, vmem, vmem, vmem],
        (pair_first, pair_second, coefficients, mp_late, blocks),
        limit=8,
        cost=BRIEF,
    )
    mp_other = swapped(gate((mp,), right_here)[0], "sub")
    left_other = swapped(left, "sub")
    c_other = swapped(gate((coefficients,), right_here)[0], "sub")

    lists = (pair_first, pair_second, pno_ranks)
    (down,) = gate((down,), mp_other, left_other, c_other, mp_below_other)
    part, right = call(
        functools.partial(sums_kernel, z),
        [(n, pairs * n), (pairs, n, fits)],
        [smem] * 4 + [vmem] * 4,
        (*lists, occ_energy, mp, left, right_here, down),
        limit=8,
    )
    if small(z):
        packs.append(None)
        packs.append(swapped(gate(packs[:1], part)[0], "sub"))
        sums = part + swapped(part, "fit")
        packs[1] = swapped(gate(packs[:1], part)[0], "fit")
        start_amps = [
            lax.all_to_all(jnp.broadcast_to(sums[None], (z.owners, *sums.shape)), "orb", 0, 0)
        ]
        start_amps.append(swapped(start_amps[0], "sub"))
        packs.append(swapped(gate(packs[1:2], start_amps[0])[0], "sub"))
    else:
        sums = lax.psum(part, "fit")
        start_amps = [lax.all_gather(sums, ("orb", "sub"), axis=0, tiled=False)]

    (right_late,) = gate((right,), part)
    left_below = shifted(gate((left,), part)[0], "orb", 1)
    (left_late,) = gate((left_below,), start_amps[0])
    right_other, left_below_other = [
        swapped(value, "sub") for value in (right_late, left_late)
    ]

    args = (
        *lists, neighbours.T, occ_energy, *start_amps, *packs,
        pno_coefficients, c_other, mp, mp_other, mp_below, mp_below_other,
        left, left_other, left_below, left_below_other, right, right_other,
    )
    square = (z.total, n, n)
    amplitudes, gradient = call(
        functools.partial(final_kernel, z),
        [(pairs, n * n), (z.orbitals, half, fits)],
        [smem] * 5 + [hbm] * (12 + len(start_amps) + len(packs)),
        args,
        [
            scratch(len(start_amps), *start_amps[0].shape),
            scratch(pairs, n * n),
            scratch(len(packs), *packs[0].shape),
            scratch(z.total, n, wide, kind=bf16),
            scratch(z.total, n, wide, kind=bf16),
            scratch(*square),
            scratch(z.total, EXTRA, wide),
            scratch(z.total if small(z) else 1, z.links // 2, n, 2 * n),
            scratch(own, n, half),
            scratch(2 * own, n, half),
            scratch(3 * own, n, fits),
            scratch(z.orbitals, half, fits),
            scratch(pairs, n, n),
            scratch(*square),
        ]
        + [scratch(*square, kind=bf16)] * 4
        + [scratch(2 * own, wide, wide, kind=bf16)] * 2
        + [scratch(z.orbitals * half, 3 * own * n, kind=bf16)] * 2
        + [pltpu.SemaphoreType.DMA((19 + -(-fits // 256),))],
        limit=60,
        out_specs=[hbm, hbm],
    )
    return (amplitudes, gradient)


def solution(mesh):
    in_specs = (
        P(("groups", "orb"), None, "fit"),
        P(("groups", "orb", "sub"), None, None),
        P(("groups", "orb", "sub"), None),
        P("groups"),
        P("groups"),
        P("groups"),
        P("groups", None),
        P(("groups", "orb", "sub"), None),
        P(("groups", "orb", "sub"), None, None),
        P(("groups", "orb", "sub"), None),
        P("groups"),
    )
    out_specs = (P(("groups", "orb", "sub"), None), P(("groups", "orb"), "sub", "fit"))
    return jax.shard_map(body, mesh=mesh, in_specs=in_specs, out_specs=out_specs, check_vma=False)
```

```python
import functools

import jax
import jax.numpy as jnp
from jax import lax
from jax.experimental import pallas as pl
from jax.experimental.pallas import tpu as pltpu
from jax.sharding import PartitionSpec as P

ITERS = 2
SMALL = 4
MIB = 1 << 20
EXTRA = 8

high = lax.Precision.HIGH
BRIEF = pl.CostEstimate(flops=1, bytes_accessed=1, transcendentals=0)
smem = pl.BlockSpec(memory_space=pltpu.SMEM)
vmem = pl.BlockSpec(memory_space=pltpu.VMEM)


def mm(a, b, contract=((1,), (0,))):
    return lax.dot_general(
        a, b, (contract, ((), ())), precision=high, preferred_element_type=jnp.float32
    )


def shifted(value, axis, steps):
    count = lax.axis_size(axis)
    initial, last = (max(0, -steps), min(count, count - steps))
    return lax.ppermute(value, axis, [(source, source + steps) for source in range(initial, last)])


def swapped(value, axis):
    return lax.ppermute(value, axis, [(0, 1), (1, 0)])


def f32(flag):
    return flag.astype(jnp.float32)


class Sizes:
    def __init__(self, blocks, pno_coefficients, couplings):
        self.orbitals, self.paos, self.fits = blocks.shape
        self.pairs, self.pnos = pno_coefficients.shape[:2]
        self.links = couplings.shape[1]
        self.subs = lax.axis_size("sub")
        self.owners = lax.axis_size("orb")
        self.fit_count = lax.axis_size("fit")
        self.own = self.pairs * self.subs
        self.total = self.own * self.owners


anywhere = pl.BlockSpec(memory_space=pl.ANY)
held_out = pl.BlockSpec(memory_space=pltpu.HBM)


def call(kernel, outs, ins, args, scratch=(), limit=16, out_specs=None, cost=None):
    return pl.pallas_call(
        kernel,
        out_shape=[jax.ShapeDtypeStruct(shape, jnp.float32) for shape in outs],
        in_specs=ins,
        out_specs=out_specs or [vmem] * len(outs),
        scratch_shapes=list(scratch),
        cost_estimate=cost,
        compiler_params=pltpu.CompilerParams(vmem_limit_bytes=limit and limit * MIB),
    )(*args)


def started(sources, targets, sems, base=0):
    copies = [
        pltpu.make_async_copy(source, target, sems.at[base + index])
        for index, (source, target) in enumerate(zip(sources, targets))
    ]
    for copy in copies:
        copy.start()
    return copies


def wait(copies):
    for copy in copies:
        copy.wait()


def side_start(z, owner, sub, side):
    return owner * z.own + (sub if side == 0 else 1 - sub) * z.pairs


def scale_of(z, pair, level, first, second, ranks, occupied):
    n = z.pnos
    row_ids = lax.broadcasted_iota(jnp.int32, (n, n), 0)
    column_ids = lax.broadcasted_iota(jnp.int32, (n, n), 1)
    level = level * jnp.ones((n, 1), jnp.float32)
    rank = ranks[pair]
    kept = f32((row_ids < rank) & (column_ids < rank))
    return kept / (level + level.T - (occupied[first[pair]] + occupied[second[pair]]))


def split(value):
    high_part = value.astype(jnp.bfloat16)
    return high_part, (value - high_part.astype(jnp.float32)).astype(jnp.bfloat16)


def mm3(a, b, contract=((1,), (0,))):
    def one(x, y):
        return lax.dot_general(x, y, (contract, ((), ())), preferred_element_type=jnp.float32)

    return one(a[0], b[0]) + (one(a[0], b[1]) + one(a[1], b[0]))


def small(z):
    return z.owners <= SMALL and z.pairs == z.fit_count == 2


def each_pair(z, action):
    if z.owners <= SMALL:
        for pair in range(z.total):
            action(pair)
    else:
        @pl.loop(0, z.total)
        def _(pair):
            action(pair)


def mapped_kernel(z, c_in, map_in, e_in, coupling_in, mp_ref, c_ref, map_ref, e_ref, coupling,
                  sems):
    n = z.pnos
    copies = started(
        [c_in, map_in, e_in, coupling_in], [c_ref, map_ref, e_ref, coupling], sems
    )
    wait(copies)
    rows = lax.broadcasted_iota(jnp.int32, (z.paos, z.paos), 0)
    lane_link = lax.broadcasted_iota(jnp.int32, (1, z.links * n), 1) // n
    for p in range(z.pairs):
        select = f32(map_ref[p : p + 1, :] == rows).astype(jnp.bfloat16)
        c_high, c_low = split(c_ref[p])
        mp_ref[p, :n, :] = lax.dot_general(
            c_high, select, (((1,), (1,)), ((), ())), preferred_element_type=jnp.float32
        ) + lax.dot_general(
            c_low, select, (((1,), (1,)), ((), ())), preferred_element_type=jnp.float32
        )
        mp_ref[p, n:, :] = jnp.zeros((EXTRA, z.paos), jnp.float32)
        mp_ref[p, n : n + 1, :n] = e_ref[p : p + 1, :]
        spread = jnp.zeros((1, z.links * n), jnp.float32)
        for k in range(z.links):
            spread = jnp.where(lane_link == k, coupling[p : p + 1, k : k + 1], spread)
        mp_ref[p, n + 1 : n + 2, :] = spread


def pack_kernel(z, s_in, mp_in, pack_ref, s_ref, mp_ref, sems):
    n = z.pnos
    line = 2 * n
    base = z.links * n // 2
    wait(started([s_in, mp_in.at[:, pl.ds(n, EXTRA), :]], [s_ref, mp_ref], sems))
    for slot in range(1 if small(z) else z.pairs):
        p = lax.axis_index("fit") if small(z) else slot
        for r in range(n // 2):
            lines = s_ref[p, :, r * line : (r + 1) * line]
            for k in range(z.links):
                row = k * n // 2 + r
                pack_ref[slot, row : row + 1, :] = lines[k : k + 1, :]
        pack_ref[slot, base:, :] = jnp.zeros((EXTRA, line), jnp.float32)
        pack_ref[slot, base : base + 1, :] = mp_ref[p, 0:1, :line]
        for k in range(z.links // 2):
            pack_ref[slot, base + 1 + k : base + 2 + k, :] = mp_ref[
                p, 1:2, k * line : (k + 1) * line
            ]
    if small(z):
        for copy in range(1, z.owners):
            pack_ref[copy] = pack_ref[0]


def below_kernel(z, second, mp_below, b_ref, touched, right_ref):
    owner, sub = lax.axis_index("orb"), lax.axis_index("sub")
    start = side_start(z, jnp.maximum(owner - 1, 0), sub, 0)
    for p in range(z.pairs):
        j = second[start + p] - owner * z.orbitals
        held = jnp.where(j >= 0, 1.0, 0.0)
        mapped = mp_below[p, : z.pnos, :] * held
        right_ref[p] = mm(mapped, b_ref[jnp.clip(j, 0, z.orbitals - 1)])


def early_kernel(z, second, mp_ref, b_ref, out_ref):
    out_ref[...] = b_ref[0, :EXTRA, :128] + mp_ref[...] + second[0].astype(jnp.float32)


def local_kernel(z, first, second, c_ref, mp_ref, b_ref, left_ref, right_ref):
    owner, sub = lax.axis_index("orb"), lax.axis_index("sub")
    start = side_start(z, owner, sub, 0)
    base = owner * z.orbitals
    for p in range(z.pairs):
        left_ref[p] = mm(c_ref[p], b_ref[first[start + p] - base])
        j = second[start + p] - base
        local = jnp.where(j < z.orbitals, 1.0, 0.0)
        right_ref[p] = mm(
            mp_ref[p, : z.pnos, :] * local, b_ref[jnp.minimum(j, z.orbitals - 1)]
        )


def sums_kernel(z, first, second, ranks, occupied, mp_ref, left_ref, here_ref, down_ref, *refs):
    sums_ref, right_ref = refs[-2:]
    owner, sub = lax.axis_index("orb"), lax.axis_index("sub")
    start = side_start(z, owner, sub, 0)
    n = z.pnos
    for p in range(z.pairs):
        right = here_ref[p] + down_ref[p]
        right_ref[p] = right
        scale = scale_of(
            z, start + p, mp_ref[p, n : n + 1, :n], first, second, ranks, occupied
        )
        part = mm(left_ref[p], right, ((1,), (1,)))
        sums_ref[:, p * n : (p + 1) * n] = -part * scale


def unpack(z, pair, block, rows, slot, s_high, s_low, scale_ref, coupling_ref, lists):
    n = z.pnos
    for k in range(0, z.links, 2):
        two = [block(k * n // 2, n // 2), block((k + 1) * n // 2, n // 2)]
        for odd in range(2):
            rows[slot, k // 2, pl.ds(odd, n // 2, 2), :] = jnp.concatenate(
                [part[:, odd * n : (odd + 1) * n] for part in two], axis=1
            )
    s = jnp.concatenate([rows[slot, k] for k in range(z.links // 2)], axis=1)
    s_high[pair], s_low[pair] = split(s)
    extra = block(z.links * n // 2, EXTRA)
    scale_ref[pair] = scale_of(z, pair, extra[0:1, :n], *lists)
    coupling_ref[pair, 0:1, :] = jnp.concatenate(
        [extra[1 + k : 2 + k, :] for k in range(z.links // 2)], axis=1
    )


def coupled_of(z, index, pair, near, s, coupling, amps_high, amps_low, diag_high, diag_low):
    n = z.pnos
    for k in range(z.links):
        row = near[k, pair]
        block = slice(k * n, (k + 1) * n)
        diag_high[index, block, block] = amps_high[row]
        diag_low[index, block, block] = amps_low[row]
    return split(mm3(s, (diag_high[index], diag_low[index])) * coupling)


def final_kernel(z, first, second, ranks, near, occupied, *refs):
    start_count, pack_count = (2, 4) if small(z) else (1, 1)
    starts_in = refs[:start_count]
    pack_in = refs[start_count : start_count + pack_count]
    (c_in, c_other, mp_in, mp_other, mp_below, mp_below_other, left_in, left_other, left_below,
     left_below_other, right_in, right_other) = refs[start_count + pack_count :][:12]
    (amp_out, grad_out, starts, amp_ref, packs, s_high, s_low, scale_ref, coupling_ref, s_rows, c_ref, m_ref, rhs,
     grad, flat, amps, amps_high, amps_low, next_high, next_low, diag_high, diag_low, rows_high,
     rows_low, sems) = refs[start_count + pack_count + 12 :]
    owner, sub = lax.axis_index("orb"), lax.axis_index("sub")
    fit = lax.axis_index("fit")
    n, pairs, own = z.pnos, z.pairs, z.own
    half = z.paos // z.subs
    at = pl.ds(pl.multiple_of(sub * half, half), half)
    lists = (first, second, ranks, occupied)

    def quarters(ref, base=0):
        return [ref.at[pl.ds(base + i * pairs, pairs)] for i in range(4)]

    start_copies = started(starts_in, [starts.at[i] for i in range(start_count)], sems, 16)
    pack_copies = started(pack_in, [packs.at[i] for i in range(pack_count)], sems)
    small_copies = started(
        [c_in.at[:, :, at], c_other.at[:, :, at]]
        + [ref.at[:, pl.ds(0, n), at] for ref in (mp_in, mp_other, mp_below, mp_below_other)],
        [c_ref.at[pl.ds(0, pairs)], c_ref.at[pl.ds(pairs, pairs)]] + quarters(m_ref),
        sems, 4,
    )
    large_copies = started(
        [right_in, right_other, left_in, left_other, left_below, left_below_other],
        [rhs.at[pl.ds(0, pairs)], rhs.at[pl.ds(pairs, pairs)]] + quarters(rhs, own),
        sems, 10,
    )
    diag_high[...] = jnp.zeros_like(diag_high)
    diag_low[...] = jnp.zeros_like(diag_low)

    wait(start_copies)

    def begin(pair, value):
        amps[pair] = value
        amps_high[pair], amps_low[pair] = split(value)

    if small(z):
        for index, side in enumerate((sub, 1 - sub)):
            for who in range(z.owners):
                for p in range(pairs):
                    begin(
                        who * own + side * pairs + p,
                        starts[index, who, :, p * n : (p + 1) * n],
                    )
    else:
        @pl.loop(0, z.owners * z.subs)
        def _(device):
            for p in range(pairs):
                begin(device * pairs + p, starts[0, device, :, p * n : (p + 1) * n])

    wait(pack_copies)
    if small(z):
        for index in range(pack_count):
            side = sub if index < 2 else 1 - sub
            which = fit if index % 2 == 0 else 1 - fit
            for who in range(z.owners):
                unpack(
                    z, who * own + side * pairs + which,
                    lambda start, size: packs[index, who, start : start + size, :], s_rows,
                    index * z.owners + who, s_high, s_low, scale_ref, coupling_ref, lists,
                )
    else:
        @pl.loop(0, z.total)
        def _(pair):
            unpack(
                z, pair, lambda start, size: packs[0, pair, pl.ds(start, size), :], s_rows, 0,
                s_high, s_low, scale_ref, coupling_ref, lists,
            )

    def s_of(pair):
        return s_high[pair], s_low[pair]

    def swept(index, pair, high_amps, low_amps):
        s = s_of(pair)
        inner = coupled_of(
            z, index, pair, near, s, coupling_ref[pair, 0:1, :], high_amps, low_amps, diag_high,
            diag_low,
        )
        return amps[pair] + mm3(inner, s, ((1,), (1,))) * scale_ref[pair]

    if z.owners <= SMALL:
        group = diag_high.shape[0]
        for base in range(0, z.total, group):
            pair_list = range(base, min(base + group, z.total))
            inner = [
                coupled_of(
                    z, index, pair, near, s_of(pair), coupling_ref[pair, 0:1, :], amps_high,
                    amps_low, diag_high, diag_low,
                )
                for index, pair in enumerate(pair_list)
            ]
            for value, pair in zip(inner, pair_list):
                coupled = mm3(value, s_of(pair), ((1,), (1,)))
                next_high[pair], next_low[pair] = split(amps[pair] + coupled * scale_ref[pair])
    else:
        @pl.loop(0, z.total)
        def _(pair):
            next_high[pair], next_low[pair] = split(swept(0, pair, amps_high, amps_low))

    pair_list = [
        side_start(z, who, sub, side) + p
        for who in (owner, jnp.maximum(owner - 1, 0))
        for side in range(z.subs)
        for p in range(pairs)
    ]
    inner = [
        coupled_of(
            z, index, pair, near, s_of(pair), coupling_ref[pair, 0:1, :], next_high, next_low,
            diag_high, diag_low,
        )
        for index, pair in enumerate(pair_list)
    ]
    found = [
        amps[pair] + mm3(value, s_of(pair), ((1,), (1,))) * scale_ref[pair]
        for value, pair in zip(inner, pair_list)
    ]
    turned = [value.T for value in found]
    wait(small_copies)
    weights = [split(2.0 * a - b) for a, b in zip(found, turned)]
    weights_turned = [split(2.0 * b - a) for a, b in zip(found[:own], turned[:own])]
    terms = (
        [mm3(w, split(c_ref[i])) for i, w in enumerate(weights_turned)]
        + [mm3(w, split(m_ref[i])) for i, w in enumerate(weights)]
    )
    orbital_list = (
        [first[pair] - owner * z.orbitals for pair in pair_list[:own]]
        + [second[pair] - owner * z.orbitals for pair in pair_list]
    )
    for index in range(0, 3 * own, 2):
        for o in range(z.orbitals):
            block = jnp.concatenate(
                [
                    jnp.where(orbital_list[i] == o, terms[i], 0.0) for i in (index, index + 1)
                ]
            ).T
            place = (slice(o * half, (o + 1) * half), slice(index * n, (index + 2) * n))
            rows_high[place], rows_low[place] = split(block)

    for p in range(pairs):
        flat[p] = found[p]
        even = flat[p, pl.ds(0, n // 2, 2), :]
        odd = flat[p, pl.ds(1, n // 2, 2), :]
        lines = jnp.concatenate([even, odd], axis=1)
        for r in range(n // 2):
            amp_ref[p : p + 1, r * 2 * n : (r + 1) * 2 * n] = lines[r : r + 1, :]
    copies = started([amp_ref], [amp_out], sems, 18)

    wait(large_copies)
    step = 256
    rows = (rows_high[...], rows_low[...])
    for index, start in enumerate(range(0, z.fits, step)):
        factor = rhs[:, :, start : start + step].reshape(3 * own * n, step)
        grad[:, :, start : start + step] = mm3(rows, split(factor)).reshape(
            z.orbitals, half, step
        )
        window = pl.ds(start, step)
        copies += started(
            [grad.at[:, :, window]], [grad_out.at[:, :, window]], sems, 19 + index
        )
    wait(copies)


def gate(values, *after):
    return lax.optimization_barrier((tuple(values), after))[0]


def body(
    blocks,
    pno_coefficients,
    domain_map,
    pair_first,
    pair_second,
    pno_ranks,
    neighbours,
    couplings,
    intersections,
    pno_energy,
    occ_energy,
):
    z = Sizes(blocks, pno_coefficients, couplings)
    n, pairs, own, fits = z.pnos, z.pairs, z.own, z.fits
    half = z.paos // z.subs
    wide = z.links * n
    hbm = held_out
    bf16 = jnp.bfloat16
    more = 0 if z.owners <= SMALL else z.owners

    def scratch(*shape, kind=jnp.float32):
        return pltpu.VMEM(shape, kind)

    pack_shape = (z.owners if small(z) else pairs, z.links * n // 2 + EXTRA, 2 * n)
    (mp,) = call(
        functools.partial(mapped_kernel, z),
        [(pairs, n + EXTRA, z.paos)],
        [hbm] * 4,
        (pno_coefficients, domain_map, pno_energy, couplings),
        [
            scratch(*pno_coefficients.shape),
            pltpu.VMEM(domain_map.shape, jnp.int32),
            scratch(*pno_energy.shape),
            scratch(*couplings.shape),
            pltpu.SemaphoreType.DMA((4,)),
        ],
        limit=None,
    )
    mp_below = shifted(mp, "orb", 1)
    (pack,) = call(
        functools.partial(pack_kernel, z),
        [pack_shape],
        [hbm] * 2,
        (intersections, mp),
        [
            scratch(*intersections.shape),
            scratch(pairs, EXTRA, z.paos),
            pltpu.SemaphoreType.DMA((2,)),
        ],
        limit=None,
    )
    if small(z):
        packs = [lax.all_to_all(pack, "orb", 0, 0)]
    else:
        packs = [lax.all_gather(pack, ("orb", "sub"), axis=0, tiled=True)]
    (touched,) = call(
        functools.partial(early_kernel, z),
        [(EXTRA, 128)],
        [smem, vmem, vmem],
        (pair_second, mp[0, :EXTRA, :128], blocks),
        limit=8,
    )
    (right_below,) = call(
        functools.partial(below_kernel, z),
        [(pairs, n, fits)],
        [smem, vmem, vmem, vmem],
        (pair_second, gate((mp_below,), pack)[0], blocks, touched),
        limit=8,
    )
    down = shifted(right_below, "orb", -1)
    mp_late, coefficients, mp_below_late = gate((mp, pno_coefficients, mp_below), right_below)
    mp_below_other = swapped(mp_below_late, "sub")
    left, right_here = call(
        functools.partial(local_kernel, z),
        [(pairs, n, fits), (pairs, n, fits)],
        [smem, smem, vmem, vmem, vmem],
        (pair_first, pair_second, coefficients, mp_late, blocks),
        limit=8,
        cost=BRIEF,
    )
    mp_other = swapped(gate((mp,), right_here)[0], "sub")
    left_other = swapped(left, "sub")
    c_other = swapped(gate((coefficients,), right_here)[0], "sub")

    lists = (pair_first, pair_second, pno_ranks)
    (down,) = gate((down,), mp_other, left_other, c_other, mp_below_other)
    part, right = call(
        functools.partial(sums_kernel, z),
        [(n, pairs * n), (pairs, n, fits)],
        [smem] * 4 + [vmem] * 4,
        (*lists, occ_energy, mp, left, right_here, down),
        limit=8,
    )
    if small(z):
        packs.append(None)
        packs.append(swapped(gate(packs[:1], part)[0], "sub"))
        sums = part + swapped(part, "fit")
        packs[1] = swapped(gate(packs[:1], part)[0], "fit")
        start_amps = [
            lax.all_to_all(jnp.broadcast_to(sums[None], (z.owners, *sums.shape)), "orb", 0, 0)
        ]
        start_amps.append(swapped(start_amps[0], "sub"))
        packs.append(swapped(gate(packs[1:2], start_amps[0])[0], "sub"))
    else:
        sums = lax.psum(part, "fit")
        start_amps = [lax.all_gather(sums, ("orb", "sub"), axis=0, tiled=False)]

    (right_late,) = gate((right,), part)
    left_below = shifted(gate((left,), part)[0], "orb", 1)
    (left_late,) = gate((left_below,), start_amps[-1])
    right_other, left_below_other = [
        swapped(value, "sub") for value in (right_late, left_late)
    ]

    args = (
        *lists, neighbours.T, occ_energy, *start_amps, *packs,
        pno_coefficients, c_other, mp, mp_other, mp_below, mp_below_other,
        left, left_other, left_below, left_below_other, right, right_other,
    )
    square = (z.total, n, n)
    amplitudes, gradient = call(
        functools.partial(final_kernel, z),
        [(pairs, n * n), (z.orbitals, half, fits)],
        [smem] * 5 + [hbm] * (12 + len(start_amps) + len(packs)),
        args,
        [
            scratch(len(start_amps), *start_amps[0].shape),
            scratch(pairs, n * n),
            scratch(len(packs), *packs[0].shape),
            scratch(z.total, n, wide, kind=bf16),
            scratch(z.total, n, wide, kind=bf16),
            scratch(*square),
            scratch(z.total, EXTRA, wide),
            scratch(z.total if small(z) else 1, z.links // 2, n, 2 * n),
            scratch(own, n, half),
            scratch(2 * own, n, half),
            scratch(3 * own, n, fits),
            scratch(z.orbitals, half, fits),
            scratch(pairs, n, n),
            scratch(*square),
        ]
        + [scratch(*square, kind=bf16)] * 4
        + [scratch(2 * own, wide, wide, kind=bf16)] * 2
        + [scratch(z.orbitals * half, 3 * own * n, kind=bf16)] * 2
        + [pltpu.SemaphoreType.DMA((19 + -(-fits // 256),))],
        limit=44,
        out_specs=[hbm, hbm],
    )
    return (amplitudes, gradient)


def solution(mesh):
    in_specs = (
        P(("groups", "orb"), None, "fit"),
        P(("groups", "orb", "sub"), None, None),
        P(("groups", "orb", "sub"), None),
        P("groups"),
        P("groups"),
        P("groups"),
        P("groups", None),
        P(("groups", "orb", "sub"), None),
        P(("groups", "orb", "sub"), None, None),
        P(("groups", "orb", "sub"), None),
        P("groups"),
    )
    out_specs = (P(("groups", "orb", "sub"), None), P(("groups", "orb"), "sub", "fit"))
    return jax.shard_map(body, mesh=mesh, in_specs=in_specs, out_specs=out_specs, check_vma=False)
```

```python
import functools

import jax
import jax.numpy as jnp
from jax import lax
from jax.experimental import pallas as pl
from jax.experimental.pallas import tpu as pltpu
from jax.sharding import PartitionSpec as P

ITERS = 2
SMALL = 4
MIB = 1 << 20
EXTRA = 8

high = lax.Precision.HIGH
BRIEF = pl.CostEstimate(flops=1, bytes_accessed=1, transcendentals=0)
smem = pl.BlockSpec(memory_space=pltpu.SMEM)
vmem = pl.BlockSpec(memory_space=pltpu.VMEM)


def mm(a, b, contract=((1,), (0,))):
    return lax.dot_general(
        a, b, (contract, ((), ())), precision=high, preferred_element_type=jnp.float32
    )


def shifted(value, axis, steps):
    count = lax.axis_size(axis)
    initial, last = (max(0, -steps), min(count, count - steps))
    return lax.ppermute(value, axis, [(source, source + steps) for source in range(initial, last)])


def swapped(value, axis):
    return lax.ppermute(value, axis, [(0, 1), (1, 0)])


def f32(flag):
    return flag.astype(jnp.float32)


class Sizes:
    def __init__(self, blocks, pno_coefficients, couplings):
        self.orbitals, self.paos, self.fits = blocks.shape
        self.pairs, self.pnos = pno_coefficients.shape[:2]
        self.links = couplings.shape[1]
        self.subs = lax.axis_size("sub")
        self.owners = lax.axis_size("orb")
        self.fit_count = lax.axis_size("fit")
        self.own = self.pairs * self.subs
        self.total = self.own * self.owners


anywhere = pl.BlockSpec(memory_space=pl.ANY)
held_out = pl.BlockSpec(memory_space=pltpu.HBM)


def call(kernel, outs, ins, args, scratch=(), limit=16, out_specs=None, cost=None):
    return pl.pallas_call(
        kernel,
        out_shape=[jax.ShapeDtypeStruct(shape, jnp.float32) for shape in outs],
        in_specs=ins,
        out_specs=out_specs or [vmem] * len(outs),
        scratch_shapes=list(scratch),
        cost_estimate=cost,
        compiler_params=pltpu.CompilerParams(vmem_limit_bytes=limit and limit * MIB),
    )(*args)


def started(sources, targets, sems, base=0):
    copies = [
        pltpu.make_async_copy(source, target, sems.at[base + index])
        for index, (source, target) in enumerate(zip(sources, targets))
    ]
    for copy in copies:
        copy.start()
    return copies


def wait(copies):
    for copy in copies:
        copy.wait()


def side_start(z, owner, sub, side):
    return owner * z.own + (sub if side == 0 else 1 - sub) * z.pairs


def scale_of(z, pair, level, first, second, ranks, occupied):
    n = z.pnos
    row_ids = lax.broadcasted_iota(jnp.int32, (n, n), 0)
    column_ids = lax.broadcasted_iota(jnp.int32, (n, n), 1)
    level = level * jnp.ones((n, 1), jnp.float32)
    rank = ranks[pair]
    kept = f32((row_ids < rank) & (column_ids < rank))
    return kept / (level + level.T - (occupied[first[pair]] + occupied[second[pair]]))


def split(value):
    high_part = value.astype(jnp.bfloat16)
    return high_part, (value - high_part.astype(jnp.float32)).astype(jnp.bfloat16)


def mm3(a, b, contract=((1,), (0,))):
    def one(x, y):
        return lax.dot_general(x, y, (contract, ((), ())), preferred_element_type=jnp.float32)

    return one(a[0], b[0]) + (one(a[0], b[1]) + one(a[1], b[0]))


def small(z):
    return z.owners <= SMALL and z.pairs == z.fit_count == 2


def each_pair(z, action):
    if z.owners <= SMALL:
        for pair in range(z.total):
            action(pair)
    else:
        @pl.loop(0, z.total)
        def _(pair):
            action(pair)


def mapped_kernel(z, c_in, map_in, e_in, coupling_in, mp_ref, c_ref, map_ref, e_ref, coupling,
                  sems):
    n = z.pnos
    copies = started(
        [c_in, map_in, e_in, coupling_in], [c_ref, map_ref, e_ref, coupling], sems
    )
    wait(copies)
    rows = lax.broadcasted_iota(jnp.int32, (z.paos, z.paos), 0)
    lane_link = lax.broadcasted_iota(jnp.int32, (1, z.links * n), 1) // n
    for p in range(z.pairs):
        select = f32(map_ref[p : p + 1, :] == rows).astype(jnp.bfloat16)
        c_high, c_low = split(c_ref[p])
        mp_ref[p, :n, :] = lax.dot_general(
            c_high, select, (((1,), (1,)), ((), ())), preferred_element_type=jnp.float32
        ) + lax.dot_general(
            c_low, select, (((1,), (1,)), ((), ())), preferred_element_type=jnp.float32
        )
        mp_ref[p, n:, :] = jnp.zeros((EXTRA, z.paos), jnp.float32)
        mp_ref[p, n : n + 1, :n] = e_ref[p : p + 1, :]
        spread = jnp.zeros((1, z.links * n), jnp.float32)
        for k in range(z.links):
            spread = jnp.where(lane_link == k, coupling[p : p + 1, k : k + 1], spread)
        mp_ref[p, n + 1 : n + 2, :] = spread


def pack_kernel(z, s_in, mp_in, pack_ref, s_ref, mp_ref, sems):
    n = z.pnos
    line = 2 * n
    base = z.links * n // 2
    wait(started([s_in, mp_in.at[:, pl.ds(n, EXTRA), :]], [s_ref, mp_ref], sems))
    for slot in range(1 if small(z) else z.pairs):
        p = lax.axis_index("fit") if small(z) else slot
        for r in range(n // 2):
            lines = s_ref[p, :, r * line : (r + 1) * line]
            for k in range(z.links):
                row = k * n // 2 + r
                pack_ref[slot, row : row + 1, :] = lines[k : k + 1, :]
        pack_ref[slot, base:, :] = jnp.zeros((EXTRA, line), jnp.float32)
        pack_ref[slot, base : base + 1, :] = mp_ref[p, 0:1, :line]
        for k in range(z.links // 2):
            pack_ref[slot, base + 1 + k : base + 2 + k, :] = mp_ref[
                p, 1:2, k * line : (k + 1) * line
            ]
    if small(z):
        for copy in range(1, z.owners):
            pack_ref[copy] = pack_ref[0]


def below_kernel(z, second, mp_below, b_ref, touched, right_ref):
    owner, sub = lax.axis_index("orb"), lax.axis_index("sub")
    start = side_start(z, jnp.maximum(owner - 1, 0), sub, 0)
    for p in range(z.pairs):
        j = second[start + p] - owner * z.orbitals
        held = jnp.where(j >= 0, 1.0, 0.0)
        mapped = mp_below[p, : z.pnos, :] * held
        right_ref[p] = mm(mapped, b_ref[jnp.clip(j, 0, z.orbitals - 1)])


def early_kernel(z, second, mp_ref, b_ref, out_ref):
    out_ref[...] = b_ref[0, :EXTRA, :128] + mp_ref[...] + second[0].astype(jnp.float32)


def local_kernel(z, first, second, c_ref, mp_ref, b_ref, left_ref, right_ref):
    owner, sub = lax.axis_index("orb"), lax.axis_index("sub")
    start = side_start(z, owner, sub, 0)
    base = owner * z.orbitals
    for p in range(z.pairs):
        left_ref[p] = mm(c_ref[p], b_ref[first[start + p] - base])
        j = second[start + p] - base
        local = jnp.where(j < z.orbitals, 1.0, 0.0)
        right_ref[p] = mm(
            mp_ref[p, : z.pnos, :] * local, b_ref[jnp.minimum(j, z.orbitals - 1)]
        )


def sums_kernel(z, first, second, ranks, occupied, mp_ref, left_ref, here_ref, down_ref, *refs):
    sums_ref, right_ref = refs[-2:]
    owner, sub = lax.axis_index("orb"), lax.axis_index("sub")
    start = side_start(z, owner, sub, 0)
    n = z.pnos
    for p in range(z.pairs):
        right = here_ref[p] + down_ref[p]
        right_ref[p] = right
        scale = scale_of(
            z, start + p, mp_ref[p, n : n + 1, :n], first, second, ranks, occupied
        )
        part = mm(left_ref[p], right, ((1,), (1,)))
        sums_ref[:, p * n : (p + 1) * n] = -part * scale


def unpack(z, pair, block, rows, slot, s_high, s_low, scale_ref, coupling_ref, lists):
    n = z.pnos
    for k in range(0, z.links, 2):
        two = [block(k * n // 2, n // 2), block((k + 1) * n // 2, n // 2)]
        for odd in range(2):
            rows[slot, k // 2, pl.ds(odd, n // 2, 2), :] = jnp.concatenate(
                [part[:, odd * n : (odd + 1) * n] for part in two], axis=1
            )
    s = jnp.concatenate([rows[slot, k] for k in range(z.links // 2)], axis=1)
    s_high[pair], s_low[pair] = split(s)
    extra = block(z.links * n // 2, EXTRA)
    scale_ref[pair] = scale_of(z, pair, extra[0:1, :n], *lists)
    coupling_ref[pair, 0:1, :] = jnp.concatenate(
        [extra[1 + k : 2 + k, :] for k in range(z.links // 2)], axis=1
    )


def coupled_of(z, index, pair, near, s, coupling, amps_high, amps_low, diag_high, diag_low):
    n = z.pnos
    for k in range(z.links):
        row = near[k, pair]
        block = slice(k * n, (k + 1) * n)
        diag_high[index, block, block] = amps_high[row]
        diag_low[index, block, block] = amps_low[row]
    return split(mm3(s, (diag_high[index], diag_low[index])) * coupling)


def final_kernel(z, first, second, ranks, near, occupied, *refs):
    start_count, pack_count = (2, 4) if small(z) else (1, 1)
    starts_in = refs[:start_count]
    pack_in = refs[start_count : start_count + pack_count]
    (c_in, c_other, mp_in, mp_other, mp_below, mp_below_other, left_in, left_other, left_below,
     left_below_other, right_in, right_other) = refs[start_count + pack_count :][:12]
    (amp_out, grad_out, starts, amp_ref, packs, s_high, s_low, scale_ref, coupling_ref, s_rows, c_ref, m_ref, rhs,
     grad, flat, amps, amps_high, amps_low, next_high, next_low, diag_high, diag_low, rows_high,
     rows_low, sems) = refs[start_count + pack_count + 12 :]
    owner, sub = lax.axis_index("orb"), lax.axis_index("sub")
    fit = lax.axis_index("fit")
    n, pairs, own = z.pnos, z.pairs, z.own
    half = z.paos // z.subs
    at = pl.ds(pl.multiple_of(sub * half, half), half)
    lists = (first, second, ranks, occupied)

    def quarters(ref, base=0):
        return [ref.at[pl.ds(base + i * pairs, pairs)] for i in range(4)]

    start_copies = started(starts_in, [starts.at[i] for i in range(start_count)], sems, 16)
    pack_copies = started(pack_in, [packs.at[i] for i in range(pack_count)], sems)
    small_copies = started(
        [c_in.at[:, :, at], c_other.at[:, :, at]]
        + [ref.at[:, pl.ds(0, n), at] for ref in (mp_in, mp_other, mp_below, mp_below_other)],
        [c_ref.at[pl.ds(0, pairs)], c_ref.at[pl.ds(pairs, pairs)]] + quarters(m_ref),
        sems, 4,
    )
    large_copies = started(
        [right_in, right_other, left_in, left_other, left_below, left_below_other],
        [rhs.at[pl.ds(0, pairs)], rhs.at[pl.ds(pairs, pairs)]] + quarters(rhs, own),
        sems, 10,
    )
    diag_high[...] = jnp.zeros_like(diag_high)
    diag_low[...] = jnp.zeros_like(diag_low)

    wait(start_copies)

    def begin(pair, value):
        amps[pair] = value
        amps_high[pair], amps_low[pair] = split(value)

    if small(z):
        for index, side in enumerate((sub, 1 - sub)):
            for who in range(z.owners):
                for p in range(pairs):
                    begin(
                        who * own + side * pairs + p,
                        starts[index, who, :, p * n : (p + 1) * n],
                    )
    else:
        @pl.loop(0, z.owners * z.subs)
        def _(device):
            for p in range(pairs):
                begin(device * pairs + p, starts[0, device, :, p * n : (p + 1) * n])

    wait(pack_copies)
    if small(z):
        for index in range(pack_count):
            side = sub if index < 2 else 1 - sub
            which = fit if index % 2 == 0 else 1 - fit
            for who in range(z.owners):
                unpack(
                    z, who * own + side * pairs + which,
                    lambda start, size: packs[index, who, start : start + size, :], s_rows,
                    index * z.owners + who, s_high, s_low, scale_ref, coupling_ref, lists,
                )
    else:
        @pl.loop(0, z.total)
        def _(pair):
            unpack(
                z, pair, lambda start, size: packs[0, pair, pl.ds(start, size), :], s_rows, 0,
                s_high, s_low, scale_ref, coupling_ref, lists,
            )

    def s_of(pair):
        return s_high[pair], s_low[pair]

    def swept(index, pair, high_amps, low_amps):
        s = s_of(pair)
        inner = coupled_of(
            z, index, pair, near, s, coupling_ref[pair, 0:1, :], high_amps, low_amps, diag_high,
            diag_low,
        )
        return amps[pair] + mm3(inner, s, ((1,), (1,))) * scale_ref[pair]

    if z.owners <= SMALL:
        group = diag_high.shape[0]
        for base in range(0, z.total, group):
            pair_list = range(base, min(base + group, z.total))
            inner = [
                coupled_of(
                    z, index, pair, near, s_of(pair), coupling_ref[pair, 0:1, :], amps_high,
                    amps_low, diag_high, diag_low,
                )
                for index, pair in enumerate(pair_list)
            ]
            for value, pair in zip(inner, pair_list):
                coupled = mm3(value, s_of(pair), ((1,), (1,)))
                next_high[pair], next_low[pair] = split(amps[pair] + coupled * scale_ref[pair])
    else:
        @pl.loop(0, z.total)
        def _(pair):
            next_high[pair], next_low[pair] = split(swept(0, pair, amps_high, amps_low))

    pair_list = [
        side_start(z, who, sub, side) + p
        for who in (owner, jnp.maximum(owner - 1, 0))
        for side in range(z.subs)
        for p in range(pairs)
    ]
    inner = [
        coupled_of(
            z, index, pair, near, s_of(pair), coupling_ref[pair, 0:1, :], next_high, next_low,
            diag_high, diag_low,
        )
        for index, pair in enumerate(pair_list)
    ]
    found = [
        amps[pair] + mm3(value, s_of(pair), ((1,), (1,))) * scale_ref[pair]
        for value, pair in zip(inner, pair_list)
    ]
    turned = [value.T for value in found]
    wait(small_copies)
    weights = [split(2.0 * a - b) for a, b in zip(found, turned)]
    weights_turned = [split(2.0 * b - a) for a, b in zip(found[:own], turned[:own])]
    terms = (
        [mm3(w, split(c_ref[i])) for i, w in enumerate(weights_turned)]
        + [mm3(w, split(m_ref[i])) for i, w in enumerate(weights)]
    )
    orbital_list = (
        [first[pair] - owner * z.orbitals for pair in pair_list[:own]]
        + [second[pair] - owner * z.orbitals for pair in pair_list]
    )
    for index in range(0, 3 * own, 2):
        for o in range(z.orbitals):
            block = jnp.concatenate(
                [
                    jnp.where(orbital_list[i] == o, terms[i], 0.0) for i in (index, index + 1)
                ]
            ).T
            place = (slice(o * half, (o + 1) * half), slice(index * n, (index + 2) * n))
            rows_high[place], rows_low[place] = split(block)

    for p in range(pairs):
        flat[p] = found[p]
        even = flat[p, pl.ds(0, n // 2, 2), :]
        odd = flat[p, pl.ds(1, n // 2, 2), :]
        lines = jnp.concatenate([even, odd], axis=1)
        for r in range(n // 2):
            amp_ref[p : p + 1, r * 2 * n : (r + 1) * 2 * n] = lines[r : r + 1, :]
    copies = started([amp_ref], [amp_out], sems, 18)

    wait(large_copies)
    step = 256
    rows = (rows_high[...], rows_low[...])
    for index, start in enumerate(range(0, z.fits, step)):
        factor = rhs[:, :, start : start + step].reshape(3 * own * n, step)
        grad[:, :, start : start + step] = mm3(rows, split(factor)).reshape(
            z.orbitals, half, step
        )
        window = pl.ds(start, step)
        copies += started(
            [grad.at[:, :, window]], [grad_out.at[:, :, window]], sems, 19 + index
        )
    wait(copies)


def gate(values, *after):
    return lax.optimization_barrier((tuple(values), after))[0]


def body(
    blocks,
    pno_coefficients,
    domain_map,
    pair_first,
    pair_second,
    pno_ranks,
    neighbours,
    couplings,
    intersections,
    pno_energy,
    occ_energy,
):
    z = Sizes(blocks, pno_coefficients, couplings)
    n, pairs, own, fits = z.pnos, z.pairs, z.own, z.fits
    half = z.paos // z.subs
    wide = z.links * n
    hbm = held_out
    bf16 = jnp.bfloat16
    more = 0 if z.owners <= SMALL else z.owners

    def scratch(*shape, kind=jnp.float32):
        return pltpu.VMEM(shape, kind)

    pack_shape = (z.owners if small(z) else pairs, z.links * n // 2 + EXTRA, 2 * n)
    (mp,) = call(
        functools.partial(mapped_kernel, z),
        [(pairs, n + EXTRA, z.paos)],
        [hbm] * 4,
        (pno_coefficients, domain_map, pno_energy, couplings),
        [
            scratch(*pno_coefficients.shape),
            pltpu.VMEM(domain_map.shape, jnp.int32),
            scratch(*pno_energy.shape),
            scratch(*couplings.shape),
            pltpu.SemaphoreType.DMA((4,)),
        ],
        limit=None,
    )
    mp_below = shifted(mp, "orb", 1)
    (pack,) = call(
        functools.partial(pack_kernel, z),
        [pack_shape],
        [hbm] * 2,
        (intersections, mp),
        [
            scratch(*intersections.shape),
            scratch(pairs, EXTRA, z.paos),
            pltpu.SemaphoreType.DMA((2,)),
        ],
        limit=None,
    )
    if small(z):
        packs = [lax.all_to_all(pack, "orb", 0, 0)]
    else:
        packs = [lax.all_gather(pack, ("orb", "sub"), axis=0, tiled=True)]
    (touched,) = call(
        functools.partial(early_kernel, z),
        [(EXTRA, 128)],
        [smem, vmem, vmem],
        (pair_second, mp[0, :EXTRA, :128], blocks),
        limit=8,
    )
    (right_below,) = call(
        functools.partial(below_kernel, z),
        [(pairs, n, fits)],
        [smem, vmem, vmem, vmem],
        (pair_second, gate((mp_below,), pack)[0], blocks, touched),
        limit=8,
    )
    down = shifted(right_below, "orb", -1)
    mp_late, coefficients, mp_below_late = gate((mp, pno_coefficients, mp_below), right_below)
    mp_below_other = swapped(mp_below_late, "sub")
    left, right_here = call(
        functools.partial(local_kernel, z),
        [(pairs, n, fits), (pairs, n, fits)],
        [smem, smem, vmem, vmem, vmem],
        (pair_first, pair_second, coefficients, mp_late, blocks),
        limit=8,
        cost=BRIEF,
    )
    mp_other = swapped(gate((mp,), right_here)[0], "sub")
    left_other = swapped(left, "sub")
    c_other = swapped(gate((coefficients,), right_here)[0], "sub")

    lists = (pair_first, pair_second, pno_ranks)
    (down,) = gate((down,), mp_other, left_other, c_other, mp_below_other)
    part, right = call(
        functools.partial(sums_kernel, z),
        [(n, pairs * n), (pairs, n, fits)],
        [smem] * 4 + [vmem] * 4,
        (*lists, occ_energy, mp, left, right_here, down),
        limit=8,
    )
    if small(z):
        packs.append(None)
        packs.append(swapped(gate(packs[:1], part)[0], "sub"))
        sums = part + swapped(part, "fit")
        packs[1] = swapped(gate(packs[:1], part)[0], "fit")
        start_amps = [
            lax.all_to_all(jnp.broadcast_to(sums[None], (z.owners, *sums.shape)), "orb", 0, 0)
        ]
        start_amps.append(swapped(start_amps[0], "sub"))
        packs.append(swapped(gate(packs[1:2], start_amps[0])[0], "sub"))
    else:
        sums = lax.psum(part, "fit")
        start_amps = [lax.all_gather(sums, ("orb", "sub"), axis=0, tiled=False)]

    (right_late,) = gate((right,), part)
    left_below = shifted(gate((left,), part)[0], "orb", 1)
    (left_late,) = gate((left_below,), start_amps[0])
    right_other, left_below_other = [
        swapped(value, "sub") for value in (right_late, left_late)
    ]

    args = (
        *lists, neighbours.T, occ_energy, *start_amps, *packs,
        pno_coefficients, c_other, mp, mp_other, mp_below, mp_below_other,
        left, left_other, left_below, left_below_other, right, right_other,
    )
    square = (z.total, n, n)
    amplitudes, gradient = call(
        functools.partial(final_kernel, z),
        [(pairs, n * n), (z.orbitals, half, fits)],
        [smem] * 5 + [hbm] * (12 + len(start_amps) + len(packs)),
        args,
        [
            scratch(len(start_amps), *start_amps[0].shape),
            scratch(pairs, n * n),
            scratch(len(packs), *packs[0].shape),
            scratch(z.total, n, wide, kind=bf16),
            scratch(z.total, n, wide, kind=bf16),
            scratch(*square),
            scratch(z.total, EXTRA, wide),
            scratch(z.total if small(z) else 1, z.links // 2, n, 2 * n),
            scratch(own, n, half),
            scratch(2 * own, n, half),
            scratch(3 * own, n, fits),
            scratch(z.orbitals, half, fits),
            scratch(pairs, n, n),
            scratch(*square),
        ]
        + [scratch(*square, kind=bf16)] * 4
        + [scratch(2 * own, wide, wide, kind=bf16)] * 2
        + [scratch(z.orbitals * half, 3 * own * n, kind=bf16)] * 2
        + [pltpu.SemaphoreType.DMA((19 + -(-fits // 256),))],
        limit=44,
        out_specs=[hbm, hbm],
    )
    return (amplitudes, gradient)


def solution(mesh):
    in_specs = (
        P(("groups", "orb"), None, "fit"),
        P(("groups", "orb", "sub"), None, None),
        P(("groups", "orb", "sub"), None),
        P("groups"),
        P("groups"),
        P("groups"),
        P("groups", None),
        P(("groups", "orb", "sub"), None),
        P(("groups", "orb", "sub"), None, None),
        P(("groups", "orb", "sub"), None),
        P("groups"),
    )
    out_specs = (P(("groups", "orb", "sub"), None), P(("groups", "orb"), "sub", "fit"))
    return jax.shard_map(body, mesh=mesh, in_specs=in_specs, out_specs=out_specs, check_vma=False)
```

```python
import functools

import jax
import jax.numpy as jnp
from jax import lax
from jax.experimental import pallas as pl
from jax.experimental.pallas import tpu as pltpu
from jax.sharding import PartitionSpec as P

ITERS = 2
SMALL = 4
MIB = 1 << 20
EXTRA = 8

high = lax.Precision.HIGH
BRIEF = pl.CostEstimate(flops=1, bytes_accessed=1, transcendentals=0)
smem = pl.BlockSpec(memory_space=pltpu.SMEM)
vmem = pl.BlockSpec(memory_space=pltpu.VMEM)


def mm(a, b, contract=((1,), (0,))):
    return lax.dot_general(
        a, b, (contract, ((), ())), precision=high, preferred_element_type=jnp.float32
    )


def shifted(value, axis, steps):
    count = lax.axis_size(axis)
    initial, last = (max(0, -steps), min(count, count - steps))
    return lax.ppermute(value, axis, [(source, source + steps) for source in range(initial, last)])


def swapped(value, axis):
    return lax.ppermute(value, axis, [(0, 1), (1, 0)])


def f32(flag):
    return flag.astype(jnp.float32)


class Sizes:
    def __init__(self, blocks, pno_coefficients, couplings):
        self.orbitals, self.paos, self.fits = blocks.shape
        self.pairs, self.pnos = pno_coefficients.shape[:2]
        self.links = couplings.shape[1]
        self.subs = lax.axis_size("sub")
        self.owners = lax.axis_size("orb")
        self.fit_count = lax.axis_size("fit")
        self.own = self.pairs * self.subs
        self.total = self.own * self.owners


anywhere = pl.BlockSpec(memory_space=pl.ANY)
held_out = pl.BlockSpec(memory_space=pltpu.HBM)


def call(kernel, outs, ins, args, scratch=(), limit=16, out_specs=None, cost=None):
    return pl.pallas_call(
        kernel,
        out_shape=[jax.ShapeDtypeStruct(shape, jnp.float32) for shape in outs],
        in_specs=ins,
        out_specs=out_specs or [vmem] * len(outs),
        scratch_shapes=list(scratch),
        cost_estimate=cost,
        compiler_params=pltpu.CompilerParams(vmem_limit_bytes=limit and limit * MIB),
    )(*args)


def started(sources, targets, sems, base=0):
    copies = [
        pltpu.make_async_copy(source, target, sems.at[base + index])
        for index, (source, target) in enumerate(zip(sources, targets))
    ]
    for copy in copies:
        copy.start()
    return copies


def wait(copies):
    for copy in copies:
        copy.wait()


def side_start(z, owner, sub, side):
    return owner * z.own + (sub if side == 0 else 1 - sub) * z.pairs


def scale_of(z, pair, level, first, second, ranks, occupied):
    n = z.pnos
    row_ids = lax.broadcasted_iota(jnp.int32, (n, n), 0)
    column_ids = lax.broadcasted_iota(jnp.int32, (n, n), 1)
    level = level * jnp.ones((n, 1), jnp.float32)
    rank = ranks[pair]
    kept = f32((row_ids < rank) & (column_ids < rank))
    return kept / (level + level.T - (occupied[first[pair]] + occupied[second[pair]]))


def split(value):
    high_part = value.astype(jnp.bfloat16)
    return high_part, (value - high_part.astype(jnp.float32)).astype(jnp.bfloat16)


def mm3(a, b, contract=((1,), (0,))):
    def one(x, y):
        return lax.dot_general(x, y, (contract, ((), ())), preferred_element_type=jnp.float32)

    return one(a[0], b[0]) + (one(a[0], b[1]) + one(a[1], b[0]))


def small(z):
    return z.owners <= SMALL and z.pairs == z.fit_count == 2


def each_pair(z, action):
    if z.owners <= SMALL:
        for pair in range(z.total):
            action(pair)
    else:
        @pl.loop(0, z.total)
        def _(pair):
            action(pair)


def mapped_kernel(z, c_in, map_in, e_in, coupling_in, mp_ref, c_ref, map_ref, e_ref, coupling,
                  sems):
    n = z.pnos
    copies = started(
        [c_in, map_in, e_in, coupling_in], [c_ref, map_ref, e_ref, coupling], sems
    )
    wait(copies)
    rows = lax.broadcasted_iota(jnp.int32, (z.paos, z.paos), 0)
    lane_link = lax.broadcasted_iota(jnp.int32, (1, z.links * n), 1) // n
    for p in range(z.pairs):
        select = f32(map_ref[p : p + 1, :] == rows).astype(jnp.bfloat16)
        c_high, c_low = split(c_ref[p])
        mp_ref[p, :n, :] = lax.dot_general(
            c_high, select, (((1,), (1,)), ((), ())), preferred_element_type=jnp.float32
        ) + lax.dot_general(
            c_low, select, (((1,), (1,)), ((), ())), preferred_element_type=jnp.float32
        )
        mp_ref[p, n:, :] = jnp.zeros((EXTRA, z.paos), jnp.float32)
        mp_ref[p, n : n + 1, :n] = e_ref[p : p + 1, :]
        spread = jnp.zeros((1, z.links * n), jnp.float32)
        for k in range(z.links):
            spread = jnp.where(lane_link == k, coupling[p : p + 1, k : k + 1], spread)
        mp_ref[p, n + 1 : n + 2, :] = spread


def pack_kernel(z, s_in, mp_in, pack_ref, s_ref, mp_ref, sems):
    n = z.pnos
    line = 2 * n
    base = z.links * n // 2
    wait(started([s_in, mp_in.at[:, pl.ds(n, EXTRA), :]], [s_ref, mp_ref], sems))
    for slot in range(1 if small(z) else z.pairs):
        p = lax.axis_index("fit") if small(z) else slot
        for r in range(n // 2):
            lines = s_ref[p, :, r * line : (r + 1) * line]
            for k in range(z.links):
                row = k * n // 2 + r
                pack_ref[slot, row : row + 1, :] = lines[k : k + 1, :]
        pack_ref[slot, base:, :] = jnp.zeros((EXTRA, line), jnp.float32)
        pack_ref[slot, base : base + 1, :] = mp_ref[p, 0:1, :line]
        for k in range(z.links // 2):
            pack_ref[slot, base + 1 + k : base + 2 + k, :] = mp_ref[
                p, 1:2, k * line : (k + 1) * line
            ]
    if small(z):
        for copy in range(1, z.owners):
            pack_ref[copy] = pack_ref[0]


def below_kernel(z, second, mp_below, b_ref, touched, right_ref):
    owner, sub = lax.axis_index("orb"), lax.axis_index("sub")
    start = side_start(z, jnp.maximum(owner - 1, 0), sub, 0)
    for p in range(z.pairs):
        j = second[start + p] - owner * z.orbitals
        held = jnp.where(j >= 0, 1.0, 0.0)
        mapped = mp_below[p, : z.pnos, :] * held
        right_ref[p] = mm(mapped, b_ref[jnp.clip(j, 0, z.orbitals - 1)])


def early_kernel(z, second, mp_ref, b_ref, out_ref):
    out_ref[...] = b_ref[0, :EXTRA, :128] + mp_ref[...] + second[0].astype(jnp.float32)


def local_kernel(z, first, second, c_ref, mp_ref, b_ref, left_ref, right_ref):
    owner, sub = lax.axis_index("orb"), lax.axis_index("sub")
    start = side_start(z, owner, sub, 0)
    base = owner * z.orbitals
    for p in range(z.pairs):
        left_ref[p] = mm(c_ref[p], b_ref[first[start + p] - base])
        j = second[start + p] - base
        local = jnp.where(j < z.orbitals, 1.0, 0.0)
        right_ref[p] = mm(
            mp_ref[p, : z.pnos, :] * local, b_ref[jnp.minimum(j, z.orbitals - 1)]
        )


def sums_kernel(z, first, second, ranks, occupied, mp_ref, left_ref, here_ref, down_ref, *refs):
    sums_ref, right_ref = refs[-2:]
    owner, sub = lax.axis_index("orb"), lax.axis_index("sub")
    start = side_start(z, owner, sub, 0)
    n = z.pnos
    for p in range(z.pairs):
        right = here_ref[p] + down_ref[p]
        right_ref[p] = right
        scale = scale_of(
            z, start + p, mp_ref[p, n : n + 1, :n], first, second, ranks, occupied
        )
        part = mm(left_ref[p], right, ((1,), (1,)))
        sums_ref[:, p * n : (p + 1) * n] = -part * scale


def unpack(z, pair, block, rows, slot, s_high, s_low, scale_ref, coupling_ref, lists):
    n = z.pnos
    for k in range(0, z.links, 2):
        two = [block(k * n // 2, n // 2), block((k + 1) * n // 2, n // 2)]
        for odd in range(2):
            rows[slot, k // 2, pl.ds(odd, n // 2, 2), :] = jnp.concatenate(
                [part[:, odd * n : (odd + 1) * n] for part in two], axis=1
            )
    s = jnp.concatenate([rows[slot, k] for k in range(z.links // 2)], axis=1)
    s_high[pair], s_low[pair] = split(s)
    extra = block(z.links * n // 2, EXTRA)
    scale_ref[pair] = scale_of(z, pair, extra[0:1, :n], *lists)
    coupling_ref[pair, 0:1, :] = jnp.concatenate(
        [extra[1 + k : 2 + k, :] for k in range(z.links // 2)], axis=1
    )


def coupled_of(z, pair, near, s, coupling, amps_high, amps_low):
    n = z.pnos
    parts = []
    for k in range(z.links):
        row = near[k, pair]
        lanes = slice(k * n, (k + 1) * n)
        parts.append(mm3((s[0][:, lanes], s[1][:, lanes]), (amps_high[row], amps_low[row])))
    return split(jnp.concatenate(parts, axis=1) * coupling)


def final_kernel(z, first, second, ranks, near, occupied, *refs):
    start_count, pack_count = (2, 4) if small(z) else (1, 1)
    starts_in = refs[:start_count]
    pack_in = refs[start_count : start_count + pack_count]
    (c_in, c_other, mp_in, mp_other, mp_below, mp_below_other, left_in, left_other, left_below,
     left_below_other, right_in, right_other) = refs[start_count + pack_count :][:12]
    (amp_out, grad_out, starts, amp_ref, packs, s_high, s_low, scale_ref, coupling_ref, s_rows, c_ref, m_ref, rhs,
     grad, flat, amps, amps_high, amps_low, next_high, next_low, rows_high, rows_low, sems) = refs[start_count + pack_count + 12 :]
    owner, sub = lax.axis_index("orb"), lax.axis_index("sub")
    fit = lax.axis_index("fit")
    n, pairs, own = z.pnos, z.pairs, z.own
    half = z.paos // z.subs
    at = pl.ds(pl.multiple_of(sub * half, half), half)
    lists = (first, second, ranks, occupied)

    def quarters(ref, base=0):
        return [ref.at[pl.ds(base + i * pairs, pairs)] for i in range(4)]

    start_copies = started(starts_in, [starts.at[i] for i in range(start_count)], sems, 16)
    pack_copies = started(pack_in, [packs.at[i] for i in range(pack_count)], sems)
    small_copies = started(
        [c_in.at[:, :, at], c_other.at[:, :, at]]
        + [ref.at[:, pl.ds(0, n), at] for ref in (mp_in, mp_other, mp_below, mp_below_other)],
        [c_ref.at[pl.ds(0, pairs)], c_ref.at[pl.ds(pairs, pairs)]] + quarters(m_ref),
        sems, 4,
    )
    large_copies = started(
        [right_in, right_other, left_in, left_other, left_below, left_below_other],
        [rhs.at[pl.ds(0, pairs)], rhs.at[pl.ds(pairs, pairs)]] + quarters(rhs, own),
        sems, 10,
    )
    wait(start_copies)

    def begin(pair, value):
        amps[pair] = value
        amps_high[pair], amps_low[pair] = split(value)

    if small(z):
        for index, side in enumerate((sub, 1 - sub)):
            for who in range(z.owners):
                for p in range(pairs):
                    begin(
                        who * own + side * pairs + p,
                        starts[index, who, :, p * n : (p + 1) * n],
                    )
    else:
        @pl.loop(0, z.owners * z.subs)
        def _(device):
            for p in range(pairs):
                begin(device * pairs + p, starts[0, device, :, p * n : (p + 1) * n])

    wait(pack_copies)
    if small(z):
        for index in range(pack_count):
            side = sub if index < 2 else 1 - sub
            which = fit if index % 2 == 0 else 1 - fit
            for who in range(z.owners):
                unpack(
                    z, who * own + side * pairs + which,
                    lambda start, size: packs[index, who, start : start + size, :], s_rows,
                    index * z.owners + who, s_high, s_low, scale_ref, coupling_ref, lists,
                )
    else:
        @pl.loop(0, z.total)
        def _(pair):
            unpack(
                z, pair, lambda start, size: packs[0, pair, pl.ds(start, size), :], s_rows, 0,
                s_high, s_low, scale_ref, coupling_ref, lists,
            )

    def s_of(pair):
        return s_high[pair], s_low[pair]

    def swept(pair, high_amps, low_amps):
        s = s_of(pair)
        inner = coupled_of(
            z, pair, near, s, coupling_ref[pair, 0:1, :], high_amps, low_amps
        )
        return amps[pair] + mm3(inner, s, ((1,), (1,))) * scale_ref[pair]

    if z.owners <= SMALL:
        group = 2 * own
        for base in range(0, z.total, group):
            pair_list = range(base, min(base + group, z.total))
            inner = [
                coupled_of(
                    z, pair, near, s_of(pair), coupling_ref[pair, 0:1, :], amps_high, amps_low
                )
                for pair in pair_list
            ]
            for value, pair in zip(inner, pair_list):
                coupled = mm3(value, s_of(pair), ((1,), (1,)))
                next_high[pair], next_low[pair] = split(amps[pair] + coupled * scale_ref[pair])
    else:
        @pl.loop(0, z.total)
        def _(pair):
            next_high[pair], next_low[pair] = split(swept(pair, amps_high, amps_low))

    pair_list = [
        side_start(z, who, sub, side) + p
        for who in (owner, jnp.maximum(owner - 1, 0))
        for side in range(z.subs)
        for p in range(pairs)
    ]
    inner = [
        coupled_of(z, pair, near, s_of(pair), coupling_ref[pair, 0:1, :], next_high, next_low)
        for pair in pair_list
    ]
    found = [
        amps[pair] + mm3(value, s_of(pair), ((1,), (1,))) * scale_ref[pair]
        for value, pair in zip(inner, pair_list)
    ]
    turned = [value.T for value in found]
    wait(small_copies)
    weights = [split(2.0 * a - b) for a, b in zip(found, turned)]
    weights_turned = [split(2.0 * b - a) for a, b in zip(found[:own], turned[:own])]
    terms = (
        [mm3(w, split(c_ref[i])) for i, w in enumerate(weights_turned)]
        + [mm3(w, split(m_ref[i])) for i, w in enumerate(weights)]
    )
    orbital_list = (
        [first[pair] - owner * z.orbitals for pair in pair_list[:own]]
        + [second[pair] - owner * z.orbitals for pair in pair_list]
    )
    for index in range(0, 3 * own, 2):
        for o in range(z.orbitals):
            block = jnp.concatenate(
                [
                    jnp.where(orbital_list[i] == o, terms[i], 0.0) for i in (index, index + 1)
                ]
            ).T
            place = (slice(o * half, (o + 1) * half), slice(index * n, (index + 2) * n))
            rows_high[place], rows_low[place] = split(block)

    for p in range(pairs):
        flat[p] = found[p]
        even = flat[p, pl.ds(0, n // 2, 2), :]
        odd = flat[p, pl.ds(1, n // 2, 2), :]
        lines = jnp.concatenate([even, odd], axis=1)
        for r in range(n // 2):
            amp_ref[p : p + 1, r * 2 * n : (r + 1) * 2 * n] = lines[r : r + 1, :]
    copies = started([amp_ref], [amp_out], sems, 18)

    wait(large_copies)
    step = 256
    rows = (rows_high[...], rows_low[...])
    for index, start in enumerate(range(0, z.fits, step)):
        factor = rhs[:, :, start : start + step].reshape(3 * own * n, step)
        grad[:, :, start : start + step] = mm3(rows, split(factor)).reshape(
            z.orbitals, half, step
        )
        window = pl.ds(start, step)
        copies += started(
            [grad.at[:, :, window]], [grad_out.at[:, :, window]], sems, 19 + index
        )
    wait(copies)


def gate(values, *after):
    return lax.optimization_barrier((tuple(values), after))[0]


def body(
    blocks,
    pno_coefficients,
    domain_map,
    pair_first,
    pair_second,
    pno_ranks,
    neighbours,
    couplings,
    intersections,
    pno_energy,
    occ_energy,
):
    z = Sizes(blocks, pno_coefficients, couplings)
    n, pairs, own, fits = z.pnos, z.pairs, z.own, z.fits
    half = z.paos // z.subs
    wide = z.links * n
    hbm = held_out
    bf16 = jnp.bfloat16
    more = 0 if z.owners <= SMALL else z.owners

    def scratch(*shape, kind=jnp.float32):
        return pltpu.VMEM(shape, kind)

    pack_shape = (z.owners if small(z) else pairs, z.links * n // 2 + EXTRA, 2 * n)
    (mp,) = call(
        functools.partial(mapped_kernel, z),
        [(pairs, n + EXTRA, z.paos)],
        [hbm] * 4,
        (pno_coefficients, domain_map, pno_energy, couplings),
        [
            scratch(*pno_coefficients.shape),
            pltpu.VMEM(domain_map.shape, jnp.int32),
            scratch(*pno_energy.shape),
            scratch(*couplings.shape),
            pltpu.SemaphoreType.DMA((4,)),
        ],
        limit=None,
    )
    mp_below = shifted(mp, "orb", 1)
    (pack,) = call(
        functools.partial(pack_kernel, z),
        [pack_shape],
        [hbm] * 2,
        (intersections, mp),
        [
            scratch(*intersections.shape),
            scratch(pairs, EXTRA, z.paos),
            pltpu.SemaphoreType.DMA((2,)),
        ],
        limit=None,
    )
    if small(z):
        packs = [lax.all_to_all(pack, "orb", 0, 0)]
    else:
        packs = [lax.all_gather(pack, ("orb", "sub"), axis=0, tiled=True)]
    (touched,) = call(
        functools.partial(early_kernel, z),
        [(EXTRA, 128)],
        [smem, vmem, vmem],
        (pair_second, mp[0, :EXTRA, :128], blocks),
        limit=8,
    )
    (right_below,) = call(
        functools.partial(below_kernel, z),
        [(pairs, n, fits)],
        [smem, vmem, vmem, vmem],
        (pair_second, gate((mp_below,), pack)[0], blocks, touched),
        limit=8,
    )
    down = shifted(right_below, "orb", -1)
    mp_late, coefficients, mp_below_late = gate((mp, pno_coefficients, mp_below), right_below)
    mp_below_other = swapped(mp_below_late, "sub")
    left, right_here = call(
        functools.partial(local_kernel, z),
        [(pairs, n, fits), (pairs, n, fits)],
        [smem, smem, vmem, vmem, vmem],
        (pair_first, pair_second, coefficients, mp_late, blocks),
        limit=8,
        cost=BRIEF,
    )
    mp_other = swapped(gate((mp,), right_here)[0], "sub")
    left_other = swapped(left, "sub")
    c_other = swapped(gate((coefficients,), right_here)[0], "sub")

    lists = (pair_first, pair_second, pno_ranks)
    (down,) = gate((down,), mp_other, left_other, c_other, mp_below_other)
    part, right = call(
        functools.partial(sums_kernel, z),
        [(n, pairs * n), (pairs, n, fits)],
        [smem] * 4 + [vmem] * 4,
        (*lists, occ_energy, mp, left, right_here, down),
        limit=8,
    )
    if small(z):
        packs.append(None)
        packs.append(swapped(gate(packs[:1], part)[0], "sub"))
        sums = part + swapped(part, "fit")
        packs[1] = swapped(gate(packs[:1], part)[0], "fit")
        start_amps = [
            lax.all_to_all(jnp.broadcast_to(sums[None], (z.owners, *sums.shape)), "orb", 0, 0)
        ]
        start_amps.append(swapped(start_amps[0], "sub"))
        packs.append(swapped(gate(packs[1:2], start_amps[0])[0], "sub"))
    else:
        sums = lax.psum(part, "fit")
        start_amps = [lax.all_gather(sums, ("orb", "sub"), axis=0, tiled=False)]

    (right_late,) = gate((right,), part)
    left_below = shifted(gate((left,), part)[0], "orb", 1)
    (left_late,) = gate((left_below,), start_amps[0])
    right_other, left_below_other = [
        swapped(value, "sub") for value in (right_late, left_late)
    ]

    args = (
        *lists, neighbours.T, occ_energy, *start_amps, *packs,
        pno_coefficients, c_other, mp, mp_other, mp_below, mp_below_other,
        left, left_other, left_below, left_below_other, right, right_other,
    )
    square = (z.total, n, n)
    amplitudes, gradient = call(
        functools.partial(final_kernel, z),
        [(pairs, n * n), (z.orbitals, half, fits)],
        [smem] * 5 + [hbm] * (12 + len(start_amps) + len(packs)),
        args,
        [
            scratch(len(start_amps), *start_amps[0].shape),
            scratch(pairs, n * n),
            scratch(len(packs), *packs[0].shape),
            scratch(z.total, n, wide, kind=bf16),
            scratch(z.total, n, wide, kind=bf16),
            scratch(*square),
            scratch(z.total, EXTRA, wide),
            scratch(z.total if small(z) else 1, z.links // 2, n, 2 * n),
            scratch(own, n, half),
            scratch(2 * own, n, half),
            scratch(3 * own, n, fits),
            scratch(z.orbitals, half, fits),
            scratch(pairs, n, n),
            scratch(*square),
        ]
        + [scratch(*square, kind=bf16)] * 4
        + [scratch(z.orbitals * half, 3 * own * n, kind=bf16)] * 2
        + [pltpu.SemaphoreType.DMA((19 + -(-fits // 256),))],
        limit=44,
        out_specs=[hbm, hbm],
    )
    return (amplitudes, gradient)


def solution(mesh):
    in_specs = (
        P(("groups", "orb"), None, "fit"),
        P(("groups", "orb", "sub"), None, None),
        P(("groups", "orb", "sub"), None),
        P("groups"),
        P("groups"),
        P("groups"),
        P("groups", None),
        P(("groups", "orb", "sub"), None),
        P(("groups", "orb", "sub"), None, None),
        P(("groups", "orb", "sub"), None),
        P("groups"),
    )
    out_specs = (P(("groups", "orb", "sub"), None), P(("groups", "orb"), "sub", "fit"))
    return jax.shard_map(body, mesh=mesh, in_specs=in_specs, out_specs=out_specs, check_vma=False)
```

```python
import functools

import jax
import jax.numpy as jnp
from jax import lax
from jax.experimental import pallas as pl
from jax.experimental.pallas import tpu as pltpu
from jax.sharding import PartitionSpec as P

ITERS = 2
SMALL = 4
MIB = 1 << 20
EXTRA = 8

high = lax.Precision.HIGH
BRIEF = pl.CostEstimate(flops=1, bytes_accessed=1, transcendentals=0)
smem = pl.BlockSpec(memory_space=pltpu.SMEM)
vmem = pl.BlockSpec(memory_space=pltpu.VMEM)


def mm(a, b, contract=((1,), (0,))):
    return lax.dot_general(
        a, b, (contract, ((), ())), precision=high, preferred_element_type=jnp.float32
    )


def shifted(value, axis, steps):
    count = lax.axis_size(axis)
    initial, last = (max(0, -steps), min(count, count - steps))
    return lax.ppermute(value, axis, [(source, source + steps) for source in range(initial, last)])


def swapped(value, axis):
    return lax.ppermute(value, axis, [(0, 1), (1, 0)])


def f32(flag):
    return flag.astype(jnp.float32)


class Sizes:
    def __init__(self, blocks, pno_coefficients, couplings):
        self.orbitals, self.paos, self.fits = blocks.shape
        self.pairs, self.pnos = pno_coefficients.shape[:2]
        self.links = couplings.shape[1]
        self.subs = lax.axis_size("sub")
        self.owners = lax.axis_size("orb")
        self.fit_count = lax.axis_size("fit")
        self.own = self.pairs * self.subs
        self.total = self.own * self.owners


anywhere = pl.BlockSpec(memory_space=pl.ANY)
held_out = pl.BlockSpec(memory_space=pltpu.HBM)


def call(kernel, outs, ins, args, scratch=(), limit=16, out_specs=None, cost=None):
    return pl.pallas_call(
        kernel,
        out_shape=[jax.ShapeDtypeStruct(shape, jnp.float32) for shape in outs],
        in_specs=ins,
        out_specs=out_specs or [vmem] * len(outs),
        scratch_shapes=list(scratch),
        cost_estimate=cost,
        compiler_params=pltpu.CompilerParams(vmem_limit_bytes=limit and limit * MIB),
    )(*args)


def started(sources, targets, sems, base=0):
    copies = [
        pltpu.make_async_copy(source, target, sems.at[base + index])
        for index, (source, target) in enumerate(zip(sources, targets))
    ]
    for copy in copies:
        copy.start()
    return copies


def wait(copies):
    for copy in copies:
        copy.wait()


def side_start(z, owner, sub, side):
    return owner * z.own + (sub if side == 0 else 1 - sub) * z.pairs


def scale_of(z, pair, level, first, second, ranks, occupied):
    n = z.pnos
    row_ids = lax.broadcasted_iota(jnp.int32, (n, n), 0)
    column_ids = lax.broadcasted_iota(jnp.int32, (n, n), 1)
    level = level * jnp.ones((n, 1), jnp.float32)
    rank = ranks[pair]
    kept = f32((row_ids < rank) & (column_ids < rank))
    return kept / (level + level.T - (occupied[first[pair]] + occupied[second[pair]]))


def split(value):
    high_part = value.astype(jnp.bfloat16)
    return high_part, (value - high_part.astype(jnp.float32)).astype(jnp.bfloat16)


def mm3(a, b, contract=((1,), (0,))):
    def one(x, y):
        return lax.dot_general(x, y, (contract, ((), ())), preferred_element_type=jnp.float32)

    return one(a[0], b[0]) + (one(a[0], b[1]) + one(a[1], b[0]))


def small(z):
    return z.owners <= SMALL and z.pairs == z.fit_count == 2


def each_pair(z, action):
    if z.owners <= SMALL:
        for pair in range(z.total):
            action(pair)
    else:
        @pl.loop(0, z.total)
        def _(pair):
            action(pair)


def mapped_kernel(z, c_in, map_in, e_in, coupling_in, mp_ref, c_ref, map_ref, e_ref, coupling,
                  sems):
    n = z.pnos
    copies = started(
        [c_in, map_in, e_in, coupling_in], [c_ref, map_ref, e_ref, coupling], sems
    )
    wait(copies)
    rows = lax.broadcasted_iota(jnp.int32, (z.paos, z.paos), 0)
    lane_link = lax.broadcasted_iota(jnp.int32, (1, z.links * n), 1) // n
    for p in range(z.pairs):
        select = f32(map_ref[p : p + 1, :] == rows).astype(jnp.bfloat16)
        c_high, c_low = split(c_ref[p])
        mp_ref[p, :n, :] = lax.dot_general(
            c_high, select, (((1,), (1,)), ((), ())), preferred_element_type=jnp.float32
        ) + lax.dot_general(
            c_low, select, (((1,), (1,)), ((), ())), preferred_element_type=jnp.float32
        )
        mp_ref[p, n:, :] = jnp.zeros((EXTRA, z.paos), jnp.float32)
        mp_ref[p, n : n + 1, :n] = e_ref[p : p + 1, :]
        spread = jnp.zeros((1, z.links * n), jnp.float32)
        for k in range(z.links):
            spread = jnp.where(lane_link == k, coupling[p : p + 1, k : k + 1], spread)
        mp_ref[p, n + 1 : n + 2, :] = spread


def pack_kernel(z, s_in, mp_in, pack_ref, s_ref, mp_ref, sems):
    n = z.pnos
    line = 2 * n
    base = z.links * n // 2
    wait(started([s_in, mp_in.at[:, pl.ds(n, EXTRA), :]], [s_ref, mp_ref], sems))
    for slot in range(1 if small(z) else z.pairs):
        p = lax.axis_index("fit") if small(z) else slot
        for r in range(n // 2):
            lines = s_ref[p, :, r * line : (r + 1) * line]
            for k in range(z.links):
                row = k * n // 2 + r
                pack_ref[slot, row : row + 1, :] = lines[k : k + 1, :]
        pack_ref[slot, base:, :] = jnp.zeros((EXTRA, line), jnp.float32)
        pack_ref[slot, base : base + 1, :] = mp_ref[p, 0:1, :line]
        for k in range(z.links // 2):
            pack_ref[slot, base + 1 + k : base + 2 + k, :] = mp_ref[
                p, 1:2, k * line : (k + 1) * line
            ]
    if small(z):
        for copy in range(1, z.owners):
            pack_ref[copy] = pack_ref[0]


def below_kernel(z, second, mp_below, b_ref, touched, right_ref):
    owner, sub = lax.axis_index("orb"), lax.axis_index("sub")
    start = side_start(z, jnp.maximum(owner - 1, 0), sub, 0)
    for p in range(z.pairs):
        j = second[start + p] - owner * z.orbitals
        held = jnp.where(j >= 0, 1.0, 0.0)
        mapped = mp_below[p, : z.pnos, :] * held
        right_ref[p] = mm(mapped, b_ref[jnp.clip(j, 0, z.orbitals - 1)])


def early_kernel(z, second, b_ref, out_ref):
    out_ref[...] = b_ref[0, :EXTRA, :128] + second[0].astype(jnp.float32)


def local_kernel(z, first, second, c_ref, mp_ref, b_ref, left_ref, right_ref):
    owner, sub = lax.axis_index("orb"), lax.axis_index("sub")
    start = side_start(z, owner, sub, 0)
    base = owner * z.orbitals
    for p in range(z.pairs):
        left_ref[p] = mm(c_ref[p], b_ref[first[start + p] - base])
        j = second[start + p] - base
        local = jnp.where(j < z.orbitals, 1.0, 0.0)
        right_ref[p] = mm(
            mp_ref[p, : z.pnos, :] * local, b_ref[jnp.minimum(j, z.orbitals - 1)]
        )


def sums_kernel(z, first, second, ranks, occupied, mp_ref, left_ref, here_ref, down_ref, *refs):
    sums_ref, right_ref = refs[-2:]
    owner, sub = lax.axis_index("orb"), lax.axis_index("sub")
    start = side_start(z, owner, sub, 0)
    n = z.pnos
    for p in range(z.pairs):
        right = here_ref[p] + down_ref[p]
        right_ref[p] = right
        scale = scale_of(
            z, start + p, mp_ref[p, n : n + 1, :n], first, second, ranks, occupied
        )
        part = mm(left_ref[p], right, ((1,), (1,)))
        sums_ref[:, p * n : (p + 1) * n] = -part * scale


def unpack(z, pair, block, rows, slot, s_high, s_low, scale_ref, coupling_ref, lists):
    n = z.pnos
    for k in range(0, z.links, 2):
        two = [block(k * n // 2, n // 2), block((k + 1) * n // 2, n // 2)]
        for odd in range(2):
            rows[slot, k // 2, pl.ds(odd, n // 2, 2), :] = jnp.concatenate(
                [part[:, odd * n : (odd + 1) * n] for part in two], axis=1
            )
    s = jnp.concatenate([rows[slot, k] for k in range(z.links // 2)], axis=1)
    s_high[pair], s_low[pair] = split(s)
    extra = block(z.links * n // 2, EXTRA)
    scale_ref[pair] = scale_of(z, pair, extra[0:1, :n], *lists)
    coupling_ref[pair, 0:1, :] = jnp.concatenate(
        [extra[1 + k : 2 + k, :] for k in range(z.links // 2)], axis=1
    )


def coupled_of(z, pair, near, s, coupling, amps_high, amps_low):
    n = z.pnos
    parts = []
    for k in range(z.links):
        row = near[k, pair]
        lanes = slice(k * n, (k + 1) * n)
        parts.append(mm3((s[0][:, lanes], s[1][:, lanes]), (amps_high[row], amps_low[row])))
    return split(jnp.concatenate(parts, axis=1) * coupling)


def final_kernel(z, first, second, ranks, near, occupied, *refs):
    start_count, pack_count = (2, 4) if small(z) else (1, 1)
    starts_in = refs[:start_count]
    pack_in = refs[start_count : start_count + pack_count]
    (c_in, c_other, mp_in, mp_other, mp_below, mp_below_other, left_in, left_other, left_below,
     left_below_other, right_in, right_other) = refs[start_count + pack_count :][:12]
    (amp_out, grad_out, starts, amp_ref, packs, s_high, s_low, scale_ref, coupling_ref, s_rows, c_ref, m_ref, rhs,
     grad, flat, amps, amps_high, amps_low, next_high, next_low, rows_high, rows_low, sems) = refs[start_count + pack_count + 12 :]
    owner, sub = lax.axis_index("orb"), lax.axis_index("sub")
    fit = lax.axis_index("fit")
    n, pairs, own = z.pnos, z.pairs, z.own
    half = z.paos // z.subs
    at = pl.ds(pl.multiple_of(sub * half, half), half)
    lists = (first, second, ranks, occupied)

    def quarters(ref, base=0):
        return [ref.at[pl.ds(base + i * pairs, pairs)] for i in range(4)]

    start_copies = started(starts_in, [starts.at[i] for i in range(start_count)], sems, 16)
    pack_copies = started(pack_in, [packs.at[i] for i in range(pack_count)], sems)
    small_copies = started(
        [c_in.at[:, :, at], c_other.at[:, :, at]]
        + [ref.at[:, pl.ds(0, n), at] for ref in (mp_in, mp_other, mp_below, mp_below_other)],
        [c_ref.at[pl.ds(0, pairs)], c_ref.at[pl.ds(pairs, pairs)]] + quarters(m_ref),
        sems, 4,
    )
    large_copies = started(
        [right_in, right_other, left_in, left_other, left_below, left_below_other],
        [rhs.at[pl.ds(0, pairs)], rhs.at[pl.ds(pairs, pairs)]] + quarters(rhs, own),
        sems, 10,
    )
    wait(start_copies)

    def begin(pair, value):
        amps[pair] = value
        amps_high[pair], amps_low[pair] = split(value)

    if small(z):
        for index, side in enumerate((sub, 1 - sub)):
            for who in range(z.owners):
                for p in range(pairs):
                    begin(
                        who * own + side * pairs + p,
                        starts[index, who, :, p * n : (p + 1) * n],
                    )
    else:
        @pl.loop(0, z.owners * z.subs)
        def _(device):
            for p in range(pairs):
                begin(device * pairs + p, starts[0, device, :, p * n : (p + 1) * n])

    wait(pack_copies)
    if small(z):
        for index in range(pack_count):
            side = sub if index < 2 else 1 - sub
            which = fit if index % 2 == 0 else 1 - fit
            for who in range(z.owners):
                unpack(
                    z, who * own + side * pairs + which,
                    lambda start, size: packs[index, who, start : start + size, :], s_rows,
                    index * z.owners + who, s_high, s_low, scale_ref, coupling_ref, lists,
                )
    else:
        @pl.loop(0, z.total)
        def _(pair):
            unpack(
                z, pair, lambda start, size: packs[0, pair, pl.ds(start, size), :], s_rows, 0,
                s_high, s_low, scale_ref, coupling_ref, lists,
            )

    def s_of(pair):
        return s_high[pair], s_low[pair]

    def swept(pair, high_amps, low_amps):
        s = s_of(pair)
        inner = coupled_of(
            z, pair, near, s, coupling_ref[pair, 0:1, :], high_amps, low_amps
        )
        return amps[pair] + mm3(inner, s, ((1,), (1,))) * scale_ref[pair]

    if z.owners <= SMALL:
        group = 2 * own
        for base in range(0, z.total, group):
            pair_list = range(base, min(base + group, z.total))
            inner = [
                coupled_of(
                    z, pair, near, s_of(pair), coupling_ref[pair, 0:1, :], amps_high, amps_low
                )
                for pair in pair_list
            ]
            for value, pair in zip(inner, pair_list):
                coupled = mm3(value, s_of(pair), ((1,), (1,)))
                next_high[pair], next_low[pair] = split(amps[pair] + coupled * scale_ref[pair])
    else:
        @pl.loop(0, z.total)
        def _(pair):
            next_high[pair], next_low[pair] = split(swept(pair, amps_high, amps_low))

    pair_list = [
        side_start(z, who, sub, side) + p
        for who in (owner, jnp.maximum(owner - 1, 0))
        for side in range(z.subs)
        for p in range(pairs)
    ]
    inner = [
        coupled_of(z, pair, near, s_of(pair), coupling_ref[pair, 0:1, :], next_high, next_low)
        for pair in pair_list
    ]
    found = [
        amps[pair] + mm3(value, s_of(pair), ((1,), (1,))) * scale_ref[pair]
        for value, pair in zip(inner, pair_list)
    ]
    turned = [value.T for value in found]
    wait(small_copies)
    weights = [split(2.0 * a - b) for a, b in zip(found, turned)]
    weights_turned = [split(2.0 * b - a) for a, b in zip(found[:own], turned[:own])]
    terms = (
        [mm3(w, split(c_ref[i])) for i, w in enumerate(weights_turned)]
        + [mm3(w, split(m_ref[i])) for i, w in enumerate(weights)]
    )
    orbital_list = (
        [first[pair] - owner * z.orbitals for pair in pair_list[:own]]
        + [second[pair] - owner * z.orbitals for pair in pair_list]
    )
    for index in range(0, 3 * own, 2):
        for o in range(z.orbitals):
            block = jnp.concatenate(
                [
                    jnp.where(orbital_list[i] == o, terms[i], 0.0) for i in (index, index + 1)
                ]
            ).T
            place = (slice(o * half, (o + 1) * half), slice(index * n, (index + 2) * n))
            rows_high[place], rows_low[place] = split(block)

    for p in range(pairs):
        flat[p] = found[p]
        even = flat[p, pl.ds(0, n // 2, 2), :]
        odd = flat[p, pl.ds(1, n // 2, 2), :]
        lines = jnp.concatenate([even, odd], axis=1)
        for r in range(n // 2):
            amp_ref[p : p + 1, r * 2 * n : (r + 1) * 2 * n] = lines[r : r + 1, :]
    copies = started([amp_ref], [amp_out], sems, 18)

    wait(large_copies)
    step = 256
    rows = (rows_high[...], rows_low[...])
    for index, start in enumerate(range(0, z.fits, step)):
        factor = rhs[:, :, start : start + step].reshape(3 * own * n, step)
        grad[:, :, start : start + step] = mm3(rows, split(factor)).reshape(
            z.orbitals, half, step
        )
        window = pl.ds(start, step)
        copies += started(
            [grad.at[:, :, window]], [grad_out.at[:, :, window]], sems, 19 + index
        )
    wait(copies)


def gate(values, *after):
    return lax.optimization_barrier((tuple(values), after))[0]


def body(
    blocks,
    pno_coefficients,
    domain_map,
    pair_first,
    pair_second,
    pno_ranks,
    neighbours,
    couplings,
    intersections,
    pno_energy,
    occ_energy,
):
    z = Sizes(blocks, pno_coefficients, couplings)
    n, pairs, own, fits = z.pnos, z.pairs, z.own, z.fits
    half = z.paos // z.subs
    wide = z.links * n
    hbm = held_out
    bf16 = jnp.bfloat16
    more = 0 if z.owners <= SMALL else z.owners

    def scratch(*shape, kind=jnp.float32):
        return pltpu.VMEM(shape, kind)

    pack_shape = (z.owners if small(z) else pairs, z.links * n // 2 + EXTRA, 2 * n)
    (mp,) = call(
        functools.partial(mapped_kernel, z),
        [(pairs, n + EXTRA, z.paos)],
        [hbm] * 4,
        (pno_coefficients, domain_map, pno_energy, couplings),
        [
            scratch(*pno_coefficients.shape),
            pltpu.VMEM(domain_map.shape, jnp.int32),
            scratch(*pno_energy.shape),
            scratch(*couplings.shape),
            pltpu.SemaphoreType.DMA((4,)),
        ],
        limit=None,
    )
    mp_below = shifted(mp, "orb", 1)
    (pack,) = call(
        functools.partial(pack_kernel, z),
        [pack_shape],
        [hbm] * 2,
        (intersections, mp),
        [
            scratch(*intersections.shape),
            scratch(pairs, EXTRA, z.paos),
            pltpu.SemaphoreType.DMA((2,)),
        ],
        limit=None,
    )
    if small(z):
        packs = [lax.all_to_all(pack, "orb", 0, 0)]
    else:
        packs = [lax.all_gather(pack, ("orb", "sub"), axis=0, tiled=True)]
    (touched,) = call(
        functools.partial(early_kernel, z),
        [(EXTRA, 128)],
        [smem, vmem],
        (gate((pair_second,), mp)[0], blocks),
        limit=8,
    )
    (right_below,) = call(
        functools.partial(below_kernel, z),
        [(pairs, n, fits)],
        [smem, vmem, vmem, vmem],
        (pair_second, gate((mp_below,), pack)[0], blocks, touched),
        limit=8,
    )
    down = shifted(right_below, "orb", -1)
    mp_late, coefficients, mp_below_late = gate((mp, pno_coefficients, mp_below), right_below)
    mp_below_other = swapped(mp_below_late, "sub")
    left, right_here = call(
        functools.partial(local_kernel, z),
        [(pairs, n, fits), (pairs, n, fits)],
        [smem, smem, vmem, vmem, vmem],
        (pair_first, pair_second, coefficients, mp_late, blocks),
        limit=8,
        cost=BRIEF,
    )
    mp_other = swapped(gate((mp,), right_here)[0], "sub")
    left_other = swapped(left, "sub")
    c_other = swapped(gate((coefficients,), right_here)[0], "sub")

    lists = (pair_first, pair_second, pno_ranks)
    (down,) = gate((down,), mp_other, left_other, c_other, mp_below_other)
    part, right = call(
        functools.partial(sums_kernel, z),
        [(n, pairs * n), (pairs, n, fits)],
        [smem] * 4 + [vmem] * 4,
        (*lists, occ_energy, mp, left, right_here, down),
        limit=8,
    )
    if small(z):
        packs.append(None)
        packs.append(swapped(gate(packs[:1], part)[0], "sub"))
        sums = part + swapped(part, "fit")
        packs[1] = swapped(gate(packs[:1], part)[0], "fit")
        start_amps = [
            lax.all_to_all(jnp.broadcast_to(sums[None], (z.owners, *sums.shape)), "orb", 0, 0)
        ]
        start_amps.append(swapped(start_amps[0], "sub"))
        packs.append(swapped(gate(packs[1:2], start_amps[0])[0], "sub"))
    else:
        sums = lax.psum(part, "fit")
        start_amps = [lax.all_gather(sums, ("orb", "sub"), axis=0, tiled=False)]

    (right_late,) = gate((right,), part)
    left_below = shifted(gate((left,), part)[0], "orb", 1)
    (left_late,) = gate((left_below,), start_amps[0])
    right_other, left_below_other = [
        swapped(value, "sub") for value in (right_late, left_late)
    ]

    args = (
        *lists, neighbours.T, occ_energy, *start_amps, *packs,
        pno_coefficients, c_other, mp, mp_other, mp_below, mp_below_other,
        left, left_other, left_below, left_below_other, right, right_other,
    )
    square = (z.total, n, n)
    amplitudes, gradient = call(
        functools.partial(final_kernel, z),
        [(pairs, n * n), (z.orbitals, half, fits)],
        [smem] * 5 + [hbm] * (12 + len(start_amps) + len(packs)),
        args,
        [
            scratch(len(start_amps), *start_amps[0].shape),
            scratch(pairs, n * n),
            scratch(len(packs), *packs[0].shape),
            scratch(z.total, n, wide, kind=bf16),
            scratch(z.total, n, wide, kind=bf16),
            scratch(*square),
            scratch(z.total, EXTRA, wide),
            scratch(z.total if small(z) else 1, z.links // 2, n, 2 * n),
            scratch(own, n, half),
            scratch(2 * own, n, half),
            scratch(3 * own, n, fits),
            scratch(z.orbitals, half, fits),
            scratch(pairs, n, n),
            scratch(*square),
        ]
        + [scratch(*square, kind=bf16)] * 4
        + [scratch(z.orbitals * half, 3 * own * n, kind=bf16)] * 2
        + [pltpu.SemaphoreType.DMA((19 + -(-fits // 256),))],
        limit=44,
        out_specs=[hbm, hbm],
    )
    return (amplitudes, gradient)


def solution(mesh):
    in_specs = (
        P(("groups", "orb"), None, "fit"),
        P(("groups", "orb", "sub"), None, None),
        P(("groups", "orb", "sub"), None),
        P("groups"),
        P("groups"),
        P("groups"),
        P("groups", None),
        P(("groups", "orb", "sub"), None),
        P(("groups", "orb", "sub"), None, None),
        P(("groups", "orb", "sub"), None),
        P("groups"),
    )
    out_specs = (P(("groups", "orb", "sub"), None), P(("groups", "orb"), "sub", "fit"))
    return jax.shard_map(body, mesh=mesh, in_specs=in_specs, out_specs=out_specs, check_vma=False)
```
